32 devices in a mesh: ctx: 4 (over x, core), fsdp: 8 (over z, y).
Axes of the slice: x: 2, y: 2, z: 4, core: 2. Of those that a mesh axis runs over, the one named last changes fastest.
Arguments:
- inputs: bfloat16 [48, 512, 1024], P('fsdp', 'ctx'), may hold values from -6 to 6
- lengths: int32 [48], P('fsdp'), may hold values from 128 to 512, as said below
- cotangent: bfloat16 [48, 512, 1024], P('fsdp', 'ctx'), may hold values from -6 to 6
- query_weight: bfloat16 [1024, 1024], P('fsdp'), may hold values from -0.1875 to 0.1875
- key_weight: bfloat16 [1024, 1024], P('fsdp'), may hold values from -0.1875 to 0.1875
- value_weight: bfloat16 [1024, 1024], P('fsdp'), may hold values from -0.1875 to 0.1875
- out_weight: bfloat16 [1024, 1024], P('fsdp'), may hold values from -3 to 3
- inner_weight: bfloat16 [1024, 4096], P('fsdp'), may hold values from -0.1875 to 0.1875
- outer_weight: bfloat16 [4096, 1024], P('fsdp'), may hold values from -0.09375 to 0.09375
- query_bias: bfloat16 [1024], P('fsdp'), may hold values from -3 to 3
- value_bias: bfloat16 [1024], P('fsdp'), may hold values from -3 to 3
- out_bias: bfloat16 [1024], P('fsdp'), may hold values from -3 to 3
- inner_bias: bfloat16 [4096], P('fsdp'), may hold values from -3 to 3
- outer_bias: bfloat16 [1024], P('fsdp'), may hold values from -3 to 3
- first_gain: bfloat16 [1024], P('fsdp'), may hold values from 0.5 to 1.5
- first_shift: bfloat16 [1024], P('fsdp'), may hold values from -3 to 3
- second_gain: bfloat16 [1024], P('fsdp'), may hold values from 0.5 to 1.5
- second_shift: bfloat16 [1024], P('fsdp'), may hold values from -3 to 3
Outputs:
- layer_out: bfloat16 [48, 512, 1024], P('fsdp', 'ctx')
- input_grad: float32 [48, 512, 1024], P('fsdp', 'ctx')
- query_weight_grad: float32 [1024, 1024], P('fsdp')
- key_weight_grad: float32 [1024, 1024], P('fsdp')
- value_weight_grad: float32 [1024, 1024], P('fsdp')
- out_weight_grad: float32 [1024, 1024], P('fsdp')
- inner_weight_grad: float32 [1024, 4096], P('fsdp')
- outer_weight_grad: float32 [4096, 1024], P('fsdp')
- query_bias_grad: float32 [1024], P('fsdp')
- value_bias_gradient: float32 [1024], P('fsdp')
- out_bias_grad: float32 [1024], P('fsdp')
- inner_bias_grad: float32 [4096], P('fsdp')
- outer_bias_grad: float32 [1024], P('fsdp')
- first_gain_grad: float32 [1024], P('fsdp')
- first_shift_grad: float32 [1024], P('fsdp')
- second_gain_grad: float32 [1024], P('fsdp')
- second_shift_grad: float32 [1024], P('fsdp')
The draws below stay inside these ranges and needn't reach their ends.
Inputs may be any that keep to these rules, and one draw needn't show every extreme that they name: Each sequence's valid slots are its first lengths[s]; some sequence is full and some holds 128.
All inputs are finite; a program needn't handle non-finite values.
Results may differ from the reference program's by a relative error of at most 0.02.
Values may be sent and summed in bfloat16 or wider, within the bound.
A program may use at most 256 MiB of HBM per device.

```python
import jax
import jax.numpy as jnp
from jax import lax

D = 1024
HEADS = 16
HD = 64
FF = 4096
L = 512
SEQ_DEV = 6
SEQS = 48
N_FSDP = 8


def draw_lengths(key, part):
    pick_key, order_key = jax.random.split(key)
    drawn = jax.random.randint(pick_key, (SEQS,), L // 4, L + 1)
    ranks = jax.random.permutation(order_key, SEQS)
    drawn = jnp.where(ranks == 0, L, drawn)
    drawn = jnp.where(ranks == 1, L // 4, drawn)
    return drawn.astype(jnp.int32)


def steps_of(own_key, dims, pieces, low, largest):
    def one(axis_at, blocks):
        heights = jax.random.uniform(jax.random.fold_in(jax.random.fold_in(own_key, 6), axis_at), (blocks,), jnp.float32, low / len(pieces), largest / len(pieces))
        return jnp.repeat(jnp.exp(heights), dims[axis_at] // blocks).reshape((-1,) + (1,) * (len(dims) - axis_at - 1))

    level = one(*pieces[0])
    for cut in pieces[1:]:
        level = level * one(*cut)
    return level


def normal_values(stream_key, dims, scale, limit, cuts=(), held_as=jnp.bfloat16):
    entries = scale * jax.random.normal(stream_key, dims, jnp.float32)
    if cuts:
        entries = entries * steps_of(stream_key, dims, cuts, -0.22, 0.18)
    return jnp.clip(entries, -limit, limit).astype(held_as)


def setup_inputs(seed: int = 0) -> dict:
    seeds = jax.random.split(jax.random.key(seed), 19)
    inputs = normal_values(seeds[0], (SEQS, L, D), 1.0, 6.0, ((0, 8), (1, 4)))
    lengths = draw_lengths(jax.random.fold_in(seeds[18], 71), 0)
    cotangent = normal_values(seeds[2], (SEQS, L, D), 1.0, 6.0, ((0, 8), (1, 4)))
    query_weight = normal_values(seeds[3], (D, D), D ** -0.5, 0.1875, ((0, 8),))
    key_weight = normal_values(seeds[4], (D, D), D ** -0.5, 0.1875, ((0, 8),))
    value_weight = normal_values(seeds[5], (D, D), D ** -0.5, 0.1875, ((0, 8),))
    out_weight = normal_values(seeds[6], (D, D), (max(D // 256, 1)) ** -0.5, 3.0, ((0, 8),))
    inner_weight = normal_values(seeds[7], (D, FF), D ** -0.5, 0.1875, ((0, 8),))
    outer_weight = normal_values(seeds[8], (FF, D), FF ** -0.5, 0.09375, ((0, 8),))
    query_bias = normal_values(seeds[9], (D,), 0.5, 3.0, ((0, 8),))
    value_bias = normal_values(seeds[10], (D,), 0.5, 3.0, ((0, 8),))
    out_bias = normal_values(seeds[11], (D,), 0.5, 3.0, ((0, 8),))
    inner_bias = normal_values(seeds[12], (FF,), 0.5, 3.0, ((0, 8),))
    outer_bias = normal_values(seeds[13], (D,), 0.5, 3.0, ((0, 8),))
    first_gain = jnp.clip(1.0 + 0.1 * jax.random.normal(seeds[14], (D,), jnp.float32), 0.5, 1.5).astype(jnp.bfloat16)
    first_shift = normal_values(seeds[15], (D,), 0.5, 3.0, ((0, 8),))
    second_gain = jnp.clip(1.0 + 0.1 * jax.random.normal(seeds[16], (D,), jnp.float32), 0.5, 1.5).astype(jnp.bfloat16)
    second_shift = normal_values(seeds[17], (D,), 0.5, 3.0, ((0, 8),))
    return {"inputs": inputs, "lengths": lengths, "cotangent": cotangent, "query_weight": query_weight, "key_weight": key_weight, "value_weight": value_weight, "out_weight": out_weight, "inner_weight": inner_weight, "outer_weight": outer_weight, "query_bias": query_bias, "value_bias": value_bias, "out_bias": out_bias, "inner_bias": inner_bias, "outer_bias": outer_bias, "first_gain": first_gain, "first_shift": first_shift, "second_gain": second_gain, "second_shift": second_shift}


NEGATIVE = -1e+30
EPSILON = 1e-05

@jax.custom_vjp
def low(v):
    return lax.optimization_barrier(v.astype(jnp.bfloat16)).astype(jnp.float32)

@jax.custom_vjp
def low_back(v):
    return v

def low_keep(v):
    return (low(v), None)

def low_pass(kept, grad):
    return (grad,)

def backward_keep_mask(v):
    return (v, None)

def back_low(kept, grad):
    return (low(grad),)
low.defvjp(low_keep, low_pass)
low_back.defvjp(backward_keep_mask, back_low)

def rounded_both(value):
    return low(low_back(value))

def matmul(first_factor_matrix, second_factor_matrix):
    return jnp.einsum('ygz,zq->ygq', first_factor_matrix, second_factor_matrix, precision=lax.Precision.HIGHEST)

def layer_norm(hidden, gain, shift):
    centre = hidden - lax.optimization_barrier(jnp.mean(hidden, -1, keepdims=True))
    spread = lax.optimization_barrier(jnp.mean(centre * centre, -1, keepdims=True))
    return centre * lax.rsqrt(spread + EPSILON) * gain + shift

def forward_pass(values_in, group_len, weights):
    query_w, key_w, value_w, out_w, inner_w, outer_w, query_b, payload_offset_entries, out_b, inner_b, outer_b, gain_one, shift_one, gain_two, shift_two = weights
    groups = values_in.shape[0]
    queries = rounded_both(matmul(values_in, query_w) + query_b)
    keys_all = rounded_both(matmul(values_in, key_w))
    values_all = rounded_both(matmul(values_in, value_w) + payload_offset_entries)
    query_four = queries.reshape(groups, L, HEADS, HD)
    key_four = keys_all.reshape(groups, L, HEADS, HD)
    value_four = values_all.reshape(groups, L, HEADS, HD)
    scores = HD ** (-0.5) * jnp.einsum('sqhd,skhd->shqk', query_four, key_four, precision=lax.Precision.HIGHEST)
    scores = low_back(scores)
    keep_keys = (jnp.arange(L)[None, :] < group_len[:, None])[:, None, None, :]
    scores = jnp.where(keep_keys, scores, NEGATIVE)
    row_top = lax.optimization_barrier(jnp.max(scores, -1, keepdims=True))
    exponent = jnp.exp(scores - row_top)
    attend = low(exponent / lax.optimization_barrier(jnp.sum(exponent, -1, keepdims=True)))
    context_rows = jnp.einsum('shqk,skhd->sqhd', attend, value_four, precision=lax.Precision.HIGHEST)
    context_rows = rounded_both(context_rows.reshape(groups, L, D))
    attn_out = low_back(matmul(context_rows, out_w) + out_b)
    standardized_activations = layer_norm(values_in + attn_out, gain_one, shift_one)
    inner_pre = low_back(matmul(low(standardized_activations), inner_w) + inner_b)
    activated = low(jax.nn.gelu(inner_pre, approximate=False))
    branch = low_back(matmul(activated, outer_w) + outer_b)
    return layer_norm(standardized_activations + branch, gain_two, shift_two)

def reference(inputs, lengths, cotangent, query_weight, key_weight, value_weight, out_weight, inner_weight, outer_weight, query_bias, value_bias, out_bias, inner_bias, outer_bias, first_gain, first_shift, second_gain, second_shift):
    params = tuple((weight.astype(jnp.float32) for weight in (query_weight, key_weight, value_weight, out_weight, inner_weight, outer_weight, query_bias, value_bias, out_bias, inner_bias, outer_bias, first_gain, first_shift, second_gain, second_shift)))
    stacked_in = inputs.astype(jnp.float32).reshape(N_FSDP, SEQ_DEV, L, D)
    stacked_cot = cotangent.astype(jnp.float32).reshape(N_FSDP, SEQ_DEV, L, D)
    stacked_len = lengths.reshape(N_FSDP, SEQ_DEV)

    def step(totals, item):
        group_in, group_cot, group_len = item
        valid = (jnp.arange(L)[None, :] < group_len[:, None]).astype(jnp.float32)[:, :, None]

        def forward_of(values_in, weights):
            return forward_pass(values_in, group_len, weights)
        result, pull = jax.vjp(forward_of, group_in, params)
        d_input, d_params = pull(group_cot * valid)
        totals = jax.tree.map(jnp.add, totals, d_params)
        return (totals, (result.astype(jnp.bfloat16), d_input))
    start = jax.tree.map(jnp.zeros_like, params)
    totals, (results, d_inputs) = lax.scan(step, start, (stacked_in, stacked_cot, stacked_len))
    return (results.reshape(SEQS, L, D), d_inputs.reshape(SEQS, L, D), totals[0], totals[1], totals[2], totals[3], totals[4], totals[5], totals[6], totals[7], totals[8], totals[9], totals[10], totals[11], totals[12], totals[13], totals[14])
```

```python
import functools

import jax
import jax.numpy as jnp
from jax import lax
from jax.experimental import pallas as pl
from jax.experimental.pallas import tpu as pltpu
from jax.sharding import PartitionSpec as P

HD = 64
EPSILON = 1e-05
BF = jnp.bfloat16
F32 = jnp.float32
ANY = pl.BlockSpec(memory_space=pl.ANY)
NT = (((1,), (1,)), ((), ()))
TN = (((0,), (0,)), ((), ()))
VMEM_LIMIT = 58 << 20


def dot(a, b):
    return jnp.dot(a, b, preferred_element_type=F32)


def dot_nt(a, b):
    return lax.dot_general(a, b, NT, preferred_element_type=F32)


def dot_tn(a, b):
    return lax.dot_general(a, b, TN, preferred_element_type=F32)


def params(**more):
    return pltpu.CompilerParams(vmem_limit_bytes=VMEM_LIMIT, **more)


def cost(flops, size, trans=0):
    return pl.CostEstimate(flops=int(flops), bytes_accessed=int(size), transcendentals=int(trans))


def qkv_kernel(n, ids, xm, xs, vec, *refs):
    pieces, (q, k, v, w), sem = refs[:n], refs[n : n + 4], refs[n + 4]
    step = pl.program_id(0)
    f = ids[1]
    rs = w.shape[1] // n

    def copies():
        out = []
        for i in range(n):
            at = pl.multiple_of((f ^ i) * rs, rs)
            for j in range(3):
                out.append(
                    pltpu.make_async_copy(
                        pieces[i].at[pl.ds(j * rs, rs)], w.at[j, pl.ds(at, rs)], sem.at[i * 3 + j]
                    )
                )
        return out

    @pl.when(step == 0)
    def _():
        todo = copies()
        for c in todo:
            c.start()
        for c in todo:
            c.wait()

    def do(x_ref):
        x = x_ref[...]
        q[0] = (dot(x, w[0]) + vec[0:1, :]).astype(BF)
        k[0] = dot(x, w[1]).astype(BF)
        v[0] = (dot(x, w[2]) + vec[1:2, :]).astype(BF)

    half = pl.num_programs(0) // 2

    @pl.when(step < half)
    def _():
        do(xm)

    @pl.when(step >= half)
    def _():
        do(xs)


def qkv_call(ids, xm, xs, vec, pieces):
    rows, width = xm.shape
    cols = pieces[0].shape[1]
    n = len(pieces)
    block = rows // 3
    grid_spec = pltpu.PrefetchScalarGridSpec(
        num_scalar_prefetch=1,
        grid=(6,),
        in_specs=[
            pl.BlockSpec((block, width), lambda i, s: (jnp.minimum(i, 2), 0)),
            pl.BlockSpec((block, width), lambda i, s: (jnp.maximum(i - 3, 0), 0)),
            pl.BlockSpec((8, cols), lambda i, s: (0, s[0] % 2)),
        ]
        + [ANY] * n,
        out_specs=[pl.BlockSpec((1, block, cols), lambda i, s: (i // 3, i % 3, 0))] * 3
        + [pl.BlockSpec((3, width, cols), lambda i, s: (0, 0, 0))],
        scratch_shapes=[pltpu.SemaphoreType.DMA((3 * n,))],
    )
    act = jax.ShapeDtypeStruct((2, rows, cols), BF)
    return pl.pallas_call(
        functools.partial(qkv_kernel, n),
        grid_spec=grid_spec,
        out_shape=[act, act, act, jax.ShapeDtypeStruct((3, width, cols), BF)],
        compiler_params=params(),
        cost_estimate=cost(2 * 2 * rows * width * cols * 3, 4 * rows * width + 12 * rows * cols),
        name="qkv",
    )(ids, xm, xs, vec, *pieces)


def lanes_of(shape, head):
    lane = lax.broadcasted_iota(jnp.int32, shape, 1)
    own = (lane < HD) if head == 0 else (lane >= HD)
    return lane, own, (HD if head == 0 else 0)


def split3(a):
    hi = a.astype(BF).astype(F32)
    mid = (a - hi).astype(BF).astype(F32)
    return hi, mid, a - hi - mid


def flat(ref):
    a = ref[...]
    return a.reshape(-1, a.shape[-1])


def attend_kernel(q_ref, k_ref, v_ref, mask_ref, cm_ref, cs_ref, lse_ref):
    q, k, v, mask = flat(q_ref), flat(k_ref), flat(v_ref), flat(mask_ref)
    out = []
    for head in range(2):
        lane, own, other = lanes_of(q.shape, head)
        qh = jnp.where(own, q * BF(HD**-0.5), jnp.where(lane == other, 1.0, 0.0).astype(BF))
        kh = jnp.where(own, k, mask)
        s = dot_nt(qh, kh)
        top = jnp.max(s, -1, keepdims=True)
        e = jnp.exp(s - top)
        total = jnp.sum(e, -1, keepdims=True)
        o = dot(e.astype(BF), v) * (1.0 / total)
        out.append((o, top + jnp.log(total), own))
    (o0, l0, own), (o1, l1, _) = out
    o = jnp.where(own, o0, o1).astype(BF)
    half = o.shape[0] // 2
    cm_ref[...] = o[:half].reshape(cm_ref.shape)
    cs_ref[...] = o[half:].reshape(cs_ref.shape)
    lse_ref[0] = jnp.where(own, l1, l0)


def attend_call(q, k, v, mask):
    slots, seqs, part, cols = q.shape
    pair = 2 * HD
    four = pl.BlockSpec((4, 1, part, pair), lambda s, h: (0, s, 0, h))
    two = pl.BlockSpec((2, 1, part, pair), lambda s, h: (0, s, 0, h))
    half = jax.ShapeDtypeStruct((2, seqs, part, cols), BF)
    full = slots * part
    return pl.pallas_call(
        attend_kernel,
        grid=(seqs, cols // pair),
        in_specs=[four, four, four, pl.BlockSpec((4, 1, part, pair), lambda s, h: (0, s, 0, 0))],
        out_specs=[two, two, pl.BlockSpec((1, full, pair), lambda s, h: (s, 0, h))],
        out_shape=[half, half, jax.ShapeDtypeStruct((seqs, full, cols), F32)],
        compiler_params=params(),
        cost_estimate=cost(
            4 * seqs * full * full * cols * 4, 14 * seqs * full * cols, seqs * full * full * cols // HD
        ),
        name="attend",
    )(q, k, v, mask)


def attend_back_kernel(
    q_ref, k_ref, v_ref, mask_ref, lse_ref, cm_ref, cs_ref, gm_ref, gs_ref, dq_ref, dk_ref, dv_ref
):
    q, k, v, mask = flat(q_ref), flat(k_ref), flat(v_ref), flat(mask_ref)
    lse = lse_ref[0]
    c = jnp.concatenate([flat(cm_ref), flat(cs_ref)], 0)
    g = jnp.concatenate([flat(gm_ref), flat(gs_ref)], 0)
    qs = q * BF(HD**-0.5)
    kt = k.T
    prod = c.astype(F32) * g.astype(F32)
    res = []
    for head in range(2):
        lane, own, o = lanes_of(q.shape, head)
        hi, mid, low = split3(-lse)
        extra = jnp.where(
            lane == o,
            1.0,
            jnp.where(
                lane == o + 1,
                hi,
                jnp.where(lane == o + 2, mid, jnp.where(lane == o + 3, low, 0.0)),
            ),
        ).astype(BF)
        qh = jnp.where(own, qs, extra)
        kh = jnp.where(own, k, jnp.where(lane == o, mask, BF(1)))
        p = jnp.exp(dot_nt(kh, qh))
        delta = jnp.sum(jnp.where(own, prod, 0.0), -1, keepdims=True)
        hi, mid, low = split3(-delta)
        extra = jnp.where(
            lane == o, hi, jnp.where(lane == o + 1, mid, jnp.where(lane == o + 2, low, 0.0))
        ).astype(BF)
        gh = jnp.where(own, g, extra)
        vh = jnp.where(own, v, BF(1))
        ds = (p * dot_nt(vh, gh)).astype(BF)
        dv = dot(p.astype(BF), g)
        dk = dot(ds, qs)
        dqt = dot(kt, ds)
        res.append((dv, dk, dqt, own))
    (dv0, dk0, dq0, own), (dv1, dk1, dq1, _) = res
    dv_ref[...] = jnp.where(own, dv0, dv1).astype(BF).reshape(dv_ref.shape)
    dk_ref[...] = jnp.where(own, dk0, dk1).astype(BF).reshape(dk_ref.shape)
    dqt = jnp.concatenate([dq0[:HD], dq1[HD:]], 0) * (HD**-0.5)
    dq_ref[...] = dqt.T.astype(BF).reshape(dq_ref.shape)


def attend_back_call(q, k, v, mask, lse, cm, cs, gm, gs):
    slots, seqs, part, cols = q.shape
    pair = 2 * HD
    four = pl.BlockSpec((4, 1, part, pair), lambda s, h: (0, s, 0, h))
    two = pl.BlockSpec((2, 1, part, pair), lambda s, h: (0, s, 0, h))
    full = slots * part
    out = jax.ShapeDtypeStruct(q.shape, BF)
    return pl.pallas_call(
        attend_back_kernel,
        grid=(seqs, cols // pair),
        in_specs=[
            four,
            four,
            four,
            pl.BlockSpec((4, 1, part, pair), lambda s, h: (0, s, 0, 0)),
            pl.BlockSpec((1, full, pair), lambda s, h: (s, 0, h)),
            two,
            two,
            two,
            two,
        ],
        out_specs=[four] * 3,
        out_shape=[out] * 3,
        compiler_params=params(),
        cost_estimate=cost(
            10 * seqs * full * full * cols * 4, 20 * seqs * full * cols, seqs * full * full * cols // HD
        ),
        name="attend_back",
    )(q, k, v, mask, lse, cm, cs, gm, gs)


def gelu_pair(u):
    e = jnp.exp(u * u * -0.5)
    t = 1.0 / (1.0 + (0.3275911 * 0.7071067811865476) * jnp.abs(u))
    poly = t * (
        0.254829592 * 0.5
        + t
        * (
            -0.284496736 * 0.5
            + t * (1.421413741 * 0.5 + t * (-1.453152027 * 0.5 + t * (1.061405429 * 0.5)))
        )
    )
    tail = poly * e
    cdf = jnp.where(u >= 0, 1.0 - tail, tail)
    ucdf = u * cdf
    return ucdf, cdf + u * (e * 0.3989422804014327)


def normalise(h):
    c = h - jnp.mean(h, -1, keepdims=True)
    r = lax.rsqrt(jnp.mean(c * c, -1, keepdims=True) + EPSILON)
    return c * r, r


def normalise_back(dyg, hat, r):
    return r * (
        dyg - jnp.mean(dyg, -1, keepdims=True) - hat * jnp.mean(dyg * hat, -1, keepdims=True)
    )


def ffn_kernel(n, ids, cm, cr, xm, cot, valid, vec, ib, *refs):
    pieces = refs[: 4 * n]
    lo, act, dout, dinn, nrm, dattn, dfirst, dco, dcs, acc = refs[4 * n : 4 * n + 10]
    wo, wi, wu, gp, sem = refs[4 * n + 10 :]
    width, ff = wi.shape
    core, f = ids[0] % 2, ids[1]
    step = pl.program_id(0)
    rs, ro = width // n, ff // n
    cq = ff // 4
    q_i, q_u, q_o = rs, ro // 4, rs // 4

    def copies(kind):
        out = []
        for e in range(4):
            qq = ids[0] ^ e
            for i in range(n):
                s = f ^ i
                ref = pieces[e * n + i]
                at = (kind * 4 + e) * n + i
                if kind == 0:
                    half = (s // (n // 2)) ^ core
                    to = half * (width // 2) + (s % (n // 2)) * rs + qq * q_o
                    src = ref.at[pl.ds(q_i + q_u, q_o)]
                    dst = wo.at[pl.ds(pl.multiple_of(to, q_o), q_o)]
                elif kind == 1:
                    src = ref.at[pl.ds(0, q_i)]
                    dst = wi.at[
                        pl.ds(pl.multiple_of(s * rs, rs), rs), pl.ds(pl.multiple_of(qq * cq, cq), cq)
                    ]
                else:
                    src = ref.at[pl.ds(q_i, q_u)]
                    dst = wu.at[pl.ds(pl.multiple_of(s * ro + qq * q_u, q_u), q_u)]
                out.append(pltpu.make_async_copy(src, dst, sem.at[at]))
        return out

    @pl.when(step == 0)
    def _():
        for kind in range(3):
            for c in copies(kind):
                c.start()
        acc[...] = jnp.zeros_like(acc)

    def arrived(kind):
        @pl.when(step == 0)
        def _():
            for c in copies(kind):
                c.wait()

    def add(row, value):
        acc[row : row + 1, :] += jnp.sum(value, 0, keepdims=True)

    arrived(0)
    hw = width // 2
    first = (
        xm[...].astype(F32) + (dot(cm[...], wo[:hw]) + dot(cr[...], wo[hw:])) + vec[2:3, :]
    )
    hat1, r1 = normalise(first)
    normed = hat1 * vec[4:5, :] + vec[5:6, :]
    low = normed.astype(BF)
    nrm[...] = low
    arrived(1)
    for j in range(4):
        cols = slice(j * cq, (j + 1) * cq)
        g, d = gelu_pair(dot(low, wi[:, cols]) + ib[:, cols])
        act[:, cols] = g.astype(BF)
        gp[:, cols] = d
    arrived(2)
    second = normed + (dot(act[...], wu[...]) + vec[3:4, :])
    hat2, r2 = normalise(second)
    lo[...] = (hat2 * vec[6:7, :] + vec[7:8, :]).astype(BF)
    og = cot[...].astype(F32) * valid[...]
    add(6, og * hat2)
    add(7, og)
    d2 = normalise_back(og * vec[6:7, :], hat2, r2)
    d2low = d2.astype(BF)
    dout[...] = d2low
    add(3, d2low.astype(F32))
    for j in range(4):
        cols = slice(j * cq, (j + 1) * cq)
        di = (dot_nt(d2low, wu[cols, :]) * gp[:, cols]).astype(BF)
        dinn[:, cols] = di
        add(8 + j, di.astype(F32))
    dn = d2 + dot_nt(dinn[...], wi[...])
    add(4, dn * hat1)
    add(5, dn)
    d1 = normalise_back(dn * vec[4:5, :], hat1, r1)
    dfirst[...] = d1
    d1low = d1.astype(BF)
    dattn[...] = d1low
    add(2, d1low.astype(F32))
    dc = dot_nt(d1low, wo[...]).astype(BF)
    dco[...] = dc[:, :hw]
    dcs[...] = dc[:, hw:]


def ffn_call(ids, cm, cr, xm, cot, valid, vec, ib, pieces):
    rows, width = xm.shape
    ff = ib.shape[1]
    n = len(pieces) // 4
    block = rows // 3
    hw = width // 2

    def by(cols):
        return pl.BlockSpec((block, cols), lambda i, s: (i, 0))

    def whole(a, b):
        return pl.BlockSpec((a, b), lambda i, s: (0, 0))

    grid_spec = pltpu.PrefetchScalarGridSpec(
        num_scalar_prefetch=1,
        grid=(3,),
        in_specs=[by(hw), by(hw), by(width), by(width), by(1), whole(8, width), whole(1, ff)]
        + [ANY] * (4 * n),
        out_specs=[
            by(width),
            by(ff),
            by(width),
            by(ff),
            by(width),
            by(width),
            by(width),
            by(hw),
            by(hw),
            whole(16, width),
        ],
        scratch_shapes=[
            pltpu.VMEM((width, width), BF),
            pltpu.VMEM((width, ff), BF),
            pltpu.VMEM((ff, width), BF),
            pltpu.VMEM((block, ff), F32),
            pltpu.SemaphoreType.DMA((12 * n,)),
        ],
    )

    def shape(cols, dtype=BF):
        return jax.ShapeDtypeStruct((rows, cols), dtype)

    return pl.pallas_call(
        functools.partial(ffn_kernel, n),
        grid_spec=grid_spec,
        out_shape=[
            shape(width),
            shape(ff),
            shape(width),
            shape(ff),
            shape(width),
            shape(width),
            shape(width, F32),
            shape(hw),
            shape(hw),
            jax.ShapeDtypeStruct((16, width), F32),
        ],
        compiler_params=params(),
        cost_estimate=cost(
            2 * rows * width * (2 * width + 4 * ff), 30 * rows * width + 2 * width * (2 * ff + width)
        ),
        name="ffn",
    )(ids, cm, cr, xm, cot, valid, vec, ib, *pieces)


def outer_grad_kernel(ids, act, dout, keep, send, tmp):
    tmp[...] = dot_tn(act[...], dout[...])
    size = keep.shape[3]
    for ec, ref in ((0, keep), (1, send)):
        for ex in range(2):
            at = pl.multiple_of((ids[0] ^ (2 * ex + ec)) * size, size)
            ref[ex, 0, 0] = tmp[pl.ds(at, size), :].astype(BF)


def outer_grad_call(ids, act, dout, n):
    rows, ff = act.shape
    width = dout.shape[1]
    ro = ff // n
    out = pl.BlockSpec((2, 1, 1, ro // 4, width), lambda i, s: (0, i % 2, i // 2, 0, 0))
    grid_spec = pltpu.PrefetchScalarGridSpec(
        num_scalar_prefetch=1,
        grid=(n,),
        in_specs=[
            pl.BlockSpec((rows, ro), lambda i, s: (0, s[1] ^ i)),
            pl.BlockSpec((rows, width), lambda i, s: (0, 0)),
        ],
        out_specs=[out, out],
        scratch_shapes=[pltpu.VMEM((ro, width), F32)],
    )
    shape = jax.ShapeDtypeStruct((2, 2, n // 2, ro // 4, width), BF)
    return pl.pallas_call(
        outer_grad_kernel,
        grid_spec=grid_spec,
        out_shape=[shape, shape],
        compiler_params=params(),
        cost_estimate=cost(2 * rows * ff * width, 2 * (rows * ff + rows * width + ff * width)),
        name="outer_grad",
    )(ids, act, dout)


def inner_grad_kernel(n, ids, nrm, dinn, keep, send, tmp):
    rs = nrm.shape[1] // n
    tmp[...] = dot_tn(nrm[...], dinn[...])

    def put(ref):
        for i in range(n):
            at = pl.multiple_of((ids[1] ^ i) * rs, rs)
            ref[0, i % 2, i // 2] = tmp[pl.ds(at, rs), :].astype(BF)

    @pl.when(pl.program_id(0) == 0)
    def _():
        put(send)

    @pl.when(pl.program_id(0) == 1)
    def _():
        put(keep)


def inner_grad_call(ids, nrm, dinn, n):
    rows, width = nrm.shape
    ff = dinn.shape[1]
    cq, rs = ff // 4, width // n
    block = (1, 2, n // 2, rs, cq)
    grid_spec = pltpu.PrefetchScalarGridSpec(
        num_scalar_prefetch=1,
        grid=(2, 2),
        in_specs=[
            pl.BlockSpec((rows, width), lambda a, ex, s: (0, 0)),
            pl.BlockSpec((rows, cq), lambda a, ex, s: (0, s[0] ^ (2 * ex + 1 - a))),
        ],
        out_specs=[
            pl.BlockSpec(block, lambda a, ex, s: (jnp.where(a == 1, ex, 0), 0, 0, 0, 0)),
            pl.BlockSpec(block, lambda a, ex, s: (jnp.where(a == 0, ex, 1), 0, 0, 0, 0)),
        ],
        scratch_shapes=[pltpu.VMEM((width, cq), F32)],
    )
    shape = jax.ShapeDtypeStruct((2, 2, n // 2, rs, cq), BF)
    return pl.pallas_call(
        functools.partial(inner_grad_kernel, n),
        grid_spec=grid_spec,
        out_shape=[shape, shape],
        compiler_params=params(),
        cost_estimate=cost(2 * rows * ff * width, 2 * (rows * ff + rows * width + ff * width)),
        name="inner_grad",
    )(ids, nrm, dinn)


def out_grad_kernel(n, ids, cm, cr, dattn, keep, send, tmp):
    width = tmp.shape[0]
    hw, rs = width // 2, width // n
    size = rs // 4
    g = dattn[...]
    tmp[:hw, :] = dot_tn(cm[...], g)
    tmp[hw:, :] = dot_tn(cr[...], g)
    for ec, ref in ((0, keep), (1, send)):
        for ex in range(2):
            for i in range(n):
                s = ids[1] ^ i
                half = (s // (n // 2)) ^ (ids[0] % 2)
                at = half * hw + (s % (n // 2)) * rs + (ids[0] ^ (2 * ex + ec)) * size
                ref[ex, i % 2, i // 2] = tmp[pl.ds(pl.multiple_of(at, size), size), :].astype(BF)


def out_grad_call(ids, cm, cr, dattn, n):
    rows, width = dattn.shape
    shape = jax.ShapeDtypeStruct((2, 2, n // 2, width // n // 4, width), BF)
    vm = pl.BlockSpec(memory_space=pltpu.VMEM)
    return pl.pallas_call(
        functools.partial(out_grad_kernel, n),
        in_specs=[pl.BlockSpec(memory_space=pltpu.SMEM), vm, vm, vm],
        out_specs=[vm, vm],
        out_shape=[shape, shape],
        scratch_shapes=[pltpu.VMEM((width, width), F32)],
        compiler_params=params(),
        cost_estimate=cost(2 * rows * width * width, 4 * rows * width + 2 * width * width),
        name="out_grad",
    )(ids, cm, cr, dattn)


def qkv_grad_kernel(n, ids, xm, xs, dm, ds, out, bias, tmp):
    tmp[...] = dot_tn(xm[...], dm[0]) + dot_tn(xs[...], ds[0])
    bias[...] = jnp.broadcast_to(
        jnp.sum(dm[0].astype(F32), 0, keepdims=True) + jnp.sum(ds[0].astype(F32), 0, keepdims=True),
        bias.shape,
    )
    rs = tmp.shape[0] // n
    for i in range(n):
        at = pl.multiple_of((ids[1] ^ i) * rs, rs)
        out[i % 2, i // 2] = tmp[pl.ds(at, rs), :].astype(BF)


def qkv_grad_call(ids, xm, xs, d, n):
    rows, width = xm.shape
    cols = d.shape[2]
    vm = pl.BlockSpec((rows, width), lambda i, s: (0, 0))
    shape = (2, n // 2, width // n, cols)
    grid_spec = pltpu.PrefetchScalarGridSpec(
        num_scalar_prefetch=1,
        grid=(1,),
        in_specs=[
            vm,
            vm,
            pl.BlockSpec((1, rows, cols), lambda i, s: (0, 0, 0)),
            pl.BlockSpec((1, rows, cols), lambda i, s: (1, 0, 0)),
        ],
        out_specs=[
            pl.BlockSpec(shape, lambda i, s: (0, 0, 0, 0)),
            pl.BlockSpec((8, cols), lambda i, s: (0, 0)),
        ],
        scratch_shapes=[pltpu.VMEM((width, cols), F32)],
    )
    return pl.pallas_call(
        functools.partial(qkv_grad_kernel, n),
        grid_spec=grid_spec,
        out_shape=[jax.ShapeDtypeStruct(shape, BF), jax.ShapeDtypeStruct((8, cols), F32)],
        compiler_params=params(),
        cost_estimate=cost(4 * rows * width * cols, 4 * rows * width + 4 * rows * cols),
        name="qkv_grad",
    )(ids, xm, xs, d, d)


def back_project_kernel(dq, dk, dv, w, out):
    out[...] = dot_nt(dq[0], w[0]) + dot_nt(dk[0], w[1]) + dot_nt(dv[0], w[2])


def back_project_call(which, dq, dk, dv, w):
    _, rows, cols = dq.shape
    width = w.shape[1]
    block = rows // 3
    one = pl.BlockSpec((1, block, cols), lambda i: (which, i, 0))
    return pl.pallas_call(
        back_project_kernel,
        grid=(3,),
        in_specs=[one, one, one, pl.BlockSpec((3, width, cols), lambda i: (0, 0, 0))],
        out_specs=pl.BlockSpec((block, width), lambda i: (i, 0)),
        out_shape=jax.ShapeDtypeStruct((rows, width), F32),
        compiler_params=params(),
        cost_estimate=cost(6 * rows * width * cols, 6 * rows * cols + 4 * rows * width + 6 * width * cols),
        name="back_project",
    )(dq, dk, dv, w)


def per_device(
    inputs,
    lengths,
    cotangent,
    query_weight,
    key_weight,
    value_weight,
    out_weight,
    inner_weight,
    outer_weight,
    query_bias,
    value_bias,
    out_bias,
    inner_bias,
    outer_bias,
    first_gain,
    first_shift,
    second_gain,
    second_shift,
):
    C = lax.axis_index("ctx")
    f = lax.axis_index("fsdp")
    nc, n = lax.axis_size("ctx"), lax.axis_size("fsdp")
    x, core = C // 2, C % 2
    ids = jnp.stack([C, f]).astype(jnp.int32)
    seqs, part, width = inputs.shape
    ff = inner_weight.shape[1]
    sh = seqs // 2
    rows = 2 * sh * part
    rs, ro = width // n, ff // n
    hw = width // 2
    A = n // 2

    def swap(a, dc, df):
        pairs = [
            (c * n + g, (c ^ dc) * n + (g ^ df)) for c in range(nc) for g in range(n)
        ]
        return lax.ppermute(a, ("ctx", "fsdp"), pairs)

    def half_seqs(a, which):
        return lax.dynamic_slice_in_dim(a, which * sh, sh, 0)

    def pick(bit, a, b):
        return jnp.where(bit == 0, a, b), jnp.where(bit == 0, b, a)

    def xor_order(items, index):
        items = list(items)
        step = 1
        while step < len(items):
            bit = (index // step) % 2
            items = [
                jnp.where(bit == 0, items[i], items[i ^ step]) for i in range(len(items))
            ]
            step *= 2
        return items

    def columns(w):
        return lax.dynamic_slice_in_dim(w, core * hw, hw, 1)

    def row_of(v):
        return jnp.pad(v.reshape(1, -1), ((0, 0), (0, hw - v.shape[0])))

    vectors = [
        query_bias,
        value_bias,
        out_bias,
        outer_bias,
        first_gain,
        first_shift,
        second_gain,
        second_shift,
        inner_bias,
    ]
    pack = jnp.concatenate(
        [columns(query_weight), columns(key_weight), columns(value_weight)]
        + [row_of(v) for v in vectors]
        + [jnp.zeros((16 - len(vectors), hw), BF)],
        0,
    )
    got = {0: pack, 1: swap(pack, 0, 1)}
    for k in range(1, A):
        got[2 * k] = swap(pack, 0, 2 * k)
    for k in range(1, A):
        got[2 * k + 1] = swap(got[2 * k], 0, 1)
    qkv_pieces = [got[i] for i in range(n)]

    x_mine, x_other = half_seqs(inputs, x), half_seqs(inputs, 1 - x)
    x_m = jnp.concatenate([x_mine[None], swap(x_other, 2, 0)[None]], 0)
    x_s = swap(x_m, 1, 0)
    xm, xs = x_m.reshape(rows, width), x_s.reshape(rows, width)

    small = xor_order([p[3 * rs : 3 * rs + 16] for p in qkv_pieces], f)
    vec = jnp.concatenate([p[:8, :rs] for p in small], 1).astype(F32)
    ib = jnp.concatenate([p[8:9, :ro] for p in small], 1).astype(F32)

    q, k, v, w_qkv = qkv_call(ids, xm, xs, vec, qkv_pieces)

    quarter_i = lax.dynamic_slice_in_dim(inner_weight, C * (ff // 4), ff // 4, 1)
    quarter_u = lax.dynamic_slice_in_dim(outer_weight, C * (ro // 4), ro // 4, 0)
    quarter_o = lax.dynamic_slice_in_dim(out_weight, C * (rs // 4), rs // 4, 0)
    ffn_pack = jnp.concatenate([quarter_i, quarter_u, quarter_o], 0)
    ffn_pack = lax.optimization_barrier((ffn_pack, got[n - 2]))[0]
    part0 = {0: ffn_pack, 1: swap(ffn_pack, 0, 1)}
    for kk in range(1, A):
        part0[2 * kk] = swap(ffn_pack, 0, 2 * kk)
    for kk in range(1, A):
        part0[2 * kk + 1] = swap(part0[2 * kk], 0, 1)
    part2 = {i: swap(part0[i], 2, 0) for i in range(n)}
    part1 = {i: swap(part0[i], 1, 0) for i in range(n)}
    part3 = {i: swap(part2[i], 1, 0) for i in range(n)}
    ffn_pieces = [p[i] for p in (part0, part1, part2, part3) for i in range(n)]

    c_mine, c_other = half_seqs(cotangent, x), half_seqs(cotangent, 1 - x)
    cot = jnp.concatenate([c_mine[None], swap(c_other, 2, 0)[None]], 0).reshape(rows, width)

    lens = half_seqs(lengths, x)
    order = jnp.stack([C ^ e for e in (0, 2, 1, 3)])
    positions = order[:, None, None] * part + jnp.arange(part)[None, None, :]
    inside = positions < lens[None, :, None]
    valid = inside[:2].astype(F32).reshape(rows, 1)
    mask = jnp.broadcast_to(
        jnp.where(inside, 0.0, -1e30).astype(BF)[..., None], (4, sh, part, 2 * HD)
    )

    four = (4, sh, part, hw)
    two = (2, sh, part, hw)
    q4, k4, v4 = q.reshape(four), k.reshape(four), v.reshape(four)
    c_m, c_s, lse = attend_call(q4, k4, v4, mask)
    c_r = swap(c_s, 1, 0)
    cm, cr = c_m.reshape(rows, hw), c_r.reshape(rows, hw)

    lo, act, dout, dinn, nrm, dattn, dfirst, dco, dcs, acc = ffn_call(
        ids, cm, cr, xm, cot, valid, vec, ib, ffn_pieces
    )

    def give_back(a):
        mine, theirs = a[0], swap(a[1], 2, 0)
        return jnp.concatenate(pick(x, mine, theirs), 0)

    layer_out = give_back(lo.reshape(2, sh, part, width))

    g_r = swap(dcs, 1, 0)

    def total(*items):
        out = items[0].astype(F32)
        for i in items[1:]:
            out = out + i.astype(F32)
        return out.astype(BF)

    def reduce_quarter(keep, send):
        got = swap(send, 1, 0)
        away = total(keep[1], got[1])
        near = total(keep[0], got[0])
        got = swap(away, 2, 0)
        away = total(near[1], got[1])
        near = total(near[0], got[0])
        got = swap(away, 0, 1)
        away = [total(near[a], got[a]) for a in range(A)]
        mine = total(away[0], *[swap(away[a], 0, 2 * a) for a in range(1, A)])
        other = swap(mine, 2, 0)
        quarters = [mine, swap(mine, 1, 0), other, swap(other, 1, 0)]
        return [a.astype(F32) for a in xor_order(quarters, C)]

    ku, su = outer_grad_call(ids, act, dout, n)
    ki, si = inner_grad_call(ids, nrm, dinn, n)
    ko, so = out_grad_call(ids, cm, cr, dattn, n)
    grad_outer = jnp.concatenate(reduce_quarter(ku, su), 0)
    grad_inner = jnp.concatenate(reduce_quarter(ki, si), 1)
    grad_out = jnp.concatenate(reduce_quarter(ko, so), 0)

    dq, dk, dv = attend_back_call(
        q4, k4, v4, mask, lse, c_m, c_s, dco.reshape(two), g_r.reshape(two)
    )
    flat3 = (2, rows, hw)
    dq, dk, dv = dq.reshape(flat3), dk.reshape(flat3), dv.reshape(flat3)

    def reduce_half(g):
        got = swap(g[1], 0, 1)
        away = [total(g[0, a], got[a]) for a in range(A)]
        mine = total(away[0], *[swap(away[a], 0, 2 * a) for a in range(1, A)])
        mine = total(mine, swap(mine, 2, 0))
        return jnp.concatenate(pick(core, mine, swap(mine, 1, 0)), 1).astype(F32)

    gq, bq = qkv_grad_call(ids, xm, xs, dq, n)
    gk, _ = qkv_grad_call(ids, xm, xs, dk, n)
    gv, bv = qkv_grad_call(ids, xm, xs, dv, n)
    grad_query, grad_key, grad_value = reduce_half(gq), reduce_half(gk), reduce_half(gv)

    halves = jnp.concatenate([bq[:1], bv[:1], jnp.zeros((14, hw), F32)], 0)
    none = jnp.zeros_like(halves)
    sums = acc + jnp.concatenate(pick(core, halves, none), 1)
    for dc, df in [(1, 0), (2, 0)] + [(0, 1 << b) for b in range(n.bit_length() - 1)]:
        sums = sums + swap(sums, dc, df)
    own = lax.dynamic_slice_in_dim(sums[:8], f * rs, rs, 1)
    own_inner = lax.dynamic_slice_in_dim(sums[8 : 8 + ff // width].reshape(ff), f * ro, ro, 0)

    theirs = back_project_call(1, dq, dk, dv, w_qkv)
    from_core = swap(theirs, 1, 0)
    own_part = back_project_call(0, dq, dk, dv, w_qkv)
    full = (dfirst + own_part + from_core).reshape(2, sh, part, width)
    away = swap(full[1].astype(BF), 2, 0).astype(F32)
    input_grad = jnp.concatenate(pick(x, full[0], away), 0)

    return (
        layer_out,
        input_grad,
        grad_query,
        grad_key,
        grad_value,
        grad_out,
        grad_inner,
        grad_outer,
        own[0],
        own[1],
        own[2],
        own_inner,
        own[3],
        own[4],
        own[5],
        own[6],
        own[7],
    )


def solution(mesh):
    rowed = P("fsdp", "ctx", None)
    matrix, vector = P("fsdp", None), P("fsdp")
    in_specs = (rowed, vector, rowed) + (matrix,) * 6 + (vector,) * 9
    out_specs = (rowed, rowed) + (matrix,) * 6 + (vector,) * 9
    return jax.shard_map(
        per_device, mesh=mesh, in_specs=in_specs, out_specs=out_specs, check_vma=False
    )
```

```python
import functools

import jax
import jax.numpy as jnp
from jax import lax
from jax.experimental import pallas as pl
from jax.experimental.pallas import tpu as pltpu
from jax.sharding import PartitionSpec as P

HD = 64
EPSILON = 1e-05
BF = jnp.bfloat16
F32 = jnp.float32
ANY = pl.BlockSpec(memory_space=pl.ANY)
NT = (((1,), (1,)), ((), ()))
TN = (((0,), (0,)), ((), ()))
VMEM_LIMIT = 58 << 20


def dot(a, b):
    return jnp.dot(a, b, preferred_element_type=F32)


def dot_nt(a, b):
    return lax.dot_general(a, b, NT, preferred_element_type=F32)


def dot_tn(a, b):
    return lax.dot_general(a, b, TN, preferred_element_type=F32)


def params(**more):
    return pltpu.CompilerParams(vmem_limit_bytes=VMEM_LIMIT, **more)


def cost(flops, size, trans=0):
    return pl.CostEstimate(flops=int(flops), bytes_accessed=int(size), transcendentals=int(trans))


MESH = pl.DeviceIdType.MESH
PACK = 16


def flip(v, mask):
    out, bit = v, 1
    while bit <= mask:
        if mask & bit:
            out = out + bit - 2 * bit * ((v // bit) % 2)
        bit *= 2
    return out


def at(index, size):
    return pl.ds(pl.multiple_of(index * size, size), size)


def spread(read, n, rs):
    per = max(128 // rs, 1)
    tiles = []
    for t in range(n // per):
        tile = read(t * per)
        for u in range(1, per):
            tile = tile + pltpu.roll(read(t * per + u), u * rs, 1)
        tiles.append(tile)
    return jnp.concatenate(tiles, 1)


def front_kernel(
    n,
    lens,
    xin,
    cin,
    wq,
    wk,
    wv,
    vecs,
    wo_in,
    wi_in,
    wu_in,
    xo,
    co,
    wqkvo,
    wio,
    wuo,
    woo,
    veco,
    qo,
    ko,
    vo,
    cxo,
    cro,
    lseo,
    X,
    W,
    VEC,
    Q,
    K,
    V,
    CX,
    LSE,
    lsem,
    ssem,
    rsem,
):
    C, f = lax.axis_index("ctx"), lax.axis_index("fsdp")
    x, core = C // 2, C % 2
    A = n // 2
    sh, part, width = X.shape[1:]
    hw = W.shape[2]
    ff = wio.shape[1]
    rs, ro, cq = width // n, ff // n, ff // 4

    partners = [(0, 2 * k) for k in range(1, A)] + [(0, 1), (2, 0), (1, 0)]

    def device(dc, df):
        return (flip(C, dc), flip(f, df))

    barrier = pltpu.get_barrier_semaphore()
    for p in partners:
        pl.semaphore_signal(barrier, inc=1, device_id=device(*p), device_id_type=MESH)

    local = []
    used = iter(range(lsem.shape[0]))

    def begin(source, target):
        c = pltpu.make_async_copy(source, target, lsem.at[next(used)])
        c.start()
        return c

    def keep(source, target):
        local.append(begin(source, target))

    x_here = begin(xin.at[pl.ds(x * sh, sh)], X.at[0])
    w_here = [begin(w.at[:, at(core, hw)], W.at[j, at(f, rs)]) for j, w in enumerate((wq, wk, wv))]
    w_here.append(begin(vecs, VEC.at[f]))

    pl.semaphore_wait(barrier, len(partners))

    def remote(source, target, sem, dev):
        return pltpu.make_async_remote_copy(
            src_ref=source,
            dst_ref=target,
            send_sem=ssem.at[sem],
            recv_sem=rsem.at[sem],
            device_id=device(*dev),
            device_id_type=MESH,
        )

    sent = []

    def send(*what):
        c = remote(*what)
        c.start()
        sent.append(c)

    seen = set()

    def arrive(target, sem, dev):
        if sem not in seen:
            seen.add(sem)
            remote(target, target, sem, dev).wait_recv()

    base_x = 12 * n + 4 * n
    X1, X2, X3, COT, CTX = (base_x + i for i in range(5))
    send(xin.at[pl.ds((1 - x) * sh, sh)], X.at[1], X1, (2, 0))

    def qkv_slot(i):
        s = flip(f, i)
        return [W.at[j, at(s, rs)] for j in range(3)] + [VEC.at[s]]

    def qkv_sem(i):
        return [12 * n + 4 * i + j for j in range(4)]

    own_qkv = [w.at[:, at(core, hw)] for w in (wq, wk, wv)] + [vecs]

    def qkv_give(tag, source_piece, source, dev):
        place = qkv_slot(source_piece)
        for j in range(4):
            send(source[j], place[j], qkv_sem(tag)[j], dev)

    def qkv_need(i):
        dev = (0, i) if i % 2 == 0 else (0, 1)
        place = qkv_slot(i)
        for j in range(4):
            arrive(place[j], qkv_sem(i)[j], dev)

    for k in range(1, A):
        qkv_give(2 * k, 0, own_qkv, (0, 2 * k))
    qkv_give(1, 0, own_qkv, (0, 1))
    x_here.wait()
    send(X.at[0], X.at[2], X2, (1, 0))

    def rest_slot(e, i):
        qq, s = flip(C, e), flip(f, i)
        return [
            woo.at[pl.ds(pl.multiple_of(s * rs + qq * (rs // 4), rs // 4), rs // 4)],
            wio.at[at(s, rs), at(qq, cq)],
            wuo.at[pl.ds(pl.multiple_of(s * ro + qq * (ro // 4), ro // 4), ro // 4)],
        ]

    def rest_sem(e, i):
        return [(e * n + i) * 3 + kind for kind in range(3)]

    def route(e, i):
        if e % 2:
            return (1, 0), (e - 1, i)
        if e:
            return (2, 0), (0, i)
        if i % 2:
            return (0, 1), (0, i - 1)
        return (0, i), (0, 0)

    def rest_copies(e, i):
        dev, (pe, pi) = route(e, i)
        place = rest_slot(pe, pi)
        source = [wo_in.at[at(C, rs // 4)], wi_in.at[:, at(C, cq)], wu_in.at[at(C, ro // 4)]]
        source = source if pi == 0 else place
        sems = rest_sem(e, i)
        return [remote(source[kind], place[kind], sems[kind], dev) for kind in range(3)]

    def rest_send(e, i):
        for c in rest_copies(e, i):
            c.start()

    def rest_need(e, i):
        dev, _ = route(e, i)
        place = rest_slot(e, i)
        for kind in range(3):
            arrive(place[kind], rest_sem(e, i)[kind], dev)

    def rest_hand_on(e, i):
        rest_need(e, i)
        if e == 0 and i % 2 == 0:
            rest_send(0, i + 1)
        if e == 0:
            rest_send(2, i)
        if e % 2 == 0:
            rest_send(e + 1, i)

    for k in range(1, A):
        qkv_need(2 * k)
        qkv_give(2 * k + 1, 2 * k, qkv_slot(2 * k), (0, 1))
    for k in range(1, A):
        rest_send(0, 2 * k)
    arrive(X.at[1], X1, (2, 0))
    send(X.at[1], X.at[3], X3, (1, 0))
    send(cin.at[pl.ds((1 - x) * sh, sh)], co.at[1], COT, (2, 0))
    rest_send(0, 1)
    keep(cin.at[pl.ds(x * sh, sh)], co.at[0])
    keep(wo_in, woo.at[at(f, rs)])
    keep(wi_in, wio.at[at(f, rs)])
    keep(wu_in, wuo.at[at(f, ro)])
    for c in w_here:
        c.wait()
    for i in range(1, n):
        qkv_need(i)
    arrive(X.at[2], X2, (1, 0))
    arrive(X.at[3], X3, (1, 0))
    keep(X, xo)
    keep(W, wqkvo)
    keep(VEC, veco)

    jobs = [(0, 1)] + [(0, i) for i in range(2, n, 2)] + [(2, 1)]
    jobs += [(0, i) for i in range(3, n, 2)] + [(2, i) for i in range(2, n)]
    slots = X.shape[0]
    pairs = hw // (2 * HD)
    steps = slots + sh * pairs
    plan = [jobs[len(jobs) * t // steps : len(jobs) * (t + 1) // steps] for t in range(steps)]

    def serve(step, base, count):
        for t in range(count):
            if plan[base + t]:

                @pl.when(step == t)
                def _():
                    for job in plan[base + t]:
                        rest_hand_on(*job)

    def bias(row):
        read = lambda s: VEC[pl.ds(core * (n // 2) + s, 1), row : row + 1, :128].reshape(1, 128).astype(F32)
        return spread(read, n // 2, rs)

    bias_q, bias_v = bias(0), bias(1)

    def project(slot, carry):
        a = X[slot].reshape(sh * part, width)
        shape = (sh, part, hw)
        Q[slot] = (dot(a, W[0]) + bias_q).astype(BF).reshape(shape)
        K[slot] = dot(a, W[1]).astype(BF).reshape(shape)
        V[slot] = (dot(a, W[2]) + bias_v).astype(BF).reshape(shape)
        serve(slot, 0, slots)
        return carry

    lax.fori_loop(0, slots, project, 0)
    keep(Q, qo)
    keep(K, ko)
    keep(V, vo)

    def attend(step, carry):
        s, pair = step // pairs, step % pairs
        cols = at(pair, 2 * HD)

        def load(ref):
            return ref[:, s, :, cols].reshape(slots * part, 2 * HD)

        q, k, v = load(Q), load(K), load(V)
        mask = key_mask(lens[x * sh + s], C, part)
        o, lse = attend_pair(q, k, v, mask)
        CX[:, s, :, cols] = o.reshape(slots, part, 2 * HD)
        LSE[s, :, cols] = lse
        serve(step, slots, sh * pairs)
        return carry

    lax.fori_loop(0, sh * pairs, attend, 0)
    send(CX.at[pl.ds(2, 2)], cro, CTX, (1, 0))
    keep(CX, cxo)
    keep(LSE, lseo)
    for e in range(4):
        for i in range(1, n):
            rest_need(e, i)
            for c in rest_copies(e, i):
                c.wait_send()
    arrive(co.at[1], COT, (2, 0))
    arrive(cro, CTX, (1, 0))
    for c in sent:
        c.wait_send()
    for c in local:
        c.wait()


def front_call(lengths, xin, cin, wq, wk, wv, vecs, wo, wi, wu, n):
    seqs, part, width = xin.shape
    sh, ff, hw = seqs // 2, wi.shape[1], width // 2

    def bf(*shape):
        return jax.ShapeDtypeStruct(shape, BF)

    def vm(*shape):
        return pltpu.VMEM(shape, BF)

    full = 4 * part
    lse = (sh, full, hw)
    four = (4, sh, part, hw)
    sems = 16 * n + 5
    return pl.pallas_call(
        functools.partial(front_kernel, n),
        in_specs=[pl.BlockSpec(memory_space=pltpu.SMEM)] + [ANY] * 9,
        out_specs=[ANY] * 13,
        out_shape=[
            bf(4, sh, part, width),
            bf(2, sh, part, width),
            bf(3, width, hw),
            bf(width, ff),
            bf(ff, width),
            bf(width, width),
            bf(n, PACK, hw),
            bf(*four),
            bf(*four),
            bf(*four),
            bf(*four),
            bf(2, sh, part, hw),
            jax.ShapeDtypeStruct(lse, F32),
        ],
        scratch_shapes=[
            vm(4, sh, part, width),
            vm(3, width, hw),
            vm(n, PACK, hw),
            vm(*four),
            vm(*four),
            vm(*four),
            vm(*four),
            pltpu.VMEM(lse, F32),
            pltpu.SemaphoreType.DMA((24,)),
            pltpu.SemaphoreType.DMA((sems,)),
            pltpu.SemaphoreType.DMA((sems,)),
        ],
        compiler_params=params(collective_id=0, has_side_effects=True),
        name="front",
    )(lengths, xin, cin, wq, wk, wv, vecs, wo, wi, wu)


def lanes_of(shape, head):
    lane = lax.broadcasted_iota(jnp.int32, shape, 1)
    own = (lane < HD) if head == 0 else (lane >= HD)
    return lane, own, (HD if head == 0 else 0)


def split3(a):
    hi = a.astype(BF).astype(F32)
    mid = (a - hi).astype(BF).astype(F32)
    return hi, mid, a - hi - mid


def flat(ref):
    a = ref[...]
    return a.reshape(-1, a.shape[-1])


def key_mask(length, C, part):
    row = lax.broadcasted_iota(jnp.int32, (part, 2 * HD), 0)
    out = []
    for e in (0, 2, 1, 3):
        inside = row + flip(C, e) * part < length
        out.append(jnp.where(inside, 0.0, -1e30).astype(BF))
    return jnp.concatenate(out, 0)


def attend_pair(q, k, v, mask):
    out = []
    for head in range(2):
        lane, own, other = lanes_of(q.shape, head)
        qh = jnp.where(own, q * BF(HD**-0.5), jnp.where(lane == other, 1.0, 0.0).astype(BF))
        kh = jnp.where(own, k, mask)
        s = dot_nt(qh, kh)
        top = jnp.max(s, -1, keepdims=True)
        e = jnp.exp(s - top)
        total = jnp.sum(e, -1, keepdims=True)
        o = dot(e.astype(BF), v) * (1.0 / total)
        out.append((o, top + jnp.log(total), own))
    (o0, l0, own), (o1, l1, _) = out
    return jnp.where(own, o0, o1).astype(BF), jnp.where(own, l1, l0)


def attend_back_kernel(
    ids, lens, q_ref, k_ref, v_ref, lse_ref, c_ref, gm_ref, gs_ref, dq_ref, dk_ref, dv_ref
):
    q, k, v, c = flat(q_ref), flat(k_ref), flat(v_ref), flat(c_ref)
    mask = key_mask(
        lens[(ids[0] // 2) * pl.num_programs(0) + pl.program_id(0)], ids[0], q_ref.shape[2]
    )
    lse = lse_ref[0]
    g = jnp.concatenate([flat(gm_ref), flat(gs_ref)], 0)
    qs = q * BF(HD**-0.5)
    kt = k.T
    prod = c.astype(F32) * g.astype(F32)
    res = []
    for head in range(2):
        lane, own, o = lanes_of(q.shape, head)
        hi, mid, low = split3(-lse)
        extra = jnp.where(
            lane == o,
            1.0,
            jnp.where(
                lane == o + 1,
                hi,
                jnp.where(lane == o + 2, mid, jnp.where(lane == o + 3, low, 0.0)),
            ),
        ).astype(BF)
        qh = jnp.where(own, qs, extra)
        kh = jnp.where(own, k, jnp.where(lane == o, mask, BF(1)))
        p = jnp.exp(dot_nt(kh, qh))
        delta = jnp.sum(jnp.where(own, prod, 0.0), -1, keepdims=True)
        hi, mid, low = split3(-delta)
        extra = jnp.where(
            lane == o, hi, jnp.where(lane == o + 1, mid, jnp.where(lane == o + 2, low, 0.0))
        ).astype(BF)
        gh = jnp.where(own, g, extra)
        vh = jnp.where(own, v, BF(1))
        ds = (p * dot_nt(vh, gh)).astype(BF)
        dv = dot(p.astype(BF), g)
        dk = dot(ds, qs)
        dqt = dot(kt, ds)
        res.append((dv, dk, dqt, own))
    (dv0, dk0, dq0, own), (dv1, dk1, dq1, _) = res
    dv_ref[...] = jnp.where(own, dv0, dv1).astype(BF).reshape(dv_ref.shape)
    dk_ref[...] = jnp.where(own, dk0, dk1).astype(BF).reshape(dk_ref.shape)
    dqt = jnp.concatenate([dq0[:HD], dq1[HD:]], 0) * (HD**-0.5)
    dq_ref[...] = dqt.T.astype(BF).reshape(dq_ref.shape)


def attend_back_call(ids, lens, q, k, v, lse, c, gm, gs):
    slots, seqs, part, cols = q.shape
    pair = 2 * HD
    four = pl.BlockSpec((4, 1, part, pair), lambda s, h, *_: (0, s, 0, h))
    two = pl.BlockSpec((2, 1, part, pair), lambda s, h, *_: (0, s, 0, h))
    full = slots * part
    out = jax.ShapeDtypeStruct(q.shape, BF)
    grid_spec = pltpu.PrefetchScalarGridSpec(
        num_scalar_prefetch=2,
        grid=(seqs, cols // pair),
        in_specs=[
            four,
            four,
            four,
            pl.BlockSpec((1, full, pair), lambda s, h, *_: (s, 0, h)),
            four,
            two,
            two,
        ],
        out_specs=[four] * 3,
    )
    return pl.pallas_call(
        attend_back_kernel,
        grid_spec=grid_spec,
        out_shape=[out] * 3,
        compiler_params=params(),
        cost_estimate=cost(
            10 * seqs * full * full * cols * 4, 20 * seqs * full * cols, seqs * full * full * cols // HD
        ),
        name="attend_back",
    )(ids, lens, q, k, v, lse, c, gm, gs)


def gelu_pair(u):
    e = jnp.exp(u * u * -0.5)
    t = 1.0 / (1.0 + (0.3275911 * 0.7071067811865476) * jnp.abs(u))
    poly = t * (
        0.254829592 * 0.5
        + t
        * (
            -0.284496736 * 0.5
            + t * (1.421413741 * 0.5 + t * (-1.453152027 * 0.5 + t * (1.061405429 * 0.5)))
        )
    )
    tail = poly * e
    cdf = jnp.where(u >= 0, 1.0 - tail, tail)
    ucdf = u * cdf
    return ucdf, cdf + u * (e * 0.3989422804014327)


def normalise(h):
    c = h - jnp.mean(h, -1, keepdims=True)
    r = lax.rsqrt(jnp.mean(c * c, -1, keepdims=True) + EPSILON)
    return c * r, r


def normalise_back(dyg, hat, r):
    return r * (
        dyg - jnp.mean(dyg, -1, keepdims=True) - hat * jnp.mean(dyg * hat, -1, keepdims=True)
    )


def ffn_kernel(n, sh, part, ids, lens, cm, cr, xm, cot, vecs, wo_in, wi_in, wu_in, *refs):
    lo, act, dout, dinn, nrm, dattn, dfirst, dco, dcs, acc = refs[:10]
    wo, wi, wu, gp, vec, ib, sem = refs[10:]
    width, ff = wi.shape
    core = ids[0] % 2
    step = pl.program_id(0)
    rs, ro = width // n, ff // n
    cq, hw = ff // 4, width // 2

    pairs = ((wo_in, wo), (wi_in, wi), (wu_in, wu))

    def copy(kind):
        return pltpu.make_async_copy(*pairs[kind], sem.at[kind])

    @pl.when(step == 0)
    def _():
        for kind in range(3):
            copy(kind).start()
        acc[...] = jnp.zeros_like(acc)
        vec[...] = spread(lambda s: vecs[s, :8, :128].astype(F32), n, rs)
        for s in range(n):
            ib[:, s * ro : (s + 1) * ro] = vecs[s, 8:9, :ro].astype(F32)

    def arrived(kind):
        @pl.when(step == 0)
        def _():
            copy(kind).wait()

    count = xm.shape[0] // part
    inside = []
    for u in range(count):
        slot = step * count + u
        ex, s = slot // sh, slot % sh
        first = (ids[0] ^ (2 * ex)) * part
        row = lax.broadcasted_iota(jnp.int32, (part, 1), 0) + first
        inside.append(jnp.where(row < lens[(ids[0] // 2) * sh + s], 1.0, 0.0))
    valid = jnp.concatenate(inside, 0)
    own, other = at(core, hw), at(1 - core, hw)

    def add(row, value):
        acc[row : row + 1, :] += jnp.sum(value, 0, keepdims=True)

    arrived(0)
    first = (
        xm[...].astype(F32) + (dot(cm[...], wo[own]) + dot(cr[...], wo[other])) + vec[2:3, :]
    )
    hat1, r1 = normalise(first)
    normed = hat1 * vec[4:5, :] + vec[5:6, :]
    low = normed.astype(BF)
    nrm[...] = low
    arrived(1)
    for j in range(4):
        cols = slice(j * cq, (j + 1) * cq)
        g, d = gelu_pair(dot(low, wi[:, cols]) + ib[:, cols])
        act[:, cols] = g.astype(BF)
        gp[:, cols] = d
    arrived(2)
    second = normed + (dot(act[...], wu[...]) + vec[3:4, :])
    hat2, r2 = normalise(second)
    lo[...] = (hat2 * vec[6:7, :] + vec[7:8, :]).astype(BF)
    og = cot[...].astype(F32) * valid
    add(6, og * hat2)
    add(7, og)
    d2 = normalise_back(og * vec[6:7, :], hat2, r2)
    d2low = d2.astype(BF)
    dout[...] = d2low
    add(3, d2low.astype(F32))
    for j in range(4):
        cols = slice(j * cq, (j + 1) * cq)
        di = (dot_nt(d2low, wu[cols, :]) * gp[:, cols]).astype(BF)
        dinn[:, cols] = di
        add(8 + j, di.astype(F32))
    dn = d2 + dot_nt(dinn[...], wi[...])
    add(4, dn * hat1)
    add(5, dn)
    d1 = normalise_back(dn * vec[4:5, :], hat1, r1)
    dfirst[...] = d1
    d1low = d1.astype(BF)
    dattn[...] = d1low
    add(2, d1low.astype(F32))
    dco[...] = dot_nt(d1low, wo[own]).astype(BF)
    dcs[...] = dot_nt(d1low, wo[other]).astype(BF)


def ffn_call(ids, lens, sh, c, cr, xall, cot, vecs, wo, wi, wu):
    width, ff = wi.shape
    n, rows = vecs.shape[0], cot.shape[0]
    block = rows // 3
    hw = width // 2

    def by(cols):
        return pl.BlockSpec((block, cols), lambda i, *_: (i, 0))

    def whole(*shape):
        return pl.BlockSpec(shape, lambda i, *_: (0,) * len(shape))

    grid_spec = pltpu.PrefetchScalarGridSpec(
        num_scalar_prefetch=2,
        grid=(3,),
        in_specs=[by(hw), by(hw), by(width), by(width), whole(*vecs.shape), ANY, ANY, ANY],
        out_specs=[
            by(width),
            by(ff),
            by(width),
            by(ff),
            by(width),
            by(width),
            by(width),
            by(hw),
            by(hw),
            whole(16, width),
        ],
        scratch_shapes=[
            pltpu.VMEM((width, width), BF),
            pltpu.VMEM((width, ff), BF),
            pltpu.VMEM((ff, width), BF),
            pltpu.VMEM((block, ff), F32),
            pltpu.VMEM((8, width), F32),
            pltpu.VMEM((1, ff), F32),
            pltpu.SemaphoreType.DMA((3,)),
        ],
    )

    def shape(cols, dtype=BF):
        return jax.ShapeDtypeStruct((rows, cols), dtype)

    return pl.pallas_call(
        functools.partial(ffn_kernel, n, sh, rows // (2 * sh)),
        grid_spec=grid_spec,
        out_shape=[
            shape(width),
            shape(ff),
            shape(width),
            shape(ff),
            shape(width),
            shape(width),
            shape(width, F32),
            shape(hw),
            shape(hw),
            jax.ShapeDtypeStruct((16, width), F32),
        ],
        compiler_params=params(),
        cost_estimate=cost(
            2 * rows * width * (2 * width + 4 * ff), 30 * rows * width + 2 * width * (2 * ff + width)
        ),
        name="ffn",
    )(ids, lens, c, cr, xall, cot, vecs, wo, wi, wu)


def outer_grad_kernel(ids, act, dout, keep, send, tmp):
    tmp[...] = dot_tn(act[...], dout[...])
    size = keep.shape[3]
    for ec, ref in ((0, keep), (1, send)):
        for ex in range(2):
            ref[ex, 0, 0] = tmp[at(ids[0] ^ (2 * ex + ec), size), :].astype(BF)


def outer_grad_call(ids, act, dout, n):
    rows, ff = act.shape
    width = dout.shape[1]
    ro = ff // n
    out = pl.BlockSpec((2, 1, 1, ro // 4, width), lambda i, s: (0, i % 2, i // 2, 0, 0))
    grid_spec = pltpu.PrefetchScalarGridSpec(
        num_scalar_prefetch=1,
        grid=(n,),
        in_specs=[
            pl.BlockSpec((rows, ro), lambda i, s: (0, s[1] ^ i)),
            pl.BlockSpec((rows, width), lambda i, s: (0, 0)),
        ],
        out_specs=[out, out],
        scratch_shapes=[pltpu.VMEM((ro, width), F32)],
    )
    shape = jax.ShapeDtypeStruct((2, 2, n // 2, ro // 4, width), BF)
    return pl.pallas_call(
        outer_grad_kernel,
        grid_spec=grid_spec,
        out_shape=[shape, shape],
        compiler_params=params(),
        cost_estimate=cost(2 * rows * ff * width, 2 * (rows * ff + rows * width + ff * width)),
        name="outer_grad",
    )(ids, act, dout)


def inner_grad_kernel(n, ids, nrm, dinn, keep, send, tmp):
    rs = nrm.shape[1] // n
    tmp[...] = dot_tn(nrm[...], dinn[...])

    def put(ref):
        for i in range(n):
            ref[0, i % 2, i // 2] = tmp[at(ids[1] ^ i, rs), :].astype(BF)

    @pl.when(pl.program_id(0) == 0)
    def _():
        put(send)

    @pl.when(pl.program_id(0) == 1)
    def _():
        put(keep)


def inner_grad_call(ids, nrm, dinn, n):
    rows, width = nrm.shape
    ff = dinn.shape[1]
    cq, rs = ff // 4, width // n
    block = (1, 2, n // 2, rs, cq)
    grid_spec = pltpu.PrefetchScalarGridSpec(
        num_scalar_prefetch=1,
        grid=(2, 2),
        in_specs=[
            pl.BlockSpec((rows, width), lambda a, ex, s: (0, 0)),
            pl.BlockSpec((rows, cq), lambda a, ex, s: (0, s[0] ^ (2 * ex + 1 - a))),
        ],
        out_specs=[
            pl.BlockSpec(block, lambda a, ex, s: (jnp.where(a == 1, ex, 0), 0, 0, 0, 0)),
            pl.BlockSpec(block, lambda a, ex, s: (jnp.where(a == 0, ex, 1), 0, 0, 0, 0)),
        ],
        scratch_shapes=[pltpu.VMEM((width, cq), F32)],
    )
    shape = jax.ShapeDtypeStruct((2, 2, n // 2, rs, cq), BF)
    return pl.pallas_call(
        functools.partial(inner_grad_kernel, n),
        grid_spec=grid_spec,
        out_shape=[shape, shape],
        compiler_params=params(),
        cost_estimate=cost(2 * rows * ff * width, 2 * (rows * ff + rows * width + ff * width)),
        name="inner_grad",
    )(ids, nrm, dinn)


def out_grad_kernel(n, ids, cm, cr, dattn, keep, send, tmp):
    width = tmp.shape[0]
    hw, rs = width // 2, width // n
    size = rs // 4
    g = dattn[...]
    core = ids[0] % 2
    tmp[at(core, hw), :] = dot_tn(cm[...], g)
    tmp[at(1 - core, hw), :] = dot_tn(cr[...], g)
    for ec, ref in ((0, keep), (1, send)):
        for ex in range(2):
            for i in range(n):
                first = (ids[1] ^ i) * rs + (ids[0] ^ (2 * ex + ec)) * size
                ref[ex, i % 2, i // 2] = tmp[pl.ds(pl.multiple_of(first, size), size), :].astype(BF)


def out_grad_call(ids, ctx, cr, dattn, n):
    rows, width = dattn.shape
    shape = jax.ShapeDtypeStruct((2, 2, n // 2, width // n // 4, width), BF)
    return pl.pallas_call(
        functools.partial(out_grad_kernel, n),
        grid_spec=pltpu.PrefetchScalarGridSpec(
            num_scalar_prefetch=1,
            grid=(1,),
            in_specs=[
                pl.BlockSpec((rows, width // 2), lambda i, s: (0, 0)),
                pl.BlockSpec((rows, width // 2), lambda i, s: (0, 0)),
                pl.BlockSpec((rows, width), lambda i, s: (0, 0)),
            ],
            out_specs=[pl.BlockSpec(shape.shape, lambda i, s: (0, 0, 0, 0, 0))] * 2,
            scratch_shapes=[pltpu.VMEM((width, width), F32)],
        ),
        out_shape=[shape, shape],
        compiler_params=params(),
        cost_estimate=cost(2 * rows * width * width, 4 * rows * width + 2 * width * width),
        name="out_grad",
    )(ids, ctx, cr, dattn)


def qkv_grad_kernel(n, ids, xm, xs, dm, ds, out, bias, tmp):
    tmp[...] = dot_tn(xm[...], dm[0]) + dot_tn(xs[...], ds[0])
    bias[...] = jnp.broadcast_to(
        jnp.sum(dm[0].astype(F32), 0, keepdims=True) + jnp.sum(ds[0].astype(F32), 0, keepdims=True),
        bias.shape,
    )
    rs = tmp.shape[0] // n
    for i in range(n):
        out[i % 2, i // 2] = tmp[at(ids[1] ^ i, rs), :].astype(BF)


def qkv_grad_call(ids, xall, d, n):
    rows, width = xall.shape[0] // 2, xall.shape[1]
    cols = d.shape[2]
    shape = (2, n // 2, width // n, cols)
    grid_spec = pltpu.PrefetchScalarGridSpec(
        num_scalar_prefetch=1,
        grid=(1,),
        in_specs=[
            pl.BlockSpec((rows, width), lambda i, s: (0, 0)),
            pl.BlockSpec((rows, width), lambda i, s: (1, 0)),
            pl.BlockSpec((1, rows, cols), lambda i, s: (0, 0, 0)),
            pl.BlockSpec((1, rows, cols), lambda i, s: (1, 0, 0)),
        ],
        out_specs=[
            pl.BlockSpec(shape, lambda i, s: (0, 0, 0, 0)),
            pl.BlockSpec((8, cols), lambda i, s: (0, 0)),
        ],
        scratch_shapes=[pltpu.VMEM((width, cols), F32)],
    )
    return pl.pallas_call(
        functools.partial(qkv_grad_kernel, n),
        grid_spec=grid_spec,
        out_shape=[jax.ShapeDtypeStruct(shape, BF), jax.ShapeDtypeStruct((8, cols), F32)],
        compiler_params=params(),
        cost_estimate=cost(4 * rows * width * cols, 4 * rows * width + 4 * rows * cols),
        name="qkv_grad",
    )(ids, xall, xall, d, d)


def back_project_kernel(dq, dk, dv, w, out):
    out[...] = dot_nt(dq[0], w[0]) + dot_nt(dk[0], w[1]) + dot_nt(dv[0], w[2])


def back_project_call(which, dq, dk, dv, w):
    _, rows, cols = dq.shape
    width = w.shape[1]
    block = rows // 3
    one = pl.BlockSpec((1, block, cols), lambda i: (which, i, 0))
    return pl.pallas_call(
        back_project_kernel,
        grid=(3,),
        in_specs=[one, one, one, pl.BlockSpec((3, width, cols), lambda i: (0, 0, 0))],
        out_specs=pl.BlockSpec((block, width), lambda i: (i, 0)),
        out_shape=jax.ShapeDtypeStruct((rows, width), F32),
        compiler_params=params(),
        cost_estimate=cost(6 * rows * width * cols, 6 * rows * cols + 4 * rows * width + 6 * width * cols),
        name="back_project",
    )(dq, dk, dv, w)


def per_device(
    inputs,
    lengths,
    cotangent,
    query_weight,
    key_weight,
    value_weight,
    out_weight,
    inner_weight,
    outer_weight,
    query_bias,
    value_bias,
    out_bias,
    inner_bias,
    outer_bias,
    first_gain,
    first_shift,
    second_gain,
    second_shift,
):
    C = lax.axis_index("ctx")
    f = lax.axis_index("fsdp")
    nc, n = lax.axis_size("ctx"), lax.axis_size("fsdp")
    x, core = C // 2, C % 2
    ids = jnp.stack([C, f]).astype(jnp.int32)
    seqs, part, width = inputs.shape
    ff = inner_weight.shape[1]
    sh = seqs // 2
    rows = 2 * sh * part
    rs, ro = width // n, ff // n
    hw = width // 2
    A = n // 2

    def swap(a, dc, df):
        pairs = [
            (c * n + g, (c ^ dc) * n + (g ^ df)) for c in range(nc) for g in range(n)
        ]
        return lax.ppermute(a, ("ctx", "fsdp"), pairs)

    def pick(bit, a, b):
        return jnp.where(bit == 0, a, b), jnp.where(bit == 0, b, a)

    def xor_order(items, index):
        items = list(items)
        step = 1
        while step < len(items):
            bit = (index // step) % 2
            items = [
                jnp.where(bit == 0, items[i], items[i ^ step]) for i in range(len(items))
            ]
            step *= 2
        return items

    def row_of(v):
        return jnp.pad(v.reshape(1, -1), ((0, 0), (0, hw - v.shape[0])))

    vectors = [
        query_bias,
        value_bias,
        out_bias,
        outer_bias,
        first_gain,
        first_shift,
        second_gain,
        second_shift,
        inner_bias,
    ]
    vecs = jnp.concatenate(
        [row_of(v) for v in vectors] + [jnp.zeros((PACK - len(vectors), hw), BF)], 0
    )
    x4, cot, w_qkv, wi, wu, wo, vecs, q4, k4, v4, c4, c_r, lse = front_call(
        lengths,
        inputs,
        cotangent,
        query_weight,
        key_weight,
        value_weight,
        vecs,
        out_weight,
        inner_weight,
        outer_weight,
        n,
    )
    xall = x4.reshape(2 * rows, width)
    ctx, cr = c4.reshape(2 * rows, hw), c_r.reshape(rows, hw)
    two = (2, sh, part, hw)
    lo, act, dout, dinn, nrm, dattn, dfirst, dco, dcs, acc = ffn_call(
        ids, lengths, sh, ctx, cr, xall, cot.reshape(rows, width), vecs, wo, wi, wu
    )

    def give_back(a):
        mine, theirs = a[0], swap(a[1], 2, 0)
        return jnp.concatenate(pick(x, mine, theirs), 0)

    layer_out = give_back(lo.reshape(2, sh, part, width))

    g_r = swap(dcs, 1, 0)

    def total(*items):
        out = items[0].astype(F32)
        for i in items[1:]:
            out = out + i.astype(F32)
        return out.astype(BF)

    def reduce_quarter(keep, send):
        got = swap(send, 1, 0)
        away = total(keep[1], got[1])
        near = total(keep[0], got[0])
        got = swap(away, 2, 0)
        away = total(near[1], got[1])
        near = total(near[0], got[0])
        got = swap(away, 0, 1)
        away = [total(near[a], got[a]) for a in range(A)]
        mine = total(away[0], *[swap(away[a], 0, 2 * a) for a in range(1, A)])
        other = swap(mine, 2, 0)
        quarters = [mine, swap(mine, 1, 0), other, swap(other, 1, 0)]
        return [a.astype(F32) for a in xor_order(quarters, C)]

    ku, su = outer_grad_call(ids, act, dout, n)
    ki, si = inner_grad_call(ids, nrm, dinn, n)
    ko, so = out_grad_call(ids, ctx, cr, dattn, n)
    grad_outer = jnp.concatenate(reduce_quarter(ku, su), 0)
    grad_inner = jnp.concatenate(reduce_quarter(ki, si), 1)
    grad_out = jnp.concatenate(reduce_quarter(ko, so), 0)

    dq, dk, dv = attend_back_call(
        ids, lengths, q4, k4, v4, lse, c4, dco.reshape(two), g_r.reshape(two)
    )
    flat3 = (2, rows, hw)
    dq, dk, dv = dq.reshape(flat3), dk.reshape(flat3), dv.reshape(flat3)

    def reduce_half(g):
        got = swap(g[1], 0, 1)
        away = [total(g[0, a], got[a]) for a in range(A)]
        mine = total(away[0], *[swap(away[a], 0, 2 * a) for a in range(1, A)])
        mine = total(mine, swap(mine, 2, 0))
        return jnp.concatenate(pick(core, mine, swap(mine, 1, 0)), 1).astype(F32)

    gq, bq = qkv_grad_call(ids, xall, dq, n)
    gk, _ = qkv_grad_call(ids, xall, dk, n)
    gv, bv = qkv_grad_call(ids, xall, dv, n)
    grad_query, grad_key, grad_value = reduce_half(gq), reduce_half(gk), reduce_half(gv)

    halves = jnp.concatenate([bq[:1], bv[:1], jnp.zeros((14, hw), F32)], 0)
    none = jnp.zeros_like(halves)
    sums = acc + jnp.concatenate(pick(core, halves, none), 1)
    for dc, df in [(1, 0), (2, 0)] + [(0, 1 << b) for b in range(n.bit_length() - 1)]:
        sums = sums + swap(sums, dc, df)
    own = lax.dynamic_slice_in_dim(sums[:8], f * rs, rs, 1)
    own_inner = lax.dynamic_slice_in_dim(sums[8 : 8 + ff // width].reshape(ff), f * ro, ro, 0)

    theirs = back_project_call(1, dq, dk, dv, w_qkv)
    from_core = swap(theirs, 1, 0)
    own_part = back_project_call(0, dq, dk, dv, w_qkv)
    full = (dfirst + own_part + from_core).reshape(2, sh, part, width)
    away = swap(full[1].astype(BF), 2, 0).astype(F32)
    input_grad = jnp.concatenate(pick(x, full[0], away), 0)

    return (
        layer_out,
        input_grad,
        grad_query,
        grad_key,
        grad_value,
        grad_out,
        grad_inner,
        grad_outer,
        own[0],
        own[1],
        own[2],
        own_inner,
        own[3],
        own[4],
        own[5],
        own[6],
        own[7],
    )


def solution(mesh):
    rowed = P("fsdp", "ctx", None)
    matrix, vector = P("fsdp", None), P("fsdp")
    in_specs = (rowed, vector, rowed) + (matrix,) * 6 + (vector,) * 9
    out_specs = (rowed, rowed) + (matrix,) * 6 + (vector,) * 9
    return jax.shard_map(
        per_device, mesh=mesh, in_specs=in_specs, out_specs=out_specs, check_vma=False
    )
```

```python
import functools

import jax
import jax.numpy as jnp
from jax import lax
from jax.experimental import pallas as pl
from jax.experimental.pallas import tpu as pltpu
from jax.sharding import PartitionSpec as P

HD = 64
EPSILON = 1e-05
BF = jnp.bfloat16
F32 = jnp.float32
ANY = pl.BlockSpec(memory_space=pl.ANY)
NT = (((1,), (1,)), ((), ()))
TN = (((0,), (0,)), ((), ()))
VMEM_LIMIT = 58 << 20
BACK_LIMIT = 60 << 20


def dot(a, b):
    return jnp.dot(a, b, preferred_element_type=F32)


def dot_nt(a, b):
    return lax.dot_general(a, b, NT, preferred_element_type=F32)


def dot_tn(a, b):
    return lax.dot_general(a, b, TN, preferred_element_type=F32)


def params(**more):
    return pltpu.CompilerParams(vmem_limit_bytes=VMEM_LIMIT, **more)


def cost(flops, size, trans=0):
    return pl.CostEstimate(flops=int(flops), bytes_accessed=int(size), transcendentals=int(trans))


MESH = pl.DeviceIdType.MESH
PACK = 16


def flip(v, mask):
    out, bit = v, 1
    while bit <= mask:
        if mask & bit:
            out = out + bit - 2 * bit * ((v // bit) % 2)
        bit *= 2
    return out


def at(index, size):
    return pl.ds(pl.multiple_of(index * size, size), size)


def spread(read, n, rs):
    per = max(128 // rs, 1)
    tiles = []
    for t in range(n // per):
        tile = read(t * per)
        for u in range(1, per):
            tile = tile + pltpu.roll(read(t * per + u), u * rs, 1)
        tiles.append(tile)
    return jnp.concatenate(tiles, 1)


def front_kernel(
    n,
    lens,
    xin,
    cin,
    wq,
    wk,
    wv,
    vecs,
    wo_in,
    wi_in,
    wu_in,
    xo,
    co,
    wqkvo,
    wio,
    wuo,
    woo,
    veco,
    qo,
    ko,
    vo,
    cxo,
    cro,
    lseo,
    X,
    W,
    VEC,
    Q,
    K,
    V,
    CX,
    LSE,
    lsem,
    ssem,
    rsem,
):
    C, f = lax.axis_index("ctx"), lax.axis_index("fsdp")
    x, core = C // 2, C % 2
    A = n // 2
    sh, part, width = X.shape[1:]
    hw = W.shape[2]
    ff = wio.shape[1]
    rs, ro, cq = width // n, ff // n, ff // 4

    partners = [(0, 2 * k) for k in range(1, A)] + [(0, 1), (2, 0), (1, 0)]

    def device(dc, df):
        return (flip(C, dc), flip(f, df))

    barrier = pltpu.get_barrier_semaphore()
    for p in partners:
        pl.semaphore_signal(barrier, inc=1, device_id=device(*p), device_id_type=MESH)

    local = []
    used = iter(range(lsem.shape[0]))

    def begin(source, target):
        c = pltpu.make_async_copy(source, target, lsem.at[next(used)])
        c.start()
        return c

    def keep(source, target):
        local.append(begin(source, target))

    x_here = begin(xin.at[pl.ds(x * sh, sh)], X.at[0])
    w_here = [begin(w.at[:, at(core, hw)], W.at[j, at(f, rs)]) for j, w in enumerate((wq, wk, wv))]
    w_here.append(begin(vecs, VEC.at[f]))

    pl.semaphore_wait(barrier, len(partners))

    def remote(source, target, sem, dev):
        return pltpu.make_async_remote_copy(
            src_ref=source,
            dst_ref=target,
            send_sem=ssem.at[sem],
            recv_sem=rsem.at[sem],
            device_id=device(*dev),
            device_id_type=MESH,
        )

    sent = []

    def send(*what):
        c = remote(*what)
        c.start()
        sent.append(c)

    seen = set()

    def arrive(target, sem, dev):
        if sem not in seen:
            seen.add(sem)
            remote(target, target, sem, dev).wait_recv()

    base_x = 12 * n + 4 * n
    X1, X2, X3, COT, CTX = (base_x + i for i in range(5))
    send(xin.at[pl.ds((1 - x) * sh, sh)], X.at[1], X1, (2, 0))

    def qkv_slot(i):
        s = flip(f, i)
        return [W.at[j, at(s, rs)] for j in range(3)] + [VEC.at[s]]

    def qkv_sem(i):
        return [12 * n + 4 * i + j for j in range(4)]

    own_qkv = [w.at[:, at(core, hw)] for w in (wq, wk, wv)] + [vecs]

    def qkv_give(tag, source_piece, source, dev):
        place = qkv_slot(source_piece)
        for j in range(4):
            send(source[j], place[j], qkv_sem(tag)[j], dev)

    def qkv_need(i):
        dev = (0, i) if i % 2 == 0 else (0, 1)
        place = qkv_slot(i)
        for j in range(4):
            arrive(place[j], qkv_sem(i)[j], dev)

    for k in range(1, A):
        qkv_give(2 * k, 0, own_qkv, (0, 2 * k))
    qkv_give(1, 0, own_qkv, (0, 1))
    x_here.wait()
    send(X.at[0], X.at[2], X2, (1, 0))

    def rest_slot(e, i):
        qq, s = flip(C, e), flip(f, i)
        return [
            woo.at[pl.ds(pl.multiple_of(s * rs + qq * (rs // 4), rs // 4), rs // 4)],
            wio.at[at(s, rs), at(qq, cq)],
            wuo.at[pl.ds(pl.multiple_of(s * ro + qq * (ro // 4), ro // 4), ro // 4)],
        ]

    def rest_sem(e, i):
        return [(e * n + i) * 3 + kind for kind in range(3)]

    def route(e, i):
        if e % 2:
            return (1, 0), (e - 1, i)
        if e:
            return (2, 0), (0, i)
        if i % 2:
            return (0, 1), (0, i - 1)
        return (0, i), (0, 0)

    def rest_copies(e, i):
        dev, (pe, pi) = route(e, i)
        place = rest_slot(pe, pi)
        source = [wo_in.at[at(C, rs // 4)], wi_in.at[:, at(C, cq)], wu_in.at[at(C, ro // 4)]]
        source = source if pi == 0 else place
        sems = rest_sem(e, i)
        return [remote(source[kind], place[kind], sems[kind], dev) for kind in range(3)]

    def rest_send(e, i):
        for c in rest_copies(e, i):
            c.start()

    def rest_need(e, i):
        dev, _ = route(e, i)
        place = rest_slot(e, i)
        for kind in range(3):
            arrive(place[kind], rest_sem(e, i)[kind], dev)

    def rest_hand_on(e, i):
        rest_need(e, i)
        if e == 0 and i % 2 == 0:
            rest_send(0, i + 1)
        if e == 0:
            rest_send(2, i)
        if e % 2 == 0:
            rest_send(e + 1, i)

    for k in range(1, A):
        qkv_need(2 * k)
        qkv_give(2 * k + 1, 2 * k, qkv_slot(2 * k), (0, 1))
    for k in range(1, A):
        rest_send(0, 2 * k)
    arrive(X.at[1], X1, (2, 0))
    send(X.at[1], X.at[3], X3, (1, 0))
    send(cin.at[pl.ds((1 - x) * sh, sh)], co.at[1], COT, (2, 0))
    rest_send(0, 1)
    keep(cin.at[pl.ds(x * sh, sh)], co.at[0])
    keep(wo_in, woo.at[at(f, rs)])
    keep(wi_in, wio.at[at(f, rs)])
    keep(wu_in, wuo.at[at(f, ro)])
    for c in w_here:
        c.wait()
    for i in range(1, n):
        qkv_need(i)
    arrive(X.at[2], X2, (1, 0))
    arrive(X.at[3], X3, (1, 0))
    keep(X, xo)
    keep(W, wqkvo)
    keep(VEC, veco)

    jobs = [(0, 1)] + [(0, i) for i in range(2, n, 2)] + [(2, 1)]
    jobs += [(0, i) for i in range(3, n, 2)] + [(2, i) for i in range(2, n)]
    slots = X.shape[0]
    pairs = hw // (2 * HD)
    steps = slots + sh * pairs
    plan = [jobs[len(jobs) * t // steps : len(jobs) * (t + 1) // steps] for t in range(steps)]

    def serve(step, base, count):
        for t in range(count):
            if plan[base + t]:

                @pl.when(step == t)
                def _():
                    for job in plan[base + t]:
                        rest_hand_on(*job)

    def bias(row):
        read = lambda s: VEC[pl.ds(core * (n // 2) + s, 1), row : row + 1, :128].reshape(1, 128).astype(F32)
        return spread(read, n // 2, rs)

    bias_q, bias_v = bias(0), bias(1)

    def project(slot, carry):
        a = X[slot].reshape(sh * part, width)
        shape = (sh, part, hw)
        Q[slot] = (dot(a, W[0]) + bias_q).astype(BF).reshape(shape)
        K[slot] = dot(a, W[1]).astype(BF).reshape(shape)
        V[slot] = (dot(a, W[2]) + bias_v).astype(BF).reshape(shape)
        serve(slot, 0, slots)
        return carry

    lax.fori_loop(0, slots, project, 0)
    keep(Q, qo)
    keep(K, ko)
    keep(V, vo)

    def attend(step, carry):
        s, pair = step // pairs, step % pairs
        cols = at(pair, 2 * HD)

        def load(ref):
            return ref[:, s, :, cols].reshape(slots * part, 2 * HD)

        q, k, v = load(Q), load(K), load(V)
        mask = key_mask(lens[x * sh + s], C, part)
        o, lse = attend_pair(q, k, v, mask)
        CX[:, s, :, cols] = o.reshape(slots, part, 2 * HD)
        LSE[s, :, cols] = lse
        serve(step, slots, sh * pairs)
        return carry

    lax.fori_loop(0, sh * pairs, attend, 0)
    send(CX.at[pl.ds(2, 2)], cro, CTX, (1, 0))
    keep(CX, cxo)
    keep(LSE, lseo)
    for e in range(4):
        for i in range(1, n):
            rest_need(e, i)
            for c in rest_copies(e, i):
                c.wait_send()
    arrive(co.at[1], COT, (2, 0))
    arrive(cro, CTX, (1, 0))
    for c in sent:
        c.wait_send()
    for c in local:
        c.wait()


def front_call(lengths, xin, cin, wq, wk, wv, vecs, wo, wi, wu, n):
    seqs, part, width = xin.shape
    sh, ff, hw = seqs // 2, wi.shape[1], width // 2

    def bf(*shape):
        return jax.ShapeDtypeStruct(shape, BF)

    def vm(*shape):
        return pltpu.VMEM(shape, BF)

    full = 4 * part
    lse = (sh, full, hw)
    four = (4, sh, part, hw)
    sems = 16 * n + 5
    return pl.pallas_call(
        functools.partial(front_kernel, n),
        in_specs=[pl.BlockSpec(memory_space=pltpu.SMEM)] + [ANY] * 9,
        out_specs=[ANY] * 13,
        out_shape=[
            bf(4, sh, part, width),
            bf(2, sh, part, width),
            bf(3, width, hw),
            bf(width, ff),
            bf(ff, width),
            bf(width, width),
            bf(n, PACK, hw),
            bf(*four),
            bf(*four),
            bf(*four),
            bf(*four),
            bf(2, sh, part, hw),
            jax.ShapeDtypeStruct(lse, F32),
        ],
        scratch_shapes=[
            vm(4, sh, part, width),
            vm(3, width, hw),
            vm(n, PACK, hw),
            vm(*four),
            vm(*four),
            vm(*four),
            vm(*four),
            pltpu.VMEM(lse, F32),
            pltpu.SemaphoreType.DMA((24,)),
            pltpu.SemaphoreType.DMA((sems,)),
            pltpu.SemaphoreType.DMA((sems,)),
        ],
        compiler_params=params(collective_id=0, has_side_effects=True),
        name="front",
    )(lengths, xin, cin, wq, wk, wv, vecs, wo, wi, wu)


def lanes_of(shape, head):
    lane = lax.broadcasted_iota(jnp.int32, shape, 1)
    own = (lane < HD) if head == 0 else (lane >= HD)
    return lane, own, (HD if head == 0 else 0)


def split3(a):
    hi = a.astype(BF).astype(F32)
    mid = (a - hi).astype(BF).astype(F32)
    return hi, mid, a - hi - mid


def flat(ref):
    a = ref[...]
    return a.reshape(-1, a.shape[-1])


def key_mask(length, C, part):
    row = lax.broadcasted_iota(jnp.int32, (part, 2 * HD), 0)
    out = []
    for e in (0, 2, 1, 3):
        inside = row + flip(C, e) * part < length
        out.append(jnp.where(inside, 0.0, -1e30).astype(BF))
    return jnp.concatenate(out, 0)


def attend_pair(q, k, v, mask):
    out = []
    for head in range(2):
        lane, own, other = lanes_of(q.shape, head)
        qh = jnp.where(own, q * BF(HD**-0.5), jnp.where(lane == other, 1.0, 0.0).astype(BF))
        kh = jnp.where(own, k, mask)
        s = dot_nt(qh, kh)
        top = jnp.max(s, -1, keepdims=True)
        e = jnp.exp(s - top)
        total = jnp.sum(e, -1, keepdims=True)
        o = dot(e.astype(BF), v) * (1.0 / total)
        out.append((o, top + jnp.log(total), own))
    (o0, l0, own), (o1, l1, _) = out
    return jnp.where(own, o0, o1).astype(BF), jnp.where(own, l1, l0)


def attend_back_pair(q, k, v, mask, lse, c, g):
    qs = q * BF(HD**-0.5)
    kt = k.T
    prod = c.astype(F32) * g.astype(F32)
    res = []
    for head in range(2):
        lane, own, o = lanes_of(q.shape, head)
        hi, mid, low = split3(-lse)
        extra = jnp.where(
            lane == o,
            1.0,
            jnp.where(
                lane == o + 1,
                hi,
                jnp.where(lane == o + 2, mid, jnp.where(lane == o + 3, low, 0.0)),
            ),
        ).astype(BF)
        qh = jnp.where(own, qs, extra)
        kh = jnp.where(own, k, jnp.where(lane == o, mask, BF(1)))
        p = jnp.exp(dot_nt(kh, qh))
        delta = jnp.sum(jnp.where(own, prod, 0.0), -1, keepdims=True)
        hi, mid, low = split3(-delta)
        extra = jnp.where(
            lane == o, hi, jnp.where(lane == o + 1, mid, jnp.where(lane == o + 2, low, 0.0))
        ).astype(BF)
        gh = jnp.where(own, g, extra)
        vh = jnp.where(own, v, BF(1))
        ds = (p * dot_nt(vh, gh)).astype(BF)
        dv = dot(p.astype(BF), g)
        dk = dot(ds, qs)
        dqt = dot(kt, ds)
        res.append((dv, dk, dqt, own))
    (dv0, dk0, dq0, own), (dv1, dk1, dq1, _) = res
    dqt = jnp.concatenate([dq0[:HD], dq1[HD:]], 0) * (HD**-0.5)
    return dqt.T.astype(BF), jnp.where(own, dk0, dk1).astype(BF), jnp.where(own, dv0, dv1).astype(BF)


def gelu_pair(u):
    e = jnp.exp(u * u * -0.5)
    t = 1.0 / (1.0 + (0.3275911 * 0.7071067811865476) * jnp.abs(u))
    poly = t * (
        0.254829592 * 0.5
        + t
        * (
            -0.284496736 * 0.5
            + t * (1.421413741 * 0.5 + t * (-1.453152027 * 0.5 + t * (1.061405429 * 0.5)))
        )
    )
    tail = poly * e
    cdf = jnp.where(u >= 0, 1.0 - tail, tail)
    ucdf = u * cdf
    return ucdf, cdf + u * (e * 0.3989422804014327)


def normalise(h):
    c = h - jnp.mean(h, -1, keepdims=True)
    r = lax.rsqrt(jnp.mean(c * c, -1, keepdims=True) + EPSILON)
    return c * r, r


def normalise_back(dyg, hat, r):
    return r * (
        dyg - jnp.mean(dyg, -1, keepdims=True) - hat * jnp.mean(dyg * hat, -1, keepdims=True)
    )


def ffn_kernel(n, sh, part, ids, lens, cm, cr, xm, cot, vecs, wo_in, wi_in, wu_in, *refs):
    lo, act, dout, dinn, nrm, dattn, dfirst, dco, dcs, acc = refs[:10]
    wo, wi, wu, gp, vec, ib, sem = refs[10:]
    width, ff = wi.shape
    core = ids[0] % 2
    step = pl.program_id(0)
    rs, ro = width // n, ff // n
    cq, hw = ff // 4, width // 2

    pairs = ((wo_in, wo), (wi_in, wi), (wu_in, wu))

    def copy(kind):
        return pltpu.make_async_copy(*pairs[kind], sem.at[kind])

    @pl.when(step == 0)
    def _():
        for kind in range(3):
            copy(kind).start()
        acc[...] = jnp.zeros_like(acc)
        vec[...] = spread(lambda s: vecs[s, :8, :128].astype(F32), n, rs)
        for s in range(n):
            ib[:, s * ro : (s + 1) * ro] = vecs[s, 8:9, :ro].astype(F32)

    def arrived(kind):
        @pl.when(step == 0)
        def _():
            copy(kind).wait()

    count = xm.shape[0] // part
    inside = []
    for u in range(count):
        slot = step * count + u
        ex, s = slot // sh, slot % sh
        first = (ids[0] ^ (2 * ex)) * part
        row = lax.broadcasted_iota(jnp.int32, (part, 1), 0) + first
        inside.append(jnp.where(row < lens[(ids[0] // 2) * sh + s], 1.0, 0.0))
    valid = jnp.concatenate(inside, 0)
    own, other = at(core, hw), at(1 - core, hw)

    def add(row, value):
        acc[row : row + 1, :] += jnp.sum(value, 0, keepdims=True)

    arrived(0)
    first = (
        xm[...].astype(F32) + (dot(cm[...], wo[own]) + dot(cr[...], wo[other])) + vec[2:3, :]
    )
    hat1, r1 = normalise(first)
    normed = hat1 * vec[4:5, :] + vec[5:6, :]
    low = normed.astype(BF)
    nrm[...] = low
    arrived(1)
    for j in range(4):
        cols = slice(j * cq, (j + 1) * cq)
        g, d = gelu_pair(dot(low, wi[:, cols]) + ib[:, cols])
        act[:, cols] = g.astype(BF)
        gp[:, cols] = d
    arrived(2)
    second = normed + (dot(act[...], wu[...]) + vec[3:4, :])
    hat2, r2 = normalise(second)
    lo[...] = (hat2 * vec[6:7, :] + vec[7:8, :]).astype(BF)
    og = cot[...].astype(F32) * valid
    add(6, og * hat2)
    add(7, og)
    d2 = normalise_back(og * vec[6:7, :], hat2, r2)
    d2low = d2.astype(BF)
    dout[...] = d2low
    add(3, d2low.astype(F32))
    for j in range(4):
        cols = slice(j * cq, (j + 1) * cq)
        di = (dot_nt(d2low, wu[cols, :]) * gp[:, cols]).astype(BF)
        dinn[:, cols] = di
        add(8 + j, di.astype(F32))
    dn = d2 + dot_nt(dinn[...], wi[...])
    add(4, dn * hat1)
    add(5, dn)
    d1 = normalise_back(dn * vec[4:5, :], hat1, r1)
    dfirst[...] = d1
    d1low = d1.astype(BF)
    dattn[...] = d1low
    add(2, d1low.astype(F32))
    dco[...] = dot_nt(d1low, wo[own]).astype(BF)
    dcs[...] = dot_nt(d1low, wo[other]).astype(BF)


def ffn_call(ids, lens, sh, c, cr, xall, cot, vecs, wo, wi, wu):
    width, ff = wi.shape
    n, rows = vecs.shape[0], cot.shape[0]
    block = rows // 3
    hw = width // 2

    def by(cols):
        return pl.BlockSpec((block, cols), lambda i, *_: (i, 0))

    def whole(*shape):
        return pl.BlockSpec(shape, lambda i, *_: (0,) * len(shape))

    grid_spec = pltpu.PrefetchScalarGridSpec(
        num_scalar_prefetch=2,
        grid=(3,),
        in_specs=[by(hw), by(hw), by(width), by(width), whole(*vecs.shape), ANY, ANY, ANY],
        out_specs=[
            by(width),
            by(ff),
            by(width),
            by(ff),
            by(width),
            by(width),
            by(width),
            by(hw),
            by(hw),
            whole(16, width),
        ],
        scratch_shapes=[
            pltpu.VMEM((width, width), BF),
            pltpu.VMEM((width, ff), BF),
            pltpu.VMEM((ff, width), BF),
            pltpu.VMEM((block, ff), F32),
            pltpu.VMEM((8, width), F32),
            pltpu.VMEM((1, ff), F32),
            pltpu.SemaphoreType.DMA((3,)),
        ],
    )

    def shape(cols, dtype=BF):
        return jax.ShapeDtypeStruct((rows, cols), dtype)

    return pl.pallas_call(
        functools.partial(ffn_kernel, n, sh, rows // (2 * sh)),
        grid_spec=grid_spec,
        out_shape=[
            shape(width),
            shape(ff),
            shape(width),
            shape(ff),
            shape(width),
            shape(width),
            shape(width, F32),
            shape(hw),
            shape(hw),
            jax.ShapeDtypeStruct((16, width), F32),
        ],
        compiler_params=params(),
        cost_estimate=cost(
            2 * rows * width * (2 * width + 4 * ff), 30 * rows * width + 2 * width * (2 * ff + width)
        ),
        name="ffn",
    )(ids, lens, c, cr, xall, cot, vecs, wo, wi, wu)


def xor(a, b, count):
    out, bit = 0, 1
    while bit < count:
        out = out + bit * ((a // bit + b // bit) % 2)
        bit *= 2
    return out


def plus(*items):
    out = items[0].astype(F32)
    for i in items[1:]:
        out = out + i.astype(F32)
    return out.astype(BF)


class Plan:
    def __init__(self):
        self.jobs = []

    def add(self, time, job):
        self.jobs.append((time, len(self.jobs), job))
        self.jobs.sort(key=lambda j: j[:2])

    def due(self, time):
        out = [j[2] for j in self.jobs if j[0] <= time]
        self.jobs = [j for j in self.jobs if j[0] > time]
        return out

    def beside(self, step, times):
        for t, time in enumerate(times):
            jobs = self.due(time)
            if jobs:

                @pl.when(step == t)
                def _():
                    for job in jobs:
                        job()


def back_kernel(
    n,
    lens,
    act,
    dout,
    nrm,
    dinn,
    dattn,
    ctx,
    ctx2,
    cr,
    xall,
    q_in,
    k_in,
    v_in,
    lse_in,
    dco,
    dcs,
    dfirst,
    w_in,
    lo,
    acc,
    o_lo,
    o_igl,
    o_igr,
    o_i,
    o_u,
    o_o,
    o_q,
    o_k,
    o_v,
    o_vec,
    act_s,
    ig_s,
    Q,
    K,
    V,
    CX,
    G,
    LSE,
    L,
    D,
    DO,
    DA,
    CO,
    W,
    PI,
    PU,
    PO,
    PQ,
    RYI,
    RZI,
    MI,
    RXI,
    RXU,
    RYU,
    RZU,
    MU,
    RYO,
    RZO,
    MO,
    RXO,
    RYQ,
    RZQ,
    MQ,
    RXQ,
    VS,
    VR,
    SB,
    IB,
    XS,
    lsem,
    ssem,
    rsem,
):
    C, f = lax.axis_index("ctx"), lax.axis_index("fsdp")
    x, core = C // 2, C % 2
    A = n // 2
    slots, sh, part, hw = Q.shape
    rows, width = nrm.shape
    ff = act.shape[1]
    rs, ro, cq, wq = width // n, ff // n, ff // 4, width // 4
    half_rows = rows // 2
    CORE, NEAR, Y = (1, 0), (2, 0), (0, 1)

    def device(dc, df):
        return (flip(C, dc), flip(f, df))

    partners = [(0, 2 * k) for k in range(1, A)] + [Y, NEAR, CORE]
    barrier = pltpu.get_barrier_semaphore()
    for p in partners:
        pl.semaphore_signal(barrier, inc=1, device_id=device(*p), device_id_type=MESH)

    locals_free = iter(range(lsem.shape[0]))
    remotes_free = iter(range(ssem.shape[0]))

    def local(make):
        sem = next(locals_free)
        return lambda: pltpu.make_async_copy(*make(), lsem.at[sem])

    def remote_at(dev, sem, make):
        source, target = make()
        return pltpu.make_async_remote_copy(
            src_ref=source,
            dst_ref=target,
            send_sem=ssem.at[sem],
            recv_sem=rsem.at[sem],
            device_id=device(*dev),
            device_id_type=MESH,
        )

    def remote(dev, make):
        sem = next(remotes_free)
        return lambda: remote_at(dev, sem, make)

    ends = []

    def go(build):
        build().start()
        ends.append(lambda: build().wait_send())

    def go_local(make):
        build = local(make)
        build().start()
        ends.append(lambda: build().wait())

    loads = {}

    def load(name, make):
        loads[name] = local(make)
        loads[name]().start()

    def need(*names):
        for name in names:
            loads.pop(name)().wait()

    load("q", lambda: (q_in, Q))
    load("k", lambda: (k_in, K))
    load("v", lambda: (v_in, V))
    load("c", lambda: (ctx, CX))
    load("g", lambda: (dco, G.at[pl.ds(0, 2)]))
    for s in range(2):
        load(("lse", s), lambda s=s: (lse_in.at[s], LSE.at[s]))
    load("nrm", lambda: (nrm, L.at[0]))
    load("vec", lambda: (acc, VS.at[0]))

    def quarters(ref, size, ex, ec):
        return ref.at[:, at(flip(C, 2 * ex + ec), size)]

    for ex in range(2):
        load(("dinn", ex), lambda ex=ex: (quarters(dinn, cq, ex, 0), D.at[ex, 0]))

    pl.semaphore_wait(barrier, len(partners))

    g_swap = remote(CORE, lambda: (dcs, G.at[pl.ds(2, 2)]))
    go(g_swap)
    lo_swap = remote(NEAR, lambda: (lo.at[1], o_lo.at[pl.ds(x * sh, sh)]))
    go(lo_swap)
    go_local(lambda: (lo.at[0], o_lo.at[pl.ds(x * sh, sh)]))
    nrm_swap = remote(CORE, lambda: (nrm, L.at[1]))
    go(nrm_swap)
    dinn_swap = [
        remote(CORE, lambda ex=ex: (quarters(dinn, cq, ex, 1), D.at[ex, 1])) for ex in range(2)
    ]
    go(dinn_swap[0])
    go(dinn_swap[1])

    for ex in range(2):
        load(
            ("dout", ex),
            lambda ex=ex: (quarters(dout, wq, ex, 0), DO.at[0, :, pl.ds(ex * wq, wq)]),
        )
        load(
            ("dattn", ex),
            lambda ex=ex: (quarters(dattn, wq, ex, 0), DA.at[0, :, pl.ds(ex * wq, wq)]),
        )
    load("co", lambda: (cr, CO.at[0]))
    load("w", lambda: (w_in, W))

    chunks = ff // 1024
    per = 1024 // ro

    def act_cols(t):
        return at(xor(f // per, t, chunks), 1024)

    dout_swap = [
        remote(
            CORE, lambda ex=ex: (quarters(dout, wq, ex, 1), DO.at[1, :, pl.ds(ex * wq, wq)])
        )
        for ex in range(2)
    ]
    act_swap = [
        remote(CORE, lambda t=t: (act.at[:, act_cols(t)], act_s.at[:, act_cols(t)]))
        for t in range(chunks)
    ]
    ctx_swap = remote(CORE, lambda: (ctx2.at[pl.ds(0, rows)], CO.at[1]))
    dattn_swap = [
        remote(
            CORE, lambda ex=ex: (quarters(dattn, wq, ex, 1), DA.at[1, :, pl.ds(ex * wq, wq)])
        )
        for ex in range(2)
    ]
    need("q", "k", "v", "c", "g")
    g_swap().wait_recv()
    for build in dout_swap + act_swap + [ctx_swap] + dattn_swap:
        go(build)

    class Unit:
        def __init__(self, P, RY, RZ, M):
            self.P, self.RY, self.RZ, self.M = P, RY, RZ, M
            self.y = [
                remote(Y, lambda a=a: (P.at[1, a], RY.at[a])) for a in range(A)
            ]
            self.z = [None] + [
                remote((0, 2 * a), lambda a=a: (P.at[0, a], RZ.at[a - 1])) for a in range(1, A)
            ]

        def start_y(self, a=None):
            for i in order if a is None else [a]:
                go(self.y[i])

        def fold_y(self, a):
            self.y[a]().wait_recv()
            self.P[0, a] = plus(self.P[0, a], self.RY[a])
            if a:
                go(self.z[a])

        def fold_z(self):
            for a in range(1, A):
                self.z[a]().wait_recv()
            self.M[...] = plus(self.P[0, 0], *[self.RZ[a - 1] for a in range(1, A)])

    order = list(range(1, A)) + [0]
    UI = [Unit(PI.at[ex], RYI.at[ex], RZI.at[ex], MI.at[ex]) for ex in range(2)]
    UU = Unit(PU.at[0], RYU, RZU, MU)
    UO = Unit(PO, RYO, RZO, MO)
    UQ = [Unit(PQ.at[j], RYQ.at[j], RZQ.at[j], MQ.at[j]) for j in range(3)]
    plan = Plan()

    xi = [remote(NEAR, lambda ex=ex: (MI.at[ex], RXI.at[ex])) for ex in range(2)]

    def inner_z(ex):
        UI[ex].fold_z()
        go(xi[ex])

    def cols_of(ref, e, size):
        return ref.at[:, at(flip(C, e), size)]

    i_core = [
        remote(CORE, lambda ex=ex: (RXI.at[1 - ex], cols_of(o_i, 2 * ex, cq))) for ex in range(2)
    ]

    def inner_x():
        for ex in range(2):
            xi[1 - ex]().wait_recv()
            RXI[1 - ex] = plus(MI[ex], RXI[1 - ex])
            go(i_core[ex])
            go_local(lambda ex=ex: (RXI.at[1 - ex], cols_of(o_i, 2 * ex, cq)))

    x_base = [next(remotes_free) for _ in range(n)][0]

    def outer_copy(i):
        return remote_at(NEAR, x_base + i, lambda: (PU.at[1, i % 2, i // 2], RXU.at[i % 2, i // 2]))

    def outer_x(i):
        outer_copy(i).wait_recv()
        PU[0, i % 2, i // 2] = plus(PU[0, i % 2, i // 2], RXU[i % 2, i // 2])
        if i % 2:
            UU.start_y(i // 2)

    u_near = remote(NEAR, lambda: (MU, cols_of(o_u, 0, wq)))
    u_core = remote(CORE, lambda: (MU, cols_of(o_u, 0, wq)))
    u_core2 = remote(CORE, lambda: (cols_of(o_u, 2, wq), cols_of(o_u, 2, wq)))

    def outer_z():
        UU.fold_z()
        go(u_near)
        go(u_core)
        go_local(lambda: (MU, cols_of(o_u, 0, wq)))

    def outer_end():
        u_near().wait_recv()
        go(u_core2)

    xo = remote(NEAR, lambda: (MO, RXO))
    o_core = [
        remote(
            CORE, lambda ex=ex: (RXO.at[pl.ds((1 - ex) * rs, rs)], cols_of(o_o, 2 * ex, wq))
        )
        for ex in range(2)
    ]

    def out_z():
        UO.fold_z()
        go(xo)

    def out_x():
        xo().wait_recv()
        for ex in range(2):
            mine, theirs = pl.ds(ex * rs, rs), pl.ds((1 - ex) * rs, rs)
            RXO[theirs] = plus(MO[mine], RXO[theirs])
            go(o_core[ex])
            go_local(
                lambda ex=ex: (RXO.at[pl.ds((1 - ex) * rs, rs)], cols_of(o_o, 2 * ex, wq))
            )

    outs = (o_q, o_k, o_v)
    xq = [remote(NEAR, lambda j=j: (MQ.at[j], RXQ.at[j])) for j in range(3)]
    q_core = [
        remote(CORE, lambda j=j: (RXQ.at[j], outs[j].at[:, at(core, hw)])) for j in range(3)
    ]

    def proj_z(j):
        UQ[j].fold_z()
        go(xq[j])

    def proj_x(j):
        xq[j]().wait_recv()
        RXQ[j] = plus(MQ[j], RXQ[j])
        go(q_core[j])
        go_local(lambda: (RXQ.at[j], outs[j].at[:, at(core, hw)]))

    hops = [CORE, NEAR] + [(0, 1 << b) for b in range(n.bit_length() - 1)]
    hop_copies = [
        remote(dev, lambda t=t: (VS.at[t], VR.at[t])) for t, dev in enumerate(hops)
    ]

    def vector_hop(t):
        if t:
            hop_copies[t - 1]().wait_recv()
            VS[t] = VS[t - 1] + VR[t - 1]
        if t < len(hops):
            go(hop_copies[t])
        else:
            go_local(lambda: (VS.at[t], o_vec))

    pairs = hw // (2 * HD)

    def attention(s, times):
        need(("lse", s))

        def body(step, carry):
            cols = at(step, 2 * HD)

            def get(ref):
                return ref[:, s, :, cols].reshape(slots * part, 2 * HD)

            mask = key_mask(lens[x * sh + s], C, part)
            dq, dk, dv = attend_back_pair(
                get(Q), get(K), get(V), mask, LSE[s % 2, :, cols], get(CX), get(G)
            )
            for ref, value in ((Q, dq), (K, dk), (V, dv)):
                ref[:, s, :, cols] = value.reshape(slots, part, 2 * HD)
            plan.beside(step, times)
            return carry

        lax.fori_loop(0, pairs, body, 0)
        if s + 2 < sh:
            load(("lse", s + 2), lambda: (lse_in.at[s + 2], LSE.at[s % 2]))

    groups = width // 256
    gsz = 256 // rs

    def weight_grad(get, P, times):
        def body(a, carry):
            cols = at(xor(f // gsz, a, groups), 256)
            r = (dot_tn(L[0, :, cols], get(0)) + dot_tn(L[1, :, cols], get(1))).astype(BF)
            for u in range(gsz):
                i = a * gsz + flip(f % gsz, u) if gsz > 1 else a
                P[i % 2, i // 2] = r[u * rs : (u + 1) * rs]
            plan.beside(a, times)
            return carry

        lax.fori_loop(0, groups, body, 0)

    def spaced(first, last, count):
        return [first + (last - first) * (t + 1) / count for t in range(count)]

    for k, a in enumerate(order):
        plan.add(27 + 6 * k, lambda a=a: UI[0].fold_y(a))
        plan.add(51 + 6 * k, lambda a=a: UI[1].fold_y(a))
        plan.add(78 + 3 * k, lambda a=a: UU.fold_y(a))
        plan.add(80 + 2 * k, lambda a=a: UO.fold_y(a))
        for j in range(3):
            plan.add(92 + 10 * j + 3 * k, lambda a=a, j=j: UQ[j].fold_y(a))
    xs_order = [t * per + il for t in range(chunks) for il in reversed(range(per))]
    for k, i in enumerate(xs_order):
        plan.add(30 + 6 * k, lambda i=i: outer_x(i))
    plan.add(72, lambda: inner_z(0))
    plan.add(88, lambda: inner_z(1))
    plan.add(98, inner_x)
    plan.add(104, outer_z)
    plan.add(112, outer_end)
    plan.add(106, out_z)
    plan.add(114, out_x)
    for j in range(3):
        plan.add(115 + 6 * j, lambda j=j: proj_z(j))
        plan.add(120 + 6 * j, lambda j=j: proj_x(j))
    for t in range(len(hops) + 1):
        plan.add(74 + 4 * t, lambda t=t: vector_hop(t))

    attention(0, spaced(5, 13, pairs))
    need("nrm", ("dinn", 0))
    nrm_swap().wait_recv()
    dinn_swap[0]().wait_recv()
    weight_grad(lambda m: D[0, m], PI.at[0], spaced(13, 17, groups))
    UI[0].start_y()

    def act_load(t):
        slot = t % 2
        return [
            pltpu.make_async_copy(act.at[:, act_cols(t)], D.at[slot, 0], lsem.at[act_sem + 2 * slot]),
            pltpu.make_async_copy(
                act_s.at[:, act_cols(t)], D.at[slot, 1], lsem.at[act_sem + 2 * slot + 1]
            ),
        ]

    act_sem = [next(locals_free) for _ in range(4)][0]

    def begin_act(t):
        for c in act_load(t):
            c.start()

    act_swap[0]().wait_recv()
    begin_act(0)
    need(("dinn", 1))
    dinn_swap[1]().wait_recv()
    weight_grad(lambda m: D[1, m], PI.at[1], spaced(17, 20, groups))
    UI[1].start_y()
    for t in range(1, chunks):
        act_swap[t]().wait_recv()
    if chunks > 1:
        begin_act(1)
    load("x0", lambda: (xall.at[pl.ds(0, rows)], L.at[0]))
    load("x1", lambda: (xall.at[pl.ds(rows, rows)], L.at[1]))
    need(("dout", 0), ("dout", 1))
    dout_swap[0]().wait_recv()
    dout_swap[1]().wait_recv()

    outer_times = spaced(20, 34, n)

    def outer_body(u, carry):
        t, il = u // per, per - 1 - u % per
        slot = t % 2

        @pl.when(u % per == 0)
        def _():
            for c in act_load(t):
                c.wait()

        cols = at(xor(f % per, il, per), ro)
        r = dot_tn(D[slot, 0, :, cols], DO[0]) + dot_tn(D[slot, 1, :, cols], DO[1])
        r = r.astype(BF)
        i = t * per + il
        for ex in range(2):
            PU[ex, i % 2, i // 2] = r[:, ex * wq : (ex + 1) * wq]
        outer_copy(i).start()

        @pl.when((u % per == per - 1) & (t + 2 < chunks))
        def _():
            begin_act(t + 2)

        plan.beside(u, outer_times)
        return carry

    lax.fori_loop(0, n, outer_body, 0)

    need("co", ("dattn", 0), ("dattn", 1))
    ctx_swap().wait_recv()
    dattn_swap[0]().wait_recv()
    dattn_swap[1]().wait_recv()
    for half in range(2):
        for g in range(hw // 256):
            lanes = slice(g * 256, (g + 1) * 256)

            def left(m):
                if half:
                    return CO[m, :, lanes]
                return CX[2 * m : 2 * m + 2, :, :, lanes].reshape(rows, 256)

            r = (dot_tn(left(0), DA[0]) + dot_tn(left(1), DA[1])).astype(BF)
            group = (core + half * (1 - 2 * core)) * (hw // 256) + g
            for u in range(gsz):
                i = xor(group * gsz + u, f, n)
                for ex in range(2):
                    PO[i % 2, i // 2, ex * rs : (ex + 1) * rs] = r[
                        u * rs : (u + 1) * rs, ex * wq : (ex + 1) * wq
                    ]
        for job in plan.due(36 + 3 * half):
            job()
    UO.start_y()

    attention(1, spaced(39, 47, pairs))
    for s in range(2, sh):
        attention(s, spaced(47, 55, pairs))

    need("x0", "x1", "vec")
    for j, ref in enumerate((Q, K, V)):

        def right(m):
            return ref[2 * m : 2 * m + 2].reshape(rows, hw)

        if j != 1:
            total = jnp.sum(right(0).astype(F32), 0, keepdims=True)
            total = total + jnp.sum(right(1).astype(F32), 0, keepdims=True)
            VS[0, j // 2 : j // 2 + 1, at(core, hw)] = total
        weight_grad(right, PQ.at[j], spaced(55 + 6 * j, 61 + 6 * j, groups))
        UQ[j].start_y()

    need("w")

    def project(slot):
        out = None
        for j, ref in enumerate((Q, K, V)):
            p = dot_nt(ref[slot].reshape(half_rows, hw), W[j])
            out = p if out is None else out + p
        return out

    ig_swap = [remote(CORE, lambda ex=ex: (SB, ig_s.at[ex])) for ex in range(2)]
    for ex in (1, 0):
        value = project(2 + ex)
        if ex == 0:
            ig_swap[1]().wait_send()
        SB[...] = value
        ig_swap[ex]().start()
        for job in plan.due(80 - 4 * ex):
            job()

    def rows_of(ex):
        return pl.ds(ex * half_rows, half_rows)

    ig_near = remote(NEAR, lambda: (XS, o_igr))
    for ex in (1, 0):
        ig_swap[ex]().wait_recv()
        load(("ig", ex), lambda ex=ex: (ig_s.at[ex], IB))
        value = project(ex)
        if ex:
            ig_swap[0]().wait_send()
        load(("df", ex), lambda ex=ex: (dfirst.at[rows_of(ex)], SB))
        need(("ig", ex), ("df", ex))
        value = value + IB[...] + SB[...]
        if ex:
            XS[...] = value.astype(BF)
            go(ig_near)
        else:
            IB[...] = value
            go_local(lambda: (IB, o_igl))
        for job in plan.due(88 - 4 * ex):
            job()

    for job in plan.due(1e9):
        job()

    lo_swap().wait_recv()
    ig_near().wait_recv()
    for build in i_core + [u_core, u_core2] + o_core + q_core:
        build().wait_recv()
    for i in range(n):
        outer_copy(i).wait_send()
    for end in ends:
        end()


def back_call(lens, n, act, dout, nrm, dinn, dattn, ctx, cr, xall, q, k, v, lse, dco, dcs, dfirst, w, lo, acc):
    rows, width = nrm.shape
    ff = act.shape[1]
    slots, sh, part, hw = q.shape
    A = n // 2
    rs, ro, cq, wq = width // n, ff // n, ff // 4, width // 4
    hops = 2 + n.bit_length() - 1

    def bf(*shape):
        return jax.ShapeDtypeStruct(shape, BF)

    def f32(*shape):
        return jax.ShapeDtypeStruct(shape, F32)

    def vm(*shape):
        return pltpu.VMEM(shape, BF)

    def vf(*shape):
        return pltpu.VMEM(shape, F32)

    four = (slots, sh, part, hw)
    return pl.pallas_call(
        functools.partial(back_kernel, n),
        in_specs=[pl.BlockSpec(memory_space=pltpu.SMEM)] + [ANY] * 19,
        out_specs=[ANY] * 12,
        out_shape=[
            bf(2 * sh, part, width),
            f32(rows // 2, width),
            bf(rows // 2, width),
            bf(rs, ff),
            bf(ro, width),
            bf(rs, width),
            bf(rs, width),
            bf(rs, width),
            bf(rs, width),
            f32(16, width),
            bf(rows, ff),
            f32(2, rows // 2, width),
        ],
        scratch_shapes=[
            vm(*four),
            vm(*four),
            vm(*four),
            vm(*four),
            vm(*four),
            vf(2, *lse.shape[1:]),
            vm(2, rows, width),
            vm(2, 2, rows, 1024),
            vm(2, rows, 2 * wq),
            vm(2, rows, 2 * wq),
            vm(2, rows, hw),
            vm(3, width, hw),
            vm(2, 2, A, rs, cq),
            vm(2, 2, A, ro, wq),
            vm(2, A, 2 * rs, wq),
            vm(3, 2, A, rs, hw),
            vm(2, A, rs, cq),
            vm(2, A - 1, rs, cq),
            vm(2, rs, cq),
            vm(2, rs, cq),
            vm(2, A, ro, wq),
            vm(A, ro, wq),
            vm(A - 1, ro, wq),
            vm(ro, wq),
            vm(A, 2 * rs, wq),
            vm(A - 1, 2 * rs, wq),
            vm(2 * rs, wq),
            vm(2 * rs, wq),
            vm(3, A, rs, hw),
            vm(3, A - 1, rs, hw),
            vm(3, rs, hw),
            vm(3, rs, hw),
            vf(hops + 1, 16, width),
            vf(hops, 16, width),
            vf(rows // 2, width),
            vf(rows // 2, width),
            vm(rows // 2, width),
            pltpu.SemaphoreType.DMA((48,)),
            pltpu.SemaphoreType.DMA((64 + 8 * n,)),
            pltpu.SemaphoreType.DMA((64 + 8 * n,)),
        ],
        compiler_params=pltpu.CompilerParams(
            vmem_limit_bytes=BACK_LIMIT, collective_id=1, has_side_effects=True
        ),
        name="back",
    )(
        lens,
        act,
        dout,
        nrm,
        dinn,
        dattn,
        ctx,
        ctx.reshape(slots * sh * part, hw),
        cr,
        xall,
        q,
        k,
        v,
        lse,
        dco,
        dcs,
        dfirst,
        w,
        lo,
        acc,
    )


def per_device(
    inputs,
    lengths,
    cotangent,
    query_weight,
    key_weight,
    value_weight,
    out_weight,
    inner_weight,
    outer_weight,
    query_bias,
    value_bias,
    out_bias,
    inner_bias,
    outer_bias,
    first_gain,
    first_shift,
    second_gain,
    second_shift,
):
    C = lax.axis_index("ctx")
    f = lax.axis_index("fsdp")
    n = lax.axis_size("fsdp")
    x, core = C // 2, C % 2
    ids = jnp.stack([C, f]).astype(jnp.int32)
    seqs, part, width = inputs.shape
    ff = inner_weight.shape[1]
    sh = seqs // 2
    rows = 2 * sh * part
    rs, ro = width // n, ff // n
    hw = width // 2

    def pick(bit, a, b):
        return jnp.where(bit == 0, a, b), jnp.where(bit == 0, b, a)

    def row_of(v):
        return jnp.pad(v.reshape(1, -1), ((0, 0), (0, hw - v.shape[0])))

    vectors = [
        query_bias,
        value_bias,
        out_bias,
        outer_bias,
        first_gain,
        first_shift,
        second_gain,
        second_shift,
        inner_bias,
    ]
    vecs = jnp.concatenate(
        [row_of(v) for v in vectors] + [jnp.zeros((PACK - len(vectors), hw), BF)], 0
    )
    x4, cot, w_qkv, wi, wu, wo, vecs, q4, k4, v4, c4, c_r, lse = front_call(
        lengths,
        inputs,
        cotangent,
        query_weight,
        key_weight,
        value_weight,
        vecs,
        out_weight,
        inner_weight,
        outer_weight,
        n,
    )
    xall = x4.reshape(2 * rows, width)
    ctx, cr = c4.reshape(2 * rows, hw), c_r.reshape(rows, hw)
    two = (2, sh, part, hw)
    lo, act, dout, dinn, nrm, dattn, dfirst, dco, dcs, acc = ffn_call(
        ids, lengths, sh, ctx, cr, xall, cot.reshape(rows, width), vecs, wo, wi, wu
    )

    layer_out, ig_here, ig_near, g_i, g_u, g_o, g_q, g_k, g_v, sums, _, _ = back_call(
        lengths,
        n,
        act,
        dout,
        nrm,
        dinn,
        dattn,
        c4,
        cr,
        xall,
        q4,
        k4,
        v4,
        lse,
        dco.reshape(two),
        dcs.reshape(two),
        dfirst,
        w_qkv,
        lo.reshape(2, sh, part, width),
        acc,
    )
    own = lax.dynamic_slice_in_dim(sums[:8], f * rs, rs, 1)
    own_inner = lax.dynamic_slice_in_dim(sums[8 : 8 + ff // width].reshape(ff), f * ro, ro, 0)
    third = (sh, part, width)
    input_grad = jnp.concatenate(
        pick(x, ig_here.reshape(third), ig_near.reshape(third).astype(F32)), 0
    )
    grad_query, grad_key, grad_value, grad_out, grad_inner, grad_outer = (
        g.astype(F32) for g in (g_q, g_k, g_v, g_o, g_i, g_u)
    )

    return (
        layer_out,
        input_grad,
        grad_query,
        grad_key,
        grad_value,
        grad_out,
        grad_inner,
        grad_outer,
        own[0],
        own[1],
        own[2],
        own_inner,
        own[3],
        own[4],
        own[5],
        own[6],
        own[7],
    )


def solution(mesh):
    rowed = P("fsdp", "ctx", None)
    matrix, vector = P("fsdp", None), P("fsdp")
    in_specs = (rowed, vector, rowed) + (matrix,) * 6 + (vector,) * 9
    out_specs = (rowed, rowed) + (matrix,) * 6 + (vector,) * 9
    return jax.shard_map(
        per_device, mesh=mesh, in_specs=in_specs, out_specs=out_specs, check_vma=False
    )
```

```python
import functools

import jax
import jax.numpy as jnp
from jax import lax
from jax.experimental import pallas as pl
from jax.experimental.pallas import tpu as pltpu
from jax.sharding import PartitionSpec as P

HD = 64
EPSILON = 1e-05
BF = jnp.bfloat16
F32 = jnp.float32
ANY = pl.BlockSpec(memory_space=pl.ANY)
NT = (((1,), (1,)), ((), ()))
TN = (((0,), (0,)), ((), ()))
VMEM_LIMIT = 58 << 20
BACK_LIMIT = 60 << 20


def dot(a, b):
    return jnp.dot(a, b, preferred_element_type=F32)


def dot_nt(a, b):
    return lax.dot_general(a, b, NT, preferred_element_type=F32)


def dot_tn(a, b):
    return lax.dot_general(a, b, TN, preferred_element_type=F32)


def params(**more):
    return pltpu.CompilerParams(vmem_limit_bytes=VMEM_LIMIT, **more)


def cost(flops, size, trans=0):
    return pl.CostEstimate(flops=int(flops), bytes_accessed=int(size), transcendentals=int(trans))


MESH = pl.DeviceIdType.MESH
PACK = 16


def flip(v, mask):
    out, bit = v, 1
    while bit <= mask:
        if mask & bit:
            out = out + bit - 2 * bit * ((v // bit) % 2)
        bit *= 2
    return out


def at(index, size):
    return pl.ds(pl.multiple_of(index * size, size), size)


def spread(read, n, rs):
    per = max(128 // rs, 1)
    tiles = []
    for t in range(n // per):
        tile = read(t * per)
        for u in range(1, per):
            tile = tile + pltpu.roll(read(t * per + u), u * rs, 1)
        tiles.append(tile)
    return jnp.concatenate(tiles, 1)


def front_kernel(
    n,
    lens,
    xin,
    cin,
    wq,
    wk,
    wv,
    vecs,
    wo_in,
    wi_in,
    wu_in,
    xo,
    co,
    wqkvo,
    wio,
    wuo,
    woo,
    veco,
    qo,
    ko,
    vo,
    cxo,
    cro,
    cso,
    lseo,
    X,
    W,
    VEC,
    Q,
    K,
    V,
    CX,
    LSE,
    lsem,
    ssem,
    rsem,
):
    C, f = lax.axis_index("ctx"), lax.axis_index("fsdp")
    x, core = C // 2, C % 2
    A = n // 2
    sh, part, width = X.shape[1:]
    hw = W.shape[2]
    ff = wio.shape[1]
    rs, ro, cq = width // n, ff // n, ff // 4

    partners = [(0, 2 * k) for k in range(1, A)] + [(0, 1), (2, 0), (1, 0)]

    def device(dc, df):
        return (flip(C, dc), flip(f, df))

    barrier = pltpu.get_barrier_semaphore()
    for p in partners:
        pl.semaphore_signal(barrier, inc=1, device_id=device(*p), device_id_type=MESH)

    local = []
    used = iter(range(lsem.shape[0]))

    def begin(source, target):
        c = pltpu.make_async_copy(source, target, lsem.at[next(used)])
        c.start()
        return c

    def keep(source, target):
        local.append(begin(source, target))

    x_here = begin(xin.at[pl.ds(x * sh, sh)], X.at[0])
    w_here = [begin(w.at[:, at(core, hw)], W.at[j, at(f, rs)]) for j, w in enumerate((wq, wk, wv))]
    w_here.append(begin(vecs, VEC.at[f]))

    pl.semaphore_wait(barrier, len(partners))

    def remote(source, target, sem, dev):
        return pltpu.make_async_remote_copy(
            src_ref=source,
            dst_ref=target,
            send_sem=ssem.at[sem],
            recv_sem=rsem.at[sem],
            device_id=device(*dev),
            device_id_type=MESH,
        )

    sent = []

    def send(*what):
        c = remote(*what)
        c.start()
        sent.append(c)

    seen = set()

    def arrive(target, sem, dev):
        if sem not in seen:
            seen.add(sem)
            remote(target, target, sem, dev).wait_recv()

    X1, X2, X3, COT, CTX, CTX2 = range(6)
    send(xin.at[pl.ds((1 - x) * sh, sh)], X.at[1], X1, (2, 0))

    def rows_at(ref, first, size):
        return ref.at[pl.ds(pl.multiple_of(first, size), size)]

    hr, hu = rs // 2, ro // 2

    def projection(j):
        w = (wq, wk, wv)[j]
        return (
            1,
            lambda e, s: [W.at[j, at(s, rs)]] + [VEC.at[s]] * (j == 0),
            lambda: [w.at[:, at(core, hw)]] + [vecs] * (j == 0),
        )

    def inner_part(h):
        return (
            4,
            lambda e, s: [wio.at[at(s * 2 + h, hr), at(flip(C, e), cq)]],
            lambda: [wi_in.at[pl.ds(h * hr, hr), at(C, cq)]],
        )

    outer_a = (
        4,
        lambda e, s: [rows_at(wuo, s * ro + flip(C, e) * (hu // 4), hu // 4)],
        lambda: [rows_at(wu_in, C * (hu // 4), hu // 4)],
    )
    out_part = (
        4,
        lambda e, s: [rows_at(woo, s * rs + flip(C, e) * (rs // 4), rs // 4)],
        lambda: [rows_at(wo_in, C * (rs // 4), rs // 4)],
    )

    def outer_b(h):
        return (
            2,
            lambda e, s: [rows_at(wuo, s * ro + hu + (flip(core, e) * 2 + h) * (hu // 4), hu // 4)],
            lambda: [rows_at(wu_in, hu + (core * 2 + h) * (hu // 4), hu // 4)],
        )

    kinds = [
        inner_part(0),
        projection(0),
        projection(1),
        projection(2),
        inner_part(1),
        outer_a,
        out_part,
        outer_b(0),
        outer_b(1),
    ]
    sems, ready = {}, 6
    for k, (parts, place, _) in enumerate(kinds):
        for e in range(parts):
            for i in range(1, n):
                for u in range(2 if k == 1 else 1):
                    sems[k, e, i, u] = ready
                    ready += 1

    def route(parts, e, i):
        if e % 2:
            return (1, 0), (e - 1, i)
        if e:
            return (2, 0), (0, i)
        if i % 2:
            return (0, 1), (0, i - 1)
        return (0, i), (0, 0)

    def copies(k, e, i):
        parts, place, own = kinds[k]
        dev, (pe, pi) = route(parts, e, i)
        target = place(pe, flip(f, pi))
        source = target if pi else own()
        return [
            remote(source[u], target[u], sems[k, e, i, u], dev) for u in range(len(target))
        ]

    issued = []

    def give(k, e, i):
        for c in copies(k, e, i):
            c.start()
        issued.append((k, e, i))

    got = set()

    def take(k, e, i):
        if (k, e, i) in got:
            return
        got.add((k, e, i))
        parts, place, _ = kinds[k]
        dev, _ = route(parts, e, i)
        for u, target in enumerate(place(e, flip(f, i))):
            remote(target, target, sems[k, e, i, u], dev).wait_recv()

    def hand_on(k, i):
        parts = kinds[k][0]
        if parts == 4:
            give(k, 2, i)
        if parts > 1:
            give(k, 1, i)

    def base(k):
        if k < len(kinds):
            for a in range(1, A):
                give(k, 0, 2 * a)
            give(k, 0, 1)

    def z_in(k):
        for a in range(1, A):
            take(k, 0, 2 * a)
            give(k, 0, 2 * a + 1)
            hand_on(k, 2 * a)

    def y_in(k):
        for i in range(1, n, 2):
            take(k, 0, i)
            hand_on(k, i)

    def x_in(k):
        if kinds[k][0] == 4:
            for i in range(1, n):
                take(k, 2, i)
                give(k, 3, i)

    base(0)
    base(1)
    x_here.wait()
    send(X.at[0], X.at[2], X2, (1, 0))
    keep(cin.at[pl.ds(x * sh, sh)], co.at[0])
    keep(wo_in, woo.at[at(f, rs)])
    keep(wi_in, wio.at[at(f, rs)])
    keep(wu_in, wuo.at[at(f, ro)])
    for c in w_here:
        c.wait()
    send(cin.at[pl.ds((1 - x) * sh, sh)], co.at[1], COT, (2, 0))

    slots = X.shape[0]
    pairs = hw // (2 * HD)

    z_in(0)
    base(2)
    arrive(X.at[1], X1, (2, 0))
    send(X.at[1], X.at[3], X3, (1, 0))
    z_in(1)
    base(3)
    y_in(0)
    arrive(X.at[2], X2, (1, 0))
    arrive(X.at[3], X3, (1, 0))
    keep(X, xo)
    z_in(2)
    base(4)
    y_in(1)
    keep(VEC, veco)

    def bias(row):
        read = lambda s: VEC[pl.ds(core * (n // 2) + s, 1), row : row + 1, :128].reshape(1, 128).astype(F32)
        return spread(read, n // 2, rs)

    shape = (sh, part, hw)

    def project(j, target, add):
        def body(slot, carry):
            value = dot(X[slot].reshape(sh * part, width), W[j])
            if add is not None:
                value = value + add
            target[slot] = value.astype(BF).reshape(shape)
            return carry

        lax.fori_loop(0, slots, body, 0)

    project(0, Q, bias(0))
    z_in(3)
    base(5)
    y_in(2)
    project(1, K, None)
    x_in(0)
    z_in(4)
    base(6)
    y_in(3)
    keep(W, wqkvo)
    project(2, V, bias(1))
    keep(Q, qo)
    keep(K, ko)
    keep(V, vo)

    jobs = [
        lambda: z_in(5),
        lambda: base(7),
        lambda: y_in(4),
        lambda: z_in(6),
        lambda: base(8),
        lambda: y_in(5),
        lambda: x_in(4),
    ]
    steps = sh * pairs

    def attend(step, carry):
        s, pair = step // pairs, step % pairs
        cols = at(pair, 2 * HD)

        def load(ref):
            return ref[:, s, :, cols].reshape(slots * part, 2 * HD)

        q, k, v = load(Q), load(K), load(V)
        mask = key_mask(lens[x * sh + s], C, part)
        o, lse = attend_pair(q, k, v, mask)
        CX[:, s, :, cols] = o.reshape(slots, part, 2 * HD)
        LSE[s, :, cols] = lse
        for t in range(steps):
            now = jobs[len(jobs) * t // steps : len(jobs) * (t + 1) // steps]
            if now:

                @pl.when(step == t)
                def _():
                    for job in now:
                        job()

        return carry

    lax.fori_loop(0, steps, attend, 0)
    send(CX.at[pl.ds(2, 2)], cro, CTX, (1, 0))
    send(CX.at[pl.ds(0, 2)], cso, CTX2, (1, 0))
    keep(CX, cxo)
    keep(LSE, lseo)
    z_in(7)
    y_in(6)
    x_in(5)
    z_in(8)
    y_in(7)
    x_in(6)
    y_in(8)
    for k, (parts, _, _) in enumerate(kinds):
        for e in range(parts):
            for i in range(1, n):
                take(k, e, i)
    arrive(co.at[1], COT, (2, 0))
    arrive(cro, CTX, (1, 0))
    arrive(cso, CTX2, (1, 0))
    for what in issued:
        for c in copies(*what):
            c.wait_send()
    for c in sent:
        c.wait_send()
    for c in local:
        c.wait()


def front_call(lengths, xin, cin, wq, wk, wv, vecs, wo, wi, wu, n):
    seqs, part, width = xin.shape
    sh, ff, hw = seqs // 2, wi.shape[1], width // 2

    def bf(*shape):
        return jax.ShapeDtypeStruct(shape, BF)

    def vm(*shape):
        return pltpu.VMEM(shape, BF)

    full = 4 * part
    lse = (sh, full, hw)
    four = (4, sh, part, hw)
    sems = 24 * n
    return pl.pallas_call(
        functools.partial(front_kernel, n),
        in_specs=[pl.BlockSpec(memory_space=pltpu.SMEM)] + [ANY] * 9,
        out_specs=[ANY] * 14,
        out_shape=[
            bf(4, sh, part, width),
            bf(2, sh, part, width),
            bf(3, width, hw),
            bf(width, ff),
            bf(ff, width),
            bf(width, width),
            bf(n, PACK, 128),
            bf(*four),
            bf(*four),
            bf(*four),
            bf(*four),
            bf(2, sh, part, hw),
            bf(2, sh, part, hw),
            jax.ShapeDtypeStruct(lse, F32),
        ],
        scratch_shapes=[
            vm(4, sh, part, width),
            vm(3, width, hw),
            vm(n, PACK, 128),
            vm(*four),
            vm(*four),
            vm(*four),
            vm(*four),
            pltpu.VMEM(lse, F32),
            pltpu.SemaphoreType.DMA((24,)),
            pltpu.SemaphoreType.DMA((sems,)),
            pltpu.SemaphoreType.DMA((sems,)),
        ],
        compiler_params=params(collective_id=0, has_side_effects=True),
        name="front",
    )(lengths, xin, cin, wq, wk, wv, vecs, wo, wi, wu)


def lanes_of(shape, head):
    lane = lax.broadcasted_iota(jnp.int32, shape, 1)
    own = (lane < HD) if head == 0 else (lane >= HD)
    return lane, own, (HD if head == 0 else 0)


def split3(a):
    hi = a.astype(BF).astype(F32)
    mid = (a - hi).astype(BF).astype(F32)
    return hi, mid, a - hi - mid


def flat(ref):
    a = ref[...]
    return a.reshape(-1, a.shape[-1])


def key_mask(length, C, part):
    row = lax.broadcasted_iota(jnp.int32, (part, 2 * HD), 0)
    out = []
    for e in (0, 2, 1, 3):
        inside = row + flip(C, e) * part < length
        out.append(jnp.where(inside, 0.0, -1e30).astype(BF))
    return jnp.concatenate(out, 0)


def attend_pair(q, k, v, mask):
    out = []
    for head in range(2):
        lane, own, other = lanes_of(q.shape, head)
        qh = jnp.where(own, q * BF(HD**-0.5), jnp.where(lane == other, 1.0, 0.0).astype(BF))
        kh = jnp.where(own, k, mask)
        s = dot_nt(qh, kh)
        top = jnp.max(s, -1, keepdims=True)
        e = jnp.exp(s - top)
        total = jnp.sum(e, -1, keepdims=True)
        o = dot(e.astype(BF), v) * (1.0 / total)
        out.append((o, top + jnp.log(total), own))
    (o0, l0, own), (o1, l1, _) = out
    return jnp.where(own, o0, o1).astype(BF), jnp.where(own, l1, l0)


def attend_back_pair(q, k, v, mask, lse, c, g):
    qs = q * BF(HD**-0.5)
    kt = k.T
    prod = c.astype(F32) * g.astype(F32)
    res = []
    for head in range(2):
        lane, own, o = lanes_of(q.shape, head)
        hi, mid, low = split3(-lse)
        extra = jnp.where(
            lane == o,
            1.0,
            jnp.where(
                lane == o + 1,
                hi,
                jnp.where(lane == o + 2, mid, jnp.where(lane == o + 3, low, 0.0)),
            ),
        ).astype(BF)
        qh = jnp.where(own, qs, extra)
        kh = jnp.where(own, k, jnp.where(lane == o, mask, BF(1)))
        p = jnp.exp(dot_nt(kh, qh))
        delta = jnp.sum(jnp.where(own, prod, 0.0), -1, keepdims=True)
        hi, mid, low = split3(-delta)
        extra = jnp.where(
            lane == o, hi, jnp.where(lane == o + 1, mid, jnp.where(lane == o + 2, low, 0.0))
        ).astype(BF)
        gh = jnp.where(own, g, extra)
        vh = jnp.where(own, v, BF(1))
        ds = (p * dot_nt(vh, gh)).astype(BF)
        dv = dot(p.astype(BF), g)
        dk = dot(ds, qs)
        dqt = dot(kt, ds)
        res.append((dv, dk, dqt, own))
    (dv0, dk0, dq0, own), (dv1, dk1, dq1, _) = res
    dqt = jnp.concatenate([dq0[:HD], dq1[HD:]], 0) * (HD**-0.5)
    return dqt.T.astype(BF), jnp.where(own, dk0, dk1).astype(BF), jnp.where(own, dv0, dv1).astype(BF)


def gelu_pair(u):
    e = jnp.exp(u * u * -0.5)
    t = 1.0 / (1.0 + (0.3275911 * 0.7071067811865476) * jnp.abs(u))
    poly = t * (
        0.254829592 * 0.5
        + t
        * (
            -0.284496736 * 0.5
            + t * (1.421413741 * 0.5 + t * (-1.453152027 * 0.5 + t * (1.061405429 * 0.5)))
        )
    )
    tail = poly * e
    cdf = jnp.where(u >= 0, 1.0 - tail, tail)
    ucdf = u * cdf
    return ucdf, cdf + u * (e * 0.3989422804014327)


def normalise(h):
    c = h - jnp.mean(h, -1, keepdims=True)
    r = lax.rsqrt(jnp.mean(c * c, -1, keepdims=True) + EPSILON)
    return c * r, r


def normalise_back(dyg, hat, r):
    return r * (
        dyg - jnp.mean(dyg, -1, keepdims=True) - hat * jnp.mean(dyg * hat, -1, keepdims=True)
    )


def ffn_kernel(n, sh, part, lens, cm, cr, xm, cot, vecs, wo_in, wi_in, wu_in, *refs):
    dfirst, dco, acc = refs[:3]
    homes, (o_lo, act_s, dout_s, dinn_s, nrm_s, dattn_s, dcs_s) = refs[3:8], refs[8:15]
    wo, wi, wu, gp, vec, ib, *twice, sem, csem, hsem, ssem, rsem = refs[15:]
    width, ff = wi.shape
    C, f = lax.axis_index("ctx"), lax.axis_index("fsdp")
    x, core = C // 2, C % 2
    step = pl.program_id(0)
    turn = 2 - step
    rs, ro = width // n, ff // n
    cq, hw = ff // 4, width // 2

    pairs = ((wo_in, wo), (wi_in, wi), (wu_in, wu))

    def copy(kind):
        return pltpu.make_async_copy(*pairs[kind], sem.at[kind])

    CORE, NEAR = flip(C, 1), flip(C, 2)
    block, wq = xm.shape[0], width // 4

    def remote(t, j, to, source, target):
        return pltpu.make_async_remote_copy(
            src_ref=source,
            dst_ref=target,
            send_sem=ssem.at[t, j],
            recv_sem=rsem.at[t, j],
            device_id=(to, f),
            device_id_type=MESH,
        )

    KINDS = ("act", "nrm", "dout0", "dout1", "dinn0", "dinn1", "dattn0", "dattn1", "dcs")

    def rows_of(t):
        return pl.ds(pl.multiple_of(t * block, block), block)

    def held(t):
        return [ref.at[(2 - t) % 2] for ref in twice]

    act, nrm, dout, dinn, dattn, dcs, lo = held(turn)
    HOME = {"act": 0, "nrm": 1, "dout": 2, "dinn": 3, "dattn": 4}

    def home(t, name):
        j = HOME[name]
        return pltpu.make_async_copy(held(t)[j], homes[j].at[rows_of(t)], hsem.at[t, j])

    def to_core(t, *names):
        out = []
        for name in names or KINDS:
            rows = rows_of(t)
            act, nrm, dout, dinn, dattn, dcs, _ = held(t)
            ex = int(name[-1]) if name[-1] in "01" else 0
            other, lanes = flip(C, 2 * ex + 1), pl.ds(ex * wq, wq)
            source, target = {
                "act": lambda: (act, act_s.at[rows]),
                "nrm": lambda: (nrm, nrm_s.at[rows]),
                "dcs": lambda: (dcs, dcs_s.at[rows]),
                "dou": lambda: (dout.at[:, at(other, wq)], dout_s.at[rows, lanes]),
                "dat": lambda: (dattn.at[:, at(other, wq)], dattn_s.at[rows, lanes]),
                "din": lambda: (dinn.at[:, at(other, cq)], dinn_s.at[ex, rows]),
            }[name[:3]]()
            out.append(remote(t, KINDS.index(name), CORE, source, target))
        return out

    def start(name):
        for c in to_core(turn, *(k for k in KINDS if k.startswith(name))):
            c.start()
        if name in HOME:
            home(turn, name).start()

    def end(t, name):
        for c in to_core(t, *(k for k in KINDS if k.startswith(name))):
            c.wait_send()
        if name in HOME:
            home(t, name).wait()

    def free(name):
        @pl.when(step == 2)
        def _():
            end(2, name)

    def slots_of(t, ex):
        count = block // part
        return [u for u in range(count) if (t * count + u) // sh == ex]

    def place(t, u):
        return held(t)[6].at[pl.ds(u * part, part)], o_lo.at[x * sh + (t * (block // part) + u) % sh]

    def to_near(t):
        return [remote(t, 9 + u, NEAR, *place(t, u)) for u in slots_of(t, 1)]

    def stay(t):
        return [pltpu.make_async_copy(*place(t, u), csem.at[t, u]) for u in slots_of(t, 0)]

    def send(t):
        for c in to_near(t) + stay(t):
            c.start()

    def sent(t):
        for c in to_near(t):
            c.wait_send()
        for c in stay(t):
            c.wait()

    def received(t):
        for c in to_core(t) + to_near(t):
            c.wait_recv()

    @pl.when(step == 0)
    def _():
        barrier = pltpu.get_barrier_semaphore()
        for to in (CORE, NEAR):
            pl.semaphore_signal(barrier, inc=1, device_id=(to, f), device_id_type=MESH)
        pl.semaphore_wait(barrier, 2)
        for kind in range(3):
            copy(kind).start()
        acc[...] = jnp.zeros_like(acc)
        vec[...] = spread(lambda s: vecs[s, :8, :128].astype(F32), n, rs)
        for s in range(n):
            for t in range(ro // 128):
                first = s * ro + t * 128
                ib[:, first : first + 128] = vecs[s, 8 + t : 9 + t, :].astype(F32)

    def arrived(kind):
        @pl.when(step == 0)
        def _():
            copy(kind).wait()

    count = xm.shape[0] // part
    inside = []
    for u in range(count):
        slot = turn * count + u
        ex, s = slot // sh, slot % sh
        first = (C + ex * (2 - 4 * x)) * part
        row = lax.broadcasted_iota(jnp.int32, (part, 1), 0) + first
        inside.append(jnp.where(row < lens[x * sh + s], 1.0, 0.0))
    valid = jnp.concatenate(inside, 0)
    own, other = at(core, hw), at(1 - core, hw)

    def add(row, value):
        acc[row : row + 1, :] += jnp.sum(value, 0, keepdims=True)

    arrived(0)
    first = (
        xm[...].astype(F32) + (dot(cm[...], wo[own]) + dot(cr[...], wo[other])) + vec[2:3, :]
    )
    hat1, r1 = normalise(first)
    normed = hat1 * vec[4:5, :] + vec[5:6, :]
    low = normed.astype(BF)
    free("act")
    free("nrm")
    nrm[...] = low
    start("nrm")
    arrived(1)
    for j in range(4):
        cols = slice(j * cq, (j + 1) * cq)
        g, d = gelu_pair(dot(low, wi[:, cols]) + ib[:, cols])
        act[:, cols] = g.astype(BF)
        gp[:, cols] = d
    start("act")
    arrived(2)
    second = normed + (dot(act[...], wu[...]) + vec[3:4, :])
    hat2, r2 = normalise(second)
    @pl.when(step == 2)
    def _():
        sent(2)

    lo[...] = (hat2 * vec[6:7, :] + vec[7:8, :]).astype(BF)
    og = cot[...].astype(F32) * valid
    add(6, og * hat2)
    add(7, og)
    d2 = normalise_back(og * vec[6:7, :], hat2, r2)
    d2low = d2.astype(BF)
    free("dout")
    dout[...] = d2low
    start("dout")
    for t in range(3):

        @pl.when(turn == t)
        def _():
            send(t)

    add(3, d2low.astype(F32))
    free("dinn")
    for j in range(4):
        cols = slice(j * cq, (j + 1) * cq)
        di = (dot_nt(d2low, wu[cols, :]) * gp[:, cols]).astype(BF)
        dinn[:, cols] = di
        add(8 + j, di.astype(F32))
    start("dinn")
    dn = d2 + dot_nt(dinn[...], wi[...])
    add(4, dn * hat1)
    add(5, dn)
    d1 = normalise_back(dn * vec[4:5, :], hat1, r1)
    dfirst[...] = d1
    d1low = d1.astype(BF)
    free("dattn")
    free("dcs")
    dattn[...] = d1low
    start("dattn")
    add(2, d1low.astype(F32))
    dcs[...] = dot_nt(d1low, wo[other]).astype(BF)
    start("dcs")
    dco[...] = dot_nt(d1low, wo[own]).astype(BF)

    @pl.when(turn == 0)
    def _():
        for t in range(2):
            for name in ("act", "nrm", "dout", "dinn", "dattn", "dcs"):
                end(t, name)
            sent(t)
        for t in range(3):
            received(t)


def ffn_call(lens, sh, c, cr, xall, cot, vecs, wo, wi, wu):
    width, ff = wi.shape
    n, rows = vecs.shape[0], cot.shape[0]
    block, part = rows // 3, rows // (2 * sh)
    hw = width // 2

    def by(cols):
        return pl.BlockSpec((block, cols), lambda i: (2 - i, 0))

    def whole(*shape):
        return pl.BlockSpec(shape, lambda i: (0,) * len(shape))

    grid_spec = pl.GridSpec(
        grid=(3,),
        in_specs=[pl.BlockSpec(memory_space=pltpu.SMEM), by(hw), by(hw), by(width), by(width), whole(*vecs.shape), ANY, ANY, ANY],
        out_specs=[by(width), by(hw), whole(16, width)] + [ANY] * 12,
        scratch_shapes=[
            pltpu.VMEM((width, width), BF),
            pltpu.VMEM((width, ff), BF),
            pltpu.VMEM((ff, width), BF),
            pltpu.VMEM((block, ff), F32),
            pltpu.VMEM((8, width), F32),
            pltpu.VMEM((1, ff), F32),
            *(
                pltpu.VMEM((2, block, cols), BF)
                for cols in (ff, width, width, ff, width, hw, width)
            ),
            pltpu.SemaphoreType.DMA((3,)),
            pltpu.SemaphoreType.DMA((3, block // part)),
            pltpu.SemaphoreType.DMA((3, 5)),
            pltpu.SemaphoreType.DMA((3, 9 + block // part)),
            pltpu.SemaphoreType.DMA((3, 9 + block // part)),
        ],
    )

    def shape(cols, dtype=BF):
        return jax.ShapeDtypeStruct((rows, cols), dtype)

    return pl.pallas_call(
        functools.partial(ffn_kernel, n, sh, part),
        grid_spec=grid_spec,
        out_shape=[
            shape(width, F32),
            shape(hw),
            jax.ShapeDtypeStruct((16, width), F32),
            shape(ff),
            shape(width),
            shape(width),
            shape(ff),
            shape(width),
            jax.ShapeDtypeStruct((2 * sh, part, width), BF),
            shape(ff),
            shape(hw),
            jax.ShapeDtypeStruct((2, rows, ff // 4), BF),
            shape(width),
            shape(hw),
            shape(hw),
        ],
        compiler_params=params(collective_id=2, has_side_effects=True),
        cost_estimate=cost(
            2 * rows * width * (2 * width + 4 * ff), 30 * rows * width + 2 * width * (2 * ff + width)
        ),
        name="ffn",
    )(lens, c, cr, xall, cot, vecs, wo, wi, wu)


def xor(a, b, count):
    out, bit = 0, 1
    while bit < count:
        out = out + bit * ((a // bit + b // bit) % 2)
        bit *= 2
    return out


def plus(*items):
    out = items[0].astype(F32)
    for i in items[1:]:
        out = out + i.astype(F32)
    return out.astype(BF)


class Plan:
    def __init__(self):
        self.jobs = []

    def add(self, time, job):
        self.jobs.append((time, len(self.jobs), job))
        self.jobs.sort(key=lambda j: j[:2])

    def due(self, time):
        out = [j[2] for j in self.jobs if j[0] <= time]
        self.jobs = [j for j in self.jobs if j[0] > time]
        return out

    def beside(self, step, times):
        for t, time in enumerate(times):
            jobs = self.due(time)
            if jobs:

                @pl.when(step == t)
                def _():
                    for job in jobs:
                        job()


def back_kernel(
    n,
    lens,
    act,
    dout,
    nrm,
    dinn,
    dattn,
    ctx,
    cr,
    xall,
    q_in,
    k_in,
    v_in,
    lse_in,
    dco,
    dfirst,
    w_in,
    acc,
    act_s,
    dout_s,
    dinn_s,
    nrm_s,
    dattn_s,
    dcs_s,
    cs,
    o_igl,
    o_igr,
    o_i,
    o_u,
    o_o,
    o_q,
    o_k,
    o_v,
    o_vec,
    ig_s,
    Q,
    K,
    V,
    CX,
    G,
    LSE,
    L,
    D,
    DO,
    DA,
    CO,
    W,
    PI,
    PU,
    PO,
    PQ,
    RYI,
    RZI,
    MI,
    RXI,
    RXU,
    RYU,
    RZU,
    MU,
    RYO,
    RZO,
    MO,
    RXO,
    RYQ,
    RZQ,
    MQ,
    RXQ,
    VS,
    VR,
    SB,
    IB,
    XS,
    lsem,
    ssem,
    rsem,
):
    C, f = lax.axis_index("ctx"), lax.axis_index("fsdp")
    x, core = C // 2, C % 2
    A = n // 2
    slots, sh, part, hw = Q.shape
    rows, width = nrm.shape
    ff = act.shape[1]
    rs, ro, cq, wq = width // n, ff // n, ff // 4, width // 4
    half_rows = rows // 2
    CORE, NEAR, Y = (1, 0), (2, 0), (0, 1)

    def device(dc, df):
        return (flip(C, dc), flip(f, df))

    partners = [(0, 2 * k) for k in range(1, A)] + [Y, NEAR, CORE]
    barrier = pltpu.get_barrier_semaphore()
    for p in partners:
        pl.semaphore_signal(barrier, inc=1, device_id=device(*p), device_id_type=MESH)

    locals_free = iter(range(lsem.shape[0]))
    remotes_free = iter(range(ssem.shape[0]))

    def local(make):
        sem = next(locals_free)
        return lambda: pltpu.make_async_copy(*make(), lsem.at[sem])

    def remote_at(dev, sem, make):
        source, target = make()
        return pltpu.make_async_remote_copy(
            src_ref=source,
            dst_ref=target,
            send_sem=ssem.at[sem],
            recv_sem=rsem.at[sem],
            device_id=device(*dev),
            device_id_type=MESH,
        )

    def remote(dev, make):
        sem = next(remotes_free)
        return lambda: remote_at(dev, sem, make)

    ends = []

    def go(build):
        build().start()
        ends.append(lambda: build().wait_send())

    def go_local(make):
        build = local(make)
        build().start()
        ends.append(lambda: build().wait())

    loads = {}

    def load(name, make):
        loads[name] = local(make)
        loads[name]().start()

    def need(*names):
        for name in names:
            loads.pop(name)().wait()

    def quarters(ref, size, ex):
        return ref.at[:, at(flip(C, 2 * ex), size)]

    load("nrm", lambda: (nrm, L.at[0]))
    load("nrm_s", lambda: (nrm_s, L.at[1]))
    for ex in range(2):
        load(("dinn", ex), lambda ex=ex: (quarters(dinn, cq, ex), D.at[ex, 0]))
        load(("dinn_s", ex), lambda ex=ex: (dinn_s.at[ex], D.at[ex, 1]))
    for ex in range(2):
        lanes = pl.ds(ex * wq, wq)
        load(("dout", ex), lambda ex=ex, lanes=lanes: (quarters(dout, wq, ex), DO.at[0, :, lanes]))
        load(
            ("dattn", ex), lambda ex=ex, lanes=lanes: (quarters(dattn, wq, ex), DA.at[0, :, lanes])
        )
    load("dout_s", lambda: (dout_s, DO.at[1]))
    load("dattn_s", lambda: (dattn_s, DA.at[1]))
    load("co", lambda: (cr, CO.at[0]))
    load("co_s", lambda: (cs, CO.at[1]))
    load("c", lambda: (ctx, CX))
    load("q", lambda: (q_in, Q))
    load("k", lambda: (k_in, K))
    load("v", lambda: (v_in, V))
    load("g", lambda: (dco, G.at[pl.ds(0, 2)]))
    load("g_s", lambda: (dcs_s, G.at[pl.ds(2, 2)]))
    for s in range(2):
        load(("lse", s), lambda s=s: (lse_in.at[s], LSE.at[s]))
    load("vec", lambda: (acc, VS.at[0]))
    load("w", lambda: (w_in, W))
    pl.semaphore_wait(barrier, len(partners))

    chunks = ff // 1024
    per = 1024 // ro

    def act_cols(t):
        return at(xor(f // per, t, chunks), 1024)

    class Unit:
        def __init__(self, P, RY, RZ, M):
            self.P, self.RY, self.RZ, self.M = P, RY, RZ, M
            self.y = [
                remote(Y, lambda a=a: (P.at[1, a], RY.at[a])) for a in range(A)
            ]
            self.z = [None] + [
                remote((0, 2 * a), lambda a=a: (P.at[0, a], RZ.at[a - 1])) for a in range(1, A)
            ]

        def start_y(self, a=None):
            for i in order if a is None else [a]:
                go(self.y[i])

        def fold_y(self, a):
            self.y[a]().wait_recv()
            self.P[0, a] = plus(self.P[0, a], self.RY[a])
            if a:
                go(self.z[a])

        def fold_z(self):
            for a in range(1, A):
                self.z[a]().wait_recv()
            self.M[...] = plus(self.P[0, 0], *[self.RZ[a - 1] for a in range(1, A)])

    order = list(range(1, A)) + [0]
    UI = [Unit(PI.at[ex], RYI.at[ex], RZI.at[ex], MI.at[ex]) for ex in range(2)]
    UU = Unit(PU.at[0], RYU, RZU, MU)
    UO = Unit(PO, RYO, RZO, MO)
    UQ = [Unit(PQ.at[j], RYQ.at[j], RZQ.at[j], MQ.at[j]) for j in range(3)]
    plan = Plan()

    xi = [remote(NEAR, lambda ex=ex: (MI.at[ex], RXI.at[ex])) for ex in range(2)]

    def inner_z(ex):
        UI[ex].fold_z()
        go(xi[ex])

    def cols_of(ref, e, size):
        return ref.at[:, at(flip(C, e), size)]

    i_core = [
        remote(CORE, lambda ex=ex: (RXI.at[1 - ex], cols_of(o_i, 2 * ex, cq))) for ex in range(2)
    ]

    def inner_x():
        for ex in range(2):
            xi[1 - ex]().wait_recv()
            RXI[1 - ex] = plus(MI[ex], RXI[1 - ex])
            go(i_core[ex])
            go_local(lambda ex=ex: (RXI.at[1 - ex], cols_of(o_i, 2 * ex, cq)))

    x_base = [next(remotes_free) for _ in range(n)][0]

    def outer_copy(i):
        return remote_at(NEAR, x_base + i, lambda: (PU.at[1, i % 2, i // 2], RXU.at[i % 2, i // 2]))

    def outer_x(i):
        outer_copy(i).wait_recv()
        PU[0, i % 2, i // 2] = plus(PU[0, i % 2, i // 2], RXU[i % 2, i // 2])
        if i % 2:
            UU.start_y(i // 2)

    u_near = remote(NEAR, lambda: (MU, cols_of(o_u, 0, wq)))
    u_core = remote(CORE, lambda: (MU, cols_of(o_u, 0, wq)))
    u_core2 = remote(CORE, lambda: (cols_of(o_u, 2, wq), cols_of(o_u, 2, wq)))

    def outer_z():
        UU.fold_z()
        go(u_near)
        go(u_core)
        go_local(lambda: (MU, cols_of(o_u, 0, wq)))

    def outer_end():
        u_near().wait_recv()
        go(u_core2)

    xo = remote(NEAR, lambda: (MO, RXO))
    o_core = [
        remote(
            CORE, lambda ex=ex: (RXO.at[pl.ds((1 - ex) * rs, rs)], cols_of(o_o, 2 * ex, wq))
        )
        for ex in range(2)
    ]

    def out_z():
        UO.fold_z()
        go(xo)

    def out_x():
        xo().wait_recv()
        for ex in range(2):
            mine, theirs = pl.ds(ex * rs, rs), pl.ds((1 - ex) * rs, rs)
            RXO[theirs] = plus(MO[mine], RXO[theirs])
            go(o_core[ex])
            go_local(
                lambda ex=ex: (RXO.at[pl.ds((1 - ex) * rs, rs)], cols_of(o_o, 2 * ex, wq))
            )

    outs = (o_q, o_k, o_v)
    xq = [remote(NEAR, lambda j=j: (MQ.at[j], RXQ.at[j])) for j in range(3)]
    q_core = [
        remote(CORE, lambda j=j: (RXQ.at[j], outs[j].at[:, at(core, hw)])) for j in range(3)
    ]

    def proj_z(j):
        UQ[j].fold_z()
        go(xq[j])

    def proj_x(j):
        xq[j]().wait_recv()
        RXQ[j] = plus(MQ[j], RXQ[j])
        go(q_core[j])
        go_local(lambda: (RXQ.at[j], outs[j].at[:, at(core, hw)]))

    hops = [CORE, NEAR] + [(0, 1 << b) for b in range(n.bit_length() - 1)]
    hop_copies = [
        remote(dev, lambda t=t: (VS.at[t], VR.at[t])) for t, dev in enumerate(hops)
    ]

    def vector_hop(t):
        if t:
            hop_copies[t - 1]().wait_recv()
            VS[t] = VS[t - 1] + VR[t - 1]
        if t < len(hops):
            go(hop_copies[t])
        else:
            go_local(lambda: (VS.at[t], o_vec))

    pairs = hw // (2 * HD)

    def attention(s, times):
        need(("lse", s))

        def body(step, carry):
            cols = at(step, 2 * HD)

            def get(ref):
                return ref[:, s, :, cols].reshape(slots * part, 2 * HD)

            mask = key_mask(lens[x * sh + s], C, part)
            dq, dk, dv = attend_back_pair(
                get(Q), get(K), get(V), mask, LSE[s % 2, :, cols], get(CX), get(G)
            )
            for ref, value in ((Q, dq), (K, dk), (V, dv)):
                ref[:, s, :, cols] = value.reshape(slots, part, 2 * HD)
            plan.beside(step, times)
            return carry

        lax.fori_loop(0, pairs, body, 0)
        if s + 2 < sh:
            load(("lse", s + 2), lambda: (lse_in.at[s + 2], LSE.at[s % 2]))

    groups = width // 256
    gsz = 256 // rs

    def weight_grad(get, P, times):
        def body(a, carry):
            cols = at(xor(f // gsz, a, groups), 256)
            r = (dot_tn(L[0, :, cols], get(0)) + dot_tn(L[1, :, cols], get(1))).astype(BF)
            for u in range(gsz):
                i = a * gsz + flip(f % gsz, u) if gsz > 1 else a
                P[i % 2, i // 2] = r[u * rs : (u + 1) * rs]
            plan.beside(a, times)
            return carry

        lax.fori_loop(0, groups, body, 0)

    def spaced(first, last, count):
        return [first + (last - first) * (t + 1) / count for t in range(count)]

    for k, a in enumerate(order):
        plan.add(15 + 6 * k, lambda a=a: UI[0].fold_y(a))
        plan.add(39 + 6 * k, lambda a=a: UI[1].fold_y(a))
        plan.add(66 + 3 * k, lambda a=a: UU.fold_y(a))
        plan.add(70 + 2 * k, lambda a=a: UO.fold_y(a))
        for j in range(3):
            plan.add(80 + 10 * j + 3 * k, lambda a=a, j=j: UQ[j].fold_y(a))
    xs_order = [t * per + il for t in range(chunks) for il in reversed(range(per))]
    for k, i in enumerate(xs_order):
        plan.add(19 + 6 * k, lambda i=i: outer_x(i))
    plan.add(60, lambda: inner_z(0))
    plan.add(76, lambda: inner_z(1))
    plan.add(86, inner_x)
    plan.add(92, outer_z)
    plan.add(100, outer_end)
    plan.add(94, out_z)
    plan.add(102, out_x)
    for j in range(3):
        plan.add(103 + 6 * j, lambda j=j: proj_z(j))
        plan.add(108 + 6 * j, lambda j=j: proj_x(j))
    for t in range(len(hops) + 1):
        plan.add(74 + 4 * t, lambda t=t: vector_hop(t))

    need("nrm", "nrm_s", ("dinn", 0), ("dinn_s", 0))
    weight_grad(lambda m: D[0, m], PI.at[0], spaced(4, 8, groups))
    UI[0].start_y()

    def act_load(t):
        slot = t % 2
        return [
            pltpu.make_async_copy(act.at[:, act_cols(t)], D.at[slot, 0], lsem.at[act_sem + 2 * slot]),
            pltpu.make_async_copy(
                act_s.at[:, act_cols(t)], D.at[slot, 1], lsem.at[act_sem + 2 * slot + 1]
            ),
        ]

    act_sem = [next(locals_free) for _ in range(4)][0]

    def begin_act(t):
        for c in act_load(t):
            c.start()

    begin_act(0)
    need(("dinn", 1), ("dinn_s", 1))
    weight_grad(lambda m: D[1, m], PI.at[1], spaced(8, 11, groups))
    UI[1].start_y()
    if chunks > 1:
        begin_act(1)
    load("x0", lambda: (xall.at[pl.ds(0, rows)], L.at[0]))
    load("x1", lambda: (xall.at[pl.ds(rows, rows)], L.at[1]))
    need(("dout", 0), ("dout", 1), "dout_s")

    outer_times = spaced(11, 25, n)

    def outer_body(u, carry):
        t, il = u // per, per - 1 - u % per
        slot = t % 2

        @pl.when(u % per == 0)
        def _():
            for c in act_load(t):
                c.wait()

        cols = at(xor(f % per, il, per), ro)
        r = dot_tn(D[slot, 0, :, cols], DO[0]) + dot_tn(D[slot, 1, :, cols], DO[1])
        r = r.astype(BF)
        i = t * per + il
        for ex in range(2):
            PU[ex, i % 2, i // 2] = r[:, ex * wq : (ex + 1) * wq]
        outer_copy(i).start()

        @pl.when((u % per == per - 1) & (t + 2 < chunks))
        def _():
            begin_act(t + 2)

        plan.beside(u, outer_times)
        return carry

    lax.fori_loop(0, n, outer_body, 0)

    need("co", "co_s", "c", ("dattn", 0), ("dattn", 1), "dattn_s")
    for half in range(2):
        for g in range(hw // 256):
            lanes = slice(g * 256, (g + 1) * 256)

            def left(m):
                if half:
                    return CO[m, :, lanes]
                return CX[2 * m : 2 * m + 2, :, :, lanes].reshape(rows, 256)

            r = (dot_tn(left(0), DA[0]) + dot_tn(left(1), DA[1])).astype(BF)
            group = (core + half * (1 - 2 * core)) * (hw // 256) + g
            for u in range(gsz):
                i = xor(group * gsz + u, f, n)
                for ex in range(2):
                    PO[i % 2, i // 2, ex * rs : (ex + 1) * rs] = r[
                        u * rs : (u + 1) * rs, ex * wq : (ex + 1) * wq
                    ]
        for job in plan.due(27 + 3 * half):
            job()
    UO.start_y()

    need("q", "k", "v", "g", "g_s")
    for s in range(sh):
        attention(s, spaced(30 + 8 * s, 38 + 8 * s, pairs))

    need("x0", "x1", "vec")
    for j, ref in enumerate((Q, K, V)):

        def right(m):
            return ref[2 * m : 2 * m + 2].reshape(rows, hw)

        if j != 1:
            total = jnp.sum(right(0).astype(F32), 0, keepdims=True)
            total = total + jnp.sum(right(1).astype(F32), 0, keepdims=True)
            VS[0, j // 2 : j // 2 + 1, at(core, hw)] = total
        weight_grad(right, PQ.at[j], spaced(54 + 6 * j, 60 + 6 * j, groups))
        UQ[j].start_y()

    need("w")

    def project(slot):
        out = None
        for j, ref in enumerate((Q, K, V)):
            p = dot_nt(ref[slot].reshape(half_rows, hw), W[j])
            out = p if out is None else out + p
        return out

    ig_swap = [remote(CORE, lambda ex=ex: (SB, ig_s.at[ex])) for ex in range(2)]
    for ex in (1, 0):
        value = project(2 + ex)
        if ex == 0:
            ig_swap[1]().wait_send()
        SB[...] = value
        ig_swap[ex]().start()
        for job in plan.due(80 - 4 * ex):
            job()

    def rows_of(ex):
        return pl.ds(ex * half_rows, half_rows)

    ig_near = remote(NEAR, lambda: (XS, o_igr))
    for ex in (1, 0):
        ig_swap[ex]().wait_recv()
        load(("ig", ex), lambda ex=ex: (ig_s.at[ex], IB))
        value = project(ex)
        if ex:
            ig_swap[0]().wait_send()
        load(("df", ex), lambda ex=ex: (dfirst.at[rows_of(ex)], SB))
        need(("ig", ex), ("df", ex))
        value = value + IB[...] + SB[...]
        if ex:
            XS[...] = value.astype(BF)
            go(ig_near)
        else:
            IB[...] = value
            go_local(lambda: (IB, o_igl))
        for job in plan.due(88 - 4 * ex):
            job()

    for job in plan.due(1e9):
        job()

    ig_near().wait_recv()
    for build in i_core + [u_core, u_core2] + o_core + q_core:
        build().wait_recv()
    for i in range(n):
        outer_copy(i).wait_send()
    for end in ends:
        end()


def back_call(lens, n, act, dout, nrm, dinn, dattn, ctx, cr, xall, q, k, v, lse, *rest):
    rows, width = nrm.shape
    ff = act.shape[1]
    slots, sh, part, hw = q.shape
    A = n // 2
    rs, ro, cq, wq = width // n, ff // n, ff // 4, width // 4
    hops = 2 + n.bit_length() - 1

    def bf(*shape):
        return jax.ShapeDtypeStruct(shape, BF)

    def f32(*shape):
        return jax.ShapeDtypeStruct(shape, F32)

    def vm(*shape):
        return pltpu.VMEM(shape, BF)

    def vf(*shape):
        return pltpu.VMEM(shape, F32)

    four = (slots, sh, part, hw)
    return pl.pallas_call(
        functools.partial(back_kernel, n),
        in_specs=[pl.BlockSpec(memory_space=pltpu.SMEM)] + [ANY] * 23,
        out_specs=[ANY] * 10,
        out_shape=[
            f32(rows // 2, width),
            bf(rows // 2, width),
            bf(rs, ff),
            bf(ro, width),
            bf(rs, width),
            bf(rs, width),
            bf(rs, width),
            bf(rs, width),
            f32(16, width),
            f32(2, rows // 2, width),
        ],
        scratch_shapes=[
            vm(*four),
            vm(*four),
            vm(*four),
            vm(*four),
            vm(*four),
            vf(2, *lse.shape[1:]),
            vm(2, rows, width),
            vm(2, 2, rows, 1024),
            vm(2, rows, 2 * wq),
            vm(2, rows, 2 * wq),
            vm(2, rows, hw),
            vm(3, width, hw),
            vm(2, 2, A, rs, cq),
            vm(2, 2, A, ro, wq),
            vm(2, A, 2 * rs, wq),
            vm(3, 2, A, rs, hw),
            vm(2, A, rs, cq),
            vm(2, A - 1, rs, cq),
            vm(2, rs, cq),
            vm(2, rs, cq),
            vm(2, A, ro, wq),
            vm(A, ro, wq),
            vm(A - 1, ro, wq),
            vm(ro, wq),
            vm(A, 2 * rs, wq),
            vm(A - 1, 2 * rs, wq),
            vm(2 * rs, wq),
            vm(2 * rs, wq),
            vm(3, A, rs, hw),
            vm(3, A - 1, rs, hw),
            vm(3, rs, hw),
            vm(3, rs, hw),
            vf(hops + 1, 16, width),
            vf(hops, 16, width),
            vf(rows // 2, width),
            vf(rows // 2, width),
            vm(rows // 2, width),
            pltpu.SemaphoreType.DMA((48,)),
            pltpu.SemaphoreType.DMA((64 + 8 * n,)),
            pltpu.SemaphoreType.DMA((64 + 8 * n,)),
        ],
        compiler_params=pltpu.CompilerParams(
            vmem_limit_bytes=BACK_LIMIT, collective_id=1, has_side_effects=True
        ),
        name="back",
    )(
        lens,
        act,
        dout,
        nrm,
        dinn,
        dattn,
        ctx,
        cr,
        xall,
        q,
        k,
        v,
        lse,
        *rest,
    )


def per_device(
    inputs,
    lengths,
    cotangent,
    query_weight,
    key_weight,
    value_weight,
    out_weight,
    inner_weight,
    outer_weight,
    query_bias,
    value_bias,
    out_bias,
    inner_bias,
    outer_bias,
    first_gain,
    first_shift,
    second_gain,
    second_shift,
):
    C = lax.axis_index("ctx")
    f = lax.axis_index("fsdp")
    n = lax.axis_size("fsdp")
    x, core = C // 2, C % 2
    seqs, part, width = inputs.shape
    ff = inner_weight.shape[1]
    sh = seqs // 2
    rows = 2 * sh * part
    rs, ro = width // n, ff // n
    hw = width // 2

    def pick(bit, a, b):
        return jnp.where(bit == 0, a, b), jnp.where(bit == 0, b, a)

    vectors = (
        query_bias,
        value_bias,
        out_bias,
        outer_bias,
        first_gain,
        first_shift,
        second_gain,
        second_shift,
    )
    vecs = jnp.concatenate([v.reshape(1, rs) for v in vectors], 0)
    if rs < 128:
        vecs = jnp.pad(vecs, ((0, 0), (0, 128 - rs)))
    vecs = jnp.concatenate(
        [vecs, inner_bias.reshape(ro // 128, 128), jnp.zeros((PACK - 8 - ro // 128, 128), BF)], 0
    )
    x4, cot, w_qkv, wi, wu, wo, vecs, q4, k4, v4, c4, c_r, c_s, lse = front_call(
        lengths,
        inputs,
        cotangent,
        query_weight,
        key_weight,
        value_weight,
        vecs,
        out_weight,
        inner_weight,
        outer_weight,
        n,
    )
    xall = x4.reshape(2 * rows, width)
    ctx, cr = c4.reshape(2 * rows, hw), c_r.reshape(rows, hw)
    two = (2, sh, part, hw)
    (
        dfirst,
        dco,
        acc,
        act,
        nrm,
        dout,
        dinn,
        dattn,
        layer_out,
        act_s,
        dout_s,
        dinn_s,
        nrm_s,
        dattn_s,
        dcs_s,
    ) = ffn_call(lengths, sh, ctx, cr, xall, cot.reshape(rows, width), vecs, wo, wi, wu)

    ig_here, ig_near, g_i, g_u, g_o, g_q, g_k, g_v, sums, _ = back_call(
        lengths,
        n,
        act,
        dout,
        nrm,
        dinn,
        dattn,
        c4,
        cr,
        xall,
        q4,
        k4,
        v4,
        lse,
        dco.reshape(two),
        dfirst,
        w_qkv,
        acc,
        act_s,
        dout_s,
        dinn_s,
        nrm_s,
        dattn_s,
        dcs_s.reshape(two),
        c_s.reshape(rows, hw),
    )
    own = lax.dynamic_slice_in_dim(sums[:8], f * rs, rs, 1)
    own_inner = lax.dynamic_slice_in_dim(sums[8 : 8 + ff // width].reshape(ff), f * ro, ro, 0)
    third = (sh, part, width)
    input_grad = jnp.concatenate(
        pick(x, ig_here.reshape(third), ig_near.reshape(third).astype(F32)), 0
    )
    grad_query, grad_key, grad_value, grad_out, grad_inner, grad_outer = (
        g.astype(F32) for g in (g_q, g_k, g_v, g_o, g_i, g_u)
    )

    return (
        layer_out,
        input_grad,
        grad_query,
        grad_key,
        grad_value,
        grad_out,
        grad_inner,
        grad_outer,
        own[0],
        own[1],
        own[2],
        own_inner,
        own[3],
        own[4],
        own[5],
        own[6],
        own[7],
    )


def solution(mesh):
    rowed = P("fsdp", "ctx", None)
    matrix, vector = P("fsdp", None), P("fsdp")
    in_specs = (rowed, vector, rowed) + (matrix,) * 6 + (vector,) * 9
    out_specs = (rowed, rowed) + (matrix,) * 6 + (vector,) * 9
    return jax.shard_map(
        per_device, mesh=mesh, in_specs=in_specs, out_specs=out_specs, check_vma=False
    )
```

```python
import functools

import jax
import jax.numpy as jnp
from jax import lax
from jax.experimental import pallas as pl
from jax.experimental.pallas import tpu as pltpu
from jax.sharding import PartitionSpec as P

HD = 64
EPSILON = 1e-05
BF = jnp.bfloat16
F32 = jnp.float32
ANY = pl.BlockSpec(memory_space=pl.ANY)
NT = (((1,), (1,)), ((), ()))
TN = (((0,), (0,)), ((), ()))
VMEM_LIMIT = 58 << 20
BACK_LIMIT = 60 << 20
WINDOW = 3


def dot(a, b):
    return jnp.dot(a, b, preferred_element_type=F32)


def dot_nt(a, b):
    return lax.dot_general(a, b, NT, preferred_element_type=F32)


def dot_tn(a, b):
    return lax.dot_general(a, b, TN, preferred_element_type=F32)


def params(**more):
    return pltpu.CompilerParams(vmem_limit_bytes=VMEM_LIMIT, **more)


def cost(flops, size, trans=0):
    return pl.CostEstimate(flops=int(flops), bytes_accessed=int(size), transcendentals=int(trans))


MESH = pl.DeviceIdType.MESH
PACK = 16


def flip(v, mask):
    out, bit = v, 1
    while bit <= mask:
        if mask & bit:
            out = out + bit - 2 * bit * ((v // bit) % 2)
        bit *= 2
    return out


def at(index, size):
    return pl.ds(pl.multiple_of(index * size, size), size)


def spread(read, n, rs):
    per = max(128 // rs, 1)
    tiles = []
    for t in range(n // per):
        tile = read(t * per)
        for u in range(1, per):
            tile = tile + pltpu.roll(read(t * per + u), u * rs, 1)
        tiles.append(tile)
    return jnp.concatenate(tiles, 1)


def front_kernel(
    n,
    lens,
    xin,
    cin,
    wq,
    wk,
    wv,
    vecs,
    wo_in,
    wi_in,
    wu_in,
    xo,
    co,
    wqkvo,
    wio,
    wuo,
    woo,
    veco,
    qo,
    ko,
    vo,
    cxo,
    cro,
    cso,
    lseo,
    X,
    W,
    VEC,
    Q,
    K,
    V,
    CX,
    LSE,
    lsem,
    ssem,
    rsem,
):
    C, f = lax.axis_index("ctx"), lax.axis_index("fsdp")
    x, core = C // 2, C % 2
    A = n // 2
    sh, part, width = X.shape[1:]
    hw = W.shape[2]
    ff = wio.shape[1]
    rs, ro, cq = width // n, ff // n, ff // 4

    partners = [(0, 2 * k) for k in range(1, A)] + [(0, 1), (2, 0), (1, 0)]

    def device(dc, df):
        return (flip(C, dc), flip(f, df))

    barrier = pltpu.get_barrier_semaphore()
    for p in partners:
        pl.semaphore_signal(barrier, inc=1, device_id=device(*p), device_id_type=MESH)

    local = []
    used = iter(range(lsem.shape[0]))

    def begin(source, target):
        c = pltpu.make_async_copy(source, target, lsem.at[next(used)])
        c.start()
        return c

    def keep(source, target):
        local.append(begin(source, target))

    x_here = begin(xin.at[pl.ds(x * sh, sh)], X.at[0])
    w_here = [begin(w.at[:, at(core, hw)], W.at[j, at(f, rs)]) for j, w in enumerate((wq, wk, wv))]
    w_here.append(begin(vecs, VEC.at[f]))

    pl.semaphore_wait(barrier, len(partners))

    def remote(source, target, sem, dev):
        return pltpu.make_async_remote_copy(
            src_ref=source,
            dst_ref=target,
            send_sem=ssem.at[sem],
            recv_sem=rsem.at[sem],
            device_id=device(*dev),
            device_id_type=MESH,
        )

    sent = []

    def send(*what):
        c = remote(*what)
        c.start()
        sent.append(c)

    seen = set()

    def arrive(target, sem, dev):
        if sem not in seen:
            seen.add(sem)
            remote(target, target, sem, dev).wait_recv()

    X1, X2, X3, COT, CTX, CTX2 = range(6)
    send(xin.at[pl.ds((1 - x) * sh, sh)], X.at[1], X1, (2, 0))

    def rows_at(ref, first, size):
        return ref.at[pl.ds(pl.multiple_of(first, size), size)]

    hr, hu = rs // 2, ro // 2

    def projection(j):
        w = (wq, wk, wv)[j]
        return (
            1,
            lambda e, s: [W.at[j, at(s, rs)]] + [VEC.at[s]] * (j == 0),
            lambda: [w.at[:, at(core, hw)]] + [vecs] * (j == 0),
        )

    def inner_part(h):
        return (
            4,
            lambda e, s: [wio.at[at(s * 2 + h, hr), at(flip(C, e), cq)]],
            lambda: [wi_in.at[pl.ds(h * hr, hr), at(C, cq)]],
        )

    outer_a = (
        4,
        lambda e, s: [rows_at(wuo, s * ro + flip(C, e) * (hu // 4), hu // 4)],
        lambda: [rows_at(wu_in, C * (hu // 4), hu // 4)],
    )
    out_part = (
        4,
        lambda e, s: [rows_at(woo, s * rs + flip(C, e) * (rs // 4), rs // 4)],
        lambda: [rows_at(wo_in, C * (rs // 4), rs // 4)],
    )

    def outer_b(h):
        return (
            2,
            lambda e, s: [rows_at(wuo, s * ro + hu + (flip(core, e) * 2 + h) * (hu // 4), hu // 4)],
            lambda: [rows_at(wu_in, hu + (core * 2 + h) * (hu // 4), hu // 4)],
        )

    kinds = [
        inner_part(0),
        projection(0),
        projection(1),
        projection(2),
        inner_part(1),
        outer_a,
        out_part,
        outer_b(0),
        outer_b(1),
    ]
    sems, ready = {}, 6
    for k, (parts, place, _) in enumerate(kinds):
        for e in range(parts):
            for i in range(1, n):
                for u in range(2 if k == 1 else 1):
                    sems[k, e, i, u] = ready
                    ready += 1

    def route(parts, e, i):
        if e % 2:
            return (1, 0), (e - 1, i)
        if e:
            return (2, 0), (0, i)
        if i % 2:
            return (0, 1), (0, i - 1)
        return (0, i), (0, 0)

    def copies(k, e, i):
        parts, place, own = kinds[k]
        dev, (pe, pi) = route(parts, e, i)
        target = place(pe, flip(f, pi))
        source = target if pi else own()
        return [
            remote(source[u], target[u], sems[k, e, i, u], dev) for u in range(len(target))
        ]

    issued = []

    def give(k, e, i):
        for c in copies(k, e, i):
            c.start()
        issued.append((k, e, i))

    got = set()

    def take(k, e, i):
        if (k, e, i) in got:
            return
        got.add((k, e, i))
        parts, place, _ = kinds[k]
        dev, _ = route(parts, e, i)
        for u, target in enumerate(place(e, flip(f, i))):
            remote(target, target, sems[k, e, i, u], dev).wait_recv()

    def hand_on(k, i):
        parts = kinds[k][0]
        if parts == 4:
            give(k, 2, i)
        if parts > 1:
            give(k, 1, i)

    def base(k):
        if k < len(kinds):
            for a in range(1, A):
                give(k, 0, 2 * a)
            give(k, 0, 1)

    def z_in(k):
        for a in range(1, A):
            take(k, 0, 2 * a)
            give(k, 0, 2 * a + 1)
            hand_on(k, 2 * a)

    def y_in(k):
        for i in range(1, n, 2):
            take(k, 0, i)
            hand_on(k, i)

    def x_in(k):
        if kinds[k][0] == 4:
            for i in range(1, n):
                take(k, 2, i)
                give(k, 3, i)

    base(0)
    base(1)
    x_here.wait()
    send(X.at[0], X.at[2], X2, (1, 0))
    keep(cin.at[pl.ds(x * sh, sh)], co.at[0])
    keep(wo_in, woo.at[at(f, rs)])
    keep(wi_in, wio.at[at(f, rs)])
    keep(wu_in, wuo.at[at(f, ro)])
    for c in w_here:
        c.wait()
    send(cin.at[pl.ds((1 - x) * sh, sh)], co.at[1], COT, (2, 0))

    slots = X.shape[0]
    pairs = hw // (2 * HD)

    z_in(0)
    base(2)
    arrive(X.at[1], X1, (2, 0))
    send(X.at[1], X.at[3], X3, (1, 0))
    z_in(1)
    base(3)
    y_in(0)
    arrive(X.at[2], X2, (1, 0))
    arrive(X.at[3], X3, (1, 0))
    keep(X, xo)
    z_in(2)
    base(4)
    y_in(1)
    keep(VEC, veco)

    def bias(row):
        read = lambda s: VEC[pl.ds(core * (n // 2) + s, 1), row : row + 1, :128].reshape(1, 128).astype(F32)
        return spread(read, n // 2, rs)

    shape = (sh, part, hw)

    def project(j, target, add):
        def body(slot, carry):
            value = dot(X[slot].reshape(sh * part, width), W[j])
            if add is not None:
                value = value + add
            target[slot] = value.astype(BF).reshape(shape)
            return carry

        lax.fori_loop(0, slots, body, 0)

    project(0, Q, bias(0))
    z_in(3)
    base(5)
    y_in(2)
    project(1, K, None)
    x_in(0)
    z_in(4)
    base(6)
    y_in(3)
    keep(W, wqkvo)
    project(2, V, bias(1))
    keep(Q, qo)
    keep(K, ko)
    keep(V, vo)

    jobs = [
        lambda: z_in(5),
        lambda: base(7),
        lambda: y_in(4),
        lambda: z_in(6),
        lambda: base(8),
        lambda: y_in(5),
        lambda: x_in(4),
    ]
    steps = sh * pairs

    def attend(step, carry):
        s, pair = step // pairs, step % pairs
        cols = at(pair, 2 * HD)

        def load(ref):
            return ref[:, s, :, cols].reshape(slots * part, 2 * HD)

        q, k, v = load(Q), load(K), load(V)
        mask = key_mask(lens[x * sh + s], C, part)
        o, lse = attend_pair(q, k, v, mask)
        CX[:, s, :, cols] = o.reshape(slots, part, 2 * HD)
        LSE[s, :, cols] = lse
        for t in range(steps):
            now = jobs[len(jobs) * t // steps : len(jobs) * (t + 1) // steps]
            if now:

                @pl.when(step == t)
                def _():
                    for job in now:
                        job()

        return carry

    lax.fori_loop(0, steps, attend, 0)
    send(CX.at[pl.ds(2, 2)], cro, CTX, (1, 0))
    send(CX.at[pl.ds(0, 2)], cso, CTX2, (1, 0))
    keep(CX, cxo)
    keep(LSE, lseo)
    z_in(7)
    y_in(6)
    x_in(5)
    z_in(8)
    y_in(7)
    x_in(6)
    y_in(8)
    for k, (parts, _, _) in enumerate(kinds):
        for e in range(parts):
            for i in range(1, n):
                take(k, e, i)
    arrive(co.at[1], COT, (2, 0))
    arrive(cro, CTX, (1, 0))
    arrive(cso, CTX2, (1, 0))
    for what in issued:
        for c in copies(*what):
            c.wait_send()
    for c in sent:
        c.wait_send()
    for c in local:
        c.wait()


def front_call(lengths, xin, cin, wq, wk, wv, vecs, wo, wi, wu, n):
    seqs, part, width = xin.shape
    sh, ff, hw = seqs // 2, wi.shape[1], width // 2

    def bf(*shape):
        return jax.ShapeDtypeStruct(shape, BF)

    def vm(*shape):
        return pltpu.VMEM(shape, BF)

    full = 4 * part
    lse = (sh, full, hw)
    four = (4, sh, part, hw)
    sems = 24 * n
    return pl.pallas_call(
        functools.partial(front_kernel, n),
        in_specs=[pl.BlockSpec(memory_space=pltpu.SMEM)] + [ANY] * 9,
        out_specs=[ANY] * 14,
        out_shape=[
            bf(4, sh, part, width),
            bf(2, sh, part, width),
            bf(3, width, hw),
            bf(width, ff),
            bf(ff, width),
            bf(width, width),
            bf(n, PACK, 128),
            bf(*four),
            bf(*four),
            bf(*four),
            bf(*four),
            bf(2, sh, part, hw),
            bf(2, sh, part, hw),
            jax.ShapeDtypeStruct(lse, F32),
        ],
        scratch_shapes=[
            vm(4, sh, part, width),
            vm(3, width, hw),
            vm(n, PACK, 128),
            vm(*four),
            vm(*four),
            vm(*four),
            vm(*four),
            pltpu.VMEM(lse, F32),
            pltpu.SemaphoreType.DMA((24,)),
            pltpu.SemaphoreType.DMA((sems,)),
            pltpu.SemaphoreType.DMA((sems,)),
        ],
        compiler_params=params(collective_id=0, has_side_effects=True),
        name="front",
    )(lengths, xin, cin, wq, wk, wv, vecs, wo, wi, wu)


def lanes_of(shape, head):
    lane = lax.broadcasted_iota(jnp.int32, shape, 1)
    own = (lane < HD) if head == 0 else (lane >= HD)
    return lane, own, (HD if head == 0 else 0)


def split3(a):
    hi = a.astype(BF).astype(F32)
    mid = (a - hi).astype(BF).astype(F32)
    return hi, mid, a - hi - mid


def flat(ref):
    a = ref[...]
    return a.reshape(-1, a.shape[-1])


def key_mask(length, C, part):
    row = lax.broadcasted_iota(jnp.int32, (part, 2 * HD), 0)
    out = []
    for e in (0, 2, 1, 3):
        inside = row + flip(C, e) * part < length
        out.append(jnp.where(inside, 0.0, -1e30).astype(BF))
    return jnp.concatenate(out, 0)


def attend_pair(q, k, v, mask):
    out = []
    for head in range(2):
        lane, own, other = lanes_of(q.shape, head)
        qh = jnp.where(own, q * BF(HD**-0.5), jnp.where(lane == other, 1.0, 0.0).astype(BF))
        kh = jnp.where(own, k, mask)
        s = dot_nt(qh, kh)
        top = jnp.max(s, -1, keepdims=True)
        e = jnp.exp(s - top)
        total = jnp.sum(e, -1, keepdims=True)
        o = dot(e.astype(BF), v) * (1.0 / total)
        out.append((o, top + jnp.log(total), own))
    (o0, l0, own), (o1, l1, _) = out
    return jnp.where(own, o0, o1).astype(BF), jnp.where(own, l1, l0)


def attend_back_pair(q, k, v, mask, lse, c, g):
    qs = q * BF(HD**-0.5)
    kt = k.T
    prod = c.astype(F32) * g.astype(F32)
    res = []
    for head in range(2):
        lane, own, o = lanes_of(q.shape, head)
        hi, mid, low = split3(-lse)
        extra = jnp.where(
            lane == o,
            1.0,
            jnp.where(
                lane == o + 1,
                hi,
                jnp.where(lane == o + 2, mid, jnp.where(lane == o + 3, low, 0.0)),
            ),
        ).astype(BF)
        qh = jnp.where(own, qs, extra)
        kh = jnp.where(own, k, jnp.where(lane == o, mask, BF(1)))
        p = jnp.exp(dot_nt(kh, qh))
        delta = jnp.sum(jnp.where(own, prod, 0.0), -1, keepdims=True)
        hi, mid, low = split3(-delta)
        extra = jnp.where(
            lane == o, hi, jnp.where(lane == o + 1, mid, jnp.where(lane == o + 2, low, 0.0))
        ).astype(BF)
        gh = jnp.where(own, g, extra)
        vh = jnp.where(own, v, BF(1))
        ds = (p * dot_nt(vh, gh)).astype(BF)
        dv = dot(p.astype(BF), g)
        dk = dot(ds, qs)
        dqt = dot(kt, ds)
        res.append((dv, dk, dqt, own))
    (dv0, dk0, dq0, own), (dv1, dk1, dq1, _) = res
    dqt = jnp.concatenate([dq0[:HD], dq1[HD:]], 0) * (HD**-0.5)
    return dqt.T.astype(BF), jnp.where(own, dk0, dk1).astype(BF), jnp.where(own, dv0, dv1).astype(BF)


def gelu_pair(u):
    e = jnp.exp(u * u * -0.5)
    t = 1.0 / (1.0 + (0.3275911 * 0.7071067811865476) * jnp.abs(u))
    poly = t * (
        0.254829592 * 0.5
        + t
        * (
            -0.284496736 * 0.5
            + t * (1.421413741 * 0.5 + t * (-1.453152027 * 0.5 + t * (1.061405429 * 0.5)))
        )
    )
    tail = poly * e
    cdf = jnp.where(u >= 0, 1.0 - tail, tail)
    ucdf = u * cdf
    return ucdf, cdf + u * (e * 0.3989422804014327)


def normalise(h):
    c = h - jnp.mean(h, -1, keepdims=True)
    r = lax.rsqrt(jnp.mean(c * c, -1, keepdims=True) + EPSILON)
    return c * r, r


def normalise_back(dyg, hat, r):
    return r * (
        dyg - jnp.mean(dyg, -1, keepdims=True) - hat * jnp.mean(dyg * hat, -1, keepdims=True)
    )


def ffn_kernel(n, sh, part, lens, cm, cr, xm, cot, vecs, wo_in, wi_in, wu_in, *refs):
    dfirst, dco, acc = refs[:3]
    homes, (o_lo, act_s, dout_s, dinn_s, nrm_s, dattn_s, dcs_s) = refs[3:8], refs[8:15]
    wo, wi, wu, gp, vec, ib, *twice, sem, csem, hsem, ssem, rsem = refs[15:]
    width, ff = wi.shape
    C, f = lax.axis_index("ctx"), lax.axis_index("fsdp")
    x, core = C // 2, C % 2
    step = pl.program_id(0)
    turn = 2 - step
    rs, ro = width // n, ff // n
    cq, hw = ff // 4, width // 2

    pairs = ((wo_in, wo), (wi_in, wi), (wu_in, wu))

    def copy(kind):
        return pltpu.make_async_copy(*pairs[kind], sem.at[kind])

    CORE, NEAR = flip(C, 1), flip(C, 2)
    block, wq = xm.shape[0], width // 4

    def remote(t, j, to, source, target):
        return pltpu.make_async_remote_copy(
            src_ref=source,
            dst_ref=target,
            send_sem=ssem.at[t, j],
            recv_sem=rsem.at[t, j],
            device_id=(to, f),
            device_id_type=MESH,
        )

    KINDS = ("act", "nrm", "dout0", "dout1", "dinn0", "dinn1", "dattn0", "dattn1", "dcs")

    def rows_of(t):
        return pl.ds(pl.multiple_of(t * block, block), block)

    def held(t):
        return [ref.at[(2 - t) % 2] for ref in twice]

    act, nrm, dout, dinn, dattn, dcs, lo = held(turn)
    HOME = {"act": 0, "nrm": 1, "dout": 2, "dinn": 3, "dattn": 4}

    def home(t, name):
        j = HOME[name]
        return pltpu.make_async_copy(held(t)[j], homes[j].at[rows_of(t)], hsem.at[t, j])

    def to_core(t, *names):
        out = []
        for name in names or KINDS:
            rows = rows_of(t)
            act, nrm, dout, dinn, dattn, dcs, _ = held(t)
            ex = int(name[-1]) if name[-1] in "01" else 0
            other, lanes = flip(C, 2 * ex + 1), pl.ds(ex * wq, wq)
            source, target = {
                "act": lambda: (act, act_s.at[rows]),
                "nrm": lambda: (nrm, nrm_s.at[rows]),
                "dcs": lambda: (dcs, dcs_s.at[rows]),
                "dou": lambda: (dout.at[:, at(other, wq)], dout_s.at[rows, lanes]),
                "dat": lambda: (dattn.at[:, at(other, wq)], dattn_s.at[rows, lanes]),
                "din": lambda: (dinn.at[:, at(other, cq)], dinn_s.at[ex, rows]),
            }[name[:3]]()
            out.append(remote(t, KINDS.index(name), CORE, source, target))
        return out

    def start(name):
        for c in to_core(turn, *(k for k in KINDS if k.startswith(name))):
            c.start()
        if name in HOME:
            home(turn, name).start()

    def end(t, name):
        for c in to_core(t, *(k for k in KINDS if k.startswith(name))):
            c.wait_send()
        if name in HOME:
            home(t, name).wait()

    def free(name):
        @pl.when(step == 2)
        def _():
            end(2, name)

    def slots_of(t, ex):
        count = block // part
        return [u for u in range(count) if (t * count + u) // sh == ex]

    def place(t, u):
        return held(t)[6].at[pl.ds(u * part, part)], o_lo.at[x * sh + (t * (block // part) + u) % sh]

    def to_near(t):
        return [remote(t, 9 + u, NEAR, *place(t, u)) for u in slots_of(t, 1)]

    def stay(t):
        return [pltpu.make_async_copy(*place(t, u), csem.at[t, u]) for u in slots_of(t, 0)]

    def send(t):
        for c in to_near(t) + stay(t):
            c.start()

    def sent(t):
        for c in to_near(t):
            c.wait_send()
        for c in stay(t):
            c.wait()

    def received(t):
        for c in to_core(t) + to_near(t):
            c.wait_recv()

    @pl.when(step == 0)
    def _():
        barrier = pltpu.get_barrier_semaphore()
        for to in (CORE, NEAR):
            pl.semaphore_signal(barrier, inc=1, device_id=(to, f), device_id_type=MESH)
        pl.semaphore_wait(barrier, 2)
        for kind in range(3):
            copy(kind).start()
        acc[...] = jnp.zeros_like(acc)
        vec[...] = spread(lambda s: vecs[s, :8, :128].astype(F32), n, rs)
        for s in range(n):
            for t in range(ro // 128):
                first = s * ro + t * 128
                ib[:, first : first + 128] = vecs[s, 8 + t : 9 + t, :].astype(F32)

    def arrived(kind):
        @pl.when(step == 0)
        def _():
            copy(kind).wait()

    count = xm.shape[0] // part
    inside = []
    for u in range(count):
        slot = turn * count + u
        ex, s = slot // sh, slot % sh
        first = (C + ex * (2 - 4 * x)) * part
        row = lax.broadcasted_iota(jnp.int32, (part, 1), 0) + first
        inside.append(jnp.where(row < lens[x * sh + s], 1.0, 0.0))
    valid = jnp.concatenate(inside, 0)
    own, other = at(core, hw), at(1 - core, hw)

    def add(row, value):
        acc[row : row + 1, :] += jnp.sum(value, 0, keepdims=True)

    arrived(0)
    first = (
        xm[...].astype(F32) + (dot(cm[...], wo[own]) + dot(cr[...], wo[other])) + vec[2:3, :]
    )
    hat1, r1 = normalise(first)
    normed = hat1 * vec[4:5, :] + vec[5:6, :]
    low = normed.astype(BF)
    free("act")
    free("nrm")
    nrm[...] = low
    start("nrm")
    arrived(1)
    for j in range(4):
        cols = slice(j * cq, (j + 1) * cq)
        g, d = gelu_pair(dot(low, wi[:, cols]) + ib[:, cols])
        act[:, cols] = g.astype(BF)
        gp[:, cols] = d
    start("act")
    arrived(2)
    second = normed + (dot(act[...], wu[...]) + vec[3:4, :])
    hat2, r2 = normalise(second)
    @pl.when(step == 2)
    def _():
        sent(2)

    lo[...] = (hat2 * vec[6:7, :] + vec[7:8, :]).astype(BF)
    og = cot[...].astype(F32) * valid
    add(6, og * hat2)
    add(7, og)
    d2 = normalise_back(og * vec[6:7, :], hat2, r2)
    d2low = d2.astype(BF)
    free("dout")
    dout[...] = d2low
    start("dout")
    for t in range(3):

        @pl.when(turn == t)
        def _():
            send(t)

    add(3, d2low.astype(F32))
    free("dinn")
    for j in range(4):
        cols = slice(j * cq, (j + 1) * cq)
        di = (dot_nt(d2low, wu[cols, :]) * gp[:, cols]).astype(BF)
        dinn[:, cols] = di
        add(8 + j, di.astype(F32))
    start("dinn")
    dn = d2 + dot_nt(dinn[...], wi[...])
    add(4, dn * hat1)
    add(5, dn)
    d1 = normalise_back(dn * vec[4:5, :], hat1, r1)
    dfirst[...] = d1
    d1low = d1.astype(BF)
    free("dattn")
    free("dcs")
    dattn[...] = d1low
    start("dattn")
    add(2, d1low.astype(F32))
    dcs[...] = dot_nt(d1low, wo[other]).astype(BF)
    start("dcs")
    dco[...] = dot_nt(d1low, wo[own]).astype(BF)

    @pl.when(turn == 0)
    def _():
        for t in range(2):
            for name in ("act", "nrm", "dout", "dinn", "dattn", "dcs"):
                end(t, name)
            sent(t)
        for t in range(3):
            received(t)


def ffn_call(lens, sh, c, cr, xall, cot, vecs, wo, wi, wu):
    width, ff = wi.shape
    n, rows = vecs.shape[0], cot.shape[0]
    block, part = rows // 3, rows // (2 * sh)
    hw = width // 2

    def by(cols):
        return pl.BlockSpec((block, cols), lambda i: (2 - i, 0))

    def whole(*shape):
        return pl.BlockSpec(shape, lambda i: (0,) * len(shape))

    grid_spec = pl.GridSpec(
        grid=(3,),
        in_specs=[pl.BlockSpec(memory_space=pltpu.SMEM), by(hw), by(hw), by(width), by(width), whole(*vecs.shape), ANY, ANY, ANY],
        out_specs=[by(width), by(hw), whole(16, width)] + [ANY] * 12,
        scratch_shapes=[
            pltpu.VMEM((width, width), BF),
            pltpu.VMEM((width, ff), BF),
            pltpu.VMEM((ff, width), BF),
            pltpu.VMEM((block, ff), F32),
            pltpu.VMEM((8, width), F32),
            pltpu.VMEM((1, ff), F32),
            *(
                pltpu.VMEM((2, block, cols), BF)
                for cols in (ff, width, width, ff, width, hw, width)
            ),
            pltpu.SemaphoreType.DMA((3,)),
            pltpu.SemaphoreType.DMA((3, block // part)),
            pltpu.SemaphoreType.DMA((3, 5)),
            pltpu.SemaphoreType.DMA((3, 9 + block // part)),
            pltpu.SemaphoreType.DMA((3, 9 + block // part)),
        ],
    )

    def shape(cols, dtype=BF):
        return jax.ShapeDtypeStruct((rows, cols), dtype)

    return pl.pallas_call(
        functools.partial(ffn_kernel, n, sh, part),
        grid_spec=grid_spec,
        out_shape=[
            shape(width, F32),
            shape(hw),
            jax.ShapeDtypeStruct((16, width), F32),
            shape(ff),
            shape(width),
            shape(width),
            shape(ff),
            shape(width),
            jax.ShapeDtypeStruct((2 * sh, part, width), BF),
            shape(ff),
            shape(hw),
            jax.ShapeDtypeStruct((2, rows, ff // 4), BF),
            shape(width),
            shape(hw),
            shape(hw),
        ],
        compiler_params=params(collective_id=2, has_side_effects=True),
        cost_estimate=cost(
            2 * rows * width * (2 * width + 4 * ff), 30 * rows * width + 2 * width * (2 * ff + width)
        ),
        name="ffn",
    )(lens, c, cr, xall, cot, vecs, wo, wi, wu)


def xor(a, b, count):
    out, bit = 0, 1
    while bit < count:
        out = out + bit * ((a // bit + b // bit) % 2)
        bit *= 2
    return out


def plus(*items):
    out = items[0].astype(F32)
    for i in items[1:]:
        out = out + i.astype(F32)
    return out.astype(BF)


class Plan:
    def __init__(self):
        self.jobs = []

    def add(self, time, job):
        self.jobs.append((time, len(self.jobs), job))
        self.jobs.sort(key=lambda j: j[:2])

    def due(self, time):
        out = [j[2] for j in self.jobs if j[0] <= time]
        self.jobs = [j for j in self.jobs if j[0] > time]
        return out

    def beside(self, step, times):
        for t, time in enumerate(times):
            jobs = self.due(time)
            if jobs:

                @pl.when(step == t)
                def _():
                    for job in jobs:
                        job()


def back_kernel(
    n,
    lens,
    act,
    dout,
    nrm,
    dinn,
    dattn,
    ctx,
    cr,
    xall,
    q_in,
    k_in,
    v_in,
    lse_in,
    dco,
    dfirst,
    w_in,
    acc,
    act_s,
    dout_s,
    dinn_s,
    nrm_s,
    dattn_s,
    dcs_s,
    cs,
    o_igl,
    o_igr,
    o_i,
    o_u,
    o_o,
    o_q,
    o_k,
    o_v,
    o_vec,
    ig_s,
    Q,
    K,
    V,
    CX,
    G,
    LSE,
    L,
    D,
    DO,
    DA,
    CO,
    W,
    PI,
    PU,
    PO,
    PQ,
    RYI,
    RZI,
    MI,
    RXI,
    RXU,
    RYU,
    RZU,
    MU,
    RYO,
    RZO,
    MO,
    RXO,
    RYQ,
    RZQ,
    MQ,
    RXQ,
    VS,
    VR,
    SB,
    IB,
    XS,
    lsem,
    ssem,
    rsem,
):
    C, f = lax.axis_index("ctx"), lax.axis_index("fsdp")
    x, core = C // 2, C % 2
    A = n // 2
    slots, sh, part, hw = Q.shape
    rows, width = nrm.shape
    ff = act.shape[1]
    rs, ro, cq, wq = width // n, ff // n, ff // 4, width // 4
    half_rows = rows // 2
    CORE, NEAR, Y = (1, 0), (2, 0), (0, 1)

    def device(dc, df):
        return (flip(C, dc), flip(f, df))

    partners = [(0, 2 * k) for k in range(1, A)] + [Y, NEAR, CORE]
    barrier = pltpu.get_barrier_semaphore()
    for p in partners:
        pl.semaphore_signal(barrier, inc=1, device_id=device(*p), device_id_type=MESH)

    locals_free = iter(range(lsem.shape[0]))
    remotes_free = iter(range(ssem.shape[0]))

    def local(make):
        sem = next(locals_free)
        return lambda: pltpu.make_async_copy(*make(), lsem.at[sem])

    def remote_at(dev, sem, make):
        source, target = make()
        return pltpu.make_async_remote_copy(
            src_ref=source,
            dst_ref=target,
            send_sem=ssem.at[sem],
            recv_sem=rsem.at[sem],
            device_id=device(*dev),
            device_id_type=MESH,
        )

    def remote(dev, make):
        sem = next(remotes_free)
        return lambda: remote_at(dev, sem, make)

    ends = []

    def go(build):
        build().start()
        ends.append(lambda: build().wait_send())

    def go_local(make):
        build = local(make)
        build().start()
        ends.append(lambda: build().wait())

    loads = {}

    def load(name, make):
        loads[name] = local(make)
        loads[name]().start()

    def need(*names):
        for name in names:
            loads.pop(name)().wait()

    def quarters(ref, size, ex):
        return ref.at[:, at(flip(C, 2 * ex), size)]

    load("nrm", lambda: (nrm, L.at[0]))
    load("nrm_s", lambda: (nrm_s, L.at[1]))
    for ex in range(2):
        load(("dinn", ex), lambda ex=ex: (quarters(dinn, cq, ex), D.at[ex, 0]))
        load(("dinn_s", ex), lambda ex=ex: (dinn_s.at[ex], D.at[ex, 1]))
    for ex in range(2):
        lanes = pl.ds(ex * wq, wq)
        load(("dout", ex), lambda ex=ex, lanes=lanes: (quarters(dout, wq, ex), DO.at[0, :, lanes]))
        load(
            ("dattn", ex), lambda ex=ex, lanes=lanes: (quarters(dattn, wq, ex), DA.at[0, :, lanes])
        )
    load("dout_s", lambda: (dout_s, DO.at[1]))
    load("dattn_s", lambda: (dattn_s, DA.at[1]))
    load("co", lambda: (cr, CO.at[0]))
    load("co_s", lambda: (cs, CO.at[1]))
    load("c", lambda: (ctx, CX))
    load("q", lambda: (q_in, Q))
    load("k", lambda: (k_in, K))
    load("v", lambda: (v_in, V))
    load("g", lambda: (dco, G.at[pl.ds(0, 2)]))
    load("g_s", lambda: (dcs_s, G.at[pl.ds(2, 2)]))
    for s in range(2):
        load(("lse", s), lambda s=s: (lse_in.at[s], LSE.at[s]))
    load("vec", lambda: (acc, VS.at[0]))
    load("w", lambda: (w_in, W))
    pl.semaphore_wait(barrier, len(partners))

    chunks = ff // 1024
    per = 1024 // ro

    def act_cols(t):
        return at(xor(f // per, t, chunks), 1024)

    class Unit:
        def __init__(self, P, RY, RZ, M):
            self.P, self.RY, self.RZ, self.M = P, RY, RZ, M
            self.left, self.then = A, []
            self.y = [
                remote(Y, lambda a=a: (P.at[1, a], RY.at[a])) for a in range(A)
            ]
            self.z = [None] + [
                remote((0, 2 * a), lambda a=a: (P.at[0, a], RZ.at[a - 1])) for a in range(1, A)
            ]

        def start_y(self, a=None):
            queue.extend((self, i) for i in (order if a is None else [a]))
            pump()

        def fold_y(self, a):
            self.y[a]().wait_recv()
            self.P[0, a] = plus(self.P[0, a], self.RY[a])
            if a:
                go(self.z[a])
            self.left -= 1

        def fold_z(self):
            for a in range(1, A):
                self.z[a]().wait_recv()
            self.M[...] = plus(self.P[0, 0], *[self.RZ[a - 1] for a in range(1, A)])

    order = list(range(1, A)) + [0]
    queue, flying, later = [], [], []

    def pump():
        while queue and len(flying) < WINDOW:
            unit, a = queue.pop(0)
            go(unit.y[a])
            flying.append((unit, a))

    def fold_next():
        if flying:
            unit, a = flying.pop(0)
            pump()
            unit.fold_y(a)
            if not unit.left:
                later.extend((3 * t + 2, job) for t, job in enumerate(unit.then))
        now = [job for t, job in later if t <= 0]
        later[:] = [(t - 1, job) for t, job in later if t > 0]
        for job in now:
            job()

    UI = [Unit(PI.at[ex], RYI.at[ex], RZI.at[ex], MI.at[ex]) for ex in range(2)]
    UU = Unit(PU.at[0], RYU, RZU, MU)
    UO = Unit(PO, RYO, RZO, MO)
    UQ = [Unit(PQ.at[j], RYQ.at[j], RZQ.at[j], MQ.at[j]) for j in range(3)]
    plan = Plan()

    xi = [remote(NEAR, lambda ex=ex: (MI.at[ex], RXI.at[ex])) for ex in range(2)]

    def inner_z(ex):
        UI[ex].fold_z()
        go(xi[ex])

    def cols_of(ref, e, size):
        return ref.at[:, at(flip(C, e), size)]

    i_core = [
        remote(CORE, lambda ex=ex: (RXI.at[1 - ex], cols_of(o_i, 2 * ex, cq))) for ex in range(2)
    ]

    def inner_x():
        for ex in range(2):
            xi[1 - ex]().wait_recv()
            RXI[1 - ex] = plus(MI[ex], RXI[1 - ex])
            go(i_core[ex])
            go_local(lambda ex=ex: (RXI.at[1 - ex], cols_of(o_i, 2 * ex, cq)))

    x_base = [next(remotes_free) for _ in range(n)][0]

    def outer_copy(i):
        return remote_at(NEAR, x_base + i, lambda: (PU.at[1, i % 2, i // 2], RXU.at[i % 2, i // 2]))

    def outer_x(i):
        outer_copy(i).wait_recv()
        PU[0, i % 2, i // 2] = plus(PU[0, i % 2, i // 2], RXU[i % 2, i // 2])
        if i % 2:
            UU.start_y(i // 2)

    u_near = remote(NEAR, lambda: (MU, cols_of(o_u, 0, wq)))
    u_core = remote(CORE, lambda: (MU, cols_of(o_u, 0, wq)))
    u_core2 = remote(CORE, lambda: (cols_of(o_u, 2, wq), cols_of(o_u, 2, wq)))

    def outer_z():
        UU.fold_z()
        go(u_near)
        go(u_core)
        go_local(lambda: (MU, cols_of(o_u, 0, wq)))

    def outer_end():
        u_near().wait_recv()
        go(u_core2)

    xo = remote(NEAR, lambda: (MO, RXO))
    o_core = [
        remote(
            CORE, lambda ex=ex: (RXO.at[pl.ds((1 - ex) * rs, rs)], cols_of(o_o, 2 * ex, wq))
        )
        for ex in range(2)
    ]

    def out_z():
        UO.fold_z()
        go(xo)

    def out_x():
        xo().wait_recv()
        for ex in range(2):
            mine, theirs = pl.ds(ex * rs, rs), pl.ds((1 - ex) * rs, rs)
            RXO[theirs] = plus(MO[mine], RXO[theirs])
            go(o_core[ex])
            go_local(
                lambda ex=ex: (RXO.at[pl.ds((1 - ex) * rs, rs)], cols_of(o_o, 2 * ex, wq))
            )

    outs = (o_q, o_k, o_v)
    xq = [remote(NEAR, lambda j=j: (MQ.at[j], RXQ.at[j])) for j in range(3)]
    q_core = [
        remote(CORE, lambda j=j: (RXQ.at[j], outs[j].at[:, at(core, hw)])) for j in range(3)
    ]

    def proj_z(j):
        UQ[j].fold_z()
        go(xq[j])

    def proj_x(j):
        xq[j]().wait_recv()
        RXQ[j] = plus(MQ[j], RXQ[j])
        go(q_core[j])
        go_local(lambda: (RXQ.at[j], outs[j].at[:, at(core, hw)]))

    hops = [CORE, NEAR] + [(0, 1 << b) for b in range(n.bit_length() - 1)]
    hop_copies = [
        remote(dev, lambda t=t: (VS.at[t], VR.at[t])) for t, dev in enumerate(hops)
    ]

    def vector_hop(t):
        if t:
            hop_copies[t - 1]().wait_recv()
            VS[t] = VS[t - 1] + VR[t - 1]
        if t < len(hops):
            go(hop_copies[t])
        else:
            go_local(lambda: (VS.at[t], o_vec))

    pairs = hw // (2 * HD)

    def attention(s, times):
        need(("lse", s))

        def body(step, carry):
            cols = at(step, 2 * HD)

            def get(ref):
                return ref[:, s, :, cols].reshape(slots * part, 2 * HD)

            mask = key_mask(lens[x * sh + s], C, part)
            dq, dk, dv = attend_back_pair(
                get(Q), get(K), get(V), mask, LSE[s % 2, :, cols], get(CX), get(G)
            )
            for ref, value in ((Q, dq), (K, dk), (V, dv)):
                ref[:, s, :, cols] = value.reshape(slots, part, 2 * HD)
            plan.beside(step, times)
            return carry

        lax.fori_loop(0, pairs, body, 0)
        if s + 2 < sh:
            load(("lse", s + 2), lambda: (lse_in.at[s + 2], LSE.at[s % 2]))

    groups = width // 256
    gsz = 256 // rs

    def weight_grad(get, P, times):
        def body(a, carry):
            cols = at(xor(f // gsz, a, groups), 256)
            r = (dot_tn(L[0, :, cols], get(0)) + dot_tn(L[1, :, cols], get(1))).astype(BF)
            for u in range(gsz):
                i = a * gsz + flip(f % gsz, u) if gsz > 1 else a
                P[i % 2, i // 2] = r[u * rs : (u + 1) * rs]
            plan.beside(a, times)
            return carry

        lax.fori_loop(0, groups, body, 0)

    def spaced(first, last, count):
        return [first + (last - first) * (t + 1) / count for t in range(count)]

    UI[0].then = [lambda: inner_z(0)]
    UI[1].then = [lambda: inner_z(1), inner_x]
    UU.then = [outer_z, outer_end]
    UO.then = [out_z, out_x]
    for j in range(3):
        UQ[j].then = [lambda j=j: proj_z(j), lambda j=j: proj_x(j)]

    xs_order = list(range(1, n, 2)) + list(range(0, n, 2))
    for k, i in enumerate(xs_order):
        if k < n // 2:
            plan.add(11 + 14 * (per * (i // per) + per - 1 - i % per + 1) / n, lambda i=i: outer_copy(i).start())
        follow = xs_order[k + n // 2] if k < n // 2 else None

        def fold_x(i=i, follow=follow):
            if follow is not None:
                outer_copy(follow).start()
            outer_x(i)

        plan.add(20 + 48 * k / n, fold_x)
    for k in range(13 * A):
        plan.add(14 + 18 * k / A, fold_next)
    for t in range(len(hops) + 1):
        plan.add(74 + 4 * t, lambda t=t: vector_hop(t))

    need("nrm", "nrm_s", ("dinn", 0), ("dinn_s", 0))
    weight_grad(lambda m: D[0, m], PI.at[0], spaced(4, 8, groups))
    UI[0].start_y()

    def act_load(t):
        slot = t % 2
        return [
            pltpu.make_async_copy(act.at[:, act_cols(t)], D.at[slot, 0], lsem.at[act_sem + 2 * slot]),
            pltpu.make_async_copy(
                act_s.at[:, act_cols(t)], D.at[slot, 1], lsem.at[act_sem + 2 * slot + 1]
            ),
        ]

    act_sem = [next(locals_free) for _ in range(4)][0]

    def begin_act(t):
        for c in act_load(t):
            c.start()

    begin_act(0)
    need(("dinn", 1), ("dinn_s", 1))
    weight_grad(lambda m: D[1, m], PI.at[1], spaced(8, 11, groups))
    UI[1].start_y()
    if chunks > 1:
        begin_act(1)
    load("x0", lambda: (xall.at[pl.ds(0, rows)], L.at[0]))
    load("x1", lambda: (xall.at[pl.ds(rows, rows)], L.at[1]))
    need(("dout", 0), ("dout", 1), "dout_s")

    outer_times = spaced(11, 25, n)

    def outer_body(u, carry):
        t, il = u // per, per - 1 - u % per
        slot = t % 2

        @pl.when(u % per == 0)
        def _():
            for c in act_load(t):
                c.wait()

        cols = at(xor(f % per, il, per), ro)
        r = dot_tn(D[slot, 0, :, cols], DO[0]) + dot_tn(D[slot, 1, :, cols], DO[1])
        r = r.astype(BF)
        i = t * per + il
        for ex in range(2):
            PU[ex, i % 2, i // 2] = r[:, ex * wq : (ex + 1) * wq]

        @pl.when((u % per == per - 1) & (t + 2 < chunks))
        def _():
            begin_act(t + 2)

        plan.beside(u, outer_times)
        return carry

    lax.fori_loop(0, n, outer_body, 0)

    need("co", "co_s", "c", ("dattn", 0), ("dattn", 1), "dattn_s")
    for half in range(2):
        for g in range(hw // 256):
            lanes = slice(g * 256, (g + 1) * 256)

            def left(m):
                if half:
                    return CO[m, :, lanes]
                return CX[2 * m : 2 * m + 2, :, :, lanes].reshape(rows, 256)

            r = (dot_tn(left(0), DA[0]) + dot_tn(left(1), DA[1])).astype(BF)
            group = (core + half * (1 - 2 * core)) * (hw // 256) + g
            for u in range(gsz):
                i = xor(group * gsz + u, f, n)
                for ex in range(2):
                    PO[i % 2, i // 2, ex * rs : (ex + 1) * rs] = r[
                        u * rs : (u + 1) * rs, ex * wq : (ex + 1) * wq
                    ]
        for job in plan.due(27 + 3 * half):
            job()
    UO.start_y()

    need("q", "k", "v", "g", "g_s")
    for s in range(sh):
        attention(s, spaced(30 + 8 * s, 38 + 8 * s, pairs))

    need("x0", "x1", "vec")
    for j, ref in enumerate((Q, K, V)):

        def right(m):
            return ref[2 * m : 2 * m + 2].reshape(rows, hw)

        if j != 1:
            total = jnp.sum(right(0).astype(F32), 0, keepdims=True)
            total = total + jnp.sum(right(1).astype(F32), 0, keepdims=True)
            VS[0, j // 2 : j // 2 + 1, at(core, hw)] = total
        weight_grad(right, PQ.at[j], spaced(54 + 6 * j, 60 + 6 * j, groups))
        UQ[j].start_y()

    need("w")

    def project(slot):
        out = None
        for j, ref in enumerate((Q, K, V)):
            p = dot_nt(ref[slot].reshape(half_rows, hw), W[j])
            out = p if out is None else out + p
        return out

    ig_swap = [remote(CORE, lambda ex=ex: (SB, ig_s.at[ex])) for ex in range(2)]
    for ex in (1, 0):
        value = project(2 + ex)
        if ex == 0:
            ig_swap[1]().wait_send()
        SB[...] = value
        ig_swap[ex]().start()
        for job in plan.due(80 - 4 * ex):
            job()

    def rows_of(ex):
        return pl.ds(ex * half_rows, half_rows)

    ig_near = remote(NEAR, lambda: (XS, o_igr))
    for ex in (1, 0):
        ig_swap[ex]().wait_recv()
        load(("ig", ex), lambda ex=ex: (ig_s.at[ex], IB))
        value = project(ex)
        if ex:
            ig_swap[0]().wait_send()
        load(("df", ex), lambda ex=ex: (dfirst.at[rows_of(ex)], SB))
        need(("ig", ex), ("df", ex))
        value = value + IB[...] + SB[...]
        if ex:
            XS[...] = value.astype(BF)
            go(ig_near)
        else:
            IB[...] = value
            go_local(lambda: (IB, o_igl))
        for job in plan.due(88 - 4 * ex):
            job()

    for job in plan.due(1e9):
        job()
    while flying or later:
        fold_next()

    ig_near().wait_recv()
    for build in i_core + [u_core, u_core2] + o_core + q_core:
        build().wait_recv()
    for i in range(n):
        outer_copy(i).wait_send()
    for end in ends:
        end()


def back_call(lens, n, act, dout, nrm, dinn, dattn, ctx, cr, xall, q, k, v, lse, *rest):
    rows, width = nrm.shape
    ff = act.shape[1]
    slots, sh, part, hw = q.shape
    A = n // 2
    rs, ro, cq, wq = width // n, ff // n, ff // 4, width // 4
    hops = 2 + n.bit_length() - 1

    def bf(*shape):
        return jax.ShapeDtypeStruct(shape, BF)

    def f32(*shape):
        return jax.ShapeDtypeStruct(shape, F32)

    def vm(*shape):
        return pltpu.VMEM(shape, BF)

    def vf(*shape):
        return pltpu.VMEM(shape, F32)

    four = (slots, sh, part, hw)
    return pl.pallas_call(
        functools.partial(back_kernel, n),
        in_specs=[pl.BlockSpec(memory_space=pltpu.SMEM)] + [ANY] * 23,
        out_specs=[ANY] * 10,
        out_shape=[
            f32(rows // 2, width),
            bf(rows // 2, width),
            bf(rs, ff),
            bf(ro, width),
            bf(rs, width),
            bf(rs, width),
            bf(rs, width),
            bf(rs, width),
            f32(16, width),
            f32(2, rows // 2, width),
        ],
        scratch_shapes=[
            vm(*four),
            vm(*four),
            vm(*four),
            vm(*four),
            vm(*four),
            vf(2, *lse.shape[1:]),
            vm(2, rows, width),
            vm(2, 2, rows, 1024),
            vm(2, rows, 2 * wq),
            vm(2, rows, 2 * wq),
            vm(2, rows, hw),
            vm(3, width, hw),
            vm(2, 2, A, rs, cq),
            vm(2, 2, A, ro, wq),
            vm(2, A, 2 * rs, wq),
            vm(3, 2, A, rs, hw),
            vm(2, A, rs, cq),
            vm(2, A - 1, rs, cq),
            vm(2, rs, cq),
            vm(2, rs, cq),
            vm(2, A, ro, wq),
            vm(A, ro, wq),
            vm(A - 1, ro, wq),
            vm(ro, wq),
            vm(A, 2 * rs, wq),
            vm(A - 1, 2 * rs, wq),
            vm(2 * rs, wq),
            vm(2 * rs, wq),
            vm(3, A, rs, hw),
            vm(3, A - 1, rs, hw),
            vm(3, rs, hw),
            vm(3, rs, hw),
            vf(hops + 1, 16, width),
            vf(hops, 16, width),
            vf(rows // 2, width),
            vf(rows // 2, width),
            vm(rows // 2, width),
            pltpu.SemaphoreType.DMA((48,)),
            pltpu.SemaphoreType.DMA((64 + 8 * n,)),
            pltpu.SemaphoreType.DMA((64 + 8 * n,)),
        ],
        compiler_params=pltpu.CompilerParams(
            vmem_limit_bytes=BACK_LIMIT, collective_id=1, has_side_effects=True
        ),
        name="back",
    )(
        lens,
        act,
        dout,
        nrm,
        dinn,
        dattn,
        ctx,
        cr,
        xall,
        q,
        k,
        v,
        lse,
        *rest,
    )


def finish_kernel(here, near, lo, *refs):
    o_ig, o_lo = refs[6:8]
    x = lax.axis_index("ctx") // 2
    o_ig[x] = here[...]
    o_ig[1 - x] = near[...].astype(F32)
    o_lo[...] = lo[...]
    for source, target in zip(refs[:6], refs[8:]):
        target[...] = source[...].astype(F32)


def finish_call(here, near, lo, *grads):
    steps = 4
    rows, width = here.shape

    def by(a):
        return pl.BlockSpec((a.shape[0] // steps, a.shape[1]), lambda i: (i, 0))

    return pl.pallas_call(
        finish_kernel,
        grid=(steps,),
        in_specs=[by(a) for a in (here, near, lo) + grads],
        out_specs=[pl.BlockSpec((2, rows // steps, width), lambda i: (0, i, 0)), by(lo)]
        + [by(g) for g in grads],
        out_shape=[jax.ShapeDtypeStruct((2, rows, width), F32), jax.ShapeDtypeStruct(lo.shape, BF)]
        + [jax.ShapeDtypeStruct(g.shape, F32) for g in grads],
        compiler_params=params(),
        name="finish",
    )(here, near, lo, *grads)


def per_device(
    inputs,
    lengths,
    cotangent,
    query_weight,
    key_weight,
    value_weight,
    out_weight,
    inner_weight,
    outer_weight,
    query_bias,
    value_bias,
    out_bias,
    inner_bias,
    outer_bias,
    first_gain,
    first_shift,
    second_gain,
    second_shift,
):
    C = lax.axis_index("ctx")
    f = lax.axis_index("fsdp")
    n = lax.axis_size("fsdp")
    x, core = C // 2, C % 2
    seqs, part, width = inputs.shape
    ff = inner_weight.shape[1]
    sh = seqs // 2
    rows = 2 * sh * part
    rs, ro = width // n, ff // n
    hw = width // 2

    def pick(bit, a, b):
        return jnp.where(bit == 0, a, b), jnp.where(bit == 0, b, a)

    vectors = (
        query_bias,
        value_bias,
        out_bias,
        outer_bias,
        first_gain,
        first_shift,
        second_gain,
        second_shift,
    )
    vecs = jnp.concatenate([v.reshape(1, rs) for v in vectors], 0)
    if rs < 128:
        vecs = jnp.pad(vecs, ((0, 0), (0, 128 - rs)))
    vecs = jnp.concatenate(
        [vecs, inner_bias.reshape(ro // 128, 128), jnp.zeros((PACK - 8 - ro // 128, 128), BF)], 0
    )
    x4, cot, w_qkv, wi, wu, wo, vecs, q4, k4, v4, c4, c_r, c_s, lse = front_call(
        lengths,
        inputs,
        cotangent,
        query_weight,
        key_weight,
        value_weight,
        vecs,
        out_weight,
        inner_weight,
        outer_weight,
        n,
    )
    xall = x4.reshape(2 * rows, width)
    ctx, cr = c4.reshape(2 * rows, hw), c_r.reshape(rows, hw)
    two = (2, sh, part, hw)
    (
        dfirst,
        dco,
        acc,
        act,
        nrm,
        dout,
        dinn,
        dattn,
        layer_out,
        act_s,
        dout_s,
        dinn_s,
        nrm_s,
        dattn_s,
        dcs_s,
    ) = ffn_call(lengths, sh, ctx, cr, xall, cot.reshape(rows, width), vecs, wo, wi, wu)

    ig_here, ig_near, g_i, g_u, g_o, g_q, g_k, g_v, sums, _ = back_call(
        lengths,
        n,
        act,
        dout,
        nrm,
        dinn,
        dattn,
        c4,
        cr,
        xall,
        q4,
        k4,
        v4,
        lse,
        dco.reshape(two),
        dfirst,
        w_qkv,
        acc,
        act_s,
        dout_s,
        dinn_s,
        nrm_s,
        dattn_s,
        dcs_s.reshape(two),
        c_s.reshape(rows, hw),
    )
    own = lax.dynamic_slice_in_dim(sums[:8], f * rs, rs, 1)
    own_inner = lax.dynamic_slice_in_dim(sums[8 : 8 + ff // width].reshape(ff), f * ro, ro, 0)
    input_grad, layer_out, *grads = finish_call(
        ig_here, ig_near, layer_out.reshape(seqs * part, width), g_q, g_k, g_v, g_o, g_i, g_u
    )
    grad_query, grad_key, grad_value, grad_out, grad_inner, grad_outer = grads
    input_grad, layer_out = input_grad.reshape(inputs.shape), layer_out.reshape(inputs.shape)

    return (
        layer_out,
        input_grad,
        grad_query,
        grad_key,
        grad_value,
        grad_out,
        grad_inner,
        grad_outer,
        own[0],
        own[1],
        own[2],
        own_inner,
        own[3],
        own[4],
        own[5],
        own[6],
        own[7],
    )


def solution(mesh):
    rowed = P("fsdp", "ctx", None)
    matrix, vector = P("fsdp", None), P("fsdp")
    in_specs = (rowed, vector, rowed) + (matrix,) * 6 + (vector,) * 9
    out_specs = (rowed, rowed) + (matrix,) * 6 + (vector,) * 9
    return jax.shard_map(
        per_device, mesh=mesh, in_specs=in_specs, out_specs=out_specs, check_vma=False
    )
```

```python
import functools

import jax
import jax.numpy as jnp
from jax import lax
from jax.experimental import pallas as pl
from jax.experimental.pallas import tpu as pltpu
from jax.sharding import PartitionSpec as P

HD = 64
EPSILON = 1e-05
BF = jnp.bfloat16
F32 = jnp.float32
ANY = pl.BlockSpec(memory_space=pl.ANY)
NT = (((1,), (1,)), ((), ()))
TN = (((0,), (0,)), ((), ()))
VMEM_LIMIT = 58 << 20
BACK_LIMIT = 60 << 20
WINDOW = 3


def dot(a, b):
    return jnp.dot(a, b, preferred_element_type=F32)


def dot_nt(a, b):
    return lax.dot_general(a, b, NT, preferred_element_type=F32)


def dot_tn(a, b):
    return lax.dot_general(a, b, TN, preferred_element_type=F32)


def params(**more):
    return pltpu.CompilerParams(vmem_limit_bytes=VMEM_LIMIT, **more)


def cost(flops, size, trans=0):
    return pl.CostEstimate(flops=int(flops), bytes_accessed=int(size), transcendentals=int(trans))


MESH = pl.DeviceIdType.MESH
PACK = 16


def flip(v, mask):
    out, bit = v, 1
    while bit <= mask:
        if mask & bit:
            out = out + bit - 2 * bit * ((v // bit) % 2)
        bit *= 2
    return out


def at(index, size):
    return pl.ds(pl.multiple_of(index * size, size), size)


def spread(read, n, rs):
    per = max(128 // rs, 1)
    tiles = []
    for t in range(n // per):
        tile = read(t * per)
        for u in range(1, per):
            tile = tile + pltpu.roll(read(t * per + u), u * rs, 1)
        tiles.append(tile)
    return jnp.concatenate(tiles, 1)


def front_kernel(
    n,
    lens,
    xin,
    cin,
    wq,
    wk,
    wv,
    vecs,
    wo_in,
    wi_in,
    wu_in,
    xo,
    co,
    wqkvo,
    wio,
    wuo,
    woo,
    veco,
    qo,
    ko,
    vo,
    cxo,
    cro,
    cso,
    lseo,
    acto,
    gpo,
    hato,
    ro_o,
    nrmo,
    X,
    W,
    VEC,
    Q,
    K,
    V,
    CX,
    LSE,
    WO,
    WI,
    CR,
    VB,
    IB,
    HAT,
    R1,
    NRM,
    ACT,
    GP,
    lsem,
    ssem,
    rsem,
):
    C, f = lax.axis_index("ctx"), lax.axis_index("fsdp")
    x, core = C // 2, C % 2
    A = n // 2
    sh, part, width = X.shape[1:]
    hw = W.shape[2]
    ff = wio.shape[1]
    rs, ro, cq = width // n, ff // n, ff // 4

    partners = [(0, 2 * k) for k in range(1, A)] + [(0, 1), (2, 0), (1, 0)]

    def device(dc, df):
        return (flip(C, dc), flip(f, df))

    barrier = pltpu.get_barrier_semaphore()
    for p in partners:
        pl.semaphore_signal(barrier, inc=1, device_id=device(*p), device_id_type=MESH)

    local = []
    used = iter(range(lsem.shape[0]))

    def begin(source, target):
        c = pltpu.make_async_copy(source, target, lsem.at[next(used)])
        c.start()
        return c

    def keep(source, target):
        local.append(begin(source, target))

    x_here = begin(xin.at[pl.ds(x * sh, sh)], X.at[0])
    w_here = [begin(w.at[:, at(core, hw)], W.at[j, at(f, rs)]) for j, w in enumerate((wq, wk, wv))]
    w_here.append(begin(vecs, VEC.at[f]))

    pl.semaphore_wait(barrier, len(partners))

    def remote(source, target, sem, dev):
        return pltpu.make_async_remote_copy(
            src_ref=source,
            dst_ref=target,
            send_sem=ssem.at[sem],
            recv_sem=rsem.at[sem],
            device_id=device(*dev),
            device_id_type=MESH,
        )

    sent = []

    def send(*what):
        c = remote(*what)
        c.start()
        sent.append(c)

    seen = set()

    def arrive(target, sem, dev):
        if sem not in seen:
            seen.add(sem)
            remote(target, target, sem, dev).wait_recv()

    X1, X2, X3, COT, CTX, CTX2 = range(6)
    send(xin.at[pl.ds((1 - x) * sh, sh)], X.at[1], X1, (2, 0))

    def rows_at(ref, first, size):
        return ref.at[pl.ds(pl.multiple_of(first, size), size)]

    hr, hu = rs // 2, ro // 2

    def projection(j):
        w = (wq, wk, wv)[j]
        return (
            1,
            lambda e, s: [W.at[j, at(s, rs)]] + [VEC.at[s]] * (j == 0),
            lambda: [w.at[:, at(core, hw)]] + [vecs] * (j == 0),
        )

    def inner_part(h):
        return (
            4,
            lambda e, s: [WI.at[at(s * 2 + h, hr), at(flip(C, e), cq)]],
            lambda: [wi_in.at[pl.ds(h * hr, hr), at(C, cq)]],
        )

    outer_a = (
        4,
        lambda e, s: [rows_at(wuo, s * ro + flip(C, e) * (hu // 4), hu // 4)],
        lambda: [rows_at(wu_in, C * (hu // 4), hu // 4)],
    )
    out_part = (
        4,
        lambda e, s: [rows_at(WO, s * rs + flip(C, e) * (rs // 4), rs // 4)],
        lambda: [rows_at(wo_in, C * (rs // 4), rs // 4)],
    )

    def outer_b(h):
        return (
            2,
            lambda e, s: [rows_at(wuo, s * ro + hu + (flip(core, e) * 2 + h) * (hu // 4), hu // 4)],
            lambda: [rows_at(wu_in, hu + (core * 2 + h) * (hu // 4), hu // 4)],
        )

    kinds = [
        out_part,
        inner_part(0),
        projection(0),
        projection(1),
        projection(2),
        inner_part(1),
        outer_a,
        outer_b(0),
        outer_b(1),
    ]
    sems, ready = {}, 6
    for k, (parts, place, _) in enumerate(kinds):
        for e in range(parts):
            for i in range(1, n):
                for u in range(2 if k == 2 else 1):
                    sems[k, e, i, u] = ready
                    ready += 1

    def route(parts, e, i):
        if e % 2:
            return (1, 0), (e - 1, i)
        if e:
            return (2, 0), (0, i)
        if i % 2:
            return (0, 1), (0, i - 1)
        return (0, i), (0, 0)

    def copies(k, e, i):
        parts, place, own = kinds[k]
        dev, (pe, pi) = route(parts, e, i)
        target = place(pe, flip(f, pi))
        source = target if pi else own()
        return [
            remote(source[u], target[u], sems[k, e, i, u], dev) for u in range(len(target))
        ]

    issued = []

    def give(k, e, i):
        for c in copies(k, e, i):
            c.start()
        issued.append((k, e, i))

    got = set()

    def take(k, e, i):
        if (k, e, i) in got:
            return
        got.add((k, e, i))
        parts, place, _ = kinds[k]
        dev, _ = route(parts, e, i)
        for u, target in enumerate(place(e, flip(f, i))):
            remote(target, target, sems[k, e, i, u], dev).wait_recv()

    def hand_on(k, i):
        parts = kinds[k][0]
        if parts == 4:
            give(k, 2, i)
        if parts > 1:
            give(k, 1, i)

    def base(k):
        if k < len(kinds):
            for a in range(1, A):
                give(k, 0, 2 * a)
            give(k, 0, 1)

    def z_in(k):
        for a in range(1, A):
            take(k, 0, 2 * a)
            give(k, 0, 2 * a + 1)
            hand_on(k, 2 * a)

    def y_in(k):
        for i in range(1, n, 2):
            take(k, 0, i)
            hand_on(k, i)

    def x_in(k):
        if kinds[k][0] == 4:
            for i in range(1, n):
                take(k, 2, i)
                give(k, 3, i)

    base(0)
    base(1)
    x_here.wait()
    send(X.at[0], X.at[2], X2, (1, 0))
    keep(cin.at[pl.ds(x * sh, sh)], co.at[0])
    w_here += [begin(wo_in, WO.at[at(f, rs)]), begin(wi_in, WI.at[at(f, rs)])]
    keep(wu_in, wuo.at[at(f, ro)])
    slots = X.shape[0]
    pairs = hw // (2 * HD)

    z_in(0)
    base(2)
    arrive(X.at[1], X1, (2, 0))
    send(X.at[1], X.at[3], X3, (1, 0))
    z_in(1)
    base(3)
    y_in(0)
    arrive(X.at[2], X2, (1, 0))
    arrive(X.at[3], X3, (1, 0))
    keep(X, xo)
    for c in w_here:
        c.wait()
    z_in(2)
    base(4)
    y_in(1)
    send(cin.at[pl.ds((1 - x) * sh, sh)], co.at[1], COT, (2, 0))
    z_in(3)
    base(5)
    y_in(2)
    x_in(0)
    keep(VEC, veco)

    def bias(row):
        read = lambda s: VEC[pl.ds(core * (n // 2) + s, 1), row : row + 1, :128].reshape(1, 128).astype(F32)
        return spread(read, n // 2, rs)

    shape = (sh, part, hw)

    def project(j, target, add):
        def body(slot, carry):
            value = dot(X[slot].reshape(sh * part, width), W[j])
            if add is not None:
                value = value + add
            target[slot] = value.astype(BF).reshape(shape)
            return carry

        lax.fori_loop(0, slots, body, 0)

    project(0, Q, bias(0))
    z_in(4)
    base(6)
    y_in(3)
    project(1, K, None)
    x_in(1)
    z_in(5)
    base(7)
    y_in(4)
    keep(W, wqkvo)
    project(2, V, bias(1))
    keep(Q, qo)
    keep(K, ko)
    keep(V, vo)

    jobs = {7: [lambda: z_in(6), lambda: base(8)], 9: [lambda: y_in(5)]}
    steps = sh * pairs

    def attend(step, carry):
        s, pair = step // pairs, step % pairs
        cols = at(pair, 2 * HD)

        def load(ref):
            return ref[:, s, :, cols].reshape(slots * part, 2 * HD)

        q, k, v = load(Q), load(K), load(V)
        mask = key_mask(lens[x * sh + s], C, part)
        o, lse = attend_pair(q, k, v, mask)
        CX[:, s, :, cols] = o.reshape(slots, part, 2 * HD)
        LSE[s, :, cols] = lse
        for t in range(steps):
            now = jobs.get(t)
            if now:

                @pl.when(step == t)
                def _():
                    for job in now:
                        job()

        return carry

    lax.fori_loop(0, steps, attend, 0)
    send(CX.at[pl.ds(2, 2)], CR, CTX, (1, 0))
    send(CX.at[pl.ds(0, 2)], cso, CTX2, (1, 0))
    keep(CX, cxo)
    keep(LSE, lseo)
    for e in range(4):
        for i in range(1, n):
            take(0, e, i)
    keep(WO, woo)
    VB[...] = spread(lambda s: VEC[s, :8, :128].astype(F32), n, rs)
    for s in range(n):
        for t in range(ro // 128):
            first = s * ro + t * 128
            IB[:, first : first + 128] = VEC[s, 8 + t : 9 + t, :].astype(F32)
    arrive(CR, CTX, (1, 0))
    keep(CR, cro)
    own_half, other_half = at(core, hw), at(1 - core, hw)
    half = sh * part

    def norm(ex, carry):
        first = (
            X[ex].reshape(half, width).astype(F32)
            + (
                dot(CX[ex].reshape(half, hw), WO[own_half])
                + dot(CR[ex].reshape(half, hw), WO[other_half])
            )
            + VB[2:3, :]
        )
        hat, r = normalise(first)
        HAT[ex] = hat
        R1[ex] = jnp.broadcast_to(r, (half, 128))
        NRM[ex] = (hat * VB[4:5, :] + VB[5:6, :]).astype(BF)
        return carry

    lax.fori_loop(0, 2, norm, 0)
    keep(HAT, hato)
    keep(R1, ro_o)
    keep(NRM, nrmo)
    plan = [
        [lambda: z_in(7), lambda: y_in(6)],
        [lambda: x_in(5)],
        [lambda: z_in(8), lambda: y_in(7)],
        [lambda: x_in(6)],
    ]
    for e in range(4):
        for job in plan[e]:
            job()
        for k in (1, 5):
            for i in range(1, n):
                take(k, e, i)
        cols = at(flip(C, e), cq)

        def inner(ex, carry):
            g, d = gelu_pair(dot(NRM[ex], WI[:, cols]) + IB[:, cols])
            ACT[ex, :, cols] = g.astype(BF)
            GP[ex, :, cols] = d.astype(BF)
            return carry

        lax.fori_loop(0, 2, inner, 0)
        keep(ACT.at[:, :, cols], acto.at[:, :, cols])
        keep(GP.at[:, :, cols], gpo.at[:, :, cols])
    y_in(8)
    keep(WI, wio)
    for k, (parts, _, _) in enumerate(kinds):
        for e in range(parts):
            for i in range(1, n):
                take(k, e, i)
    arrive(co.at[1], COT, (2, 0))
    arrive(cso, CTX2, (1, 0))
    for what in issued:
        for c in copies(*what):
            c.wait_send()
    for c in sent:
        c.wait_send()
    for c in local:
        c.wait()


def front_call(lengths, xin, cin, wq, wk, wv, vecs, wo, wi, wu, n):
    seqs, part, width = xin.shape
    sh, ff, hw = seqs // 2, wi.shape[1], width // 2

    def bf(*shape):
        return jax.ShapeDtypeStruct(shape, BF)

    def vm(*shape):
        return pltpu.VMEM(shape, BF)

    full = 4 * part
    lse = (sh, full, hw)
    half = sh * part
    four = (4, sh, part, hw)
    sems = 24 * n
    return pl.pallas_call(
        functools.partial(front_kernel, n),
        in_specs=[pl.BlockSpec(memory_space=pltpu.SMEM)] + [ANY] * 9,
        out_specs=[ANY] * 19,
        out_shape=[
            bf(4, sh, part, width),
            bf(2, sh, part, width),
            bf(3, width, hw),
            bf(width, ff),
            bf(ff, width),
            bf(width, width),
            bf(n, PACK, 128),
            bf(*four),
            bf(*four),
            bf(*four),
            bf(*four),
            bf(2, sh, part, hw),
            bf(2, sh, part, hw),
            jax.ShapeDtypeStruct(lse, F32),
            bf(2, half, ff),
            bf(2, half, ff),
            jax.ShapeDtypeStruct((2, half, width), F32),
            jax.ShapeDtypeStruct((2, half, 128), F32),
            bf(2, half, width),
        ],
        scratch_shapes=[
            vm(4, sh, part, width),
            vm(3, width, hw),
            vm(n, PACK, 128),
            vm(*four),
            vm(*four),
            vm(*four),
            vm(*four),
            pltpu.VMEM(lse, F32),
            vm(width, width),
            vm(width, ff),
            vm(2, sh, part, hw),
            pltpu.VMEM((8, width), F32),
            pltpu.VMEM((1, ff), F32),
            pltpu.VMEM((2, half, width), F32),
            pltpu.VMEM((2, half, 128), F32),
            vm(2, half, width),
            vm(2, half, ff),
            vm(2, half, ff),
            pltpu.SemaphoreType.DMA((40,)),
            pltpu.SemaphoreType.DMA((sems,)),
            pltpu.SemaphoreType.DMA((sems,)),
        ],
        compiler_params=params(collective_id=0, has_side_effects=True),
        name="front",
    )(lengths, xin, cin, wq, wk, wv, vecs, wo, wi, wu)


def lanes_of(shape, head):
    lane = lax.broadcasted_iota(jnp.int32, shape, 1)
    own = (lane < HD) if head == 0 else (lane >= HD)
    return lane, own, (HD if head == 0 else 0)


def split3(a):
    hi = a.astype(BF).astype(F32)
    mid = (a - hi).astype(BF).astype(F32)
    return hi, mid, a - hi - mid


def flat(ref):
    a = ref[...]
    return a.reshape(-1, a.shape[-1])


def key_mask(length, C, part):
    row = lax.broadcasted_iota(jnp.int32, (part, 2 * HD), 0)
    out = []
    for e in (0, 2, 1, 3):
        inside = row + flip(C, e) * part < length
        out.append(jnp.where(inside, 0.0, -1e30).astype(BF))
    return jnp.concatenate(out, 0)


def attend_pair(q, k, v, mask):
    out = []
    for head in range(2):
        lane, own, other = lanes_of(q.shape, head)
        qh = jnp.where(own, q * BF(HD**-0.5), jnp.where(lane == other, 1.0, 0.0).astype(BF))
        kh = jnp.where(own, k, mask)
        s = dot_nt(qh, kh)
        top = jnp.max(s, -1, keepdims=True)
        e = jnp.exp(s - top)
        total = jnp.sum(e, -1, keepdims=True)
        o = dot(e.astype(BF), v) * (1.0 / total)
        out.append((o, top + jnp.log(total), own))
    (o0, l0, own), (o1, l1, _) = out
    return jnp.where(own, o0, o1).astype(BF), jnp.where(own, l1, l0)


def attend_back_pair(q, k, v, mask, lse, c, g):
    qs = q * BF(HD**-0.5)
    kt = k.T
    prod = c.astype(F32) * g.astype(F32)
    res = []
    for head in range(2):
        lane, own, o = lanes_of(q.shape, head)
        hi, mid, low = split3(-lse)
        extra = jnp.where(
            lane == o,
            1.0,
            jnp.where(
                lane == o + 1,
                hi,
                jnp.where(lane == o + 2, mid, jnp.where(lane == o + 3, low, 0.0)),
            ),
        ).astype(BF)
        qh = jnp.where(own, qs, extra)
        kh = jnp.where(own, k, jnp.where(lane == o, mask, BF(1)))
        p = jnp.exp(dot_nt(kh, qh))
        delta = jnp.sum(jnp.where(own, prod, 0.0), -1, keepdims=True)
        hi, mid, low = split3(-delta)
        extra = jnp.where(
            lane == o, hi, jnp.where(lane == o + 1, mid, jnp.where(lane == o + 2, low, 0.0))
        ).astype(BF)
        gh = jnp.where(own, g, extra)
        vh = jnp.where(own, v, BF(1))
        ds = (p * dot_nt(vh, gh)).astype(BF)
        dv = dot(p.astype(BF), g)
        dk = dot(ds, qs)
        dqt = dot(kt, ds)
        res.append((dv, dk, dqt, own))
    (dv0, dk0, dq0, own), (dv1, dk1, dq1, _) = res
    dqt = jnp.concatenate([dq0[:HD], dq1[HD:]], 0) * (HD**-0.5)
    return dqt.T.astype(BF), jnp.where(own, dk0, dk1).astype(BF), jnp.where(own, dv0, dv1).astype(BF)


def gelu_pair(u):
    e = jnp.exp(u * u * -0.5)
    t = 1.0 / (1.0 + (0.3275911 * 0.7071067811865476) * jnp.abs(u))
    poly = t * (
        0.254829592 * 0.5
        + t
        * (
            -0.284496736 * 0.5
            + t * (1.421413741 * 0.5 + t * (-1.453152027 * 0.5 + t * (1.061405429 * 0.5)))
        )
    )
    tail = poly * e
    cdf = jnp.where(u >= 0, 1.0 - tail, tail)
    ucdf = u * cdf
    return ucdf, cdf + u * (e * 0.3989422804014327)


def normalise(h):
    c = h - jnp.mean(h, -1, keepdims=True)
    r = lax.rsqrt(jnp.mean(c * c, -1, keepdims=True) + EPSILON)
    return c * r, r


def normalise_back(dyg, hat, r):
    return r * (
        dyg - jnp.mean(dyg, -1, keepdims=True) - hat * jnp.mean(dyg * hat, -1, keepdims=True)
    )


def ffn_kernel(
    n, sh, part, lens, act, gp, hat1_ref, r1_ref, cot, vecs, act_in, nrm_in, wo_in, wi_in, wu_in, *refs
):
    dfirst, dco, acc = refs[:3]
    homes, (o_lo, act_s, dout_s, dinn_s, nrm_s, dattn_s, dcs_s) = refs[3:6], refs[6:13]
    wo, wi, wu, vec, *twice, sem, csem, hsem, ssem, rsem = refs[13:]
    width, ff = wi.shape
    C, f = lax.axis_index("ctx"), lax.axis_index("fsdp")
    x, core = C // 2, C % 2
    step = pl.program_id(0)
    turn = 2 - step
    rs, ro = width // n, ff // n
    cq, hw = ff // 4, width // 2

    pairs = ((wo_in, wo), (wi_in, wi), (wu_in, wu))

    def copy(kind):
        return pltpu.make_async_copy(*pairs[kind], sem.at[kind])

    CORE, NEAR = flip(C, 1), flip(C, 2)
    block, wq = cot.shape[0], width // 4

    def remote(t, j, to, source, target):
        return pltpu.make_async_remote_copy(
            src_ref=source,
            dst_ref=target,
            send_sem=ssem.at[t, j],
            recv_sem=rsem.at[t, j],
            device_id=(to, f),
            device_id_type=MESH,
        )

    KINDS = ("dout0", "dout1", "dinn0", "dinn1", "dattn0", "dattn1", "dcs")

    def rows_of(t):
        return pl.ds(pl.multiple_of(t * block, block), block)

    def held(t):
        return [ref.at[(2 - t) % 2] for ref in twice]

    dout, dinn, dattn, dcs, lo = held(turn)
    HOME = {"dout": 0, "dinn": 1, "dattn": 2}

    def whole(t):
        pair = ((act_in, act_s), (nrm_in, nrm_s))[t]
        return remote(t, 7, CORE, *pair)

    def home(t, name):
        j = HOME[name]
        return pltpu.make_async_copy(held(t)[j], homes[j].at[rows_of(t)], hsem.at[t, j])

    def to_core(t, *names):
        out = []
        for name in names or KINDS:
            rows = rows_of(t)
            dout, dinn, dattn, dcs, _ = held(t)
            ex = int(name[-1]) if name[-1] in "01" else 0
            other, lanes = flip(C, 2 * ex + 1), pl.ds(ex * wq, wq)
            source, target = {
                "dcs": lambda: (dcs, dcs_s.at[rows]),
                "dou": lambda: (dout.at[:, at(other, wq)], dout_s.at[rows, lanes]),
                "dat": lambda: (dattn.at[:, at(other, wq)], dattn_s.at[rows, lanes]),
                "din": lambda: (dinn.at[:, at(other, cq)], dinn_s.at[ex, rows]),
            }[name[:3]]()
            out.append(remote(t, KINDS.index(name), CORE, source, target))
        return out

    def start(name):
        for c in to_core(turn, *(k for k in KINDS if k.startswith(name))):
            c.start()
        if name in HOME:
            home(turn, name).start()

    def end(t, name):
        for c in to_core(t, *(k for k in KINDS if k.startswith(name))):
            c.wait_send()
        if name in HOME:
            home(t, name).wait()

    def free(name):
        @pl.when(step == 2)
        def _():
            end(2, name)

    def slots_of(t, ex):
        count = block // part
        return [u for u in range(count) if (t * count + u) // sh == ex]

    def place(t, u):
        return held(t)[4].at[pl.ds(u * part, part)], o_lo.at[x * sh + (t * (block // part) + u) % sh]

    def to_near(t):
        return [remote(t, 8 + u, NEAR, *place(t, u)) for u in slots_of(t, 1)]

    def stay(t):
        return [pltpu.make_async_copy(*place(t, u), csem.at[t, u]) for u in slots_of(t, 0)]

    def send(t):
        for c in to_near(t) + stay(t):
            c.start()

    def sent(t):
        for c in to_near(t):
            c.wait_send()
        for c in stay(t):
            c.wait()

    def received(t):
        for c in to_core(t) + to_near(t):
            c.wait_recv()

    @pl.when(step == 0)
    def _():
        barrier = pltpu.get_barrier_semaphore()
        for to in (CORE, NEAR):
            pl.semaphore_signal(barrier, inc=1, device_id=(to, f), device_id_type=MESH)
        for kind in (2, 1, 0):
            copy(kind).start()
        pl.semaphore_wait(barrier, 2)
        whole(1).start()
        whole(0).start()
        acc[...] = jnp.zeros_like(acc)
        vec[...] = spread(lambda s: vecs[s, :8, :128].astype(F32), n, rs)

    def arrived(kind):
        @pl.when(step == 0)
        def _():
            copy(kind).wait()

    count = block // part
    inside = []
    for u in range(count):
        slot = turn * count + u
        ex, s = slot // sh, slot % sh
        first = (C + ex * (2 - 4 * x)) * part
        row = lax.broadcasted_iota(jnp.int32, (part, 1), 0) + first
        inside.append(jnp.where(row < lens[x * sh + s], 1.0, 0.0))
    valid = jnp.concatenate(inside, 0)
    own, other = at(core, hw), at(1 - core, hw)

    def add(row, value):
        acc[row : row + 1, :] += jnp.sum(value, 0, keepdims=True)

    hat1, r1 = hat1_ref[...], r1_ref[:, :1]
    normed = hat1 * vec[4:5, :] + vec[5:6, :]
    arrived(2)
    second = normed + (dot(act[...], wu[...]) + vec[3:4, :])
    hat2, r2 = normalise(second)
    @pl.when(step == 2)
    def _():
        sent(2)

    lo[...] = (hat2 * vec[6:7, :] + vec[7:8, :]).astype(BF)
    og = cot[...].astype(F32) * valid
    add(6, og * hat2)
    add(7, og)
    d2 = normalise_back(og * vec[6:7, :], hat2, r2)
    d2low = d2.astype(BF)
    free("dout")
    dout[...] = d2low
    start("dout")
    for t in range(3):

        @pl.when(turn == t)
        def _():
            send(t)

    add(3, d2low.astype(F32))
    free("dinn")
    arrived(1)
    for j in range(4):
        cols = slice(j * cq, (j + 1) * cq)
        di = (dot_nt(d2low, wu[cols, :]) * gp[:, cols]).astype(BF)
        dinn[:, cols] = di
        add(8 + j, di.astype(F32))
    start("dinn")
    dn = d2 + dot_nt(dinn[...], wi[...])
    add(4, dn * hat1)
    add(5, dn)
    d1 = normalise_back(dn * vec[4:5, :], hat1, r1)
    dfirst[...] = d1
    d1low = d1.astype(BF)
    arrived(0)
    free("dattn")
    free("dcs")
    dattn[...] = d1low
    start("dattn")
    add(2, d1low.astype(F32))
    dcs[...] = dot_nt(d1low, wo[other]).astype(BF)
    start("dcs")
    dco[...] = dot_nt(d1low, wo[own]).astype(BF)

    @pl.when(turn == 0)
    def _():
        for t in range(2):
            for name in ("dout", "dinn", "dattn", "dcs"):
                end(t, name)
            sent(t)
            whole(t).wait()
        for t in range(3):
            received(t)


def ffn_call(lens, sh, act, gp, hat, r, nrm, cot, vecs, wo, wi, wu):
    width, ff = wi.shape
    n, rows = vecs.shape[0], cot.shape[0]
    block, part = rows // 3, rows // (2 * sh)
    hw = width // 2

    def by(cols):
        return pl.BlockSpec((block, cols), lambda i: (2 - i, 0))

    def whole(*shape):
        return pl.BlockSpec(shape, lambda i: (0,) * len(shape))

    grid_spec = pl.GridSpec(
        grid=(3,),
        in_specs=[
            pl.BlockSpec(memory_space=pltpu.SMEM),
            by(ff),
            by(ff),
            by(width),
            by(128),
            by(width),
            whole(*vecs.shape),
        ]
        + [ANY] * 5,
        out_specs=[by(width), by(hw), whole(16, width)] + [ANY] * 10,
        scratch_shapes=[
            pltpu.VMEM((width, width), BF),
            pltpu.VMEM((width, ff), BF),
            pltpu.VMEM((ff, width), BF),
            pltpu.VMEM((8, width), F32),
            *(pltpu.VMEM((2, block, cols), BF) for cols in (width, ff, width, hw, width)),
            pltpu.SemaphoreType.DMA((3,)),
            pltpu.SemaphoreType.DMA((3, block // part)),
            pltpu.SemaphoreType.DMA((3, 3)),
            pltpu.SemaphoreType.DMA((3, 8 + block // part)),
            pltpu.SemaphoreType.DMA((3, 8 + block // part)),
        ],
    )

    def shape(cols, dtype=BF):
        return jax.ShapeDtypeStruct((rows, cols), dtype)

    return pl.pallas_call(
        functools.partial(ffn_kernel, n, sh, part),
        grid_spec=grid_spec,
        out_shape=[
            shape(width, F32),
            shape(hw),
            jax.ShapeDtypeStruct((16, width), F32),
            shape(width),
            shape(ff),
            shape(width),
            jax.ShapeDtypeStruct((2 * sh, part, width), BF),
            shape(ff),
            shape(hw),
            jax.ShapeDtypeStruct((2, rows, ff // 4), BF),
            shape(width),
            shape(hw),
            shape(hw),
        ],
        compiler_params=params(collective_id=2, has_side_effects=True),
        cost_estimate=cost(
            2 * rows * width * (2 * width + 4 * ff), 30 * rows * width + 2 * width * (2 * ff + width)
        ),
        name="ffn",
    )(lens, act, gp, hat, r, cot, vecs, act, nrm, wo, wi, wu)


def xor(a, b, count):
    out, bit = 0, 1
    while bit < count:
        out = out + bit * ((a // bit + b // bit) % 2)
        bit *= 2
    return out


def plus(*items):
    out = items[0].astype(F32)
    for i in items[1:]:
        out = out + i.astype(F32)
    return out.astype(BF)


class Plan:
    def __init__(self):
        self.jobs = []

    def add(self, time, job):
        self.jobs.append((time, len(self.jobs), job))
        self.jobs.sort(key=lambda j: j[:2])

    def due(self, time):
        out = [j[2] for j in self.jobs if j[0] <= time]
        self.jobs = [j for j in self.jobs if j[0] > time]
        return out

    def beside(self, step, times):
        for t, time in enumerate(times):
            jobs = self.due(time)
            if jobs:

                @pl.when(step == t)
                def _():
                    for job in jobs:
                        job()


def back_kernel(
    n,
    lens,
    act,
    dout,
    nrm,
    dinn,
    dattn,
    ctx,
    cr,
    xall,
    q_in,
    k_in,
    v_in,
    lse_in,
    dco,
    dfirst,
    w_in,
    acc,
    act_s,
    dout_s,
    dinn_s,
    nrm_s,
    dattn_s,
    dcs_s,
    cs,
    o_igl,
    o_igr,
    o_i,
    o_u,
    o_o,
    o_q,
    o_k,
    o_v,
    o_vec,
    ig_s,
    Q,
    K,
    V,
    CX,
    G,
    LSE,
    L,
    D,
    DO,
    DA,
    CO,
    W,
    PI,
    PU,
    PO,
    PQ,
    RYI,
    RZI,
    MI,
    RXI,
    RXU,
    RYU,
    RZU,
    MU,
    RYO,
    RZO,
    MO,
    RXO,
    RYQ,
    RZQ,
    MQ,
    RXQ,
    VS,
    VR,
    SB,
    IB,
    XS,
    lsem,
    ssem,
    rsem,
):
    C, f = lax.axis_index("ctx"), lax.axis_index("fsdp")
    x, core = C // 2, C % 2
    A = n // 2
    slots, sh, part, hw = Q.shape
    rows, width = nrm.shape
    ff = act.shape[1]
    rs, ro, cq, wq = width // n, ff // n, ff // 4, width // 4
    half_rows = rows // 2
    CORE, NEAR, Y = (1, 0), (2, 0), (0, 1)

    def device(dc, df):
        return (flip(C, dc), flip(f, df))

    partners = [(0, 2 * k) for k in range(1, A)] + [Y, NEAR, CORE]
    barrier = pltpu.get_barrier_semaphore()
    for p in partners:
        pl.semaphore_signal(barrier, inc=1, device_id=device(*p), device_id_type=MESH)

    locals_free = iter(range(lsem.shape[0]))
    remotes_free = iter(range(ssem.shape[0]))

    def local(make):
        sem = next(locals_free)
        return lambda: pltpu.make_async_copy(*make(), lsem.at[sem])

    def remote_at(dev, sem, make):
        source, target = make()
        return pltpu.make_async_remote_copy(
            src_ref=source,
            dst_ref=target,
            send_sem=ssem.at[sem],
            recv_sem=rsem.at[sem],
            device_id=device(*dev),
            device_id_type=MESH,
        )

    def remote(dev, make):
        sem = next(remotes_free)
        return lambda: remote_at(dev, sem, make)

    ends = []

    def go(build):
        build().start()
        ends.append(lambda: build().wait_send())

    def go_local(make):
        build = local(make)
        build().start()
        ends.append(lambda: build().wait())

    loads = {}

    def load(name, make):
        loads[name] = local(make)
        loads[name]().start()

    def need(*names):
        for name in names:
            loads.pop(name)().wait()

    def quarters(ref, size, ex):
        return ref.at[:, at(flip(C, 2 * ex), size)]

    load("nrm", lambda: (nrm, L.at[0]))
    load("nrm_s", lambda: (nrm_s, L.at[1]))
    for ex in range(2):
        load(("dinn", ex), lambda ex=ex: (quarters(dinn, cq, ex), D.at[ex, 0]))
        load(("dinn_s", ex), lambda ex=ex: (dinn_s.at[ex], D.at[ex, 1]))
    for ex in range(2):
        lanes = pl.ds(ex * wq, wq)
        load(("dout", ex), lambda ex=ex, lanes=lanes: (quarters(dout, wq, ex), DO.at[0, :, lanes]))
        load(
            ("dattn", ex), lambda ex=ex, lanes=lanes: (quarters(dattn, wq, ex), DA.at[0, :, lanes])
        )
    load("dout_s", lambda: (dout_s, DO.at[1]))
    load("dattn_s", lambda: (dattn_s, DA.at[1]))
    load("co", lambda: (cr, CO.at[0]))
    load("co_s", lambda: (cs, CO.at[1]))
    load("c", lambda: (ctx, CX))
    load("q", lambda: (q_in, Q))
    load("k", lambda: (k_in, K))
    load("v", lambda: (v_in, V))
    load("g", lambda: (dco, G.at[pl.ds(0, 2)]))
    load("g_s", lambda: (dcs_s, G.at[pl.ds(2, 2)]))
    for s in range(2):
        load(("lse", s), lambda s=s: (lse_in.at[s], LSE.at[s]))
    load("vec", lambda: (acc, VS.at[0]))
    load("w", lambda: (w_in, W))
    pl.semaphore_wait(barrier, len(partners))

    chunks = ff // 1024
    per = 1024 // ro

    def act_cols(t):
        return at(xor(f // per, t, chunks), 1024)

    class Unit:
        def __init__(self, P, RY, RZ, M):
            self.P, self.RY, self.RZ, self.M = P, RY, RZ, M
            self.left, self.then = A, []
            self.y = [
                remote(Y, lambda a=a: (P.at[1, a], RY.at[a])) for a in range(A)
            ]
            self.z = [None] + [
                remote((0, 2 * a), lambda a=a: (P.at[0, a], RZ.at[a - 1])) for a in range(1, A)
            ]

        def start_y(self, a=None):
            queue.extend((self, i) for i in (order if a is None else [a]))
            pump()

        def fold_y(self, a):
            self.y[a]().wait_recv()
            self.P[0, a] = plus(self.P[0, a], self.RY[a])
            if a:
                go(self.z[a])
            self.left -= 1

        def fold_z(self):
            for a in range(1, A):
                self.z[a]().wait_recv()
            self.M[...] = plus(self.P[0, 0], *[self.RZ[a - 1] for a in range(1, A)])

    order = list(range(1, A)) + [0]
    queue, flying, later = [], [], []

    def pump():
        while queue and len(flying) < WINDOW:
            unit, a = queue.pop(0)
            go(unit.y[a])
            flying.append((unit, a))

    def fold_next():
        if flying:
            unit, a = flying.pop(0)
            pump()
            unit.fold_y(a)
            if not unit.left:
                later.extend((3 * t + 2, job) for t, job in enumerate(unit.then))
        now = [job for t, job in later if t <= 0]
        later[:] = [(t - 1, job) for t, job in later if t > 0]
        for job in now:
            job()

    UI = [Unit(PI.at[ex], RYI.at[ex], RZI.at[ex], MI.at[ex]) for ex in range(2)]
    UU = Unit(PU.at[0], RYU, RZU, MU)
    UO = Unit(PO, RYO, RZO, MO)
    UQ = [Unit(PQ.at[j], RYQ.at[j], RZQ.at[j], MQ.at[j]) for j in range(3)]
    plan = Plan()

    xi = [remote(NEAR, lambda ex=ex: (MI.at[ex], RXI.at[ex])) for ex in range(2)]

    def inner_z(ex):
        UI[ex].fold_z()
        go(xi[ex])

    def cols_of(ref, e, size):
        return ref.at[:, at(flip(C, e), size)]

    i_core = [
        remote(CORE, lambda ex=ex: (RXI.at[1 - ex], cols_of(o_i, 2 * ex, cq))) for ex in range(2)
    ]

    def inner_x():
        for ex in range(2):
            xi[1 - ex]().wait_recv()
            RXI[1 - ex] = plus(MI[ex], RXI[1 - ex])
            go(i_core[ex])
            go_local(lambda ex=ex: (RXI.at[1 - ex], cols_of(o_i, 2 * ex, cq)))

    x_base = [next(remotes_free) for _ in range(n)][0]

    def outer_copy(i):
        return remote_at(NEAR, x_base + i, lambda: (PU.at[1, i % 2, i // 2], RXU.at[i % 2, i // 2]))

    def outer_x(i):
        outer_copy(i).wait_recv()
        PU[0, i % 2, i // 2] = plus(PU[0, i % 2, i // 2], RXU[i % 2, i // 2])
        if i % 2:
            UU.start_y(i // 2)

    u_near = remote(NEAR, lambda: (MU, cols_of(o_u, 0, wq)))
    u_core = remote(CORE, lambda: (MU, cols_of(o_u, 0, wq)))
    u_core2 = remote(CORE, lambda: (cols_of(o_u, 2, wq), cols_of(o_u, 2, wq)))

    def outer_z():
        UU.fold_z()
        go(u_near)
        go(u_core)
        go_local(lambda: (MU, cols_of(o_u, 0, wq)))

    def outer_end():
        u_near().wait_recv()
        go(u_core2)

    xo = remote(NEAR, lambda: (MO, RXO))
    o_core = [
        remote(
            CORE, lambda ex=ex: (RXO.at[pl.ds((1 - ex) * rs, rs)], cols_of(o_o, 2 * ex, wq))
        )
        for ex in range(2)
    ]

    def out_z():
        UO.fold_z()
        go(xo)

    def out_x():
        xo().wait_recv()
        for ex in range(2):
            mine, theirs = pl.ds(ex * rs, rs), pl.ds((1 - ex) * rs, rs)
            RXO[theirs] = plus(MO[mine], RXO[theirs])
            go(o_core[ex])
            go_local(
                lambda ex=ex: (RXO.at[pl.ds((1 - ex) * rs, rs)], cols_of(o_o, 2 * ex, wq))
            )

    outs = (o_q, o_k, o_v)
    xq = [remote(NEAR, lambda j=j: (MQ.at[j], RXQ.at[j])) for j in range(3)]
    q_core = [
        remote(CORE, lambda j=j: (RXQ.at[j], outs[j].at[:, at(core, hw)])) for j in range(3)
    ]

    def proj_z(j):
        UQ[j].fold_z()
        go(xq[j])

    def proj_x(j):
        xq[j]().wait_recv()
        RXQ[j] = plus(MQ[j], RXQ[j])
        go(q_core[j])
        go_local(lambda: (RXQ.at[j], outs[j].at[:, at(core, hw)]))

    hops = [CORE, NEAR] + [(0, 1 << b) for b in range(n.bit_length() - 1)]
    hop_copies = [
        remote(dev, lambda t=t: (VS.at[t], VR.at[t])) for t, dev in enumerate(hops)
    ]

    def vector_hop(t):
        if t:
            hop_copies[t - 1]().wait_recv()
            VS[t] = VS[t - 1] + VR[t - 1]
        if t < len(hops):
            go(hop_copies[t])
        else:
            go_local(lambda: (VS.at[t], o_vec))

    pairs = hw // (2 * HD)

    def attention(s, times):
        need(("lse", s))

        def body(step, carry):
            cols = at(step, 2 * HD)

            def get(ref):
                return ref[:, s, :, cols].reshape(slots * part, 2 * HD)

            mask = key_mask(lens[x * sh + s], C, part)
            dq, dk, dv = attend_back_pair(
                get(Q), get(K), get(V), mask, LSE[s % 2, :, cols], get(CX), get(G)
            )
            for ref, value in ((Q, dq), (K, dk), (V, dv)):
                ref[:, s, :, cols] = value.reshape(slots, part, 2 * HD)
            plan.beside(step, times)
            return carry

        lax.fori_loop(0, pairs, body, 0)
        if s + 2 < sh:
            load(("lse", s + 2), lambda: (lse_in.at[s + 2], LSE.at[s % 2]))

    groups = width // 256
    gsz = 256 // rs

    def weight_grad(get, P, times):
        def body(a, carry):
            cols = at(xor(f // gsz, a, groups), 256)
            r = (dot_tn(L[0, :, cols], get(0)) + dot_tn(L[1, :, cols], get(1))).astype(BF)
            for u in range(gsz):
                i = a * gsz + flip(f % gsz, u) if gsz > 1 else a
                P[i % 2, i // 2] = r[u * rs : (u + 1) * rs]
            plan.beside(a, times)
            return carry

        lax.fori_loop(0, groups, body, 0)

    def spaced(first, last, count):
        return [first + (last - first) * (t + 1) / count for t in range(count)]

    UI[0].then = [lambda: inner_z(0)]
    UI[1].then = [lambda: inner_z(1), inner_x]
    UU.then = [outer_z, outer_end]
    UO.then = [out_z, out_x]
    for j in range(3):
        UQ[j].then = [lambda j=j: proj_z(j), lambda j=j: proj_x(j)]

    xs_order = list(range(1, n, 2)) + list(range(0, n, 2))
    for k, i in enumerate(xs_order):
        if k < n // 2:
            plan.add(11 + 14 * (per * (i // per) + per - 1 - i % per + 1) / n, lambda i=i: outer_copy(i).start())
        follow = xs_order[k + n // 2] if k < n // 2 else None

        def fold_x(i=i, follow=follow):
            if follow is not None:
                outer_copy(follow).start()
            outer_x(i)

        plan.add(20 + 48 * k / n, fold_x)
    for k in range(13 * A):
        plan.add(14 + 18 * k / A, fold_next)
    for t in range(len(hops) + 1):
        plan.add(74 + 4 * t, lambda t=t: vector_hop(t))

    need("nrm", "nrm_s", ("dinn", 0), ("dinn_s", 0))
    weight_grad(lambda m: D[0, m], PI.at[0], spaced(4, 8, groups))
    UI[0].start_y()

    def act_load(t):
        slot = t % 2
        return [
            pltpu.make_async_copy(act.at[:, act_cols(t)], D.at[slot, 0], lsem.at[act_sem + 2 * slot]),
            pltpu.make_async_copy(
                act_s.at[:, act_cols(t)], D.at[slot, 1], lsem.at[act_sem + 2 * slot + 1]
            ),
        ]

    act_sem = [next(locals_free) for _ in range(4)][0]

    def begin_act(t):
        for c in act_load(t):
            c.start()

    begin_act(0)
    need(("dinn", 1), ("dinn_s", 1))
    weight_grad(lambda m: D[1, m], PI.at[1], spaced(8, 11, groups))
    UI[1].start_y()
    if chunks > 1:
        begin_act(1)
    load("x0", lambda: (xall.at[pl.ds(0, rows)], L.at[0]))
    load("x1", lambda: (xall.at[pl.ds(rows, rows)], L.at[1]))
    need(("dout", 0), ("dout", 1), "dout_s")

    outer_times = spaced(11, 25, n)

    def outer_body(u, carry):
        t, il = u // per, per - 1 - u % per
        slot = t % 2

        @pl.when(u % per == 0)
        def _():
            for c in act_load(t):
                c.wait()

        cols = at(xor(f % per, il, per), ro)
        r = dot_tn(D[slot, 0, :, cols], DO[0]) + dot_tn(D[slot, 1, :, cols], DO[1])
        r = r.astype(BF)
        i = t * per + il
        for ex in range(2):
            PU[ex, i % 2, i // 2] = r[:, ex * wq : (ex + 1) * wq]

        @pl.when((u % per == per - 1) & (t + 2 < chunks))
        def _():
            begin_act(t + 2)

        plan.beside(u, outer_times)
        return carry

    lax.fori_loop(0, n, outer_body, 0)

    need("co", "co_s", "c", ("dattn", 0), ("dattn", 1), "dattn_s")
    for half in range(2):
        for g in range(hw // 256):
            lanes = slice(g * 256, (g + 1) * 256)

            def left(m):
                if half:
                    return CO[m, :, lanes]
                return CX[2 * m : 2 * m + 2, :, :, lanes].reshape(rows, 256)

            r = (dot_tn(left(0), DA[0]) + dot_tn(left(1), DA[1])).astype(BF)
            group = (core + half * (1 - 2 * core)) * (hw // 256) + g
            for u in range(gsz):
                i = xor(group * gsz + u, f, n)
                for ex in range(2):
                    PO[i % 2, i // 2, ex * rs : (ex + 1) * rs] = r[
                        u * rs : (u + 1) * rs, ex * wq : (ex + 1) * wq
                    ]
        for job in plan.due(27 + 3 * half):
            job()
    UO.start_y()

    need("q", "k", "v", "g", "g_s")
    for s in range(sh):
        attention(s, spaced(30 + 8 * s, 38 + 8 * s, pairs))

    need("x0", "x1", "vec")
    for j, ref in enumerate((Q, K, V)):

        def right(m):
            return ref[2 * m : 2 * m + 2].reshape(rows, hw)

        if j != 1:
            total = jnp.sum(right(0).astype(F32), 0, keepdims=True)
            total = total + jnp.sum(right(1).astype(F32), 0, keepdims=True)
            VS[0, j // 2 : j // 2 + 1, at(core, hw)] = total
        weight_grad(right, PQ.at[j], spaced(54 + 6 * j, 60 + 6 * j, groups))
        UQ[j].start_y()

    need("w")

    def project(slot):
        out = None
        for j, ref in enumerate((Q, K, V)):
            p = dot_nt(ref[slot].reshape(half_rows, hw), W[j])
            out = p if out is None else out + p
        return out

    ig_swap = [remote(CORE, lambda ex=ex: (SB, ig_s.at[ex])) for ex in range(2)]
    for ex in (1, 0):
        value = project(2 + ex)
        if ex == 0:
            ig_swap[1]().wait_send()
        SB[...] = value
        ig_swap[ex]().start()
        for job in plan.due(80 - 4 * ex):
            job()

    def rows_of(ex):
        return pl.ds(ex * half_rows, half_rows)

    ig_near = remote(NEAR, lambda: (XS, o_igr))
    for ex in (1, 0):
        ig_swap[ex]().wait_recv()
        load(("ig", ex), lambda ex=ex: (ig_s.at[ex], IB))
        value = project(ex)
        if ex:
            ig_swap[0]().wait_send()
        load(("df", ex), lambda ex=ex: (dfirst.at[rows_of(ex)], SB))
        need(("ig", ex), ("df", ex))
        value = value + IB[...] + SB[...]
        if ex:
            XS[...] = value.astype(BF)
            go(ig_near)
        else:
            IB[...] = value
            go_local(lambda: (IB, o_igl))
        for job in plan.due(88 - 4 * ex):
            job()

    for job in plan.due(1e9):
        job()
    while flying or later:
        fold_next()

    ig_near().wait_recv()
    for build in i_core + [u_core, u_core2] + o_core + q_core:
        build().wait_recv()
    for i in range(n):
        outer_copy(i).wait_send()
    for end in ends:
        end()


def back_call(lens, n, act, dout, nrm, dinn, dattn, ctx, cr, xall, q, k, v, lse, *rest):
    rows, width = nrm.shape
    ff = act.shape[1]
    slots, sh, part, hw = q.shape
    A = n // 2
    rs, ro, cq, wq = width // n, ff // n, ff // 4, width // 4
    hops = 2 + n.bit_length() - 1

    def bf(*shape):
        return jax.ShapeDtypeStruct(shape, BF)

    def f32(*shape):
        return jax.ShapeDtypeStruct(shape, F32)

    def vm(*shape):
        return pltpu.VMEM(shape, BF)

    def vf(*shape):
        return pltpu.VMEM(shape, F32)

    four = (slots, sh, part, hw)
    return pl.pallas_call(
        functools.partial(back_kernel, n),
        in_specs=[pl.BlockSpec(memory_space=pltpu.SMEM)] + [ANY] * 23,
        out_specs=[ANY] * 10,
        out_shape=[
            f32(rows // 2, width),
            bf(rows // 2, width),
            bf(rs, ff),
            bf(ro, width),
            bf(rs, width),
            bf(rs, width),
            bf(rs, width),
            bf(rs, width),
            f32(16, width),
            f32(2, rows // 2, width),
        ],
        scratch_shapes=[
            vm(*four),
            vm(*four),
            vm(*four),
            vm(*four),
            vm(*four),
            vf(2, *lse.shape[1:]),
            vm(2, rows, width),
            vm(2, 2, rows, 1024),
            vm(2, rows, 2 * wq),
            vm(2, rows, 2 * wq),
            vm(2, rows, hw),
            vm(3, width, hw),
            vm(2, 2, A, rs, cq),
            vm(2, 2, A, ro, wq),
            vm(2, A, 2 * rs, wq),
            vm(3, 2, A, rs, hw),
            vm(2, A, rs, cq),
            vm(2, A - 1, rs, cq),
            vm(2, rs, cq),
            vm(2, rs, cq),
            vm(2, A, ro, wq),
            vm(A, ro, wq),
            vm(A - 1, ro, wq),
            vm(ro, wq),
            vm(A, 2 * rs, wq),
            vm(A - 1, 2 * rs, wq),
            vm(2 * rs, wq),
            vm(2 * rs, wq),
            vm(3, A, rs, hw),
            vm(3, A - 1, rs, hw),
            vm(3, rs, hw),
            vm(3, rs, hw),
            vf(hops + 1, 16, width),
            vf(hops, 16, width),
            vf(rows // 2, width),
            vf(rows // 2, width),
            vm(rows // 2, width),
            pltpu.SemaphoreType.DMA((48,)),
            pltpu.SemaphoreType.DMA((64 + 8 * n,)),
            pltpu.SemaphoreType.DMA((64 + 8 * n,)),
        ],
        compiler_params=pltpu.CompilerParams(
            vmem_limit_bytes=BACK_LIMIT, collective_id=1, has_side_effects=True
        ),
        name="back",
    )(
        lens,
        act,
        dout,
        nrm,
        dinn,
        dattn,
        ctx,
        cr,
        xall,
        q,
        k,
        v,
        lse,
        *rest,
    )


def finish_kernel(here, near, lo, *refs):
    o_ig, o_lo = refs[6:8]
    x = lax.axis_index("ctx") // 2
    o_ig[x] = here[...]
    o_ig[1 - x] = near[...].astype(F32)
    o_lo[...] = lo[...]
    for source, target in zip(refs[:6], refs[8:]):
        target[...] = source[...].astype(F32)


def finish_call(here, near, lo, *grads):
    steps = 4
    rows, width = here.shape

    def by(a):
        return pl.BlockSpec((a.shape[0] // steps, a.shape[1]), lambda i: (i, 0))

    return pl.pallas_call(
        finish_kernel,
        grid=(steps,),
        in_specs=[by(a) for a in (here, near, lo) + grads],
        out_specs=[pl.BlockSpec((2, rows // steps, width), lambda i: (0, i, 0)), by(lo)]
        + [by(g) for g in grads],
        out_shape=[jax.ShapeDtypeStruct((2, rows, width), F32), jax.ShapeDtypeStruct(lo.shape, BF)]
        + [jax.ShapeDtypeStruct(g.shape, F32) for g in grads],
        compiler_params=params(),
        name="finish",
    )(here, near, lo, *grads)


def per_device(
    inputs,
    lengths,
    cotangent,
    query_weight,
    key_weight,
    value_weight,
    out_weight,
    inner_weight,
    outer_weight,
    query_bias,
    value_bias,
    out_bias,
    inner_bias,
    outer_bias,
    first_gain,
    first_shift,
    second_gain,
    second_shift,
):
    C = lax.axis_index("ctx")
    f = lax.axis_index("fsdp")
    n = lax.axis_size("fsdp")
    x, core = C // 2, C % 2
    seqs, part, width = inputs.shape
    ff = inner_weight.shape[1]
    sh = seqs // 2
    rows = 2 * sh * part
    rs, ro = width // n, ff // n
    hw = width // 2

    def pick(bit, a, b):
        return jnp.where(bit == 0, a, b), jnp.where(bit == 0, b, a)

    vectors = (
        query_bias,
        value_bias,
        out_bias,
        outer_bias,
        first_gain,
        first_shift,
        second_gain,
        second_shift,
    )
    vecs = jnp.concatenate([v.reshape(1, rs) for v in vectors], 0)
    if rs < 128:
        vecs = jnp.pad(vecs, ((0, 0), (0, 128 - rs)))
    vecs = jnp.concatenate(
        [vecs, inner_bias.reshape(ro // 128, 128), jnp.zeros((PACK - 8 - ro // 128, 128), BF)], 0
    )
    x4, cot, w_qkv, wi, wu, wo, vecs, q4, k4, v4, c4, c_r, c_s, lse, *norm = front_call(
        lengths,
        inputs,
        cotangent,
        query_weight,
        key_weight,
        value_weight,
        vecs,
        out_weight,
        inner_weight,
        outer_weight,
        n,
    )
    xall = x4.reshape(2 * rows, width)
    cr = c_r.reshape(rows, hw)
    norm = [a.reshape(rows, a.shape[2]) for a in norm]
    two = (2, sh, part, hw)
    (
        dfirst,
        dco,
        acc,
        dout,
        dinn,
        dattn,
        layer_out,
        act_s,
        dout_s,
        dinn_s,
        nrm_s,
        dattn_s,
        dcs_s,
    ) = ffn_call(lengths, sh, *norm, cot.reshape(rows, width), vecs, wo, wi, wu)
    act, nrm = norm[0], norm[4]

    ig_here, ig_near, g_i, g_u, g_o, g_q, g_k, g_v, sums, _ = back_call(
        lengths,
        n,
        act,
        dout,
        nrm,
        dinn,
        dattn,
        c4,
        cr,
        xall,
        q4,
        k4,
        v4,
        lse,
        dco.reshape(two),
        dfirst,
        w_qkv,
        acc,
        act_s,
        dout_s,
        dinn_s,
        nrm_s,
        dattn_s,
        dcs_s.reshape(two),
        c_s.reshape(rows, hw),
    )
    own = lax.dynamic_slice_in_dim(sums[:8], f * rs, rs, 1)
    own_inner = lax.dynamic_slice_in_dim(sums[8 : 8 + ff // width].reshape(ff), f * ro, ro, 0)
    input_grad, layer_out, *grads = finish_call(
        ig_here, ig_near, layer_out.reshape(seqs * part, width), g_q, g_k, g_v, g_o, g_i, g_u
    )
    grad_query, grad_key, grad_value, grad_out, grad_inner, grad_outer = grads
    input_grad, layer_out = input_grad.reshape(inputs.shape), layer_out.reshape(inputs.shape)

    return (
        layer_out,
        input_grad,
        grad_query,
        grad_key,
        grad_value,
        grad_out,
        grad_inner,
        grad_outer,
        own[0],
        own[1],
        own[2],
        own_inner,
        own[3],
        own[4],
        own[5],
        own[6],
        own[7],
    )


def solution(mesh):
    rowed = P("fsdp", "ctx", None)
    matrix, vector = P("fsdp", None), P("fsdp")
    in_specs = (rowed, vector, rowed) + (matrix,) * 6 + (vector,) * 9
    out_specs = (rowed, rowed) + (matrix,) * 6 + (vector,) * 9
    return jax.shard_map(
        per_device, mesh=mesh, in_specs=in_specs, out_specs=out_specs, check_vma=False
    )
```

```python
import functools

import jax
import jax.numpy as jnp
from jax import lax
from jax.experimental import pallas as pl
from jax.experimental.pallas import tpu as pltpu
from jax.sharding import PartitionSpec as P

HD = 64
EPSILON = 1e-05
BF = jnp.bfloat16
F32 = jnp.float32
ANY = pl.BlockSpec(memory_space=pl.ANY)
NT = (((1,), (1,)), ((), ()))
TN = (((0,), (0,)), ((), ()))
VMEM_LIMIT = 58 << 20
BACK_LIMIT = 60 << 20
WINDOW = 2


def dot(a, b):
    return jnp.dot(a, b, preferred_element_type=F32)


def dot_nt(a, b):
    return lax.dot_general(a, b, NT, preferred_element_type=F32)


def dot_tn(a, b):
    return lax.dot_general(a, b, TN, preferred_element_type=F32)


def params(**more):
    return pltpu.CompilerParams(vmem_limit_bytes=VMEM_LIMIT, **more)


def cost(flops, size, trans=0):
    return pl.CostEstimate(flops=int(flops), bytes_accessed=int(size), transcendentals=int(trans))


MESH = pl.DeviceIdType.MESH
PACK = 16


def flip(v, mask):
    out, bit = v, 1
    while bit <= mask:
        if mask & bit:
            out = out + bit - 2 * bit * ((v // bit) % 2)
        bit *= 2
    return out


def at(index, size):
    return pl.ds(pl.multiple_of(index * size, size), size)


def spread(read, n, rs):
    per = max(128 // rs, 1)
    tiles = []
    for t in range(n // per):
        tile = read(t * per)
        for u in range(1, per):
            tile = tile + pltpu.roll(read(t * per + u), u * rs, 1)
        tiles.append(tile)
    return jnp.concatenate(tiles, 1)


def front_kernel(
    n,
    lens,
    xin,
    cin,
    wq,
    wk,
    wv,
    vecs,
    wo_in,
    wi_in,
    wu_in,
    xo,
    co,
    wqkvo,
    wio,
    wuo,
    woo,
    veco,
    qo,
    ko,
    vo,
    cxo,
    cro,
    cso,
    lseo,
    acto,
    gpo,
    hato,
    ro_o,
    nrmo,
    X,
    W,
    VEC,
    Q,
    K,
    V,
    CX,
    LSE,
    WO,
    WI,
    CR,
    VB,
    IB,
    HAT,
    R1,
    NRM,
    ACT,
    GP,
    lsem,
    ssem,
    rsem,
):
    C, f = lax.axis_index("ctx"), lax.axis_index("fsdp")
    x, core = C // 2, C % 2
    A = n // 2
    sh, part, width = X.shape[1:]
    hw = W.shape[2]
    ff = wio.shape[1]
    rs, ro, cq = width // n, ff // n, ff // 4

    partners = [(0, 2 * k) for k in range(1, A)] + [(0, 1), (2, 0), (1, 0)]

    def device(dc, df):
        return (flip(C, dc), flip(f, df))

    barrier = pltpu.get_barrier_semaphore()
    for p in partners:
        pl.semaphore_signal(barrier, inc=1, device_id=device(*p), device_id_type=MESH)

    local = []
    used = iter(range(lsem.shape[0]))

    def begin(source, target):
        c = pltpu.make_async_copy(source, target, lsem.at[next(used)])
        c.start()
        return c

    def keep(source, target):
        local.append(begin(source, target))

    x_here = begin(xin.at[pl.ds(x * sh, sh)], X.at[0])
    w_here = [begin(w.at[:, at(core, hw)], W.at[j, at(f, rs)]) for j, w in enumerate((wq, wk, wv))]
    w_here.append(begin(vecs, VEC.at[f]))

    pl.semaphore_wait(barrier, len(partners))

    def remote(source, target, sem, dev):
        return pltpu.make_async_remote_copy(
            src_ref=source,
            dst_ref=target,
            send_sem=ssem.at[sem],
            recv_sem=rsem.at[sem],
            device_id=device(*dev),
            device_id_type=MESH,
        )

    sent = []

    def send(*what):
        c = remote(*what)
        c.start()
        sent.append(c)

    seen = set()

    def arrive(target, sem, dev):
        if sem not in seen:
            seen.add(sem)
            remote(target, target, sem, dev).wait_recv()

    X1, X2, X3, COT, CTX, CTX2 = range(6)
    send(xin.at[pl.ds((1 - x) * sh, sh)], X.at[1], X1, (2, 0))

    def rows_at(ref, first, size):
        return ref.at[pl.ds(pl.multiple_of(first, size), size)]

    hr, hu = rs // 2, ro // 2

    def projection(j):
        w = (wq, wk, wv)[j]
        return (
            1,
            lambda e, s: [W.at[j, at(s, rs)]] + [VEC.at[s]] * (j == 0),
            lambda: [w.at[:, at(core, hw)]] + [vecs] * (j == 0),
        )

    def inner_part(h):
        return (
            4,
            lambda e, s: [WI.at[at(s * 2 + h, hr), at(flip(C, e), cq)]],
            lambda: [wi_in.at[pl.ds(h * hr, hr), at(C, cq)]],
        )

    outer_a = (
        4,
        lambda e, s: [rows_at(wuo, s * ro + flip(C, e) * (hu // 4), hu // 4)],
        lambda: [rows_at(wu_in, C * (hu // 4), hu // 4)],
    )
    out_part = (
        4,
        lambda e, s: [rows_at(WO, s * rs + flip(C, e) * (rs // 4), rs // 4)],
        lambda: [rows_at(wo_in, C * (rs // 4), rs // 4)],
    )

    def outer_b(h):
        return (
            2,
            lambda e, s: [rows_at(wuo, s * ro + hu + (flip(core, e) * 2 + h) * (hu // 4), hu // 4)],
            lambda: [rows_at(wu_in, hu + (core * 2 + h) * (hu // 4), hu // 4)],
        )

    kinds = [
        out_part,
        inner_part(0),
        projection(0),
        projection(1),
        projection(2),
        inner_part(1),
        outer_a,
        outer_b(0),
        outer_b(1),
    ]
    sems, ready = {}, 6
    for k, (parts, place, _) in enumerate(kinds):
        for e in range(parts):
            for i in range(1, n):
                for u in range(2 if k == 2 else 1):
                    sems[k, e, i, u] = ready
                    ready += 1

    def route(parts, e, i):
        if e % 2:
            return (1, 0), (e - 1, i)
        if e:
            return (2, 0), (0, i)
        if i % 2:
            return (0, 1), (0, i - 1)
        return (0, i), (0, 0)

    def copies(k, e, i):
        parts, place, own = kinds[k]
        dev, (pe, pi) = route(parts, e, i)
        target = place(pe, flip(f, pi))
        source = target if pi else own()
        return [
            remote(source[u], target[u], sems[k, e, i, u], dev) for u in range(len(target))
        ]

    issued = []

    def give(k, e, i):
        for c in copies(k, e, i):
            c.start()
        issued.append((k, e, i))

    got = set()

    def take(k, e, i):
        if (k, e, i) in got:
            return
        got.add((k, e, i))
        parts, place, _ = kinds[k]
        dev, _ = route(parts, e, i)
        for u, target in enumerate(place(e, flip(f, i))):
            remote(target, target, sems[k, e, i, u], dev).wait_recv()

    def hand_on(k, i):
        parts = kinds[k][0]
        if parts == 4:
            give(k, 2, i)
        if parts > 1:
            give(k, 1, i)

    def base(k):
        if k < len(kinds):
            for a in range(1, A):
                give(k, 0, 2 * a)
            give(k, 0, 1)

    def z_in(k):
        for a in range(1, A):
            take(k, 0, 2 * a)
            give(k, 0, 2 * a + 1)
            hand_on(k, 2 * a)

    def y_in(k):
        for i in range(1, n, 2):
            take(k, 0, i)
            hand_on(k, i)

    def x_in(k):
        if kinds[k][0] == 4:
            for i in range(1, n):
                take(k, 2, i)
                give(k, 3, i)

    base(0)
    base(1)
    x_here.wait()
    send(X.at[0], X.at[2], X2, (1, 0))
    keep(cin.at[pl.ds(x * sh, sh)], co.at[0])
    w_here += [begin(wo_in, WO.at[at(f, rs)]), begin(wi_in, WI.at[at(f, rs)])]
    keep(wu_in, wuo.at[at(f, ro)])
    slots = X.shape[0]
    pairs = hw // (2 * HD)

    z_in(0)
    base(2)
    arrive(X.at[1], X1, (2, 0))
    send(X.at[1], X.at[3], X3, (1, 0))
    z_in(1)
    base(3)
    y_in(0)
    arrive(X.at[2], X2, (1, 0))
    arrive(X.at[3], X3, (1, 0))
    keep(X, xo)
    for c in w_here:
        c.wait()
    z_in(2)
    base(4)
    y_in(1)
    send(cin.at[pl.ds((1 - x) * sh, sh)], co.at[1], COT, (2, 0))
    z_in(3)
    base(5)
    y_in(2)
    x_in(0)
    keep(VEC, veco)

    def bias(row):
        read = lambda s: VEC[pl.ds(core * (n // 2) + s, 1), row : row + 1, :128].reshape(1, 128).astype(F32)
        return spread(read, n // 2, rs)

    shape = (sh, part, hw)

    def project(j, target, add):
        def body(slot, carry):
            value = dot(X[slot].reshape(sh * part, width), W[j])
            if add is not None:
                value = value + add
            target[slot] = value.astype(BF).reshape(shape)
            return carry

        lax.fori_loop(0, slots, body, 0)

    project(0, Q, bias(0))
    z_in(4)
    base(6)
    y_in(3)
    project(1, K, None)
    x_in(1)
    z_in(5)
    base(7)
    y_in(4)
    keep(W, wqkvo)
    project(2, V, bias(1))
    keep(Q, qo)
    keep(K, ko)
    keep(V, vo)

    jobs = {7: [lambda: z_in(6), lambda: base(8)], 9: [lambda: y_in(5)]}
    steps = sh * pairs

    def attend(step, carry):
        s, pair = step // pairs, step % pairs
        cols = at(pair, 2 * HD)

        def load(ref):
            return ref[:, s, :, cols].reshape(slots * part, 2 * HD)

        q, k, v = load(Q), load(K), load(V)
        mask = key_mask(lens[x * sh + s], C, part)
        o, lse = attend_pair(q, k, v, mask)
        CX[:, s, :, cols] = o.reshape(slots, part, 2 * HD)
        LSE[s, :, cols] = lse
        for t in range(steps):
            now = jobs.get(t)
            if now:

                @pl.when(step == t)
                def _():
                    for job in now:
                        job()

        return carry

    lax.fori_loop(0, steps, attend, 0)
    send(CX.at[pl.ds(2, 2)], CR, CTX, (1, 0))
    send(CX.at[pl.ds(0, 2)], cso, CTX2, (1, 0))
    keep(CX, cxo)
    keep(LSE, lseo)
    for e in range(4):
        for i in range(1, n):
            take(0, e, i)
    keep(WO, woo)
    VB[...] = spread(lambda s: VEC[s, :8, :128].astype(F32), n, rs)
    for s in range(n):
        for t in range(ro // 128):
            first = s * ro + t * 128
            IB[:, first : first + 128] = VEC[s, 8 + t : 9 + t, :].astype(F32)
    arrive(CR, CTX, (1, 0))
    keep(CR, cro)
    own_half, other_half = at(core, hw), at(1 - core, hw)
    half = sh * part

    def norm(ex, carry):
        first = (
            X[ex].reshape(half, width).astype(F32)
            + (
                dot(CX[ex].reshape(half, hw), WO[own_half])
                + dot(CR[ex].reshape(half, hw), WO[other_half])
            )
            + VB[2:3, :]
        )
        hat, r = normalise(first)
        HAT[ex] = hat
        R1[ex] = jnp.broadcast_to(r, (half, 128))
        NRM[ex] = (hat * VB[4:5, :] + VB[5:6, :]).astype(BF)
        return carry

    lax.fori_loop(0, 2, norm, 0)
    keep(HAT, hato)
    keep(R1, ro_o)
    keep(NRM, nrmo)
    plan = [
        [lambda: z_in(7), lambda: y_in(6)],
        [lambda: x_in(5)],
        [lambda: z_in(8), lambda: y_in(7)],
        [lambda: x_in(6)],
    ]
    for e in range(4):
        for job in plan[e]:
            job()
        for k in (1, 5):
            for i in range(1, n):
                take(k, e, i)
        cols = at(flip(C, e), cq)

        def inner(ex, carry):
            g, d = gelu_pair(dot(NRM[ex], WI[:, cols]) + IB[:, cols])
            ACT[ex, :, cols] = g.astype(BF)
            GP[ex, :, cols] = d.astype(BF)
            return carry

        lax.fori_loop(0, 2, inner, 0)
        keep(ACT.at[:, :, cols], acto.at[:, :, cols])
        keep(GP.at[:, :, cols], gpo.at[:, :, cols])
    y_in(8)
    keep(WI, wio)
    for k, (parts, _, _) in enumerate(kinds):
        for e in range(parts):
            for i in range(1, n):
                take(k, e, i)
    arrive(co.at[1], COT, (2, 0))
    arrive(cso, CTX2, (1, 0))
    for what in issued:
        for c in copies(*what):
            c.wait_send()
    for c in sent:
        c.wait_send()
    for c in local:
        c.wait()


def front_call(lengths, xin, cin, wq, wk, wv, vecs, wo, wi, wu, n):
    seqs, part, width = xin.shape
    sh, ff, hw = seqs // 2, wi.shape[1], width // 2

    def bf(*shape):
        return jax.ShapeDtypeStruct(shape, BF)

    def vm(*shape):
        return pltpu.VMEM(shape, BF)

    full = 4 * part
    lse = (sh, full, hw)
    half = sh * part
    four = (4, sh, part, hw)
    sems = 24 * n
    return pl.pallas_call(
        functools.partial(front_kernel, n),
        in_specs=[pl.BlockSpec(memory_space=pltpu.SMEM)] + [ANY] * 9,
        out_specs=[ANY] * 19,
        out_shape=[
            bf(4, sh, part, width),
            bf(2, sh, part, width),
            bf(3, width, hw),
            bf(width, ff),
            bf(ff, width),
            bf(width, width),
            bf(n, PACK, 128),
            bf(*four),
            bf(*four),
            bf(*four),
            bf(*four),
            bf(2, sh, part, hw),
            bf(2, sh, part, hw),
            jax.ShapeDtypeStruct(lse, F32),
            bf(2, half, ff),
            bf(2, half, ff),
            jax.ShapeDtypeStruct((2, half, width), F32),
            jax.ShapeDtypeStruct((2, half, 128), F32),
            bf(2, half, width),
        ],
        scratch_shapes=[
            vm(4, sh, part, width),
            vm(3, width, hw),
            vm(n, PACK, 128),
            vm(*four),
            vm(*four),
            vm(*four),
            vm(*four),
            pltpu.VMEM(lse, F32),
            vm(width, width),
            vm(width, ff),
            vm(2, sh, part, hw),
            pltpu.VMEM((8, width), F32),
            pltpu.VMEM((1, ff), F32),
            pltpu.VMEM((2, half, width), F32),
            pltpu.VMEM((2, half, 128), F32),
            vm(2, half, width),
            vm(2, half, ff),
            vm(2, half, ff),
            pltpu.SemaphoreType.DMA((40,)),
            pltpu.SemaphoreType.DMA((sems,)),
            pltpu.SemaphoreType.DMA((sems,)),
        ],
        compiler_params=params(collective_id=0, has_side_effects=True),
        name="front",
    )(lengths, xin, cin, wq, wk, wv, vecs, wo, wi, wu)


def lanes_of(shape, head):
    lane = lax.broadcasted_iota(jnp.int32, shape, 1)
    own = (lane < HD) if head == 0 else (lane >= HD)
    return lane, own, (HD if head == 0 else 0)


def split3(a):
    hi = a.astype(BF).astype(F32)
    mid = (a - hi).astype(BF).astype(F32)
    return hi, mid, a - hi - mid


def flat(ref):
    a = ref[...]
    return a.reshape(-1, a.shape[-1])


def key_mask(length, C, part):
    row = lax.broadcasted_iota(jnp.int32, (part, 2 * HD), 0)
    out = []
    for e in (0, 2, 1, 3):
        inside = row + flip(C, e) * part < length
        out.append(jnp.where(inside, 0.0, -1e30).astype(BF))
    return jnp.concatenate(out, 0)


def attend_pair(q, k, v, mask):
    out = []
    for head in range(2):
        lane, own, other = lanes_of(q.shape, head)
        qh = jnp.where(own, q * BF(HD**-0.5), jnp.where(lane == other, 1.0, 0.0).astype(BF))
        kh = jnp.where(own, k, mask)
        s = dot_nt(qh, kh)
        top = jnp.max(s, -1, keepdims=True)
        e = jnp.exp(s - top)
        total = jnp.sum(e, -1, keepdims=True)
        o = dot(e.astype(BF), v) * (1.0 / total)
        out.append((o, top + jnp.log(total), own))
    (o0, l0, own), (o1, l1, _) = out
    return jnp.where(own, o0, o1).astype(BF), jnp.where(own, l1, l0)


def attend_back_pair(q, k, v, mask, lse, c, g):
    qs = q * BF(HD**-0.5)
    kt = k.T
    prod = c.astype(F32) * g.astype(F32)
    res = []
    for head in range(2):
        lane, own, o = lanes_of(q.shape, head)
        hi, mid, low = split3(-lse)
        extra = jnp.where(
            lane == o,
            1.0,
            jnp.where(
                lane == o + 1,
                hi,
                jnp.where(lane == o + 2, mid, jnp.where(lane == o + 3, low, 0.0)),
            ),
        ).astype(BF)
        qh = jnp.where(own, qs, extra)
        kh = jnp.where(own, k, jnp.where(lane == o, mask, BF(1)))
        p = jnp.exp(dot_nt(kh, qh))
        delta = jnp.sum(jnp.where(own, prod, 0.0), -1, keepdims=True)
        hi, mid, low = split3(-delta)
        extra = jnp.where(
            lane == o, hi, jnp.where(lane == o + 1, mid, jnp.where(lane == o + 2, low, 0.0))
        ).astype(BF)
        gh = jnp.where(own, g, extra)
        vh = jnp.where(own, v, BF(1))
        ds = (p * dot_nt(vh, gh)).astype(BF)
        dv = dot(p.astype(BF), g)
        dk = dot(ds, qs)
        dqt = dot(kt, ds)
        res.append((dv, dk, dqt, own))
    (dv0, dk0, dq0, own), (dv1, dk1, dq1, _) = res
    dqt = jnp.concatenate([dq0[:HD], dq1[HD:]], 0) * (HD**-0.5)
    return dqt.T.astype(BF), jnp.where(own, dk0, dk1).astype(BF), jnp.where(own, dv0, dv1).astype(BF)


def gelu_pair(u):
    e = jnp.exp(u * u * -0.5)
    t = 1.0 / (1.0 + (0.3275911 * 0.7071067811865476) * jnp.abs(u))
    poly = t * (
        0.254829592 * 0.5
        + t
        * (
            -0.284496736 * 0.5
            + t * (1.421413741 * 0.5 + t * (-1.453152027 * 0.5 + t * (1.061405429 * 0.5)))
        )
    )
    tail = poly * e
    cdf = jnp.where(u >= 0, 1.0 - tail, tail)
    ucdf = u * cdf
    return ucdf, cdf + u * (e * 0.3989422804014327)


def normalise(h):
    c = h - jnp.mean(h, -1, keepdims=True)
    r = lax.rsqrt(jnp.mean(c * c, -1, keepdims=True) + EPSILON)
    return c * r, r


def normalise_back(dyg, hat, r):
    return r * (
        dyg - jnp.mean(dyg, -1, keepdims=True) - hat * jnp.mean(dyg * hat, -1, keepdims=True)
    )


def ffn_kernel(
    n, sh, part, lens, act, gp, hat1_ref, r1_ref, cot, vecs, act_in, nrm_in, wo_in, wi_in, wu_in, *refs
):
    dfirst, dco, acc = refs[:3]
    homes, (o_lo, act_s, dout_s, dinn_s, nrm_s, dattn_s, dcs_s) = refs[3:6], refs[6:13]
    wo, wi, wu, vec, *twice, sem, csem, hsem, ssem, rsem = refs[13:]
    width, ff = wi.shape
    C, f = lax.axis_index("ctx"), lax.axis_index("fsdp")
    x, core = C // 2, C % 2
    step = pl.program_id(0)
    turn = 2 - step
    rs, ro = width // n, ff // n
    cq, hw = ff // 4, width // 2

    pairs = ((wo_in, wo), (wi_in, wi), (wu_in, wu))

    def copy(kind):
        return pltpu.make_async_copy(*pairs[kind], sem.at[kind])

    CORE, NEAR = flip(C, 1), flip(C, 2)
    block, wq = cot.shape[0], width // 4

    def remote(t, j, to, source, target):
        return pltpu.make_async_remote_copy(
            src_ref=source,
            dst_ref=target,
            send_sem=ssem.at[t, j],
            recv_sem=rsem.at[t, j],
            device_id=(to, f),
            device_id_type=MESH,
        )

    KINDS = ("dout0", "dout1", "dinn0", "dinn1", "dattn0", "dattn1", "dcs")

    def rows_of(t):
        return pl.ds(pl.multiple_of(t * block, block), block)

    def held(t):
        return [ref.at[(2 - t) % 2] for ref in twice]

    dout, dinn, dattn, dcs, lo = held(turn)
    HOME = {"dout": 0, "dinn": 1, "dattn": 2}

    def whole(t):
        pair = ((act_in, act_s), (nrm_in, nrm_s))[t]
        return remote(t, 7, CORE, *pair)

    def home(t, name):
        j = HOME[name]
        return pltpu.make_async_copy(held(t)[j], homes[j].at[rows_of(t)], hsem.at[t, j])

    def to_core(t, *names):
        out = []
        for name in names or KINDS:
            rows = rows_of(t)
            dout, dinn, dattn, dcs, _ = held(t)
            ex = int(name[-1]) if name[-1] in "01" else 0
            other, lanes = flip(C, 2 * ex + 1), pl.ds(ex * wq, wq)
            source, target = {
                "dcs": lambda: (dcs, dcs_s.at[rows]),
                "dou": lambda: (dout.at[:, at(other, wq)], dout_s.at[rows, lanes]),
                "dat": lambda: (dattn.at[:, at(other, wq)], dattn_s.at[rows, lanes]),
                "din": lambda: (dinn.at[:, at(other, cq)], dinn_s.at[ex, rows]),
            }[name[:3]]()
            out.append(remote(t, KINDS.index(name), CORE, source, target))
        return out

    def start(name):
        for c in to_core(turn, *(k for k in KINDS if k.startswith(name))):
            c.start()
        if name in HOME:
            home(turn, name).start()

    def end(t, name):
        for c in to_core(t, *(k for k in KINDS if k.startswith(name))):
            c.wait_send()
        if name in HOME:
            home(t, name).wait()

    def free(name):
        @pl.when(step == 2)
        def _():
            end(2, name)

    def slots_of(t, ex):
        count = block // part
        return [u for u in range(count) if (t * count + u) // sh == ex]

    def place(t, u):
        return held(t)[4].at[pl.ds(u * part, part)], o_lo.at[x * sh + (t * (block // part) + u) % sh]

    def to_near(t):
        return [remote(t, 8 + u, NEAR, *place(t, u)) for u in slots_of(t, 1)]

    def stay(t):
        return [pltpu.make_async_copy(*place(t, u), csem.at[t, u]) for u in slots_of(t, 0)]

    def send(t):
        for c in to_near(t) + stay(t):
            c.start()

    def sent(t):
        for c in to_near(t):
            c.wait_send()
        for c in stay(t):
            c.wait()

    def received(t):
        for c in to_core(t) + to_near(t):
            c.wait_recv()

    @pl.when(step == 0)
    def _():
        barrier = pltpu.get_barrier_semaphore()
        for to in (CORE, NEAR):
            pl.semaphore_signal(barrier, inc=1, device_id=(to, f), device_id_type=MESH)
        copy(2).start()
        pl.semaphore_wait(barrier, 2)
        acc[...] = jnp.zeros_like(acc)
        vec[...] = spread(lambda s: vecs[s, :8, :128].astype(F32), n, rs)

    def arrived(kind):
        @pl.when(step == 0)
        def _():
            copy(kind).wait()

    count = block // part
    inside = []
    for u in range(count):
        slot = turn * count + u
        ex, s = slot // sh, slot % sh
        first = (C + ex * (2 - 4 * x)) * part
        row = lax.broadcasted_iota(jnp.int32, (part, 1), 0) + first
        inside.append(jnp.where(row < lens[x * sh + s], 1.0, 0.0))
    valid = jnp.concatenate(inside, 0)
    own, other = at(core, hw), at(1 - core, hw)

    def add(row, value):
        acc[row : row + 1, :] += jnp.sum(value, 0, keepdims=True)

    hat1, r1 = hat1_ref[...], r1_ref[:, :1]
    normed = hat1 * vec[4:5, :] + vec[5:6, :]
    arrived(2)

    @pl.when(step == 0)
    def _():
        copy(1).start()
        copy(0).start()
        whole(1).start()
        whole(0).start()

    second = normed + (dot(act[...], wu[...]) + vec[3:4, :])
    hat2, r2 = normalise(second)
    @pl.when(step == 2)
    def _():
        sent(2)

    lo[...] = (hat2 * vec[6:7, :] + vec[7:8, :]).astype(BF)
    og = cot[...].astype(F32) * valid
    add(6, og * hat2)
    add(7, og)
    d2 = normalise_back(og * vec[6:7, :], hat2, r2)
    d2low = d2.astype(BF)
    free("dout")
    dout[...] = d2low
    start("dout")
    for t in range(3):

        @pl.when(turn == t)
        def _():
            send(t)

    add(3, d2low.astype(F32))
    free("dinn")
    arrived(1)
    for j in range(4):
        cols = slice(j * cq, (j + 1) * cq)
        di = (dot_nt(d2low, wu[cols, :]) * gp[:, cols]).astype(BF)
        dinn[:, cols] = di
        add(8 + j, di.astype(F32))
    start("dinn")
    dn = d2 + dot_nt(dinn[...], wi[...])
    add(4, dn * hat1)
    add(5, dn)
    d1 = normalise_back(dn * vec[4:5, :], hat1, r1)
    dfirst[...] = d1
    d1low = d1.astype(BF)
    arrived(0)
    free("dattn")
    free("dcs")
    dattn[...] = d1low
    start("dattn")
    add(2, d1low.astype(F32))
    dcs[...] = dot_nt(d1low, wo[other]).astype(BF)
    start("dcs")
    dco[...] = dot_nt(d1low, wo[own]).astype(BF)

    @pl.when(turn == 0)
    def _():
        for t in range(2):
            for name in ("dout", "dinn", "dattn", "dcs"):
                end(t, name)
            sent(t)
            whole(t).wait()
        for t in range(3):
            received(t)


def ffn_call(lens, sh, act, gp, hat, r, nrm, cot, vecs, wo, wi, wu):
    width, ff = wi.shape
    n, rows = vecs.shape[0], cot.shape[0]
    block, part = rows // 3, rows // (2 * sh)
    hw = width // 2

    def by(cols):
        return pl.BlockSpec((block, cols), lambda i: (2 - i, 0))

    def whole(*shape):
        return pl.BlockSpec(shape, lambda i: (0,) * len(shape))

    grid_spec = pl.GridSpec(
        grid=(3,),
        in_specs=[
            pl.BlockSpec(memory_space=pltpu.SMEM),
            by(ff),
            by(ff),
            by(width),
            by(128),
            by(width),
            whole(*vecs.shape),
        ]
        + [ANY] * 5,
        out_specs=[by(width), by(hw), whole(16, width)] + [ANY] * 10,
        scratch_shapes=[
            pltpu.VMEM((width, width), BF),
            pltpu.VMEM((width, ff), BF),
            pltpu.VMEM((ff, width), BF),
            pltpu.VMEM((8, width), F32),
            *(pltpu.VMEM((2, block, cols), BF) for cols in (width, ff, width, hw, width)),
            pltpu.SemaphoreType.DMA((3,)),
            pltpu.SemaphoreType.DMA((3, block // part)),
            pltpu.SemaphoreType.DMA((3, 3)),
            pltpu.SemaphoreType.DMA((3, 8 + block // part)),
            pltpu.SemaphoreType.DMA((3, 8 + block // part)),
        ],
    )

    def shape(cols, dtype=BF):
        return jax.ShapeDtypeStruct((rows, cols), dtype)

    return pl.pallas_call(
        functools.partial(ffn_kernel, n, sh, part),
        grid_spec=grid_spec,
        out_shape=[
            shape(width, F32),
            shape(hw),
            jax.ShapeDtypeStruct((16, width), F32),
            shape(width),
            shape(ff),
            shape(width),
            jax.ShapeDtypeStruct((2 * sh, part, width), BF),
            shape(ff),
            shape(hw),
            jax.ShapeDtypeStruct((2, rows, ff // 4), BF),
            shape(width),
            shape(hw),
            shape(hw),
        ],
        compiler_params=params(collective_id=2, has_side_effects=True),
        cost_estimate=cost(
            2 * rows * width * (2 * width + 4 * ff), 30 * rows * width + 2 * width * (2 * ff + width)
        ),
        name="ffn",
    )(lens, act, gp, hat, r, cot, vecs, act, nrm, wo, wi, wu)


def xor(a, b, count):
    out, bit = 0, 1
    while bit < count:
        out = out + bit * ((a // bit + b // bit) % 2)
        bit *= 2
    return out


def plus(*items):
    out = items[0].astype(F32)
    for i in items[1:]:
        out = out + i.astype(F32)
    return out.astype(BF)


class Plan:
    def __init__(self):
        self.jobs = []

    def add(self, time, job):
        self.jobs.append((time, len(self.jobs), job))
        self.jobs.sort(key=lambda j: j[:2])

    def due(self, time):
        out = [j[2] for j in self.jobs if j[0] <= time]
        self.jobs = [j for j in self.jobs if j[0] > time]
        return out

    def beside(self, step, times):
        for t, time in enumerate(times):
            jobs = self.due(time)
            if jobs:

                @pl.when(step == t)
                def _():
                    for job in jobs:
                        job()


def back_kernel(
    n,
    lens,
    act,
    dout,
    nrm,
    dinn,
    dattn,
    ctx,
    cr,
    xall,
    q_in,
    k_in,
    v_in,
    lse_in,
    dco,
    dfirst,
    w_in,
    acc,
    act_s,
    dout_s,
    dinn_s,
    nrm_s,
    dattn_s,
    dcs_s,
    cs,
    o_igl,
    o_igr,
    o_i,
    o_u,
    o_o,
    o_q,
    o_k,
    o_v,
    o_vec,
    ig_s,
    Q,
    K,
    V,
    CX,
    G,
    LSE,
    L,
    D,
    DO,
    DA,
    CO,
    W,
    PI,
    PU,
    PO,
    PQ,
    RYI,
    RZI,
    MI,
    RXI,
    RXU,
    RYU,
    RZU,
    MU,
    RYO,
    RZO,
    MO,
    RXO,
    PH,
    RYH,
    RZH,
    MH,
    RXH,
    RYQ,
    RZQ,
    MQ,
    RXQ,
    VS,
    VR,
    SB,
    IB,
    XS,
    lsem,
    ssem,
    rsem,
):
    C, f = lax.axis_index("ctx"), lax.axis_index("fsdp")
    x, core = C // 2, C % 2
    A = n // 2
    slots, sh, part, hw = Q.shape
    rows, width = nrm.shape
    ff = act.shape[1]
    rs, ro, cq, wq = width // n, ff // n, ff // 4, width // 4
    half_rows = rows // 2
    CORE, NEAR, Y = (1, 0), (2, 0), (0, 1)

    def device(dc, df):
        return (flip(C, dc), flip(f, df))

    partners = [(0, 2 * k) for k in range(1, A)] + [Y, NEAR, CORE]
    barrier = pltpu.get_barrier_semaphore()
    for p in partners:
        pl.semaphore_signal(barrier, inc=1, device_id=device(*p), device_id_type=MESH)

    locals_free = iter(range(lsem.shape[0]))
    remotes_free = iter(range(ssem.shape[0]))

    def local(make):
        sem = next(locals_free)
        return lambda: pltpu.make_async_copy(*make(), lsem.at[sem])

    def remote_at(dev, sem, make):
        source, target = make()
        return pltpu.make_async_remote_copy(
            src_ref=source,
            dst_ref=target,
            send_sem=ssem.at[sem],
            recv_sem=rsem.at[sem],
            device_id=device(*dev),
            device_id_type=MESH,
        )

    def remote(dev, make):
        sem = next(remotes_free)
        return lambda: remote_at(dev, sem, make)

    ends = []

    def go(build):
        build().start()
        ends.append(lambda: build().wait_send())

    def go_local(make):
        build = local(make)
        build().start()
        ends.append(lambda: build().wait())

    loads = {}

    def load(name, make):
        loads[name] = local(make)
        loads[name]().start()

    def need(*names):
        for name in names:
            loads.pop(name)().wait()

    def quarters(ref, size, ex):
        return ref.at[:, at(flip(C, 2 * ex), size)]

    def load_dinn(ex):
        load(("dinn", ex), lambda: (quarters(dinn, cq, ex), D.at[ex, 0]))
        load(("dinn_s", ex), lambda: (dinn_s.at[ex], D.at[ex, 1]))

    load("nrm", lambda: (nrm, L.at[0]))
    load("nrm_s", lambda: (nrm_s, L.at[1]))
    load_dinn(0)
    pl.semaphore_wait(barrier, len(partners))
    need("nrm", "nrm_s", ("dinn", 0), ("dinn_s", 0))
    load_dinn(1)
    for ex in range(2):
        lanes = pl.ds(ex * wq, wq)
        load(("dout", ex), lambda ex=ex, lanes=lanes: (quarters(dout, wq, ex), DO.at[0, :, lanes]))
        load(
            ("dattn", ex), lambda ex=ex, lanes=lanes: (quarters(dattn, wq, ex), DA.at[0, :, lanes])
        )
    load("dout_s", lambda: (dout_s, DO.at[1]))
    load("dattn_s", lambda: (dattn_s, DA.at[1]))
    load("co", lambda: (cr, CO.at[0]))
    load("co_s", lambda: (cs, CO.at[1]))
    load("c", lambda: (ctx, CX))
    load("q", lambda: (q_in, Q))
    load("k", lambda: (k_in, K))
    load("v", lambda: (v_in, V))
    load("g", lambda: (dco, G.at[pl.ds(0, 2)]))
    load("g_s", lambda: (dcs_s, G.at[pl.ds(2, 2)]))
    for s in range(2):
        load(("lse", s), lambda s=s: (lse_in.at[s], LSE.at[s]))
    load("vec", lambda: (acc, VS.at[0]))
    load("w", lambda: (w_in, W))

    chunks = ff // 1024
    per = 1024 // ro

    def act_cols(t):
        return at(xor(f // per, t, chunks), 1024)

    class Unit:
        def __init__(self, P, RY, RZ, M, merged=False):
            self.P, self.RY, self.RZ, self.M, self.merged = P, RY, RZ, M, merged
            self.left, self.then = 1 if merged else A, []
            self.all_y = remote(Y, lambda: (P.at[1], RY)) if merged else None
            self.y = [
                remote(Y, lambda a=a: (P.at[1, a], RY.at[a])) for a in range(0 if merged else A)
            ]
            self.z = [None] + [
                remote((0, 2 * a), lambda a=a: (P.at[0, a], RZ.at[a - 1])) for a in range(1, A)
            ]

        def start_y(self, a=None):
            if self.merged:
                queue.append((self, None))
            else:
                queue.extend((self, i) for i in (order if a is None else [a]))
            pump()

        def fold_y(self, a):
            (self.all_y if self.merged else self.y[a])().wait_recv()
            for i in order if self.merged else [a]:
                self.P[0, i] = plus(self.P[0, i], self.RY[i])
                if i:
                    go(self.z[i])
            self.left -= 1

        def fold_z(self):
            for a in range(1, A):
                self.z[a]().wait_recv()
            self.M[...] = plus(self.P[0, 0], *[self.RZ[a - 1] for a in range(1, A)])

    order = list(range(1, A)) + [0]
    queue, flying, later = [], [], []

    def pump():
        while queue and len(flying) < WINDOW:
            unit, a = queue.pop(0)
            go(unit.all_y if unit.merged else unit.y[a])
            flying.append((unit, a))

    def fold_next():
        if flying:
            unit, a = flying.pop(0)
            pump()
            unit.fold_y(a)
            if not unit.left:
                later.extend((3 * t + 2, job) for t, job in enumerate(unit.then))
        now = [job for t, job in later if t <= 0]
        later[:] = [(t - 1, job) for t, job in later if t > 0]
        for job in now:
            job()

    UI = [Unit(PI.at[ex], RYI.at[ex], RZI.at[ex], MI.at[ex]) for ex in range(2)]
    UU = Unit(PU.at[0], RYU, RZU, MU)
    UO = Unit(PO.at[0], RYO, RZO, MO, merged=True)
    UH = Unit(PH.at[0], RYH, RZH, MH, merged=True)
    UQ = [None] + [Unit(PQ.at[j], RYQ.at[j], RZQ.at[j], MQ.at[j]) for j in range(2)]
    plan = Plan()

    xi = [remote(NEAR, lambda ex=ex: (MI.at[ex], RXI.at[ex])) for ex in range(2)]

    def inner_z(ex):
        UI[ex].fold_z()
        go(xi[ex])

    def cols_of(ref, e, size):
        return ref.at[:, at(flip(C, e), size)]

    i_core = [
        remote(CORE, lambda ex=ex: (RXI.at[1 - ex], cols_of(o_i, 2 * ex, cq))) for ex in range(2)
    ]

    def inner_x():
        for ex in range(2):
            xi[1 - ex]().wait_recv()
            RXI[1 - ex] = plus(MI[ex], RXI[1 - ex])
            go(i_core[ex])
            go_local(lambda ex=ex: (RXI.at[1 - ex], cols_of(o_i, 2 * ex, cq)))

    x_base = [next(remotes_free) for _ in range(n)][0]

    def outer_copy(i):
        return remote_at(NEAR, x_base + i, lambda: (PU.at[1, i % 2, i // 2], RXU.at[i % 2, i // 2]))

    def outer_x(i):
        outer_copy(i).wait_recv()
        PU[0, i % 2, i // 2] = plus(PU[0, i % 2, i // 2], RXU[i % 2, i // 2])
        if i % 2:
            UU.start_y(i // 2)

    class Finish:
        def __init__(self, unit, M, place):
            self.unit, self.M, self.place = unit, M, place
            self.near = remote(NEAR, lambda: (M, place(0)))
            self.core = remote(CORE, lambda: (M, place(0)))
            self.core2 = remote(CORE, lambda: (place(2), place(2)))

        def first(self):
            self.unit.fold_z()
            go(self.near)
            go(self.core)
            go_local(lambda: (self.M, self.place(0)))

        def second(self):
            self.near().wait_recv()
            go(self.core2)

    FU = Finish(UU, MU, lambda e: cols_of(o_u, e, wq))
    FO = Finish(UO, MO, lambda e: cols_of(o_o, e, wq))

    def query_place(e):
        to = flip(C, e)
        return o_q.at[at(to // 2, rs // 2), at(to % 2, hw)]

    FH = Finish(UH, MH, query_place)

    xo = remote(NEAR, lambda: (PO.at[1], RXO))
    xh = remote(NEAR, lambda: (PH.at[1], RXH))

    def fold_near(build, P, R, unit):
        build().wait_recv()
        for ib in (1, 0):
            for ia in range(A):
                P[0, ib, ia] = plus(P[0, ib, ia], R[ib, ia])
            if ib:
                unit.start_y()

    outs = (o_k, o_v)
    xq = [remote(NEAR, lambda j=j: (MQ.at[j], RXQ.at[j])) for j in range(2)]
    q_core = [
        remote(CORE, lambda j=j: (RXQ.at[j], outs[j].at[:, at(core, hw)])) for j in range(2)
    ]

    def proj_z(j):
        UQ[j + 1].fold_z()
        go(xq[j])

    def proj_x(j):
        xq[j]().wait_recv()
        RXQ[j] = plus(MQ[j], RXQ[j])
        go(q_core[j])
        go_local(lambda: (RXQ.at[j], outs[j].at[:, at(core, hw)]))

    hops = [CORE, NEAR] + [(0, 1 << b) for b in range(n.bit_length() - 1)]
    hop_copies = [
        remote(dev, lambda t=t: (VS.at[t], VR.at[t])) for t, dev in enumerate(hops)
    ]

    def vector_hop(t):
        if t:
            hop_copies[t - 1]().wait_recv()
            VS[t] = VS[t - 1] + VR[t - 1]
        if t < len(hops):
            go(hop_copies[t])
        else:
            go_local(lambda: (VS.at[t], o_vec))

    pairs = hw // (2 * HD)

    def attention(s, times):
        need(("lse", s))

        def body(step, carry):
            cols = at(step, 2 * HD)

            def get(ref):
                return ref[:, s, :, cols].reshape(slots * part, 2 * HD)

            mask = key_mask(lens[x * sh + s], C, part)
            dq, dk, dv = attend_back_pair(
                get(Q), get(K), get(V), mask, LSE[s % 2, :, cols], get(CX), get(G)
            )
            for ref, value in ((Q, dq), (K, dk), (V, dv)):
                ref[:, s, :, cols] = value.reshape(slots, part, 2 * HD)
            plan.beside(step, times)
            return carry

        lax.fori_loop(0, pairs, body, 0)
        if s + 2 < sh:
            load(("lse", s + 2), lambda: (lse_in.at[s + 2], LSE.at[s % 2]))

    groups = width // 256
    gsz = 256 // rs

    def weight_grad(get, put, times, unit=None):
        def body(step, carry):
            a = (step + 1) % groups
            cols = at(xor(f // gsz, a, groups), 256)
            r = (dot_tn(L[0, :, cols], get(0)) + dot_tn(L[1, :, cols], get(1))).astype(BF)
            for u in range(gsz):
                i = a * gsz + flip(f % gsz, u)
                put(i, r[u * rs : (u + 1) * rs])
            if unit is not None and groups == A:
                for t in range(groups):

                    @pl.when(step == t)
                    def _():
                        unit.start_y((t + 1) % groups)

            plan.beside(step, times)
            return carry

        lax.fori_loop(0, groups, body, 0)
        if unit is not None and groups != A:
            unit.start_y()

    def into(P):
        def put(i, value):
            P[i % 2, i // 2] = value

        return put

    def put_query(i, value):
        for h in range(2):
            PH[(h + x) % 2, i % 2, i // 2] = value[h * (rs // 2) : (h + 1) * (rs // 2)]

    def spaced(first, last, count):
        return [first + (last - first) * (t + 1) / count for t in range(count)]

    UI[0].then = [lambda: inner_z(0)]
    UI[1].then = [lambda: inner_z(1), inner_x]
    UU.then = [FU.first, FU.second]
    UO.then = [FO.first, FO.second]
    UH.then = [FH.first, FH.second]
    for j in range(2):
        UQ[j + 1].then = [lambda j=j: proj_z(j), lambda j=j: proj_x(j)]

    xs_order = list(range(1, n, 2)) + list(range(0, n, 2))
    for k, i in enumerate(xs_order):
        if k < n // 2:
            plan.add(11 + 14 * (per * (i // per) + per - 1 - i % per + 1) / n, lambda i=i: outer_copy(i).start())
        follow = xs_order[k + n // 2] if k < n // 2 else None

        def fold_x(i=i, follow=follow):
            if follow is not None:
                outer_copy(follow).start()
            outer_x(i)

        plan.add(20 + 48 * k / n, fold_x)
    for k in range(13 * A):
        plan.add(14 + 18 * k / A, fold_next)
    for t in range(len(hops) + 1):
        plan.add(74 + 4 * t, lambda t=t: vector_hop(t))

    weight_grad(lambda m: D[0, m], into(PI.at[0]), spaced(4, 8, groups), UI[0])

    def act_load(t):
        slot = t % 2
        return [
            pltpu.make_async_copy(act.at[:, act_cols(t)], D.at[slot, 0], lsem.at[act_sem + 2 * slot]),
            pltpu.make_async_copy(
                act_s.at[:, act_cols(t)], D.at[slot, 1], lsem.at[act_sem + 2 * slot + 1]
            ),
        ]

    act_sem = [next(locals_free) for _ in range(4)][0]

    def begin_act(t):
        for c in act_load(t):
            c.start()

    begin_act(0)
    need(("dinn", 1), ("dinn_s", 1))
    weight_grad(lambda m: D[1, m], into(PI.at[1]), spaced(8, 11, groups), UI[1])
    if chunks > 1:
        begin_act(1)
    load("x0", lambda: (xall.at[pl.ds(0, rows)], L.at[0]))
    load("x1", lambda: (xall.at[pl.ds(rows, rows)], L.at[1]))
    need(("dout", 0), ("dout", 1), "dout_s")

    outer_times = spaced(11, 25, n)

    def outer_body(u, carry):
        t, il = u // per, per - 1 - u % per
        slot = t % 2

        @pl.when(u % per == 0)
        def _():
            for c in act_load(t):
                c.wait()

        cols = at(xor(f % per, il, per), ro)
        r = dot_tn(D[slot, 0, :, cols], DO[0]) + dot_tn(D[slot, 1, :, cols], DO[1])
        r = r.astype(BF)
        i = t * per + il
        for ex in range(2):
            PU[ex, i % 2, i // 2] = r[:, ex * wq : (ex + 1) * wq]

        @pl.when((u % per == per - 1) & (t + 2 < chunks))
        def _():
            begin_act(t + 2)

        plan.beside(u, outer_times)
        return carry

    lax.fori_loop(0, n, outer_body, 0)

    need("co", "co_s", "c", ("dattn", 0), ("dattn", 1), "dattn_s")
    for half in range(2):
        for g in range(hw // 256):
            lanes = slice(g * 256, (g + 1) * 256)

            def left(m):
                if half:
                    return CO[m, :, lanes]
                return CX[2 * m : 2 * m + 2, :, :, lanes].reshape(rows, 256)

            r = (dot_tn(left(0), DA[0]) + dot_tn(left(1), DA[1])).astype(BF)
            group = (core + half * (1 - 2 * core)) * (hw // 256) + g
            for u in range(gsz):
                i = xor(group * gsz + u, f, n)
                for ex in range(2):
                    PO[ex, i % 2, i // 2] = r[u * rs : (u + 1) * rs, ex * wq : (ex + 1) * wq]
        for job in plan.due(27 + 3 * half):
            job()
    go(xo)
    plan.add(64, lambda: fold_near(xo, PO, RXO, UO))

    need("q", "k", "v", "g", "g_s")
    for s in range(sh):
        attention(s, spaced(30 + 8 * s, 38 + 8 * s, pairs))

    need("x0", "x1", "vec")
    for j, ref in enumerate((Q, K, V)):

        def right(m):
            return ref[2 * m : 2 * m + 2].reshape(rows, hw)

        if j != 1:
            total = jnp.sum(right(0).astype(F32), 0, keepdims=True)
            total = total + jnp.sum(right(1).astype(F32), 0, keepdims=True)
            VS[0, j // 2 : j // 2 + 1, at(core, hw)] = total
        times = spaced(54 + 6 * j, 60 + 6 * j, groups)
        if j:
            weight_grad(right, into(PQ.at[j - 1]), times, UQ[j])
        else:
            weight_grad(right, put_query, times)
            go(xh)
            plan.add(76, lambda: fold_near(xh, PH, RXH, UH))

    need("w")

    def project(slot):
        out = None
        for j, ref in enumerate((Q, K, V)):
            p = dot_nt(ref[slot].reshape(half_rows, hw), W[j])
            out = p if out is None else out + p
        return out

    ig_swap = [remote(CORE, lambda ex=ex: (SB, ig_s.at[ex])) for ex in range(2)]
    for ex in (1, 0):
        value = project(2 + ex)
        if ex == 0:
            ig_swap[1]().wait_send()
        SB[...] = value
        ig_swap[ex]().start()
        for job in plan.due(80 - 4 * ex):
            job()

    def rows_of(ex):
        return pl.ds(ex * half_rows, half_rows)

    ig_near = remote(NEAR, lambda: (XS, o_igr))
    for ex in (1, 0):
        ig_swap[ex]().wait_recv()
        load(("ig", ex), lambda ex=ex: (ig_s.at[ex], IB))
        value = project(ex)
        if ex:
            ig_swap[0]().wait_send()
        load(("df", ex), lambda ex=ex: (dfirst.at[rows_of(ex)], SB))
        need(("ig", ex), ("df", ex))
        value = value + IB[...] + SB[...]
        if ex:
            XS[...] = value.astype(BF)
            go(ig_near)
        else:
            IB[...] = value
            go_local(lambda: (IB, o_igl))
        for job in plan.due(88 - 4 * ex):
            job()

    for job in plan.due(1e9):
        job()
    while queue or flying or later:
        fold_next()

    ig_near().wait_recv()
    for build in i_core + q_core + [b for F in (FU, FO, FH) for b in (F.core, F.core2)]:
        build().wait_recv()
    for i in range(n):
        outer_copy(i).wait_send()
    for end in ends:
        end()


def back_call(lens, n, act, dout, nrm, dinn, dattn, ctx, cr, xall, q, k, v, lse, *rest):
    rows, width = nrm.shape
    ff = act.shape[1]
    slots, sh, part, hw = q.shape
    A = n // 2
    rs, ro, cq, wq = width // n, ff // n, ff // 4, width // 4
    hops = 2 + n.bit_length() - 1

    def bf(*shape):
        return jax.ShapeDtypeStruct(shape, BF)

    def f32(*shape):
        return jax.ShapeDtypeStruct(shape, F32)

    def vm(*shape):
        return pltpu.VMEM(shape, BF)

    def vf(*shape):
        return pltpu.VMEM(shape, F32)

    four = (slots, sh, part, hw)
    return pl.pallas_call(
        functools.partial(back_kernel, n),
        in_specs=[pl.BlockSpec(memory_space=pltpu.SMEM)] + [ANY] * 23,
        out_specs=[ANY] * 10,
        out_shape=[
            f32(rows // 2, width),
            bf(rows // 2, width),
            bf(rs, ff),
            bf(ro, width),
            bf(rs, width),
            bf(rs, width),
            bf(rs, width),
            bf(rs, width),
            f32(16, width),
            f32(2, rows // 2, width),
        ],
        scratch_shapes=[
            vm(*four),
            vm(*four),
            vm(*four),
            vm(*four),
            vm(*four),
            vf(2, *lse.shape[1:]),
            vm(2, rows, width),
            vm(2, 2, rows, 1024),
            vm(2, rows, 2 * wq),
            vm(2, rows, 2 * wq),
            vm(2, rows, hw),
            vm(3, width, hw),
            vm(2, 2, A, rs, cq),
            vm(2, 2, A, ro, wq),
            vm(2, 2, A, rs, wq),
            vm(2, 2, A, rs, hw),
            vm(2, A, rs, cq),
            vm(2, A - 1, rs, cq),
            vm(2, rs, cq),
            vm(2, rs, cq),
            vm(2, A, ro, wq),
            vm(A, ro, wq),
            vm(A - 1, ro, wq),
            vm(ro, wq),
            vm(A, rs, wq),
            vm(A - 1, rs, wq),
            vm(rs, wq),
            vm(2, A, rs, wq),
            vm(2, 2, A, rs // 2, hw),
            vm(A, rs // 2, hw),
            vm(A - 1, rs // 2, hw),
            vm(rs // 2, hw),
            vm(2, A, rs // 2, hw),
            vm(2, A, rs, hw),
            vm(2, A - 1, rs, hw),
            vm(2, rs, hw),
            vm(2, rs, hw),
            vf(hops + 1, 16, width),
            vf(hops, 16, width),
            vf(rows // 2, width),
            vf(rows // 2, width),
            vm(rows // 2, width),
            pltpu.SemaphoreType.DMA((48,)),
            pltpu.SemaphoreType.DMA((64 + 8 * n,)),
            pltpu.SemaphoreType.DMA((64 + 8 * n,)),
        ],
        compiler_params=pltpu.CompilerParams(
            vmem_limit_bytes=BACK_LIMIT, collective_id=1, has_side_effects=True
        ),
        name="back",
    )(
        lens,
        act,
        dout,
        nrm,
        dinn,
        dattn,
        ctx,
        cr,
        xall,
        q,
        k,
        v,
        lse,
        *rest,
    )


def finish_kernel(here, near, lo, *refs):
    o_ig, o_lo = refs[6:8]
    x = lax.axis_index("ctx") // 2
    o_ig[x] = here[...]
    o_ig[1 - x] = near[...].astype(F32)
    o_lo[...] = lo[...]
    for source, target in zip(refs[:6], refs[8:]):
        target[...] = source[...].astype(F32)


def finish_call(here, near, lo, *grads):
    rows, width = here.shape
    steps = 2

    def by(a):
        return pl.BlockSpec((a.shape[0] // steps, a.shape[1]), lambda i: (i, 0))

    return pl.pallas_call(
        finish_kernel,
        grid=(steps,),
        in_specs=[by(a) for a in (here, near, lo) + grads],
        out_specs=[pl.BlockSpec((2, rows // steps, width), lambda i: (0, i, 0)), by(lo)]
        + [by(g) for g in grads],
        out_shape=[jax.ShapeDtypeStruct((2, rows, width), F32), jax.ShapeDtypeStruct(lo.shape, BF)]
        + [jax.ShapeDtypeStruct(g.shape, F32) for g in grads],
        compiler_params=params(),
        name="finish",
    )(here, near, lo, *grads)


def per_device(
    inputs,
    lengths,
    cotangent,
    query_weight,
    key_weight,
    value_weight,
    out_weight,
    inner_weight,
    outer_weight,
    query_bias,
    value_bias,
    out_bias,
    inner_bias,
    outer_bias,
    first_gain,
    first_shift,
    second_gain,
    second_shift,
):
    C = lax.axis_index("ctx")
    f = lax.axis_index("fsdp")
    n = lax.axis_size("fsdp")
    x, core = C // 2, C % 2
    seqs, part, width = inputs.shape
    ff = inner_weight.shape[1]
    sh = seqs // 2
    rows = 2 * sh * part
    rs, ro = width // n, ff // n
    hw = width // 2

    def pick(bit, a, b):
        return jnp.where(bit == 0, a, b), jnp.where(bit == 0, b, a)

    vectors = (
        query_bias,
        value_bias,
        out_bias,
        outer_bias,
        first_gain,
        first_shift,
        second_gain,
        second_shift,
    )
    vecs = jnp.concatenate([v.reshape(1, rs) for v in vectors], 0)
    if rs < 128:
        vecs = jnp.pad(vecs, ((0, 0), (0, 128 - rs)))
    vecs = jnp.concatenate(
        [vecs, inner_bias.reshape(ro // 128, 128), jnp.zeros((PACK - 8 - ro // 128, 128), BF)], 0
    )
    x4, cot, w_qkv, wi, wu, wo, vecs, q4, k4, v4, c4, c_r, c_s, lse, *norm = front_call(
        lengths,
        inputs,
        cotangent,
        query_weight,
        key_weight,
        value_weight,
        vecs,
        out_weight,
        inner_weight,
        outer_weight,
        n,
    )
    xall = x4.reshape(2 * rows, width)
    cr = c_r.reshape(rows, hw)
    norm = [a.reshape(rows, a.shape[2]) for a in norm]
    two = (2, sh, part, hw)
    (
        dfirst,
        dco,
        acc,
        dout,
        dinn,
        dattn,
        layer_out,
        act_s,
        dout_s,
        dinn_s,
        nrm_s,
        dattn_s,
        dcs_s,
    ) = ffn_call(lengths, sh, *norm, cot.reshape(rows, width), vecs, wo, wi, wu)
    act, nrm = norm[0], norm[4]

    ig_here, ig_near, g_i, g_u, g_o, g_q, g_k, g_v, sums, _ = back_call(
        lengths,
        n,
        act,
        dout,
        nrm,
        dinn,
        dattn,
        c4,
        cr,
        xall,
        q4,
        k4,
        v4,
        lse,
        dco.reshape(two),
        dfirst,
        w_qkv,
        acc,
        act_s,
        dout_s,
        dinn_s,
        nrm_s,
        dattn_s,
        dcs_s.reshape(two),
        c_s.reshape(rows, hw),
    )
    own = lax.dynamic_slice_in_dim(sums[:8], f * rs, rs, 1)
    own_inner = lax.dynamic_slice_in_dim(sums[8 : 8 + ff // width].reshape(ff), f * ro, ro, 0)
    input_grad, layer_out, *grads = finish_call(
        ig_here, ig_near, layer_out.reshape(seqs * part, width), g_q, g_k, g_v, g_o, g_i, g_u
    )
    grad_query, grad_key, grad_value, grad_out, grad_inner, grad_outer = grads
    input_grad, layer_out = input_grad.reshape(inputs.shape), layer_out.reshape(inputs.shape)

    return (
        layer_out,
        input_grad,
        grad_query,
        grad_key,
        grad_value,
        grad_out,
        grad_inner,
        grad_outer,
        own[0],
        own[1],
        own[2],
        own_inner,
        own[3],
        own[4],
        own[5],
        own[6],
        own[7],
    )


def solution(mesh):
    rowed = P("fsdp", "ctx", None)
    matrix, vector = P("fsdp", None), P("fsdp")
    in_specs = (rowed, vector, rowed) + (matrix,) * 6 + (vector,) * 9
    out_specs = (rowed, rowed) + (matrix,) * 6 + (vector,) * 9
    return jax.shard_map(
        per_device, mesh=mesh, in_specs=in_specs, out_specs=out_specs, check_vma=False
    )
```

```python
import functools

import jax
import jax.numpy as jnp
from jax import lax
from jax.experimental import pallas as pl
from jax.experimental.pallas import tpu as pltpu
from jax.sharding import PartitionSpec as P

HD = 64
EPSILON = 1e-05
BF = jnp.bfloat16
F32 = jnp.float32
ANY = pl.BlockSpec(memory_space=pl.ANY)
NT = (((1,), (1,)), ((), ()))
TN = (((0,), (0,)), ((), ()))
VMEM_LIMIT = 58 << 20
BACK_LIMIT = 60 << 20
WINDOW = 2


def dot(a, b):
    return jnp.dot(a, b, preferred_element_type=F32)


def dot_nt(a, b):
    return lax.dot_general(a, b, NT, preferred_element_type=F32)


def dot_tn(a, b):
    return lax.dot_general(a, b, TN, preferred_element_type=F32)


def params(**more):
    return pltpu.CompilerParams(vmem_limit_bytes=VMEM_LIMIT, **more)


def cost(flops, size, trans=0):
    return pl.CostEstimate(flops=int(flops), bytes_accessed=int(size), transcendentals=int(trans))


MESH = pl.DeviceIdType.MESH
PACK = 16


def flip(v, mask):
    out, bit = v, 1
    while bit <= mask:
        if mask & bit:
            out = out + bit - 2 * bit * ((v // bit) % 2)
        bit *= 2
    return out


def at(index, size):
    return pl.ds(pl.multiple_of(index * size, size), size)


def spread(read, n, rs):
    per = max(128 // rs, 1)
    tiles = []
    for t in range(n // per):
        tile = read(t * per)
        for u in range(1, per):
            tile = tile + pltpu.roll(read(t * per + u), u * rs, 1)
        tiles.append(tile)
    return jnp.concatenate(tiles, 1)


def front_kernel(
    n,
    lens,
    xin,
    cin,
    wq,
    wk,
    wv,
    vecs,
    wo_in,
    wi_in,
    wu_in,
    xo,
    co,
    wqkvo,
    wio,
    wuo,
    woo,
    veco,
    qo,
    ko,
    vo,
    cxo,
    cro,
    cso,
    lseo,
    acto,
    gpo,
    hato,
    ro_o,
    nrmo,
    X,
    W,
    VEC,
    Q,
    K,
    V,
    CX,
    LSE,
    WO,
    WI,
    CR,
    VB,
    IB,
    HAT,
    R1,
    NRM,
    ACT,
    GP,
    lsem,
    ssem,
    rsem,
):
    C, f = lax.axis_index("ctx"), lax.axis_index("fsdp")
    x, core = C // 2, C % 2
    A = n // 2
    sh, part, width = X.shape[1:]
    hw = W.shape[2]
    ff = wio.shape[1]
    rs, ro, cq = width // n, ff // n, ff // 4

    partners = [(0, 2 * k) for k in range(1, A)] + [(0, 1), (2, 0), (1, 0)]

    def device(dc, df):
        return (flip(C, dc), flip(f, df))

    barrier = pltpu.get_barrier_semaphore()
    for p in partners:
        pl.semaphore_signal(barrier, inc=1, device_id=device(*p), device_id_type=MESH)

    local = []
    used = iter(range(lsem.shape[0]))

    def begin(source, target):
        c = pltpu.make_async_copy(source, target, lsem.at[next(used)])
        c.start()
        return c

    def keep(source, target):
        local.append(begin(source, target))

    x_here = begin(xin.at[pl.ds(x * sh, sh)], X.at[0])
    w_here = [begin(w.at[:, at(core, hw)], W.at[j, at(f, rs)]) for j, w in enumerate((wq, wk, wv))]
    w_here.append(begin(vecs, VEC.at[f]))

    pl.semaphore_wait(barrier, len(partners))

    def remote(source, target, sem, dev):
        return pltpu.make_async_remote_copy(
            src_ref=source,
            dst_ref=target,
            send_sem=ssem.at[sem],
            recv_sem=rsem.at[sem],
            device_id=device(*dev),
            device_id_type=MESH,
        )

    sent = []

    def send(*what):
        c = remote(*what)
        c.start()
        sent.append(c)

    seen = set()

    def arrive(target, sem, dev):
        if sem not in seen:
            seen.add(sem)
            remote(target, target, sem, dev).wait_recv()

    X1, X2, X3, COT, CTX, CTX2 = range(6)
    send(xin.at[pl.ds((1 - x) * sh, sh)], X.at[1], X1, (2, 0))

    def rows_at(ref, first, size):
        return ref.at[pl.ds(pl.multiple_of(first, size), size)]

    hr, hu = rs // 2, ro // 2

    def projection(j):
        w = (wq, wk, wv)[j]
        return (
            1,
            lambda e, s: [W.at[j, at(s, rs)]] + [VEC.at[s]] * (j == 0),
            lambda: [w.at[:, at(core, hw)]] + [vecs] * (j == 0),
        )

    def inner_part(h):
        return (
            4,
            lambda e, s: [WI.at[at(s * 2 + h, hr), at(flip(C, e), cq)]],
            lambda: [wi_in.at[pl.ds(h * hr, hr), at(C, cq)]],
        )

    outer_a = (
        4,
        lambda e, s: [rows_at(wuo, s * ro + flip(C, e) * (hu // 4), hu // 4)],
        lambda: [rows_at(wu_in, C * (hu // 4), hu // 4)],
    )
    out_part = (
        4,
        lambda e, s: [rows_at(WO, s * rs + flip(C, e) * (rs // 4), rs // 4)],
        lambda: [rows_at(wo_in, C * (rs // 4), rs // 4)],
    )

    def outer_b(h):
        return (
            2,
            lambda e, s: [rows_at(wuo, s * ro + hu + (flip(core, e) * 2 + h) * (hu // 4), hu // 4)],
            lambda: [rows_at(wu_in, hu + (core * 2 + h) * (hu // 4), hu // 4)],
        )

    kinds = [
        out_part,
        inner_part(0),
        projection(0),
        projection(1),
        projection(2),
        inner_part(1),
        outer_a,
        outer_b(0),
        outer_b(1),
    ]
    sems, ready = {}, 6
    for k, (parts, place, _) in enumerate(kinds):
        for e in range(parts):
            for i in range(1, n):
                for u in range(2 if k == 2 else 1):
                    sems[k, e, i, u] = ready
                    ready += 1

    def route(parts, e, i):
        if e % 2:
            return (1, 0), (e - 1, i)
        if e:
            return (2, 0), (0, i)
        if i % 2:
            return (0, 1), (0, i - 1)
        return (0, i), (0, 0)

    def copies(k, e, i):
        parts, place, own = kinds[k]
        dev, (pe, pi) = route(parts, e, i)
        target = place(pe, flip(f, pi))
        source = target if pi else own()
        return [
            remote(source[u], target[u], sems[k, e, i, u], dev) for u in range(len(target))
        ]

    issued = []

    def give(k, e, i):
        for c in copies(k, e, i):
            c.start()
        issued.append((k, e, i))

    got = set()

    def take(k, e, i):
        if (k, e, i) in got:
            return
        got.add((k, e, i))
        parts, place, _ = kinds[k]
        dev, _ = route(parts, e, i)
        for u, target in enumerate(place(e, flip(f, i))):
            remote(target, target, sems[k, e, i, u], dev).wait_recv()

    def hand_on(k, i):
        parts = kinds[k][0]
        if parts == 4:
            give(k, 2, i)
        if parts > 1:
            give(k, 1, i)

    def base(k):
        if k < len(kinds):
            for a in range(A - 1, 0, -1):
                give(k, 0, 2 * a)
            give(k, 0, 1)

    def z_in(k):
        for a in range(1, A):
            take(k, 0, 2 * a)
            give(k, 0, 2 * a + 1)
            hand_on(k, 2 * a)

    def y_in(k):
        for i in range(1, n, 2):
            take(k, 0, i)
            hand_on(k, i)

    def x_in(k):
        if kinds[k][0] == 4:
            for i in range(1, n):
                take(k, 2, i)
                give(k, 3, i)

    base(0)
    base(1)
    x_here.wait()
    send(X.at[0], X.at[2], X2, (1, 0))
    keep(cin.at[pl.ds(x * sh, sh)], co.at[0])
    w_here += [begin(wo_in, WO.at[at(f, rs)]), begin(wi_in, WI.at[at(f, rs)])]
    keep(wu_in, wuo.at[at(f, ro)])
    slots = X.shape[0]
    pairs = hw // (2 * HD)

    z_in(0)
    base(2)
    arrive(X.at[1], X1, (2, 0))
    send(X.at[1], X.at[3], X3, (1, 0))
    z_in(1)
    base(3)
    y_in(0)
    arrive(X.at[2], X2, (1, 0))
    arrive(X.at[3], X3, (1, 0))
    keep(X, xo)
    for c in w_here:
        c.wait()
    z_in(2)
    base(4)
    y_in(1)
    send(cin.at[pl.ds((1 - x) * sh, sh)], co.at[1], COT, (2, 0))
    z_in(3)
    base(5)
    y_in(2)
    x_in(0)
    keep(VEC, veco)

    def bias(row):
        read = lambda s: VEC[pl.ds(core * (n // 2) + s, 1), row : row + 1, :128].reshape(1, 128).astype(F32)
        return spread(read, n // 2, rs)

    shape = (sh, part, hw)

    def project(j, target, add):
        def body(slot, carry):
            value = dot(X[slot].reshape(sh * part, width), W[j])
            if add is not None:
                value = value + add
            target[slot] = value.astype(BF).reshape(shape)
            return carry

        lax.fori_loop(0, slots, body, 0)

    project(0, Q, bias(0))
    z_in(4)
    base(6)
    y_in(3)
    project(1, K, None)
    x_in(1)
    z_in(5)
    base(7)
    y_in(4)
    keep(W, wqkvo)
    project(2, V, bias(1))
    keep(Q, qo)
    keep(K, ko)
    keep(V, vo)

    jobs = {7: [lambda: z_in(6), lambda: base(8)], 9: [lambda: y_in(5)]}
    steps = sh * pairs

    def attend(step, carry):
        s, pair = step // pairs, step % pairs
        cols = at(pair, 2 * HD)

        def load(ref):
            return ref[:, s, :, cols].reshape(slots * part, 2 * HD)

        q, k, v = load(Q), load(K), load(V)
        mask = key_mask(lens[x * sh + s], C, part)
        o, lse = attend_pair(q, k, v, mask)
        CX[:, s, :, cols] = o.reshape(slots, part, 2 * HD)
        LSE[s, :, cols] = lse
        for t in range(steps):
            now = jobs.get(t)
            if now:

                @pl.when(step == t)
                def _():
                    for job in now:
                        job()

        return carry

    lax.fori_loop(0, steps, attend, 0)
    send(CX.at[pl.ds(2, 2)], CR, CTX, (1, 0))
    send(CX.at[pl.ds(0, 2)], cso, CTX2, (1, 0))
    keep(CX, cxo)
    keep(LSE, lseo)
    for e in range(4):
        for i in range(1, n):
            take(0, e, i)
    keep(WO, woo)
    VB[...] = spread(lambda s: VEC[s, :8, :128].astype(F32), n, rs)
    for s in range(n):
        for t in range(ro // 128):
            first = s * ro + t * 128
            IB[:, first : first + 128] = VEC[s, 8 + t : 9 + t, :].astype(F32)
    arrive(CR, CTX, (1, 0))
    keep(CR, cro)
    own_half, other_half = at(core, hw), at(1 - core, hw)
    half = sh * part

    def norm(ex, carry):
        first = (
            X[ex].reshape(half, width).astype(F32)
            + (
                dot(CX[ex].reshape(half, hw), WO[own_half])
                + dot(CR[ex].reshape(half, hw), WO[other_half])
            )
            + VB[2:3, :]
        )
        hat, r = normalise(first)
        HAT[ex] = hat
        R1[ex] = jnp.broadcast_to(r, (half, 128))
        NRM[ex] = (hat * VB[4:5, :] + VB[5:6, :]).astype(BF)
        return carry

    lax.fori_loop(0, 2, norm, 0)
    keep(HAT, hato)
    keep(R1, ro_o)
    keep(NRM, nrmo)
    plan = [
        [lambda: z_in(7), lambda: y_in(6)],
        [lambda: x_in(5)],
        [lambda: z_in(8), lambda: y_in(7)],
        [lambda: x_in(6)],
    ]
    for e in range(4):
        for job in plan[e]:
            job()
        for k in (1, 5):
            for i in range(1, n):
                take(k, e, i)
        cols = at(flip(C, e), cq)

        def inner(ex, carry):
            g, d = gelu_pair(dot(NRM[ex], WI[:, cols]) + IB[:, cols])
            ACT[ex, :, cols] = g.astype(BF)
            GP[ex, :, cols] = d.astype(BF)
            return carry

        lax.fori_loop(0, 2, inner, 0)
        keep(ACT.at[:, :, cols], acto.at[:, :, cols])
        keep(GP.at[:, :, cols], gpo.at[:, :, cols])
    y_in(8)
    keep(WI, wio)
    for k, (parts, _, _) in enumerate(kinds):
        for e in range(parts):
            for i in range(1, n):
                take(k, e, i)
    arrive(co.at[1], COT, (2, 0))
    arrive(cso, CTX2, (1, 0))
    for what in issued:
        for c in copies(*what):
            c.wait_send()
    for c in sent:
        c.wait_send()
    for c in local:
        c.wait()


def front_call(lengths, xin, cin, wq, wk, wv, vecs, wo, wi, wu, n):
    seqs, part, width = xin.shape
    sh, ff, hw = seqs // 2, wi.shape[1], width // 2

    def bf(*shape):
        return jax.ShapeDtypeStruct(shape, BF)

    def vm(*shape):
        return pltpu.VMEM(shape, BF)

    full = 4 * part
    lse = (sh, full, hw)
    half = sh * part
    four = (4, sh, part, hw)
    sems = 24 * n
    return pl.pallas_call(
        functools.partial(front_kernel, n),
        in_specs=[pl.BlockSpec(memory_space=pltpu.SMEM)] + [ANY] * 9,
        out_specs=[ANY] * 19,
        out_shape=[
            bf(4, sh, part, width),
            bf(2, sh, part, width),
            bf(3, width, hw),
            bf(width, ff),
            bf(ff, width),
            bf(width, width),
            bf(n, PACK, 128),
            bf(*four),
            bf(*four),
            bf(*four),
            bf(*four),
            bf(2, sh, part, hw),
            bf(2, sh, part, hw),
            jax.ShapeDtypeStruct(lse, F32),
            bf(2, half, ff),
            bf(2, half, ff),
            jax.ShapeDtypeStruct((2, half, width), F32),
            jax.ShapeDtypeStruct((2, half, 128), F32),
            bf(2, half, width),
        ],
        scratch_shapes=[
            vm(4, sh, part, width),
            vm(3, width, hw),
            vm(n, PACK, 128),
            vm(*four),
            vm(*four),
            vm(*four),
            vm(*four),
            pltpu.VMEM(lse, F32),
            vm(width, width),
            vm(width, ff),
            vm(2, sh, part, hw),
            pltpu.VMEM((8, width), F32),
            pltpu.VMEM((1, ff), F32),
            pltpu.VMEM((2, half, width), F32),
            pltpu.VMEM((2, half, 128), F32),
            vm(2, half, width),
            vm(2, half, ff),
            vm(2, half, ff),
            pltpu.SemaphoreType.DMA((40,)),
            pltpu.SemaphoreType.DMA((sems,)),
            pltpu.SemaphoreType.DMA((sems,)),
        ],
        compiler_params=params(collective_id=0, has_side_effects=True),
        name="front",
    )(lengths, xin, cin, wq, wk, wv, vecs, wo, wi, wu)


def lanes_of(shape, head):
    lane = lax.broadcasted_iota(jnp.int32, shape, 1)
    own = (lane < HD) if head == 0 else (lane >= HD)
    return lane, own, (HD if head == 0 else 0)


def split3(a):
    hi = a.astype(BF).astype(F32)
    mid = (a - hi).astype(BF).astype(F32)
    return hi, mid, a - hi - mid


def flat(ref):
    a = ref[...]
    return a.reshape(-1, a.shape[-1])


def key_mask(length, C, part):
    row = lax.broadcasted_iota(jnp.int32, (part, 2 * HD), 0)
    out = []
    for e in (0, 2, 1, 3):
        inside = row + flip(C, e) * part < length
        out.append(jnp.where(inside, 0.0, -1e30).astype(BF))
    return jnp.concatenate(out, 0)


def attend_pair(q, k, v, mask):
    out = []
    for head in range(2):
        lane, own, other = lanes_of(q.shape, head)
        qh = jnp.where(own, q * BF(HD**-0.5), jnp.where(lane == other, 1.0, 0.0).astype(BF))
        kh = jnp.where(own, k, mask)
        s = dot_nt(qh, kh)
        top = jnp.max(s, -1, keepdims=True)
        e = jnp.exp(s - top)
        total = jnp.sum(e, -1, keepdims=True)
        o = dot(e.astype(BF), v) * (1.0 / total)
        out.append((o, top + jnp.log(total), own))
    (o0, l0, own), (o1, l1, _) = out
    return jnp.where(own, o0, o1).astype(BF), jnp.where(own, l1, l0)


def attend_back_pair(q, k, v, mask, lse, c, g):
    qs = q * BF(HD**-0.5)
    kt = k.T
    prod = c.astype(F32) * g.astype(F32)
    res = []
    for head in range(2):
        lane, own, o = lanes_of(q.shape, head)
        hi, mid, low = split3(-lse)
        extra = jnp.where(
            lane == o,
            1.0,
            jnp.where(
                lane == o + 1,
                hi,
                jnp.where(lane == o + 2, mid, jnp.where(lane == o + 3, low, 0.0)),
            ),
        ).astype(BF)
        qh = jnp.where(own, qs, extra)
        kh = jnp.where(own, k, jnp.where(lane == o, mask, BF(1)))
        p = jnp.exp(dot_nt(kh, qh))
        delta = jnp.sum(jnp.where(own, prod, 0.0), -1, keepdims=True)
        hi, mid, low = split3(-delta)
        extra = jnp.where(
            lane == o, hi, jnp.where(lane == o + 1, mid, jnp.where(lane == o + 2, low, 0.0))
        ).astype(BF)
        gh = jnp.where(own, g, extra)
        vh = jnp.where(own, v, BF(1))
        ds = (p * dot_nt(vh, gh)).astype(BF)
        dv = dot(p.astype(BF), g)
        dk = dot(ds, qs)
        dqt = dot(kt, ds)
        res.append((dv, dk, dqt, own))
    (dv0, dk0, dq0, own), (dv1, dk1, dq1, _) = res
    dqt = jnp.concatenate([dq0[:HD], dq1[HD:]], 0) * (HD**-0.5)
    return dqt.T.astype(BF), jnp.where(own, dk0, dk1).astype(BF), jnp.where(own, dv0, dv1).astype(BF)


def gelu_pair(u):
    e = jnp.exp(u * u * -0.5)
    t = 1.0 / (1.0 + (0.3275911 * 0.7071067811865476) * jnp.abs(u))
    poly = t * (
        0.254829592 * 0.5
        + t
        * (
            -0.284496736 * 0.5
            + t * (1.421413741 * 0.5 + t * (-1.453152027 * 0.5 + t * (1.061405429 * 0.5)))
        )
    )
    tail = poly * e
    cdf = jnp.where(u >= 0, 1.0 - tail, tail)
    ucdf = u * cdf
    return ucdf, cdf + u * (e * 0.3989422804014327)


def normalise(h):
    c = h - jnp.mean(h, -1, keepdims=True)
    r = lax.rsqrt(jnp.mean(c * c, -1, keepdims=True) + EPSILON)
    return c * r, r


def normalise_back(dyg, hat, r):
    return r * (
        dyg - jnp.mean(dyg, -1, keepdims=True) - hat * jnp.mean(dyg * hat, -1, keepdims=True)
    )


def ffn_kernel(
    n, sh, part, lens, act, gp, hat1_ref, r1_ref, cot, vecs, act_in, nrm_in, wo_in, wi_in, wu_in, *refs
):
    dfirst, dco, acc = refs[:3]
    homes, (o_lo, act_s, dout_s, dinn_s, nrm_s, dattn_s, dcs_s) = refs[3:6], refs[6:13]
    wo, wi, wu, vec, *twice, sem, csem, hsem, ssem, rsem = refs[13:]
    width, ff = wi.shape
    C, f = lax.axis_index("ctx"), lax.axis_index("fsdp")
    x, core = C // 2, C % 2
    step = pl.program_id(0)
    turn = 2 - step
    rs, ro = width // n, ff // n
    cq, hw = ff // 4, width // 2

    pairs = ((wo_in, wo), (wi_in, wi), (wu_in, wu))

    def copy(kind):
        return pltpu.make_async_copy(*pairs[kind], sem.at[kind])

    CORE, NEAR = flip(C, 1), flip(C, 2)
    block, wq = cot.shape[0], width // 4

    def remote(t, j, to, source, target):
        return pltpu.make_async_remote_copy(
            src_ref=source,
            dst_ref=target,
            send_sem=ssem.at[t, j],
            recv_sem=rsem.at[t, j],
            device_id=(to, f),
            device_id_type=MESH,
        )

    KINDS = ("dout0", "dout1", "dinn0", "dinn1", "dattn0", "dattn1", "dcs")

    def rows_of(t):
        return pl.ds(pl.multiple_of(t * block, block), block)

    def held(t):
        return [ref.at[(2 - t) % 2] for ref in twice]

    dout, dinn, dattn, dcs, lo = held(turn)
    HOME = {"dout": 0, "dinn": 1, "dattn": 2}

    def whole(t):
        pair = ((act_in, act_s), (nrm_in, nrm_s))[t]
        return remote(t, 7, CORE, *pair)

    def home(t, name):
        j = HOME[name]
        return pltpu.make_async_copy(held(t)[j], homes[j].at[rows_of(t)], hsem.at[t, j])

    def to_core(t, *names):
        out = []
        for name in names or KINDS:
            rows = rows_of(t)
            dout, dinn, dattn, dcs, _ = held(t)
            ex = int(name[-1]) if name[-1] in "01" else 0
            other, lanes = flip(C, 2 * ex + 1), pl.ds(ex * wq, wq)
            source, target = {
                "dcs": lambda: (dcs, dcs_s.at[rows]),
                "dou": lambda: (dout.at[:, at(other, wq)], dout_s.at[rows, lanes]),
                "dat": lambda: (dattn.at[:, at(other, wq)], dattn_s.at[rows, lanes]),
                "din": lambda: (dinn.at[:, at(other, cq)], dinn_s.at[ex, rows]),
            }[name[:3]]()
            out.append(remote(t, KINDS.index(name), CORE, source, target))
        return out

    def start(name):
        for c in to_core(turn, *(k for k in KINDS if k.startswith(name))):
            c.start()
        if name in HOME:
            home(turn, name).start()

    def end(t, name):
        for c in to_core(t, *(k for k in KINDS if k.startswith(name))):
            c.wait_send()
        if name in HOME:
            home(t, name).wait()

    def free(name):
        @pl.when(step == 2)
        def _():
            end(2, name)

    def slots_of(t, ex):
        count = block // part
        return [u for u in range(count) if (t * count + u) // sh == ex]

    def place(t, u):
        return held(t)[4].at[pl.ds(u * part, part)], o_lo.at[x * sh + (t * (block // part) + u) % sh]

    def to_near(t):
        return [remote(t, 8 + u, NEAR, *place(t, u)) for u in slots_of(t, 1)]

    def stay(t):
        return [pltpu.make_async_copy(*place(t, u), csem.at[t, u]) for u in slots_of(t, 0)]

    def send(t):
        for c in to_near(t) + stay(t):
            c.start()

    def sent(t):
        for c in to_near(t):
            c.wait_send()
        for c in stay(t):
            c.wait()

    def received(t):
        for c in to_core(t) + to_near(t):
            c.wait_recv()

    @pl.when(step == 0)
    def _():
        barrier = pltpu.get_barrier_semaphore()
        for to in (CORE, NEAR):
            pl.semaphore_signal(barrier, inc=1, device_id=(to, f), device_id_type=MESH)
        copy(2).start()
        pl.semaphore_wait(barrier, 2)
        acc[...] = jnp.zeros_like(acc)
        vec[...] = spread(lambda s: vecs[s, :8, :128].astype(F32), n, rs)

    def arrived(kind):
        @pl.when(step == 0)
        def _():
            copy(kind).wait()

    count = block // part
    inside = []
    for u in range(count):
        slot = turn * count + u
        ex, s = slot // sh, slot % sh
        first = (C + ex * (2 - 4 * x)) * part
        row = lax.broadcasted_iota(jnp.int32, (part, 1), 0) + first
        inside.append(jnp.where(row < lens[x * sh + s], 1.0, 0.0))
    valid = jnp.concatenate(inside, 0)
    own, other = at(core, hw), at(1 - core, hw)

    def add(row, value):
        acc[row : row + 1, :] += jnp.sum(value, 0, keepdims=True)

    hat1, r1 = hat1_ref[...], r1_ref[:, :1]
    normed = hat1 * vec[4:5, :] + vec[5:6, :]
    arrived(2)

    @pl.when(step == 0)
    def _():
        copy(1).start()
        copy(0).start()
        whole(1).start()
        whole(0).start()

    second = normed + (dot(act[...], wu[...]) + vec[3:4, :])
    hat2, r2 = normalise(second)
    @pl.when(step == 2)
    def _():
        sent(2)

    lo[...] = (hat2 * vec[6:7, :] + vec[7:8, :]).astype(BF)
    og = cot[...].astype(F32) * valid
    add(6, og * hat2)
    add(7, og)
    d2 = normalise_back(og * vec[6:7, :], hat2, r2)
    d2low = d2.astype(BF)
    free("dout")
    dout[...] = d2low
    start("dout")
    for t in range(3):

        @pl.when(turn == t)
        def _():
            send(t)

    add(3, d2low.astype(F32))
    free("dinn")
    arrived(1)
    for j in range(4):
        cols = slice(j * cq, (j + 1) * cq)
        di = (dot_nt(d2low, wu[cols, :]) * gp[:, cols]).astype(BF)
        dinn[:, cols] = di
        add(8 + j, di.astype(F32))
    start("dinn")
    dn = d2 + dot_nt(dinn[...], wi[...])
    add(4, dn * hat1)
    add(5, dn)
    d1 = normalise_back(dn * vec[4:5, :], hat1, r1)
    dfirst[...] = d1
    d1low = d1.astype(BF)
    arrived(0)
    free("dattn")
    free("dcs")
    dattn[...] = d1low
    start("dattn")
    add(2, d1low.astype(F32))
    dcs[...] = dot_nt(d1low, wo[other]).astype(BF)
    start("dcs")
    dco[...] = dot_nt(d1low, wo[own]).astype(BF)

    @pl.when(turn == 0)
    def _():
        for t in range(2):
            for name in ("dout", "dinn", "dattn", "dcs"):
                end(t, name)
            sent(t)
            whole(t).wait()
        for t in range(3):
            received(t)


def ffn_call(lens, sh, act, gp, hat, r, nrm, cot, vecs, wo, wi, wu):
    width, ff = wi.shape
    n, rows = vecs.shape[0], cot.shape[0]
    block, part = rows // 3, rows // (2 * sh)
    hw = width // 2

    def by(cols):
        return pl.BlockSpec((block, cols), lambda i: (2 - i, 0))

    def whole(*shape):
        return pl.BlockSpec(shape, lambda i: (0,) * len(shape))

    grid_spec = pl.GridSpec(
        grid=(3,),
        in_specs=[
            pl.BlockSpec(memory_space=pltpu.SMEM),
            by(ff),
            by(ff),
            by(width),
            by(128),
            by(width),
            whole(*vecs.shape),
        ]
        + [ANY] * 5,
        out_specs=[by(width), by(hw), whole(16, width)] + [ANY] * 10,
        scratch_shapes=[
            pltpu.VMEM((width, width), BF),
            pltpu.VMEM((width, ff), BF),
            pltpu.VMEM((ff, width), BF),
            pltpu.VMEM((8, width), F32),
            *(pltpu.VMEM((2, block, cols), BF) for cols in (width, ff, width, hw, width)),
            pltpu.SemaphoreType.DMA((3,)),
            pltpu.SemaphoreType.DMA((3, block // part)),
            pltpu.SemaphoreType.DMA((3, 3)),
            pltpu.SemaphoreType.DMA((3, 8 + block // part)),
            pltpu.SemaphoreType.DMA((3, 8 + block // part)),
        ],
    )

    def shape(cols, dtype=BF):
        return jax.ShapeDtypeStruct((rows, cols), dtype)

    return pl.pallas_call(
        functools.partial(ffn_kernel, n, sh, part),
        grid_spec=grid_spec,
        out_shape=[
            shape(width, F32),
            shape(hw),
            jax.ShapeDtypeStruct((16, width), F32),
            shape(width),
            shape(ff),
            shape(width),
            jax.ShapeDtypeStruct((2 * sh, part, width), BF),
            shape(ff),
            shape(hw),
            jax.ShapeDtypeStruct((2, rows, ff // 4), BF),
            shape(width),
            shape(hw),
            shape(hw),
        ],
        compiler_params=params(collective_id=2, has_side_effects=True),
        cost_estimate=cost(
            2 * rows * width * (2 * width + 4 * ff), 30 * rows * width + 2 * width * (2 * ff + width)
        ),
        name="ffn",
    )(lens, act, gp, hat, r, cot, vecs, act, nrm, wo, wi, wu)


def xor(a, b, count):
    out, bit = 0, 1
    while bit < count:
        out = out + bit * ((a // bit + b // bit) % 2)
        bit *= 2
    return out


def plus(*items):
    out = items[0].astype(F32)
    for i in items[1:]:
        out = out + i.astype(F32)
    return out.astype(BF)


class Plan:
    def __init__(self):
        self.jobs = []

    def add(self, time, job):
        self.jobs.append((time, len(self.jobs), job))
        self.jobs.sort(key=lambda j: j[:2])

    def due(self, time):
        out = [j[2] for j in self.jobs if j[0] <= time]
        self.jobs = [j for j in self.jobs if j[0] > time]
        return out

    def beside(self, step, times):
        for t, time in enumerate(times):
            jobs = self.due(time)
            if jobs:

                @pl.when(step == t)
                def _():
                    for job in jobs:
                        job()


def back_kernel(
    n,
    lens,
    act,
    dout,
    nrm,
    dinn,
    dattn,
    ctx,
    cr,
    xall,
    q_in,
    k_in,
    v_in,
    lse_in,
    dco,
    dfirst,
    w_in,
    acc,
    act_s,
    dout_s,
    dinn_s,
    nrm_s,
    dattn_s,
    dcs_s,
    cs,
    o_igl,
    o_igr,
    o_i,
    o_u,
    o_o,
    o_q,
    o_k,
    o_v,
    o_vec,
    ig_s,
    Q,
    K,
    V,
    CX,
    G,
    LSE,
    L,
    D,
    DO,
    DA,
    CO,
    W,
    PI,
    PU,
    PO,
    PQ,
    RYI,
    RZI,
    MI,
    RXI,
    RXU,
    RYU,
    RZU,
    MU,
    RYO,
    RZO,
    MO,
    RXO,
    PH,
    RYH,
    RZH,
    MH,
    RXH,
    RYQ,
    RZQ,
    MQ,
    RXQ,
    VS,
    VR,
    SB,
    IB,
    XS,
    lsem,
    ssem,
    rsem,
):
    C, f = lax.axis_index("ctx"), lax.axis_index("fsdp")
    x, core = C // 2, C % 2
    A = n // 2
    slots, sh, part, hw = Q.shape
    rows, width = nrm.shape
    ff = act.shape[1]
    rs, ro, cq, wq = width // n, ff // n, ff // 4, width // 4
    half_rows = rows // 2
    CORE, NEAR, Y = (1, 0), (2, 0), (0, 1)

    def device(dc, df):
        return (flip(C, dc), flip(f, df))

    partners = [(0, 2 * k) for k in range(1, A)] + [Y, NEAR, CORE]
    barrier = pltpu.get_barrier_semaphore()
    for p in partners:
        pl.semaphore_signal(barrier, inc=1, device_id=device(*p), device_id_type=MESH)

    locals_free = iter(range(lsem.shape[0]))
    remotes_free = iter(range(ssem.shape[0]))

    def local(make):
        sem = next(locals_free)
        return lambda: pltpu.make_async_copy(*make(), lsem.at[sem])

    def remote_at(dev, sem, make):
        source, target = make()
        return pltpu.make_async_remote_copy(
            src_ref=source,
            dst_ref=target,
            send_sem=ssem.at[sem],
            recv_sem=rsem.at[sem],
            device_id=device(*dev),
            device_id_type=MESH,
        )

    def remote(dev, make):
        sem = next(remotes_free)
        return lambda: remote_at(dev, sem, make)

    ends = []

    def go(build):
        build().start()
        ends.append(lambda: build().wait_send())

    def go_local(make):
        build = local(make)
        build().start()
        ends.append(lambda: build().wait())

    loads = {}

    def load(name, make):
        loads[name] = local(make)
        loads[name]().start()

    def need(*names):
        for name in names:
            loads.pop(name)().wait()

    def quarters(ref, size, ex):
        return ref.at[:, at(flip(C, 2 * ex), size)]

    def load_dinn(ex):
        load(("dinn", ex), lambda: (quarters(dinn, cq, ex), D.at[ex, 0]))
        load(("dinn_s", ex), lambda: (dinn_s.at[ex], D.at[ex, 1]))

    load("nrm", lambda: (nrm, L.at[0]))
    load("nrm_s", lambda: (nrm_s, L.at[1]))
    load_dinn(0)
    pl.semaphore_wait(barrier, len(partners))
    need("nrm", "nrm_s", ("dinn", 0), ("dinn_s", 0))
    load_dinn(1)
    for ex in range(2):
        lanes = pl.ds(ex * wq, wq)
        load(("dout", ex), lambda ex=ex, lanes=lanes: (quarters(dout, wq, ex), DO.at[0, :, lanes]))
        load(
            ("dattn", ex), lambda ex=ex, lanes=lanes: (quarters(dattn, wq, ex), DA.at[0, :, lanes])
        )
    load("dout_s", lambda: (dout_s, DO.at[1]))
    load("dattn_s", lambda: (dattn_s, DA.at[1]))
    load("co", lambda: (cr, CO.at[0]))
    load("co_s", lambda: (cs, CO.at[1]))
    load("c", lambda: (ctx, CX))
    load("q", lambda: (q_in, Q))
    load("k", lambda: (k_in, K))
    load("v", lambda: (v_in, V))
    load("g", lambda: (dco, G.at[pl.ds(0, 2)]))
    load("g_s", lambda: (dcs_s, G.at[pl.ds(2, 2)]))
    for s in range(2):
        load(("lse", s), lambda s=s: (lse_in.at[s], LSE.at[s]))
    load("vec", lambda: (acc, VS.at[0]))
    load("w", lambda: (w_in, W))

    chunks = ff // 1024
    per = 1024 // ro

    def act_cols(t):
        return at(xor(f // per, t, chunks), 1024)

    class Unit:
        def __init__(self, P, RY, RZ, M, merged=False):
            self.P, self.RY, self.RZ, self.M, self.merged = P, RY, RZ, M, merged
            self.left, self.then = 1 if merged else A, []
            self.all_y = remote(Y, lambda: (P.at[1], RY)) if merged else None
            self.y = [
                remote(Y, lambda a=a: (P.at[1, a], RY.at[a])) for a in range(0 if merged else A)
            ]
            self.z = [None] + [
                remote((0, 2 * a), lambda a=a: (P.at[0, a], RZ.at[a - 1])) for a in range(1, A)
            ]

        def start_y(self, a=None):
            if self.merged:
                queue.append((self, None))
            else:
                queue.extend((self, i) for i in (order if a is None else [a]))
            pump()

        def fold_y(self, a):
            (self.all_y if self.merged else self.y[a])().wait_recv()
            for i in order if self.merged else [a]:
                self.P[0, i] = plus(self.P[0, i], self.RY[i])
                if i:
                    go(self.z[i])
            self.left -= 1

        def fold_z(self):
            for a in range(1, A):
                self.z[a]().wait_recv()
            self.M[...] = plus(self.P[0, 0], *[self.RZ[a - 1] for a in range(1, A)])

    order = list(range(A - 1, -1, -1))
    queue, flying, later = [], [], []

    def pump():
        while queue and len(flying) < WINDOW:
            unit, a = queue.pop(0)
            go(unit.all_y if unit.merged else unit.y[a])
            flying.append((unit, a))

    def fold_next():
        if flying:
            unit, a = flying.pop(0)
            pump()
            unit.fold_y(a)
            if not unit.left:
                later.extend((3 * t + 2, job) for t, job in enumerate(unit.then))
        now = [job for t, job in later if t <= 0]
        later[:] = [(t - 1, job) for t, job in later if t > 0]
        for job in now:
            job()

    UI = [Unit(PI.at[ex], RYI.at[ex], RZI.at[ex], MI.at[ex]) for ex in range(2)]
    UU = Unit(PU.at[0], RYU, RZU, MU)
    UO = Unit(PO.at[0], RYO, RZO, MO, merged=True)
    UH = Unit(PH.at[0], RYH, RZH, MH, merged=True)
    UQ = [None] + [Unit(PQ.at[j], RYQ.at[j], RZQ.at[j], MQ.at[j]) for j in range(2)]
    plan = Plan()

    xi = [remote(NEAR, lambda ex=ex: (MI.at[ex], RXI.at[ex])) for ex in range(2)]

    def inner_z(ex):
        UI[ex].fold_z()
        go(xi[ex])

    def cols_of(ref, e, size):
        return ref.at[:, at(flip(C, e), size)]

    i_core = [
        remote(CORE, lambda ex=ex: (RXI.at[1 - ex], cols_of(o_i, 2 * ex, cq))) for ex in range(2)
    ]

    def inner_x():
        for ex in range(2):
            xi[1 - ex]().wait_recv()
            RXI[1 - ex] = plus(MI[ex], RXI[1 - ex])
            go(i_core[ex])
            go_local(lambda ex=ex: (RXI.at[1 - ex], cols_of(o_i, 2 * ex, cq)))

    x_base = [next(remotes_free) for _ in range(n)][0]

    def outer_copy(i):
        return remote_at(NEAR, x_base + i, lambda: (PU.at[1, i % 2, i // 2], RXU.at[i % 2, i // 2]))

    def outer_x(i):
        outer_copy(i).wait_recv()
        PU[0, i % 2, i // 2] = plus(PU[0, i % 2, i // 2], RXU[i % 2, i // 2])
        if i % 2:
            UU.start_y(i // 2)

    class Finish:
        def __init__(self, unit, M, place):
            self.unit, self.M, self.place = unit, M, place
            self.near = remote(NEAR, lambda: (M, place(0)))
            self.core = remote(CORE, lambda: (M, place(0)))
            self.core2 = remote(CORE, lambda: (place(2), place(2)))

        def first(self):
            self.unit.fold_z()
            go(self.near)
            go(self.core)
            go_local(lambda: (self.M, self.place(0)))

        def second(self):
            self.near().wait_recv()
            go(self.core2)

    FU = Finish(UU, MU, lambda e: cols_of(o_u, e, wq))
    FO = Finish(UO, MO, lambda e: cols_of(o_o, e, wq))

    def query_place(e):
        to = flip(C, e)
        return o_q.at[at(to // 2, rs // 2), at(to % 2, hw)]

    FH = Finish(UH, MH, query_place)

    xo = remote(NEAR, lambda: (PO.at[1], RXO))
    xh = remote(NEAR, lambda: (PH.at[1], RXH))

    def fold_near(build, P, R, unit):
        build().wait_recv()
        for ib in (1, 0):
            for ia in range(A):
                P[0, ib, ia] = plus(P[0, ib, ia], R[ib, ia])
            if ib:
                unit.start_y()

    outs = (o_k, o_v)
    xq = [remote(NEAR, lambda j=j: (MQ.at[j], RXQ.at[j])) for j in range(2)]
    q_core = [
        remote(CORE, lambda j=j: (RXQ.at[j], outs[j].at[:, at(core, hw)])) for j in range(2)
    ]

    def proj_z(j):
        UQ[j + 1].fold_z()
        go(xq[j])

    def proj_x(j):
        xq[j]().wait_recv()
        RXQ[j] = plus(MQ[j], RXQ[j])
        go(q_core[j])
        go_local(lambda: (RXQ.at[j], outs[j].at[:, at(core, hw)]))

    hops = [CORE, NEAR] + [(0, 1 << b) for b in range(n.bit_length() - 1)]
    hop_copies = [
        remote(dev, lambda t=t: (VS.at[t], VR.at[t])) for t, dev in enumerate(hops)
    ]

    def vector_hop(t):
        if t:
            hop_copies[t - 1]().wait_recv()
            VS[t] = VS[t - 1] + VR[t - 1]
        if t < len(hops):
            go(hop_copies[t])
        else:
            go_local(lambda: (VS.at[t], o_vec))

    pairs = hw // (2 * HD)

    def attention(s, times):
        need(("lse", s))

        def body(step, carry):
            cols = at(step, 2 * HD)

            def get(ref):
                return ref[:, s, :, cols].reshape(slots * part, 2 * HD)

            mask = key_mask(lens[x * sh + s], C, part)
            dq, dk, dv = attend_back_pair(
                get(Q), get(K), get(V), mask, LSE[s % 2, :, cols], get(CX), get(G)
            )
            for ref, value in ((Q, dq), (K, dk), (V, dv)):
                ref[:, s, :, cols] = value.reshape(slots, part, 2 * HD)
            plan.beside(step, times)
            return carry

        lax.fori_loop(0, pairs, body, 0)
        if s + 2 < sh:
            load(("lse", s + 2), lambda: (lse_in.at[s + 2], LSE.at[s % 2]))

    groups = width // 256
    gsz = 256 // rs

    def weight_grad(get, put, times, unit=None):
        def body(step, carry):
            a = groups - 1 - step
            cols = at(xor(f // gsz, a, groups), 256)
            r = (dot_tn(L[0, :, cols], get(0)) + dot_tn(L[1, :, cols], get(1))).astype(BF)
            for u in range(gsz):
                i = a * gsz + flip(f % gsz, u)
                put(i, r[u * rs : (u + 1) * rs])
            if unit is not None and groups == A:
                for t in range(groups):

                    @pl.when(step == t)
                    def _():
                        unit.start_y(groups - 1 - t)

            plan.beside(step, times)
            return carry

        lax.fori_loop(0, groups, body, 0)
        if unit is not None and groups != A:
            unit.start_y()

    def into(P):
        def put(i, value):
            P[i % 2, i // 2] = value

        return put

    def put_query(i, value):
        for h in range(2):
            PH[(h + x) % 2, i % 2, i // 2] = value[h * (rs // 2) : (h + 1) * (rs // 2)]

    def spaced(first, last, count):
        return [first + (last - first) * (t + 1) / count for t in range(count)]

    UI[0].then = [lambda: inner_z(0)]
    UI[1].then = [lambda: inner_z(1), inner_x]
    UU.then = [FU.first, FU.second]
    UO.then = [FO.first, FO.second]
    UH.then = [FH.first, FH.second]
    for j in range(2):
        UQ[j + 1].then = [lambda j=j: proj_z(j), lambda j=j: proj_x(j)]

    xs_order = list(range(1, n, 2)) + list(range(0, n, 2))
    for k, i in enumerate(xs_order):
        if k < n // 2:
            plan.add(11 + 14 * (per * (i // per) + per - 1 - i % per + 1) / n, lambda i=i: outer_copy(i).start())
        follow = xs_order[k + n // 2] if k < n // 2 else None

        def fold_x(i=i, follow=follow):
            if follow is not None:
                outer_copy(follow).start()
            outer_x(i)

        plan.add(20 + 48 * k / n, fold_x)
    for k in range(13 * A):
        plan.add(14 + 18 * k / A, fold_next)
    for t in range(len(hops) + 1):
        plan.add(74 + 4 * t, lambda t=t: vector_hop(t))

    weight_grad(lambda m: D[0, m], into(PI.at[0]), spaced(4, 8, groups), UI[0])

    def act_load(t):
        slot = t % 2
        return [
            pltpu.make_async_copy(act.at[:, act_cols(t)], D.at[slot, 0], lsem.at[act_sem + 2 * slot]),
            pltpu.make_async_copy(
                act_s.at[:, act_cols(t)], D.at[slot, 1], lsem.at[act_sem + 2 * slot + 1]
            ),
        ]

    act_sem = [next(locals_free) for _ in range(4)][0]

    def begin_act(t):
        for c in act_load(t):
            c.start()

    begin_act(0)
    need(("dinn", 1), ("dinn_s", 1))
    weight_grad(lambda m: D[1, m], into(PI.at[1]), spaced(8, 11, groups), UI[1])
    if chunks > 1:
        begin_act(1)
    load("x0", lambda: (xall.at[pl.ds(0, rows)], L.at[0]))
    load("x1", lambda: (xall.at[pl.ds(rows, rows)], L.at[1]))
    need(("dout", 0), ("dout", 1), "dout_s")

    outer_times = spaced(11, 25, n)

    def outer_body(u, carry):
        t, il = u // per, per - 1 - u % per
        slot = t % 2

        @pl.when(u % per == 0)
        def _():
            for c in act_load(t):
                c.wait()

        cols = at(xor(f % per, il, per), ro)
        r = dot_tn(D[slot, 0, :, cols], DO[0]) + dot_tn(D[slot, 1, :, cols], DO[1])
        r = r.astype(BF)
        i = t * per + il
        for ex in range(2):
            PU[ex, i % 2, i // 2] = r[:, ex * wq : (ex + 1) * wq]

        @pl.when((u % per == per - 1) & (t + 2 < chunks))
        def _():
            begin_act(t + 2)

        plan.beside(u, outer_times)
        return carry

    lax.fori_loop(0, n, outer_body, 0)

    need("co", "co_s", "c", ("dattn", 0), ("dattn", 1), "dattn_s")
    for half in range(2):
        for g in range(hw // 256):
            lanes = slice(g * 256, (g + 1) * 256)

            def left(m):
                if half:
                    return CO[m, :, lanes]
                return CX[2 * m : 2 * m + 2, :, :, lanes].reshape(rows, 256)

            r = (dot_tn(left(0), DA[0]) + dot_tn(left(1), DA[1])).astype(BF)
            group = (core + half * (1 - 2 * core)) * (hw // 256) + g
            for u in range(gsz):
                i = xor(group * gsz + u, f, n)
                for ex in range(2):
                    PO[ex, i % 2, i // 2] = r[u * rs : (u + 1) * rs, ex * wq : (ex + 1) * wq]
        for job in plan.due(27 + 3 * half):
            job()
    go(xo)
    plan.add(64, lambda: fold_near(xo, PO, RXO, UO))

    need("q", "k", "v", "g", "g_s")
    for s in range(sh):
        attention(s, spaced(30 + 8 * s, 38 + 8 * s, pairs))

    need("x0", "x1", "vec")
    for j, ref in enumerate((Q, K, V)):

        def right(m):
            return ref[2 * m : 2 * m + 2].reshape(rows, hw)

        if j != 1:
            total = jnp.sum(right(0).astype(F32), 0, keepdims=True)
            total = total + jnp.sum(right(1).astype(F32), 0, keepdims=True)
            VS[0, j // 2 : j // 2 + 1, at(core, hw)] = total
        times = spaced(54 + 6 * j, 60 + 6 * j, groups)
        if j:
            weight_grad(right, into(PQ.at[j - 1]), times, UQ[j])
        else:
            weight_grad(right, put_query, times)
            go(xh)
            plan.add(76, lambda: fold_near(xh, PH, RXH, UH))

    need("w")

    def project(slot):
        out = None
        for j, ref in enumerate((Q, K, V)):
            p = dot_nt(ref[slot].reshape(half_rows, hw), W[j])
            out = p if out is None else out + p
        return out

    ig_swap = [remote(CORE, lambda ex=ex: (SB, ig_s.at[ex])) for ex in range(2)]
    for ex in (1, 0):
        value = project(2 + ex)
        if ex == 0:
            ig_swap[1]().wait_send()
        SB[...] = value
        ig_swap[ex]().start()
        for job in plan.due(80 - 4 * ex):
            job()

    def rows_of(ex):
        return pl.ds(ex * half_rows, half_rows)

    ig_near = remote(NEAR, lambda: (XS, o_igr))
    for ex in (1, 0):
        ig_swap[ex]().wait_recv()
        load(("ig", ex), lambda ex=ex: (ig_s.at[ex], IB))
        value = project(ex)
        if ex:
            ig_swap[0]().wait_send()
        load(("df", ex), lambda ex=ex: (dfirst.at[rows_of(ex)], SB))
        need(("ig", ex), ("df", ex))
        value = value + IB[...] + SB[...]
        if ex:
            XS[...] = value.astype(BF)
            go(ig_near)
        else:
            IB[...] = value
            go_local(lambda: (IB, o_igl))
        for job in plan.due(88 - 4 * ex):
            job()

    for job in plan.due(1e9):
        job()
    while queue or flying or later:
        fold_next()

    ig_near().wait_recv()
    for build in i_core + q_core + [b for F in (FU, FO, FH) for b in (F.core, F.core2)]:
        build().wait_recv()
    for i in range(n):
        outer_copy(i).wait_send()
    for end in ends:
        end()


def back_call(lens, n, act, dout, nrm, dinn, dattn, ctx, cr, xall, q, k, v, lse, *rest):
    rows, width = nrm.shape
    ff = act.shape[1]
    slots, sh, part, hw = q.shape
    A = n // 2
    rs, ro, cq, wq = width // n, ff // n, ff // 4, width // 4
    hops = 2 + n.bit_length() - 1

    def bf(*shape):
        return jax.ShapeDtypeStruct(shape, BF)

    def f32(*shape):
        return jax.ShapeDtypeStruct(shape, F32)

    def vm(*shape):
        return pltpu.VMEM(shape, BF)

    def vf(*shape):
        return pltpu.VMEM(shape, F32)

    four = (slots, sh, part, hw)
    return pl.pallas_call(
        functools.partial(back_kernel, n),
        in_specs=[pl.BlockSpec(memory_space=pltpu.SMEM)] + [ANY] * 23,
        out_specs=[ANY] * 10,
        out_shape=[
            f32(rows // 2, width),
            bf(rows // 2, width),
            bf(rs, ff),
            bf(ro, width),
            bf(rs, width),
            bf(rs, width),
            bf(rs, width),
            bf(rs, width),
            f32(16, width),
            f32(2, rows // 2, width),
        ],
        scratch_shapes=[
            vm(*four),
            vm(*four),
            vm(*four),
            vm(*four),
            vm(*four),
            vf(2, *lse.shape[1:]),
            vm(2, rows, width),
            vm(2, 2, rows, 1024),
            vm(2, rows, 2 * wq),
            vm(2, rows, 2 * wq),
            vm(2, rows, hw),
            vm(3, width, hw),
            vm(2, 2, A, rs, cq),
            vm(2, 2, A, ro, wq),
            vm(2, 2, A, rs, wq),
            vm(2, 2, A, rs, hw),
            vm(2, A, rs, cq),
            vm(2, A - 1, rs, cq),
            vm(2, rs, cq),
            vm(2, rs, cq),
            vm(2, A, ro, wq),
            vm(A, ro, wq),
            vm(A - 1, ro, wq),
            vm(ro, wq),
            vm(A, rs, wq),
            vm(A - 1, rs, wq),
            vm(rs, wq),
            vm(2, A, rs, wq),
            vm(2, 2, A, rs // 2, hw),
            vm(A, rs // 2, hw),
            vm(A - 1, rs // 2, hw),
            vm(rs // 2, hw),
            vm(2, A, rs // 2, hw),
            vm(2, A, rs, hw),
            vm(2, A - 1, rs, hw),
            vm(2, rs, hw),
            vm(2, rs, hw),
            vf(hops + 1, 16, width),
            vf(hops, 16, width),
            vf(rows // 2, width),
            vf(rows // 2, width),
            vm(rows // 2, width),
            pltpu.SemaphoreType.DMA((48,)),
            pltpu.SemaphoreType.DMA((64 + 8 * n,)),
            pltpu.SemaphoreType.DMA((64 + 8 * n,)),
        ],
        compiler_params=pltpu.CompilerParams(
            vmem_limit_bytes=BACK_LIMIT, collective_id=1, has_side_effects=True
        ),
        name="back",
    )(
        lens,
        act,
        dout,
        nrm,
        dinn,
        dattn,
        ctx,
        cr,
        xall,
        q,
        k,
        v,
        lse,
        *rest,
    )


def finish_kernel(here, near, lo, *refs):
    o_ig, o_lo = refs[6:8]
    x = lax.axis_index("ctx") // 2
    o_ig[x] = here[...]
    o_ig[1 - x] = near[...].astype(F32)
    o_lo[...] = lo[...]
    for source, target in zip(refs[:6], refs[8:]):
        target[...] = source[...].astype(F32)


def finish_call(here, near, lo, *grads):
    rows, width = here.shape
    steps = 2

    def by(a):
        return pl.BlockSpec((a.shape[0] // steps, a.shape[1]), lambda i: (i, 0))

    return pl.pallas_call(
        finish_kernel,
        grid=(steps,),
        in_specs=[by(a) for a in (here, near, lo) + grads],
        out_specs=[pl.BlockSpec((2, rows // steps, width), lambda i: (0, i, 0)), by(lo)]
        + [by(g) for g in grads],
        out_shape=[jax.ShapeDtypeStruct((2, rows, width), F32), jax.ShapeDtypeStruct(lo.shape, BF)]
        + [jax.ShapeDtypeStruct(g.shape, F32) for g in grads],
        compiler_params=params(),
        name="finish",
    )(here, near, lo, *grads)


def per_device(
    inputs,
    lengths,
    cotangent,
    query_weight,
    key_weight,
    value_weight,
    out_weight,
    inner_weight,
    outer_weight,
    query_bias,
    value_bias,
    out_bias,
    inner_bias,
    outer_bias,
    first_gain,
    first_shift,
    second_gain,
    second_shift,
):
    C = lax.axis_index("ctx")
    f = lax.axis_index("fsdp")
    n = lax.axis_size("fsdp")
    x, core = C // 2, C % 2
    seqs, part, width = inputs.shape
    ff = inner_weight.shape[1]
    sh = seqs // 2
    rows = 2 * sh * part
    rs, ro = width // n, ff // n
    hw = width // 2

    def pick(bit, a, b):
        return jnp.where(bit == 0, a, b), jnp.where(bit == 0, b, a)

    vectors = (
        query_bias,
        value_bias,
        out_bias,
        outer_bias,
        first_gain,
        first_shift,
        second_gain,
        second_shift,
    )
    vecs = jnp.concatenate([v.reshape(1, rs) for v in vectors], 0)
    if rs < 128:
        vecs = jnp.pad(vecs, ((0, 0), (0, 128 - rs)))
    vecs = jnp.concatenate(
        [vecs, inner_bias.reshape(ro // 128, 128), jnp.zeros((PACK - 8 - ro // 128, 128), BF)], 0
    )
    x4, cot, w_qkv, wi, wu, wo, vecs, q4, k4, v4, c4, c_r, c_s, lse, *norm = front_call(
        lengths,
        inputs,
        cotangent,
        query_weight,
        key_weight,
        value_weight,
        vecs,
        out_weight,
        inner_weight,
        outer_weight,
        n,
    )
    xall = x4.reshape(2 * rows, width)
    cr = c_r.reshape(rows, hw)
    norm = [a.reshape(rows, a.shape[2]) for a in norm]
    two = (2, sh, part, hw)
    (
        dfirst,
        dco,
        acc,
        dout,
        dinn,
        dattn,
        layer_out,
        act_s,
        dout_s,
        dinn_s,
        nrm_s,
        dattn_s,
        dcs_s,
    ) = ffn_call(lengths, sh, *norm, cot.reshape(rows, width), vecs, wo, wi, wu)
    act, nrm = norm[0], norm[4]

    ig_here, ig_near, g_i, g_u, g_o, g_q, g_k, g_v, sums, _ = back_call(
        lengths,
        n,
        act,
        dout,
        nrm,
        dinn,
        dattn,
        c4,
        cr,
        xall,
        q4,
        k4,
        v4,
        lse,
        dco.reshape(two),
        dfirst,
        w_qkv,
        acc,
        act_s,
        dout_s,
        dinn_s,
        nrm_s,
        dattn_s,
        dcs_s.reshape(two),
        c_s.reshape(rows, hw),
    )
    own = lax.dynamic_slice_in_dim(sums[:8], f * rs, rs, 1)
    own_inner = lax.dynamic_slice_in_dim(sums[8 : 8 + ff // width].reshape(ff), f * ro, ro, 0)
    input_grad, layer_out, *grads = finish_call(
        ig_here, ig_near, layer_out.reshape(seqs * part, width), g_q, g_k, g_v, g_o, g_i, g_u
    )
    grad_query, grad_key, grad_value, grad_out, grad_inner, grad_outer = grads
    input_grad, layer_out = input_grad.reshape(inputs.shape), layer_out.reshape(inputs.shape)

    return (
        layer_out,
        input_grad,
        grad_query,
        grad_key,
        grad_value,
        grad_out,
        grad_inner,
        grad_outer,
        own[0],
        own[1],
        own[2],
        own_inner,
        own[3],
        own[4],
        own[5],
        own[6],
        own[7],
    )


def solution(mesh):
    rowed = P("fsdp", "ctx", None)
    matrix, vector = P("fsdp", None), P("fsdp")
    in_specs = (rowed, vector, rowed) + (matrix,) * 6 + (vector,) * 9
    out_specs = (rowed, rowed) + (matrix,) * 6 + (vector,) * 9
    return jax.shard_map(
        per_device, mesh=mesh, in_specs=in_specs, out_specs=out_specs, check_vma=False
    )
```

```python
import functools

import jax
import jax.numpy as jnp
from jax import lax
from jax.experimental import pallas as pl
from jax.experimental.pallas import tpu as pltpu
from jax.sharding import PartitionSpec as P

HD = 64
EPSILON = 1e-05
BF = jnp.bfloat16
F32 = jnp.float32
ANY = pl.BlockSpec(memory_space=pl.ANY)
NT = (((1,), (1,)), ((), ()))
TN = (((0,), (0,)), ((), ()))
VMEM_LIMIT = 58 << 20
BACK_LIMIT = 60 << 20
WINDOW = 2


def dot(a, b):
    return jnp.dot(a, b, preferred_element_type=F32)


def dot_nt(a, b):
    return lax.dot_general(a, b, NT, preferred_element_type=F32)


def dot_tn(a, b):
    return lax.dot_general(a, b, TN, preferred_element_type=F32)


def params(**more):
    return pltpu.CompilerParams(vmem_limit_bytes=VMEM_LIMIT, **more)


def cost(flops, size, trans=0):
    return pl.CostEstimate(flops=int(flops), bytes_accessed=int(size), transcendentals=int(trans))


MESH = pl.DeviceIdType.MESH
PACK = 16


def flip(v, mask):
    out, bit = v, 1
    while bit <= mask:
        if mask & bit:
            out = out + bit - 2 * bit * ((v // bit) % 2)
        bit *= 2
    return out


def at(index, size):
    return pl.ds(pl.multiple_of(index * size, size), size)


def spread(read, n, rs):
    per = max(128 // rs, 1)
    tiles = []
    for t in range(n // per):
        tile = read(t * per)
        for u in range(1, per):
            tile = tile + pltpu.roll(read(t * per + u), u * rs, 1)
        tiles.append(tile)
    return jnp.concatenate(tiles, 1)


def front_kernel(
    n,
    lens,
    xin,
    cin,
    wq,
    wk,
    wv,
    wo_in,
    wi_in,
    wu_in,
    *refs,
):
    vectors, refs = refs[:9], refs[9:]
    (
    xo,
    co,
    wqkvo,
    wio,
    wuo,
    woo,
    veco,
    qo,
    ko,
    vo,
    cxo,
    cro,
    cso,
    lseo,
    acto,
    gpo,
    hato,
    ro_o,
    nrmo,
    X,
    W,
    VEC,
    Q,
    K,
    V,
    CX,
    LSE,
    WO,
    WI,
    CR,
    VB,
    IB,
    HAT,
    R1,
    NRM,
    ACT,
    GP,
    lsem,
    ssem,
    rsem,
    vecs,
    ) = refs
    C, f = lax.axis_index("ctx"), lax.axis_index("fsdp")
    x, core = C // 2, C % 2
    A = n // 2
    sh, part, width = X.shape[1:]
    hw = W.shape[2]
    ff = wio.shape[1]
    rs, ro, cq = width // n, ff // n, ff // 4

    partners = [(0, 2 * k) for k in range(1, A)] + [(0, 1), (2, 0), (1, 0)]

    def device(dc, df):
        return (flip(C, dc), flip(f, df))

    barrier = pltpu.get_barrier_semaphore()
    for p in partners:
        pl.semaphore_signal(barrier, inc=1, device_id=device(*p), device_id_type=MESH)

    vecs[...] = jnp.zeros_like(vecs)
    for j, ref in enumerate(vectors[:8]):
        vecs[j : j + 1, : ref.shape[0]] = ref[...].reshape(1, -1)
    inner_bias = vectors[8][...].reshape(1, -1)
    for t in range(inner_bias.shape[1] // 128):
        vecs[8 + t : 9 + t, :] = inner_bias[:, t * 128 : (t + 1) * 128]

    local = []
    used = iter(range(lsem.shape[0]))

    def begin(source, target):
        c = pltpu.make_async_copy(source, target, lsem.at[next(used)])
        c.start()
        return c

    def keep(source, target):
        local.append(begin(source, target))

    x_here = begin(xin.at[pl.ds(x * sh, sh)], X.at[0])
    w_here = [begin(w.at[:, at(core, hw)], W.at[j, at(f, rs)]) for j, w in enumerate((wq, wk, wv))]
    w_here.append(begin(vecs, VEC.at[f]))

    pl.semaphore_wait(barrier, len(partners))

    def remote(source, target, sem, dev):
        return pltpu.make_async_remote_copy(
            src_ref=source,
            dst_ref=target,
            send_sem=ssem.at[sem],
            recv_sem=rsem.at[sem],
            device_id=device(*dev),
            device_id_type=MESH,
        )

    sent = []

    def send(*what):
        c = remote(*what)
        c.start()
        sent.append(c)

    seen = set()

    def arrive(target, sem, dev):
        if sem not in seen:
            seen.add(sem)
            remote(target, target, sem, dev).wait_recv()

    X1, X2, X3, COT, CTX, CTX2 = range(6)
    send(xin.at[pl.ds((1 - x) * sh, sh)], X.at[1], X1, (2, 0))

    def rows_at(ref, first, size):
        return ref.at[pl.ds(pl.multiple_of(first, size), size)]

    hr, hu = rs // 2, ro // 2

    def projection(j):
        w = (wq, wk, wv)[j]
        return (
            1,
            lambda e, s: [W.at[j, at(s, rs)]] + [VEC.at[s]] * (j == 0),
            lambda: [w.at[:, at(core, hw)]] + [vecs] * (j == 0),
        )

    def inner_part(h):
        return (
            4,
            lambda e, s: [WI.at[at(s * 2 + h, hr), at(flip(C, e), cq)]],
            lambda: [wi_in.at[pl.ds(h * hr, hr), at(C, cq)]],
        )

    outer_a = (
        4,
        lambda e, s: [rows_at(wuo, s * ro + flip(C, e) * (hu // 4), hu // 4)],
        lambda: [rows_at(wu_in, C * (hu // 4), hu // 4)],
    )
    out_part = (
        4,
        lambda e, s: [rows_at(WO, s * rs + flip(C, e) * (rs // 4), rs // 4)],
        lambda: [rows_at(wo_in, C * (rs // 4), rs // 4)],
    )

    def outer_b(h):
        return (
            2,
            lambda e, s: [rows_at(wuo, s * ro + hu + (flip(core, e) * 2 + h) * (hu // 4), hu // 4)],
            lambda: [rows_at(wu_in, hu + (core * 2 + h) * (hu // 4), hu // 4)],
        )

    kinds = [
        out_part,
        inner_part(0),
        projection(0),
        projection(1),
        projection(2),
        inner_part(1),
        outer_a,
        outer_b(0),
        outer_b(1),
    ]
    sems, ready = {}, 6
    for k, (parts, place, _) in enumerate(kinds):
        for e in range(parts):
            for i in range(1, n):
                for u in range(2 if k == 2 else 1):
                    sems[k, e, i, u] = ready
                    ready += 1

    def route(parts, e, i):
        if e % 2:
            return (1, 0), (e - 1, i)
        if e:
            return (2, 0), (0, i)
        if i % 2:
            return (0, 1), (0, i - 1)
        return (0, i), (0, 0)

    def copies(k, e, i):
        parts, place, own = kinds[k]
        dev, (pe, pi) = route(parts, e, i)
        target = place(pe, flip(f, pi))
        source = target if pi else own()
        return [
            remote(source[u], target[u], sems[k, e, i, u], dev) for u in range(len(target))
        ]

    issued = []

    def give(k, e, i):
        for c in copies(k, e, i):
            c.start()
        issued.append((k, e, i))

    got = set()

    def take(k, e, i):
        if (k, e, i) in got:
            return
        got.add((k, e, i))
        parts, place, _ = kinds[k]
        dev, _ = route(parts, e, i)
        for u, target in enumerate(place(e, flip(f, i))):
            remote(target, target, sems[k, e, i, u], dev).wait_recv()

    def hand_on(k, i):
        parts = kinds[k][0]
        if parts == 4:
            give(k, 2, i)
        if parts > 1:
            give(k, 1, i)

    def base(k):
        if k < len(kinds):
            for a in range(A - 1, 0, -1):
                give(k, 0, 2 * a)
            give(k, 0, 1)

    def z_in(k):
        for a in range(1, A):
            take(k, 0, 2 * a)
            give(k, 0, 2 * a + 1)
            hand_on(k, 2 * a)

    def y_in(k):
        for i in range(1, n, 2):
            take(k, 0, i)
            hand_on(k, i)

    def x_in(k):
        if kinds[k][0] == 4:
            for i in range(1, n):
                take(k, 2, i)
                give(k, 3, i)

    base(0)
    base(1)
    x_here.wait()
    send(X.at[0], X.at[2], X2, (1, 0))
    keep(cin.at[pl.ds(x * sh, sh)], co.at[0])
    w_here += [begin(wo_in, WO.at[at(f, rs)]), begin(wi_in, WI.at[at(f, rs)])]
    keep(wu_in, wuo.at[at(f, ro)])
    slots = X.shape[0]
    pairs = hw // (2 * HD)

    z_in(0)
    base(2)
    arrive(X.at[1], X1, (2, 0))
    send(X.at[1], X.at[3], X3, (1, 0))
    z_in(1)
    base(3)
    y_in(0)
    arrive(X.at[2], X2, (1, 0))
    arrive(X.at[3], X3, (1, 0))
    keep(X, xo)
    for c in w_here:
        c.wait()
    z_in(2)
    base(4)
    y_in(1)
    send(cin.at[pl.ds((1 - x) * sh, sh)], co.at[1], COT, (2, 0))
    z_in(3)
    base(5)
    y_in(2)
    x_in(0)
    keep(VEC, veco)

    def bias(row):
        read = lambda s: VEC[pl.ds(core * (n // 2) + s, 1), row : row + 1, :128].reshape(1, 128).astype(F32)
        return spread(read, n // 2, rs)

    shape = (sh, part, hw)

    def project(j, target, add):
        def body(slot, carry):
            value = dot(X[slot].reshape(sh * part, width), W[j])
            if add is not None:
                value = value + add
            target[slot] = value.astype(BF).reshape(shape)
            return carry

        lax.fori_loop(0, slots, body, 0)

    project(0, Q, bias(0))
    z_in(4)
    base(6)
    y_in(3)
    project(1, K, None)
    x_in(1)
    z_in(5)
    base(7)
    y_in(4)
    keep(W, wqkvo)
    project(2, V, bias(1))
    keep(Q, qo)
    keep(K, ko)
    keep(V, vo)

    jobs = {7: [lambda: z_in(6), lambda: base(8)], 9: [lambda: y_in(5)]}
    steps = sh * pairs

    def attend(step, carry):
        s, pair = step // pairs, step % pairs
        cols = at(pair, 2 * HD)

        def load(ref):
            return ref[:, s, :, cols].reshape(slots * part, 2 * HD)

        q, k, v = load(Q), load(K), load(V)
        mask = key_mask(lens[x * sh + s], C, part)
        o, lse = attend_pair(q, k, v, mask)
        CX[:, s, :, cols] = o.reshape(slots, part, 2 * HD)
        LSE[s, :, cols] = lse
        for t in range(steps):
            now = jobs.get(t)
            if now:

                @pl.when(step == t)
                def _():
                    for job in now:
                        job()

        return carry

    lax.fori_loop(0, steps, attend, 0)
    send(CX.at[pl.ds(2, 2)], CR, CTX, (1, 0))
    send(CX.at[pl.ds(0, 2)], cso, CTX2, (1, 0))
    keep(CX, cxo)
    keep(LSE, lseo)
    for e in range(4):
        for i in range(1, n):
            take(0, e, i)
    keep(WO, woo)
    VB[...] = spread(lambda s: VEC[s, :8, :128].astype(F32), n, rs)
    for s in range(n):
        for t in range(ro // 128):
            first = s * ro + t * 128
            IB[:, first : first + 128] = VEC[s, 8 + t : 9 + t, :].astype(F32)
    arrive(CR, CTX, (1, 0))
    keep(CR, cro)
    own_half, other_half = at(core, hw), at(1 - core, hw)
    half = sh * part

    def norm(ex, carry):
        first = (
            X[ex].reshape(half, width).astype(F32)
            + (
                dot(CX[ex].reshape(half, hw), WO[own_half])
                + dot(CR[ex].reshape(half, hw), WO[other_half])
            )
            + VB[2:3, :]
        )
        hat, r = normalise(first)
        HAT[ex] = hat
        R1[ex] = jnp.broadcast_to(r, (half, 128))
        NRM[ex] = (hat * VB[4:5, :] + VB[5:6, :]).astype(BF)
        return carry

    lax.fori_loop(0, 2, norm, 0)
    keep(HAT, hato)
    keep(R1, ro_o)
    keep(NRM, nrmo)
    plan = [
        [lambda: z_in(7), lambda: y_in(6)],
        [lambda: x_in(5)],
        [lambda: z_in(8), lambda: y_in(7)],
        [lambda: x_in(6)],
    ]
    for e in range(4):
        for job in plan[e]:
            job()
        for k in (1, 5):
            for i in range(1, n):
                take(k, e, i)
        cols = at(flip(C, e), cq)

        def inner(ex, carry):
            g, d = gelu_pair(dot(NRM[ex], WI[:, cols]) + IB[:, cols])
            ACT[ex, :, cols] = g.astype(BF)
            GP[ex, :, cols] = d.astype(BF)
            return carry

        lax.fori_loop(0, 2, inner, 0)
        keep(ACT.at[:, :, cols], acto.at[:, :, cols])
        keep(GP.at[:, :, cols], gpo.at[:, :, cols])
    y_in(8)
    keep(WI, wio)
    for k, (parts, _, _) in enumerate(kinds):
        for e in range(parts):
            for i in range(1, n):
                take(k, e, i)
    arrive(co.at[1], COT, (2, 0))
    arrive(cso, CTX2, (1, 0))
    for what in issued:
        for c in copies(*what):
            c.wait_send()
    for c in sent:
        c.wait_send()
    for c in local:
        c.wait()


def front_call(lengths, xin, cin, wq, wk, wv, wo, wi, wu, vectors, n):
    seqs, part, width = xin.shape
    sh, ff, hw = seqs // 2, wi.shape[1], width // 2

    def bf(*shape):
        return jax.ShapeDtypeStruct(shape, BF)

    def vm(*shape):
        return pltpu.VMEM(shape, BF)

    full = 4 * part
    lse = (sh, full, hw)
    half = sh * part
    four = (4, sh, part, hw)
    sems = 24 * n
    return pl.pallas_call(
        functools.partial(front_kernel, n),
        in_specs=[pl.BlockSpec(memory_space=pltpu.SMEM)] + [ANY] * 8 + [pl.BlockSpec(memory_space=pltpu.VMEM)] * 9,
        out_specs=[ANY] * 19,
        out_shape=[
            bf(4, sh, part, width),
            bf(2, sh, part, width),
            bf(3, width, hw),
            bf(width, ff),
            bf(ff, width),
            bf(width, width),
            bf(n, PACK, 128),
            bf(*four),
            bf(*four),
            bf(*four),
            bf(*four),
            bf(2, sh, part, hw),
            bf(2, sh, part, hw),
            jax.ShapeDtypeStruct(lse, F32),
            bf(2, half, ff),
            bf(2, half, ff),
            jax.ShapeDtypeStruct((2, half, width), F32),
            jax.ShapeDtypeStruct((2, half, 128), F32),
            bf(2, half, width),
        ],
        scratch_shapes=[
            vm(4, sh, part, width),
            vm(3, width, hw),
            vm(n, PACK, 128),
            vm(*four),
            vm(*four),
            vm(*four),
            vm(*four),
            pltpu.VMEM(lse, F32),
            vm(width, width),
            vm(width, ff),
            vm(2, sh, part, hw),
            pltpu.VMEM((8, width), F32),
            pltpu.VMEM((1, ff), F32),
            pltpu.VMEM((2, half, width), F32),
            pltpu.VMEM((2, half, 128), F32),
            vm(2, half, width),
            vm(2, half, ff),
            vm(2, half, ff),
            pltpu.SemaphoreType.DMA((40,)),
            pltpu.SemaphoreType.DMA((sems,)),
            pltpu.SemaphoreType.DMA((sems,)),
            vm(PACK, 128),
        ],
        compiler_params=params(collective_id=0, has_side_effects=True),
        name="front",
    )(lengths, xin, cin, wq, wk, wv, wo, wi, wu, *vectors)


def lanes_of(shape, head):
    lane = lax.broadcasted_iota(jnp.int32, shape, 1)
    own = (lane < HD) if head == 0 else (lane >= HD)
    return lane, own, (HD if head == 0 else 0)


def split3(a):
    hi = a.astype(BF).astype(F32)
    mid = (a - hi).astype(BF).astype(F32)
    return hi, mid, a - hi - mid


def flat(ref):
    a = ref[...]
    return a.reshape(-1, a.shape[-1])


def key_mask(length, C, part):
    row = lax.broadcasted_iota(jnp.int32, (part, 2 * HD), 0)
    out = []
    for e in (0, 2, 1, 3):
        inside = row + flip(C, e) * part < length
        out.append(jnp.where(inside, 0.0, -1e30).astype(BF))
    return jnp.concatenate(out, 0)


def attend_pair(q, k, v, mask):
    out = []
    for head in range(2):
        lane, own, other = lanes_of(q.shape, head)
        qh = jnp.where(own, q * BF(HD**-0.5), jnp.where(lane == other, 1.0, 0.0).astype(BF))
        kh = jnp.where(own, k, mask)
        s = dot_nt(qh, kh)
        top = jnp.max(s, -1, keepdims=True)
        e = jnp.exp(s - top)
        total = jnp.sum(e, -1, keepdims=True)
        o = dot(e.astype(BF), v) * (1.0 / total)
        out.append((o, top + jnp.log(total), own))
    (o0, l0, own), (o1, l1, _) = out
    return jnp.where(own, o0, o1).astype(BF), jnp.where(own, l1, l0)


def attend_back_pair(q, k, v, mask, lse, c, g):
    qs = q * BF(HD**-0.5)
    kt = k.T
    prod = c.astype(F32) * g.astype(F32)
    res = []
    for head in range(2):
        lane, own, o = lanes_of(q.shape, head)
        hi, mid, low = split3(-lse)
        extra = jnp.where(
            lane == o,
            1.0,
            jnp.where(
                lane == o + 1,
                hi,
                jnp.where(lane == o + 2, mid, jnp.where(lane == o + 3, low, 0.0)),
            ),
        ).astype(BF)
        qh = jnp.where(own, qs, extra)
        kh = jnp.where(own, k, jnp.where(lane == o, mask, BF(1)))
        p = jnp.exp(dot_nt(kh, qh))
        delta = jnp.sum(jnp.where(own, prod, 0.0), -1, keepdims=True)
        hi, mid, low = split3(-delta)
        extra = jnp.where(
            lane == o, hi, jnp.where(lane == o + 1, mid, jnp.where(lane == o + 2, low, 0.0))
        ).astype(BF)
        gh = jnp.where(own, g, extra)
        vh = jnp.where(own, v, BF(1))
        ds = (p * dot_nt(vh, gh)).astype(BF)
        dv = dot(p.astype(BF), g)
        dk = dot(ds, qs)
        dqt = dot(kt, ds)
        res.append((dv, dk, dqt, own))
    (dv0, dk0, dq0, own), (dv1, dk1, dq1, _) = res
    dqt = jnp.concatenate([dq0[:HD], dq1[HD:]], 0) * (HD**-0.5)
    return dqt.T.astype(BF), jnp.where(own, dk0, dk1).astype(BF), jnp.where(own, dv0, dv1).astype(BF)


def gelu_pair(u):
    e = jnp.exp(u * u * -0.5)
    t = 1.0 / (1.0 + (0.3275911 * 0.7071067811865476) * jnp.abs(u))
    poly = t * (
        0.254829592 * 0.5
        + t
        * (
            -0.284496736 * 0.5
            + t * (1.421413741 * 0.5 + t * (-1.453152027 * 0.5 + t * (1.061405429 * 0.5)))
        )
    )
    tail = poly * e
    cdf = jnp.where(u >= 0, 1.0 - tail, tail)
    ucdf = u * cdf
    return ucdf, cdf + u * (e * 0.3989422804014327)


def normalise(h):
    c = h - jnp.mean(h, -1, keepdims=True)
    r = lax.rsqrt(jnp.mean(c * c, -1, keepdims=True) + EPSILON)
    return c * r, r


def normalise_back(dyg, hat, r):
    return r * (
        dyg - jnp.mean(dyg, -1, keepdims=True) - hat * jnp.mean(dyg * hat, -1, keepdims=True)
    )


def ffn_kernel(
    n, sh, part, lens, act, gp, hat1_ref, r1_ref, cot, vecs, act_in, nrm_in, wo_in, wi_in, wu_in, *refs
):
    dfirst, dco, acc = refs[:3]
    homes, (o_lo, act_s, dout_s, dinn_s, nrm_s, dattn_s, dcs_s) = refs[3:6], refs[6:13]
    wo, wi, wu, vec, *twice, sem, csem, hsem, ssem, rsem = refs[13:]
    width, ff = wi.shape
    C, f = lax.axis_index("ctx"), lax.axis_index("fsdp")
    x, core = C // 2, C % 2
    step = pl.program_id(0)
    turn = 2 - step
    rs, ro = width // n, ff // n
    cq, hw = ff // 4, width // 2

    pairs = ((wo_in, wo), (wi_in, wi), (wu_in, wu))

    def copy(kind):
        return pltpu.make_async_copy(*pairs[kind], sem.at[kind])

    CORE, NEAR = flip(C, 1), flip(C, 2)
    block, wq = cot.shape[0], width // 4

    def remote(t, j, to, source, target):
        return pltpu.make_async_remote_copy(
            src_ref=source,
            dst_ref=target,
            send_sem=ssem.at[t, j],
            recv_sem=rsem.at[t, j],
            device_id=(to, f),
            device_id_type=MESH,
        )

    KINDS = ("dout0", "dout1", "dinn0", "dinn1", "dattn0", "dattn1", "dcs")

    def rows_of(t):
        return pl.ds(pl.multiple_of(t * block, block), block)

    def held(t):
        return [ref.at[(2 - t) % 2] for ref in twice]

    dout, dinn, dattn, dcs, lo = held(turn)
    HOME = {"dout": 0, "dinn": 1, "dattn": 2}

    def whole(t):
        pair = ((act_in, act_s), (nrm_in, nrm_s))[t]
        return remote(t, 7, CORE, *pair)

    def home(t, name):
        j = HOME[name]
        return pltpu.make_async_copy(held(t)[j], homes[j].at[rows_of(t)], hsem.at[t, j])

    def to_core(t, *names):
        out = []
        for name in names or KINDS:
            rows = rows_of(t)
            dout, dinn, dattn, dcs, _ = held(t)
            ex = int(name[-1]) if name[-1] in "01" else 0
            other, lanes = flip(C, 2 * ex + 1), pl.ds(ex * wq, wq)
            source, target = {
                "dcs": lambda: (dcs, dcs_s.at[rows]),
                "dou": lambda: (dout.at[:, at(other, wq)], dout_s.at[rows, lanes]),
                "dat": lambda: (dattn.at[:, at(other, wq)], dattn_s.at[rows, lanes]),
                "din": lambda: (dinn.at[:, at(other, cq)], dinn_s.at[ex, rows]),
            }[name[:3]]()
            out.append(remote(t, KINDS.index(name), CORE, source, target))
        return out

    def start(name):
        for c in to_core(turn, *(k for k in KINDS if k.startswith(name))):
            c.start()
        if name in HOME:
            home(turn, name).start()

    def end(t, name):
        for c in to_core(t, *(k for k in KINDS if k.startswith(name))):
            c.wait_send()
        if name in HOME:
            home(t, name).wait()

    def free(name):
        @pl.when(step == 2)
        def _():
            end(2, name)

    def slots_of(t, ex):
        count = block // part
        return [u for u in range(count) if (t * count + u) // sh == ex]

    def place(t, u):
        return held(t)[4].at[pl.ds(u * part, part)], o_lo.at[x * sh + (t * (block // part) + u) % sh]

    def to_near(t):
        return [remote(t, 8 + u, NEAR, *place(t, u)) for u in slots_of(t, 1)]

    def stay(t):
        return [pltpu.make_async_copy(*place(t, u), csem.at[t, u]) for u in slots_of(t, 0)]

    def send(t):
        for c in to_near(t) + stay(t):
            c.start()

    def sent(t):
        for c in to_near(t):
            c.wait_send()
        for c in stay(t):
            c.wait()

    def received(t):
        for c in to_core(t) + to_near(t):
            c.wait_recv()

    @pl.when(step == 0)
    def _():
        barrier = pltpu.get_barrier_semaphore()
        for to in (CORE, NEAR):
            pl.semaphore_signal(barrier, inc=1, device_id=(to, f), device_id_type=MESH)
        copy(2).start()
        pl.semaphore_wait(barrier, 2)
        acc[...] = jnp.zeros_like(acc)
        vec[...] = spread(lambda s: vecs[s, :8, :128].astype(F32), n, rs)

    def arrived(kind):
        @pl.when(step == 0)
        def _():
            copy(kind).wait()

    count = block // part
    inside = []
    for u in range(count):
        slot = turn * count + u
        ex, s = slot // sh, slot % sh
        first = (C + ex * (2 - 4 * x)) * part
        row = lax.broadcasted_iota(jnp.int32, (part, 1), 0) + first
        inside.append(jnp.where(row < lens[x * sh + s], 1.0, 0.0))
    valid = jnp.concatenate(inside, 0)
    own, other = at(core, hw), at(1 - core, hw)

    def add(row, value):
        acc[row : row + 1, :] += jnp.sum(value, 0, keepdims=True)

    hat1, r1 = hat1_ref[...], r1_ref[:, :1]
    normed = hat1 * vec[4:5, :] + vec[5:6, :]
    arrived(2)

    @pl.when(step == 0)
    def _():
        copy(1).start()
        copy(0).start()
        whole(1).start()
        whole(0).start()

    second = normed + (dot(act[...], wu[...]) + vec[3:4, :])
    hat2, r2 = normalise(second)
    @pl.when(step == 2)
    def _():
        sent(2)

    lo[...] = (hat2 * vec[6:7, :] + vec[7:8, :]).astype(BF)
    og = cot[...].astype(F32) * valid
    add(6, og * hat2)
    add(7, og)
    d2 = normalise_back(og * vec[6:7, :], hat2, r2)
    d2low = d2.astype(BF)
    free("dout")
    dout[...] = d2low
    start("dout")
    for t in range(3):

        @pl.when(turn == t)
        def _():
            send(t)

    add(3, d2low.astype(F32))
    free("dinn")
    arrived(1)
    for j in range(4):
        cols = slice(j * cq, (j + 1) * cq)
        di = (dot_nt(d2low, wu[cols, :]) * gp[:, cols]).astype(BF)
        dinn[:, cols] = di
        add(8 + j, di.astype(F32))
    start("dinn")
    dn = d2 + dot_nt(dinn[...], wi[...])
    add(4, dn * hat1)
    add(5, dn)
    d1 = normalise_back(dn * vec[4:5, :], hat1, r1)
    dfirst[...] = d1
    d1low = d1.astype(BF)
    arrived(0)
    free("dattn")
    free("dcs")
    dattn[...] = d1low
    start("dattn")
    add(2, d1low.astype(F32))
    dcs[...] = dot_nt(d1low, wo[other]).astype(BF)
    start("dcs")
    dco[...] = dot_nt(d1low, wo[own]).astype(BF)

    @pl.when(turn == 0)
    def _():
        for t in range(2):
            for name in ("dout", "dinn", "dattn", "dcs"):
                end(t, name)
            sent(t)
            whole(t).wait()
        for t in range(3):
            received(t)


def ffn_call(lens, sh, act, gp, hat, r, nrm, cot, vecs, wo, wi, wu):
    width, ff = wi.shape
    n, rows = vecs.shape[0], cot.shape[0]
    block, part = rows // 3, rows // (2 * sh)
    hw = width // 2

    def by(cols):
        return pl.BlockSpec((block, cols), lambda i: (2 - i, 0))

    def whole(*shape):
        return pl.BlockSpec(shape, lambda i: (0,) * len(shape))

    grid_spec = pl.GridSpec(
        grid=(3,),
        in_specs=[
            pl.BlockSpec(memory_space=pltpu.SMEM),
            by(ff),
            by(ff),
            by(width),
            by(128),
            by(width),
            whole(*vecs.shape),
        ]
        + [ANY] * 5,
        out_specs=[by(width), by(hw), whole(16, width)] + [ANY] * 10,
        scratch_shapes=[
            pltpu.VMEM((width, width), BF),
            pltpu.VMEM((width, ff), BF),
            pltpu.VMEM((ff, width), BF),
            pltpu.VMEM((8, width), F32),
            *(pltpu.VMEM((2, block, cols), BF) for cols in (width, ff, width, hw, width)),
            pltpu.SemaphoreType.DMA((3,)),
            pltpu.SemaphoreType.DMA((3, block // part)),
            pltpu.SemaphoreType.DMA((3, 3)),
            pltpu.SemaphoreType.DMA((3, 8 + block // part)),
            pltpu.SemaphoreType.DMA((3, 8 + block // part)),
        ],
    )

    def shape(cols, dtype=BF):
        return jax.ShapeDtypeStruct((rows, cols), dtype)

    return pl.pallas_call(
        functools.partial(ffn_kernel, n, sh, part),
        grid_spec=grid_spec,
        out_shape=[
            shape(width, F32),
            shape(hw),
            jax.ShapeDtypeStruct((16, width), F32),
            shape(width),
            shape(ff),
            shape(width),
            jax.ShapeDtypeStruct((2 * sh, part, width), BF),
            shape(ff),
            shape(hw),
            jax.ShapeDtypeStruct((2, rows, ff // 4), BF),
            shape(width),
            shape(hw),
            shape(hw),
        ],
        compiler_params=params(collective_id=2, has_side_effects=True),
        cost_estimate=cost(
            2 * rows * width * (2 * width + 4 * ff), 30 * rows * width + 2 * width * (2 * ff + width)
        ),
        name="ffn",
    )(lens, act, gp, hat, r, cot, vecs, act, nrm, wo, wi, wu)


def xor(a, b, count):
    out, bit = 0, 1
    while bit < count:
        out = out + bit * ((a // bit + b // bit) % 2)
        bit *= 2
    return out


def plus(*items):
    out = items[0].astype(F32)
    for i in items[1:]:
        out = out + i.astype(F32)
    return out.astype(BF)


class Plan:
    def __init__(self):
        self.jobs = []

    def add(self, time, job):
        self.jobs.append((time, len(self.jobs), job))
        self.jobs.sort(key=lambda j: j[:2])

    def due(self, time):
        out = [j[2] for j in self.jobs if j[0] <= time]
        self.jobs = [j for j in self.jobs if j[0] > time]
        return out

    def beside(self, step, times):
        for t, time in enumerate(times):
            jobs = self.due(time)
            if jobs:

                @pl.when(step == t)
                def _():
                    for job in jobs:
                        job()


def back_kernel(
    n,
    lens,
    act,
    dout,
    nrm,
    dinn,
    dattn,
    ctx,
    cr,
    xall,
    q_in,
    k_in,
    v_in,
    lse_in,
    dco,
    dfirst,
    w_in,
    acc,
    act_s,
    dout_s,
    dinn_s,
    nrm_s,
    dattn_s,
    dcs_s,
    cs,
    o_igl,
    o_igr,
    o_i,
    o_u,
    o_o,
    o_q,
    o_k,
    o_v,
    o_vec,
    ig_s,
    Q,
    K,
    V,
    CX,
    G,
    LSE,
    L,
    D,
    DO,
    DA,
    CO,
    W,
    PI,
    PU,
    PO,
    PQ,
    RYI,
    RZI,
    MI,
    RXI,
    RXU,
    RYU,
    RZU,
    MU,
    RYO,
    RZO,
    MO,
    RXO,
    PH,
    RYH,
    RZH,
    MH,
    RXH,
    RYQ,
    RZQ,
    MQ,
    RXQ,
    VS,
    VR,
    SB,
    IB,
    XS,
    lsem,
    ssem,
    rsem,
):
    C, f = lax.axis_index("ctx"), lax.axis_index("fsdp")
    x, core = C // 2, C % 2
    A = n // 2
    slots, sh, part, hw = Q.shape
    rows, width = nrm.shape
    ff = act.shape[1]
    rs, ro, cq, wq = width // n, ff // n, ff // 4, width // 4
    half_rows = rows // 2
    CORE, NEAR, Y = (1, 0), (2, 0), (0, 1)

    def device(dc, df):
        return (flip(C, dc), flip(f, df))

    partners = [(0, 2 * k) for k in range(1, A)] + [Y, NEAR, CORE]
    barrier = pltpu.get_barrier_semaphore()
    for p in partners:
        pl.semaphore_signal(barrier, inc=1, device_id=device(*p), device_id_type=MESH)

    locals_free = iter(range(lsem.shape[0]))
    remotes_free = iter(range(ssem.shape[0]))

    def local(make):
        sem = next(locals_free)
        return lambda: pltpu.make_async_copy(*make(), lsem.at[sem])

    def remote_at(dev, sem, make):
        source, target = make()
        return pltpu.make_async_remote_copy(
            src_ref=source,
            dst_ref=target,
            send_sem=ssem.at[sem],
            recv_sem=rsem.at[sem],
            device_id=device(*dev),
            device_id_type=MESH,
        )

    def remote(dev, make):
        sem = next(remotes_free)
        return lambda: remote_at(dev, sem, make)

    ends = []

    def go(build):
        build().start()
        ends.append(lambda: build().wait_send())

    def go_local(make):
        build = local(make)
        build().start()
        ends.append(lambda: build().wait())

    loads = {}

    def load(name, make):
        loads[name] = local(make)
        loads[name]().start()

    def need(*names):
        for name in names:
            loads.pop(name)().wait()

    def quarters(ref, size, ex):
        return ref.at[:, at(flip(C, 2 * ex), size)]

    def load_dinn(ex):
        load(("dinn", ex), lambda: (quarters(dinn, cq, ex), D.at[ex, 0]))
        load(("dinn_s", ex), lambda: (dinn_s.at[ex], D.at[ex, 1]))

    load("nrm", lambda: (nrm, L.at[0]))
    load("nrm_s", lambda: (nrm_s, L.at[1]))
    load_dinn(0)
    pl.semaphore_wait(barrier, len(partners))
    need("nrm", "nrm_s", ("dinn", 0), ("dinn_s", 0))
    load_dinn(1)
    for ex in range(2):
        lanes = pl.ds(ex * wq, wq)
        load(("dout", ex), lambda ex=ex, lanes=lanes: (quarters(dout, wq, ex), DO.at[0, :, lanes]))
        load(
            ("dattn", ex), lambda ex=ex, lanes=lanes: (quarters(dattn, wq, ex), DA.at[0, :, lanes])
        )
    load("dout_s", lambda: (dout_s, DO.at[1]))
    load("dattn_s", lambda: (dattn_s, DA.at[1]))
    load("co", lambda: (cr, CO.at[0]))
    load("co_s", lambda: (cs, CO.at[1]))
    load("c", lambda: (ctx, CX))
    load("q", lambda: (q_in, Q))
    load("k", lambda: (k_in, K))
    load("v", lambda: (v_in, V))
    load("g", lambda: (dco, G.at[pl.ds(0, 2)]))
    load("g_s", lambda: (dcs_s, G.at[pl.ds(2, 2)]))
    for s in range(2):
        load(("lse", s), lambda s=s: (lse_in.at[s], LSE.at[s]))
    load("vec", lambda: (acc, VS.at[0]))
    load("w", lambda: (w_in, W))

    chunks = ff // 1024
    per = 1024 // ro

    def act_cols(t):
        return at(xor(f // per, t, chunks), 1024)

    class Unit:
        def __init__(self, P, RY, RZ, M, merged=False):
            self.P, self.RY, self.RZ, self.M, self.merged = P, RY, RZ, M, merged
            self.left, self.then = 1 if merged else A, []
            self.all_y = remote(Y, lambda: (P.at[1], RY)) if merged else None
            self.y = [
                remote(Y, lambda a=a: (P.at[1, a], RY.at[a])) for a in range(0 if merged else A)
            ]
            self.z = [None] + [
                remote((0, 2 * a), lambda a=a: (P.at[0, a], RZ.at[a - 1])) for a in range(1, A)
            ]

        def start_y(self, a=None):
            if self.merged:
                queue.append((self, None))
            else:
                queue.extend((self, i) for i in (order if a is None else [a]))
            pump()

        def fold_y(self, a):
            (self.all_y if self.merged else self.y[a])().wait_recv()
            for i in order if self.merged else [a]:
                self.P[0, i] = plus(self.P[0, i], self.RY[i])
                if i:
                    go(self.z[i])
            self.left -= 1

        def fold_z(self):
            for a in range(1, A):
                self.z[a]().wait_recv()
            self.M[...] = plus(self.P[0, 0], *[self.RZ[a - 1] for a in range(1, A)])

    order = list(range(A - 1, -1, -1))
    queue, flying, later = [], [], []

    def pump():
        while queue and len(flying) < WINDOW:
            unit, a = queue.pop(0)
            go(unit.all_y if unit.merged else unit.y[a])
            flying.append((unit, a))

    def fold_next():
        if flying:
            unit, a = flying.pop(0)
            pump()
            unit.fold_y(a)
            if not unit.left:
                later.extend((3 * t + 2, job) for t, job in enumerate(unit.then))
        now = [job for t, job in later if t <= 0]
        later[:] = [(t - 1, job) for t, job in later if t > 0]
        for job in now:
            job()

    UI = [Unit(PI.at[ex], RYI.at[ex], RZI.at[ex], MI.at[ex]) for ex in range(2)]
    UU = Unit(PU.at[0], RYU, RZU, MU)
    UO = Unit(PO.at[0], RYO, RZO, MO, merged=True)
    UH = Unit(PH.at[0], RYH, RZH, MH, merged=True)
    UQ = [None] + [Unit(PQ.at[j], RYQ.at[j], RZQ.at[j], MQ.at[j]) for j in range(2)]
    plan = Plan()

    xi = [remote(NEAR, lambda ex=ex: (MI.at[ex], RXI.at[ex])) for ex in range(2)]

    def inner_z(ex):
        UI[ex].fold_z()
        go(xi[ex])

    def cols_of(ref, e, size):
        return ref.at[:, at(flip(C, e), size)]

    i_core = [
        remote(CORE, lambda ex=ex: (RXI.at[1 - ex], cols_of(o_i, 2 * ex, cq))) for ex in range(2)
    ]

    def inner_x():
        for ex in range(2):
            xi[1 - ex]().wait_recv()
            RXI[1 - ex] = plus(MI[ex], RXI[1 - ex])
            go(i_core[ex])
            go_local(lambda ex=ex: (RXI.at[1 - ex], cols_of(o_i, 2 * ex, cq)))

    x_base = [next(remotes_free) for _ in range(n)][0]

    def outer_copy(i):
        return remote_at(NEAR, x_base + i, lambda: (PU.at[1, i % 2, i // 2], RXU.at[i % 2, i // 2]))

    def outer_x(i):
        outer_copy(i).wait_recv()
        PU[0, i % 2, i // 2] = plus(PU[0, i % 2, i // 2], RXU[i % 2, i // 2])
        if i % 2:
            UU.start_y(i // 2)

    class Finish:
        def __init__(self, unit, M, place):
            self.unit, self.M, self.place = unit, M, place
            self.near = remote(NEAR, lambda: (M, place(0)))
            self.core = remote(CORE, lambda: (M, place(0)))
            self.core2 = remote(CORE, lambda: (place(2), place(2)))

        def first(self):
            self.unit.fold_z()
            go(self.near)
            go(self.core)
            go_local(lambda: (self.M, self.place(0)))

        def second(self):
            self.near().wait_recv()
            go(self.core2)

    FU = Finish(UU, MU, lambda e: cols_of(o_u, e, wq))
    FO = Finish(UO, MO, lambda e: cols_of(o_o, e, wq))

    def query_place(e):
        to = flip(C, e)
        return o_q.at[at(to // 2, rs // 2), at(to % 2, hw)]

    FH = Finish(UH, MH, query_place)

    xo = remote(NEAR, lambda: (PO.at[1], RXO))
    xh = remote(NEAR, lambda: (PH.at[1], RXH))

    def fold_near(build, P, R, unit):
        build().wait_recv()
        for ib in (1, 0):
            for ia in range(A):
                P[0, ib, ia] = plus(P[0, ib, ia], R[ib, ia])
            if ib:
                unit.start_y()

    outs = (o_k, o_v)
    xq = [remote(NEAR, lambda j=j: (MQ.at[j], RXQ.at[j])) for j in range(2)]
    q_core = [
        remote(CORE, lambda j=j: (RXQ.at[j], outs[j].at[:, at(core, hw)])) for j in range(2)
    ]

    def proj_z(j):
        UQ[j + 1].fold_z()
        go(xq[j])

    def proj_x(j):
        xq[j]().wait_recv()
        RXQ[j] = plus(MQ[j], RXQ[j])
        go(q_core[j])
        go_local(lambda: (RXQ.at[j], outs[j].at[:, at(core, hw)]))

    hops = [CORE, NEAR] + [(0, 1 << b) for b in range(n.bit_length() - 1)]
    hop_copies = [
        remote(dev, lambda t=t: (VS.at[t], VR.at[t])) for t, dev in enumerate(hops)
    ]

    def vector_hop(t):
        if t:
            hop_copies[t - 1]().wait_recv()
            VS[t] = VS[t - 1] + VR[t - 1]
        if t < len(hops):
            go(hop_copies[t])
        else:
            go_local(lambda: (VS.at[t], o_vec))

    pairs = hw // (2 * HD)

    def attention(s, times):
        need(("lse", s))

        def body(step, carry):
            cols = at(step, 2 * HD)

            def get(ref):
                return ref[:, s, :, cols].reshape(slots * part, 2 * HD)

            mask = key_mask(lens[x * sh + s], C, part)
            dq, dk, dv = attend_back_pair(
                get(Q), get(K), get(V), mask, LSE[s % 2, :, cols], get(CX), get(G)
            )
            for ref, value in ((Q, dq), (K, dk), (V, dv)):
                ref[:, s, :, cols] = value.reshape(slots, part, 2 * HD)
            plan.beside(step, times)
            return carry

        lax.fori_loop(0, pairs, body, 0)
        if s + 2 < sh:
            load(("lse", s + 2), lambda: (lse_in.at[s + 2], LSE.at[s % 2]))

    groups = width // 256
    gsz = 256 // rs

    def weight_grad(get, put, times, unit=None):
        def body(step, carry):
            a = groups - 1 - step
            cols = at(xor(f // gsz, a, groups), 256)
            r = (dot_tn(L[0, :, cols], get(0)) + dot_tn(L[1, :, cols], get(1))).astype(BF)
            for u in range(gsz):
                i = a * gsz + flip(f % gsz, u)
                put(i, r[u * rs : (u + 1) * rs])
            if unit is not None and groups == A:
                for t in range(groups):

                    @pl.when(step == t)
                    def _():
                        unit.start_y(groups - 1 - t)

            plan.beside(step, times)
            return carry

        lax.fori_loop(0, groups, body, 0)
        if unit is not None and groups != A:
            unit.start_y()

    def into(P):
        def put(i, value):
            P[i % 2, i // 2] = value

        return put

    def put_query(i, value):
        for h in range(2):
            PH[(h + x) % 2, i % 2, i // 2] = value[h * (rs // 2) : (h + 1) * (rs // 2)]

    def spaced(first, last, count):
        return [first + (last - first) * (t + 1) / count for t in range(count)]

    UI[0].then = [lambda: inner_z(0)]
    UI[1].then = [lambda: inner_z(1), inner_x]
    UU.then = [FU.first, FU.second]
    UO.then = [FO.first, FO.second]
    UH.then = [FH.first, FH.second]
    for j in range(2):
        UQ[j + 1].then = [lambda j=j: proj_z(j), lambda j=j: proj_x(j)]

    xs_order = list(range(1, n, 2)) + list(range(0, n, 2))
    for k, i in enumerate(xs_order):
        if k < n // 2:
            plan.add(11 + 14 * (per * (i // per) + per - 1 - i % per + 1) / n, lambda i=i: outer_copy(i).start())
        follow = xs_order[k + n // 2] if k < n // 2 else None

        def fold_x(i=i, follow=follow):
            if follow is not None:
                outer_copy(follow).start()
            outer_x(i)

        plan.add(20 + 48 * k / n, fold_x)
    for k in range(13 * A):
        plan.add(14 + 18 * k / A, fold_next)
    for t in range(len(hops) + 1):
        plan.add(74 + 4 * t, lambda t=t: vector_hop(t))

    weight_grad(lambda m: D[0, m], into(PI.at[0]), spaced(4, 8, groups), UI[0])

    def act_load(t):
        slot = t % 2
        return [
            pltpu.make_async_copy(act.at[:, act_cols(t)], D.at[slot, 0], lsem.at[act_sem + 2 * slot]),
            pltpu.make_async_copy(
                act_s.at[:, act_cols(t)], D.at[slot, 1], lsem.at[act_sem + 2 * slot + 1]
            ),
        ]

    act_sem = [next(locals_free) for _ in range(4)][0]

    def begin_act(t):
        for c in act_load(t):
            c.start()

    begin_act(0)
    need(("dinn", 1), ("dinn_s", 1))
    weight_grad(lambda m: D[1, m], into(PI.at[1]), spaced(8, 11, groups), UI[1])
    if chunks > 1:
        begin_act(1)
    load("x0", lambda: (xall.at[pl.ds(0, rows)], L.at[0]))
    load("x1", lambda: (xall.at[pl.ds(rows, rows)], L.at[1]))
    need(("dout", 0), ("dout", 1), "dout_s")

    outer_times = spaced(11, 25, n)

    def outer_body(u, carry):
        t, il = u // per, per - 1 - u % per
        slot = t % 2

        @pl.when(u % per == 0)
        def _():
            for c in act_load(t):
                c.wait()

        cols = at(xor(f % per, il, per), ro)
        r = dot_tn(D[slot, 0, :, cols], DO[0]) + dot_tn(D[slot, 1, :, cols], DO[1])
        r = r.astype(BF)
        i = t * per + il
        for ex in range(2):
            PU[ex, i % 2, i // 2] = r[:, ex * wq : (ex + 1) * wq]

        @pl.when((u % per == per - 1) & (t + 2 < chunks))
        def _():
            begin_act(t + 2)

        plan.beside(u, outer_times)
        return carry

    lax.fori_loop(0, n, outer_body, 0)

    need("co", "co_s", "c", ("dattn", 0), ("dattn", 1), "dattn_s")
    for half in range(2):
        for g in range(hw // 256):
            lanes = slice(g * 256, (g + 1) * 256)

            def left(m):
                if half:
                    return CO[m, :, lanes]
                return CX[2 * m : 2 * m + 2, :, :, lanes].reshape(rows, 256)

            r = (dot_tn(left(0), DA[0]) + dot_tn(left(1), DA[1])).astype(BF)
            group = (core + half * (1 - 2 * core)) * (hw // 256) + g
            for u in range(gsz):
                i = xor(group * gsz + u, f, n)
                for ex in range(2):
                    PO[ex, i % 2, i // 2] = r[u * rs : (u + 1) * rs, ex * wq : (ex + 1) * wq]
        for job in plan.due(27 + 3 * half):
            job()
    go(xo)
    plan.add(64, lambda: fold_near(xo, PO, RXO, UO))

    need("q", "k", "v", "g", "g_s")
    for s in range(sh):
        attention(s, spaced(30 + 8 * s, 38 + 8 * s, pairs))

    need("x0", "x1", "vec")
    for j, ref in enumerate((Q, K, V)):

        def right(m):
            return ref[2 * m : 2 * m + 2].reshape(rows, hw)

        if j != 1:
            total = jnp.sum(right(0).astype(F32), 0, keepdims=True)
            total = total + jnp.sum(right(1).astype(F32), 0, keepdims=True)
            VS[0, j // 2 : j // 2 + 1, at(core, hw)] = total
        times = spaced(54 + 6 * j, 60 + 6 * j, groups)
        if j:
            weight_grad(right, into(PQ.at[j - 1]), times, UQ[j])
        else:
            weight_grad(right, put_query, times)
            go(xh)
            plan.add(76, lambda: fold_near(xh, PH, RXH, UH))

    need("w")

    def project(slot):
        out = None
        for j, ref in enumerate((Q, K, V)):
            p = dot_nt(ref[slot].reshape(half_rows, hw), W[j])
            out = p if out is None else out + p
        return out

    ig_swap = [remote(CORE, lambda ex=ex: (SB, ig_s.at[ex])) for ex in range(2)]
    for ex in (1, 0):
        value = project(2 + ex)
        if ex == 0:
            ig_swap[1]().wait_send()
        SB[...] = value
        ig_swap[ex]().start()
        for job in plan.due(80 - 4 * ex):
            job()

    def rows_of(ex):
        return pl.ds(ex * half_rows, half_rows)

    ig_near = remote(NEAR, lambda: (XS, o_igr))
    for ex in (1, 0):
        ig_swap[ex]().wait_recv()
        load(("ig", ex), lambda ex=ex: (ig_s.at[ex], IB))
        value = project(ex)
        if ex:
            ig_swap[0]().wait_send()
        load(("df", ex), lambda ex=ex: (dfirst.at[rows_of(ex)], SB))
        need(("ig", ex), ("df", ex))
        value = value + IB[...] + SB[...]
        if ex:
            XS[...] = value.astype(BF)
            go(ig_near)
        else:
            IB[...] = value
            go_local(lambda: (IB, o_igl))
        for job in plan.due(88 - 4 * ex):
            job()

    for job in plan.due(1e9):
        job()
    while queue or flying or later:
        fold_next()

    ig_near().wait_recv()
    for build in i_core + q_core + [b for F in (FU, FO, FH) for b in (F.core, F.core2)]:
        build().wait_recv()
    for i in range(n):
        outer_copy(i).wait_send()
    for end in ends:
        end()


def back_call(lens, n, act, dout, nrm, dinn, dattn, ctx, cr, xall, q, k, v, lse, *rest):
    rows, width = nrm.shape
    ff = act.shape[1]
    slots, sh, part, hw = q.shape
    A = n // 2
    rs, ro, cq, wq = width // n, ff // n, ff // 4, width // 4
    hops = 2 + n.bit_length() - 1

    def bf(*shape):
        return jax.ShapeDtypeStruct(shape, BF)

    def f32(*shape):
        return jax.ShapeDtypeStruct(shape, F32)

    def vm(*shape):
        return pltpu.VMEM(shape, BF)

    def vf(*shape):
        return pltpu.VMEM(shape, F32)

    four = (slots, sh, part, hw)
    return pl.pallas_call(
        functools.partial(back_kernel, n),
        in_specs=[pl.BlockSpec(memory_space=pltpu.SMEM)] + [ANY] * 23,
        out_specs=[ANY] * 10,
        out_shape=[
            f32(rows // 2, width),
            bf(rows // 2, width),
            bf(rs, ff),
            bf(ro, width),
            bf(rs, width),
            bf(rs, width),
            bf(rs, width),
            bf(rs, width),
            f32(16, width),
            f32(2, rows // 2, width),
        ],
        scratch_shapes=[
            vm(*four),
            vm(*four),
            vm(*four),
            vm(*four),
            vm(*four),
            vf(2, *lse.shape[1:]),
            vm(2, rows, width),
            vm(2, 2, rows, 1024),
            vm(2, rows, 2 * wq),
            vm(2, rows, 2 * wq),
            vm(2, rows, hw),
            vm(3, width, hw),
            vm(2, 2, A, rs, cq),
            vm(2, 2, A, ro, wq),
            vm(2, 2, A, rs, wq),
            vm(2, 2, A, rs, hw),
            vm(2, A, rs, cq),
            vm(2, A - 1, rs, cq),
            vm(2, rs, cq),
            vm(2, rs, cq),
            vm(2, A, ro, wq),
            vm(A, ro, wq),
            vm(A - 1, ro, wq),
            vm(ro, wq),
            vm(A, rs, wq),
            vm(A - 1, rs, wq),
            vm(rs, wq),
            vm(2, A, rs, wq),
            vm(2, 2, A, rs // 2, hw),
            vm(A, rs // 2, hw),
            vm(A - 1, rs // 2, hw),
            vm(rs // 2, hw),
            vm(2, A, rs // 2, hw),
            vm(2, A, rs, hw),
            vm(2, A - 1, rs, hw),
            vm(2, rs, hw),
            vm(2, rs, hw),
            vf(hops + 1, 16, width),
            vf(hops, 16, width),
            vf(rows // 2, width),
            vf(rows // 2, width),
            vm(rows // 2, width),
            pltpu.SemaphoreType.DMA((48,)),
            pltpu.SemaphoreType.DMA((64 + 8 * n,)),
            pltpu.SemaphoreType.DMA((64 + 8 * n,)),
        ],
        compiler_params=pltpu.CompilerParams(
            vmem_limit_bytes=BACK_LIMIT, collective_id=1, has_side_effects=True
        ),
        name="back",
    )(
        lens,
        act,
        dout,
        nrm,
        dinn,
        dattn,
        ctx,
        cr,
        xall,
        q,
        k,
        v,
        lse,
        *rest,
    )


def finish_kernel(here, near, lo, *refs):
    o_ig, o_lo = refs[6:8]
    x = lax.axis_index("ctx") // 2
    o_ig[x] = here[...]
    o_ig[1 - x] = near[...].astype(F32)
    o_lo[...] = lo[...]
    for source, target in zip(refs[:6], refs[8:]):
        target[...] = source[...].astype(F32)


def finish_call(here, near, lo, *grads):
    rows, width = here.shape
    steps = 2

    def by(a):
        return pl.BlockSpec((a.shape[0] // steps, a.shape[1]), lambda i: (i, 0))

    return pl.pallas_call(
        finish_kernel,
        grid=(steps,),
        in_specs=[by(a) for a in (here, near, lo) + grads],
        out_specs=[pl.BlockSpec((2, rows // steps, width), lambda i: (0, i, 0)), by(lo)]
        + [by(g) for g in grads],
        out_shape=[jax.ShapeDtypeStruct((2, rows, width), F32), jax.ShapeDtypeStruct(lo.shape, BF)]
        + [jax.ShapeDtypeStruct(g.shape, F32) for g in grads],
        compiler_params=params(),
        name="finish",
    )(here, near, lo, *grads)


def per_device(
    inputs,
    lengths,
    cotangent,
    query_weight,
    key_weight,
    value_weight,
    out_weight,
    inner_weight,
    outer_weight,
    query_bias,
    value_bias,
    out_bias,
    inner_bias,
    outer_bias,
    first_gain,
    first_shift,
    second_gain,
    second_shift,
):
    C = lax.axis_index("ctx")
    f = lax.axis_index("fsdp")
    n = lax.axis_size("fsdp")
    x, core = C // 2, C % 2
    seqs, part, width = inputs.shape
    ff = inner_weight.shape[1]
    sh = seqs // 2
    rows = 2 * sh * part
    rs, ro = width // n, ff // n
    hw = width // 2

    def pick(bit, a, b):
        return jnp.where(bit == 0, a, b), jnp.where(bit == 0, b, a)

    vectors = (
        query_bias,
        value_bias,
        out_bias,
        outer_bias,
        first_gain,
        first_shift,
        second_gain,
        second_shift,
        inner_bias,
    )
    x4, cot, w_qkv, wi, wu, wo, vecs, q4, k4, v4, c4, c_r, c_s, lse, *norm = front_call(
        lengths,
        inputs,
        cotangent,
        query_weight,
        key_weight,
        value_weight,
        out_weight,
        inner_weight,
        outer_weight,
        vectors,
        n,
    )
    xall = x4.reshape(2 * rows, width)
    cr = c_r.reshape(rows, hw)
    norm = [a.reshape(rows, a.shape[2]) for a in norm]
    two = (2, sh, part, hw)
    (
        dfirst,
        dco,
        acc,
        dout,
        dinn,
        dattn,
        layer_out,
        act_s,
        dout_s,
        dinn_s,
        nrm_s,
        dattn_s,
        dcs_s,
    ) = ffn_call(lengths, sh, *norm, cot.reshape(rows, width), vecs, wo, wi, wu)
    act, nrm = norm[0], norm[4]

    ig_here, ig_near, g_i, g_u, g_o, g_q, g_k, g_v, sums, _ = back_call(
        lengths,
        n,
        act,
        dout,
        nrm,
        dinn,
        dattn,
        c4,
        cr,
        xall,
        q4,
        k4,
        v4,
        lse,
        dco.reshape(two),
        dfirst,
        w_qkv,
        acc,
        act_s,
        dout_s,
        dinn_s,
        nrm_s,
        dattn_s,
        dcs_s.reshape(two),
        c_s.reshape(rows, hw),
    )
    own = lax.dynamic_slice_in_dim(sums[:8], f * rs, rs, 1)
    own_inner = lax.dynamic_slice_in_dim(sums[8 : 8 + ff // width].reshape(ff), f * ro, ro, 0)
    input_grad, layer_out, *grads = finish_call(
        ig_here, ig_near, layer_out.reshape(seqs * part, width), g_q, g_k, g_v, g_o, g_i, g_u
    )
    grad_query, grad_key, grad_value, grad_out, grad_inner, grad_outer = grads
    input_grad, layer_out = input_grad.reshape(inputs.shape), layer_out.reshape(inputs.shape)

    return (
        layer_out,
        input_grad,
        grad_query,
        grad_key,
        grad_value,
        grad_out,
        grad_inner,
        grad_outer,
        own[0],
        own[1],
        own[2],
        own_inner,
        own[3],
        own[4],
        own[5],
        own[6],
        own[7],
    )


def solution(mesh):
    rowed = P("fsdp", "ctx", None)
    matrix, vector = P("fsdp", None), P("fsdp")
    in_specs = (rowed, vector, rowed) + (matrix,) * 6 + (vector,) * 9
    out_specs = (rowed, rowed) + (matrix,) * 6 + (vector,) * 9
    return jax.shard_map(
        per_device, mesh=mesh, in_specs=in_specs, out_specs=out_specs, check_vma=False
    )
```
